32 devices in a mesh: ctx: 8 (over z, x), head: 4 (over y, core).
Axes of the slice: x: 2, y: 2, z: 4, core: 2. Of those that a mesh axis runs over, the one named last changes fastest.
Arguments:
- q_pre: bfloat16 [2048, 2560], P('ctx', 'head'), may hold values from -48 to 48
- k_pre: bfloat16 [2048, 2560], P('ctx', 'head'), may hold values from -48 to 48
- values: bfloat16 [2048, 2560], P('ctx', 'head'), may hold values from -6 to 6
- out_grad: bfloat16 [2048, 2560], P('ctx', 'head'), may hold values from -192 to 192
- q_gain: float32 [2560], P('head'), may hold values from 0.25 to 1.75
- k_gain: float32 [2560], P('head'), may hold values from 0.25 to 1.75
- selected: int32 [16, 20, 7], P('ctx', 'head'), may hold values from 0 to 15, as said below
Outputs:
- dq_pre: bfloat16 [2048, 2560], P('ctx', 'head')
- dk_pre: bfloat16 [2048, 2560], P('ctx', 'head')
- dv: bfloat16 [2048, 2560], P('ctx', 'head')
The draws below stay inside these ranges and needn't reach their ends.
Inputs may be any that keep to these rules, and one draw needn't show every extreme that they name: `selected`: entry [i, h, c] names a tile outside the block of query tile i; the 7 entries of one row lie in 7 different blocks. All query tiles of one block have equal rows for each head. Over the heads of one group of 5 consecutive heads starting at a multiple of 5, the rows of one block name no other block more than 5 times in all, and some block exactly 5 times.
All inputs are finite; a program needn't handle non-finite values.
Results may differ from the reference program's by a relative error of at most 0.011.
Values may be sent and summed in bfloat16 or wider, within the bound.
No kernel may reach another device: no remote copies, remote signals or barrier semaphores. Data moves between devices by JAX's collectives and lax.ppermute only.
A program may use at most 128 MiB of HBM per device.

```python
import math
import jax
import jax.numpy as jnp
from jax import lax

HEADS = 20
HD = 128
TILE = 128
REM = 7
QT_DEV = 2
TOKENS = 2048
QTILES = 16
HEADS_DEV = 5
WIDTH = 2560


def shared_pair(key):
    streams = jax.random.split(jax.random.fold_in(key, 31), 4)
    columns = jnp.arange(WIDTH, dtype=jnp.int32)
    rise = jnp.sqrt(1.0 + 2.0 * columns.astype(jnp.float32) / (WIDTH - 1))
    q_cols = jnp.exp(jnp.log(10.0) * jax.random.uniform(streams[0], (WIDTH,))) * rise / 6.0
    k_cols = jnp.exp(jnp.log(10.0) * jax.random.uniform(streams[1], (WIDTH,))) * rise / 6.0
    queries = jnp.clip(jax.random.normal(streams[2], (TOKENS, WIDTH)), -6.0, 6.0) * q_cols
    keyrows = jnp.clip(jax.random.normal(streams[3], (TOKENS, WIDTH)), -6.0, 6.0) * k_cols
    return (jnp.clip(queries, -48.0, 48.0), jnp.clip(keyrows, -48.0, 48.0))


def draw_q_pre(key, part):
    return shared_pair(key)[0].astype(jnp.bfloat16)


def draw_k_pre(key, part):
    return shared_pair(key)[1].astype(jnp.bfloat16)


def draw_selected(key, part):
    n_dev = QTILES // QT_DEV
    groups = HEADS // HEADS_DEV
    per_group = HEADS_DEV * REM
    streams = jax.random.split(jax.random.fold_in(key, 11), 2)
    others = jnp.arange(n_dev - 1, dtype=jnp.int32)
    scores = jax.random.randint(streams[0], (n_dev, groups, n_dev - 1), 0, 1 << 20) * n_dev + others
    sigma = jnp.argsort(scores, axis=-1, stable=True).astype(jnp.int32)
    slots = jnp.arange(per_group, dtype=jnp.int32)
    picked = sigma[:, :, slots % (n_dev - 1)]
    owners = (jnp.arange(n_dev, dtype=jnp.int32)[:, None, None] + 1 + picked) % n_dev
    inside = jax.random.randint(streams[1], (n_dev, groups, per_group), 0, QT_DEV)
    tiles = (owners * QT_DEV + inside).reshape(n_dev, 1, groups, HEADS_DEV, REM)
    tiles = jnp.broadcast_to(tiles, (n_dev, QT_DEV, groups, HEADS_DEV, REM))
    return tiles.reshape(QTILES, HEADS, REM).astype(jnp.int32)


def steps_of(own_key, dims, shards, smallest, high):
    loudness = 1.0
    for axis_at, blocks in shards:
        heights = jax.random.uniform(jax.random.fold_in(jax.random.fold_in(own_key, 6), axis_at), (blocks,), jnp.float32, smallest / len(shards), high / len(shards))
        loudness = loudness * jnp.repeat(jnp.exp(heights), dims[axis_at] // blocks).reshape((-1,) + (1,) * (len(dims) - 1 - axis_at))
    return loudness


def bell_draw(key, shape, deviation, reach, shards=(), kind=jnp.bfloat16):
    drawn = deviation * jax.random.normal(key, shape, jnp.float32)
    if shards:
        drawn = drawn * steps_of(key, shape, shards, -0.22, 0.18)
    return jnp.clip(drawn, -reach, reach).astype(kind)


def setup_inputs(seed: int = 0) -> dict:
    seeds = jax.random.split(jax.random.key(seed), 8)
    q_pre = draw_q_pre(jax.random.fold_in(seeds[7], 71), 0)
    k_pre = draw_k_pre(jax.random.fold_in(seeds[7], 71), 0)
    values = bell_draw(seeds[2], (TOKENS, WIDTH), 1.0, 6.0, ((0, 8), (1, 4)))
    out_grad = bell_draw(seeds[3], (TOKENS, WIDTH), 32.0, 192.0, ((0, 8), (1, 4)))
    q_gain = jnp.clip(1.0 + 0.15 * jax.random.normal(seeds[4], (WIDTH,), jnp.float32), 0.25, 1.75)
    k_gain = jnp.clip(1.0 + 0.15 * jax.random.normal(seeds[5], (WIDTH,), jnp.float32), 0.25, 1.75)
    selected = draw_selected(jax.random.fold_in(seeds[7], 71), 0)
    return {"q_pre": q_pre, "k_pre": k_pre, "values": values, "out_grad": out_grad, "q_gain": q_gain, "k_gain": k_gain, "selected": selected}


epsilon = 1e-06

def rms_normed(pre, gain):
    wide = pre.astype(jnp.float32)
    scale = lax.rsqrt(lax.optimization_barrier(jnp.mean(wide * wide, axis=1, keepdims=True)) + epsilon)
    return (wide, scale, (wide * scale * gain).astype(jnp.bfloat16))

def per_head(array):
    return array.reshape(QTILES, TILE, HEADS, HD).transpose(2, 0, 1, 3)

def rounded_back(array):
    return lax.optimization_barrier(array.astype(jnp.bfloat16)).astype(jnp.float32)

def norm_back(wide, scale, gain, grad):
    dot_mean = lax.optimization_barrier(jnp.mean(gain * grad * wide, axis=1, keepdims=True))
    return (scale * gain * grad - wide * scale ** 3 * dot_mean).astype(jnp.bfloat16)

def reference(q_pre, k_pre, values, out_grad, q_gain, k_gain, selected):
    q_wide, q_scale, q_normed = rms_normed(q_pre, q_gain)
    k_wide, k_scale, k_normed = rms_normed(k_pre, k_gain)
    q_heads = per_head(q_normed)
    k_heads = per_head(k_normed)
    v_heads = per_head(values)
    g_heads = per_head(out_grad)
    head_index = jnp.arange(HEADS, dtype=jnp.int32)[:, None]
    factor = 1.0 / math.sqrt(HD)

    def visit(carry, tile_index):
        dk_all, dv_all = carry
        start = tile_index // QT_DEV * QT_DEV
        near_k = lax.dynamic_slice_in_dim(k_heads, start, QT_DEV, 1).reshape(HEADS, QT_DEV * TILE, HD)
        near_v = lax.dynamic_slice_in_dim(v_heads, start, QT_DEV, 1).reshape(HEADS, QT_DEV * TILE, HD)
        picks = lax.dynamic_index_in_dim(selected, tile_index, 0, keepdims=False).astype(jnp.int32)
        far_k = k_heads[head_index, picks].reshape(HEADS, REM * TILE, HD)
        far_v = v_heads[head_index, picks].reshape(HEADS, REM * TILE, HD)
        keys_all = jnp.concatenate((near_k, far_k), axis=1).astype(jnp.float32)
        vals_all = jnp.concatenate((near_v, far_v), axis=1).astype(jnp.float32)
        query = lax.dynamic_index_in_dim(q_heads, tile_index, 1, keepdims=False).astype(jnp.float32)
        grad = lax.dynamic_index_in_dim(g_heads, tile_index, 1, keepdims=False).astype(jnp.float32)
        scores = jnp.einsum('hqd,hkd->hqk', query, keys_all) * factor
        row_top = lax.optimization_barrier(jnp.max(scores, axis=-1))
        lse = row_top + jnp.log(lax.optimization_barrier(jnp.sum(jnp.exp(scores - row_top[..., None]), axis=-1)))
        probs = jnp.exp(scores - lse[..., None])
        dprob = jnp.einsum('hqd,hkd->hqk', grad, vals_all)
        delta = lax.optimization_barrier(jnp.sum(probs * dprob, axis=-1))
        dscore = rounded_back(probs * (dprob - delta[..., None]) * factor)
        probs_b = rounded_back(probs)
        dq_tile = jnp.einsum('hqk,hkd->hqd', dscore, keys_all)
        dk_part = jnp.einsum('hqk,hqd->hkd', dscore, query)
        dv_part = jnp.einsum('hqk,hqd->hkd', probs_b, grad)
        cut = QT_DEV * TILE
        near_dk = dk_part[:, :cut].reshape(HEADS, QT_DEV, TILE, HD)
        near_dv = dv_part[:, :cut].reshape(HEADS, QT_DEV, TILE, HD)
        dk_all = lax.dynamic_update_slice_in_dim(dk_all, lax.dynamic_slice_in_dim(dk_all, start, QT_DEV, 1) + near_dk, start, 1)
        dv_all = lax.dynamic_update_slice_in_dim(dv_all, lax.dynamic_slice_in_dim(dv_all, start, QT_DEV, 1) + near_dv, start, 1)
        dk_all = dk_all.at[head_index, picks].add(dk_part[:, cut:].reshape(HEADS, REM, TILE, HD))
        dv_all = dv_all.at[head_index, picks].add(dv_part[:, cut:].reshape(HEADS, REM, TILE, HD))
        return ((dk_all, dv_all), dq_tile)
    zeros = jnp.zeros((HEADS, QTILES, TILE, HD), jnp.float32)
    (dk_all, dv_all), dq_tiles = lax.scan(visit, (zeros, zeros), jnp.arange(QTILES, dtype=jnp.int32))
    dq_wide = dq_tiles.transpose(0, 2, 1, 3).reshape(TOKENS, WIDTH)
    dk_wide = dk_all.transpose(1, 2, 0, 3).reshape(TOKENS, WIDTH)
    dv_out = dv_all.transpose(1, 2, 0, 3).reshape(TOKENS, WIDTH).astype(jnp.bfloat16)
    dq_out = norm_back(q_wide, q_scale, q_gain, dq_wide)
    dk_out = norm_back(k_wide, k_scale, k_gain, dk_wide)
    return (dq_out, dk_out, dv_out)
```

```python
import functools
import math

import jax
import jax.numpy as jnp
import numpy as np
from jax import lax
from jax.experimental import pallas as pl
from jax.experimental.pallas import tpu as pltpu
from jax.sharding import PartitionSpec as P

HD = 128
TILE = 128


epsilon = 1e-06


def split_heads(array, heads_dev):
    return array.reshape(array.shape[0], heads_dev, HD).transpose(1, 0, 2)


def merge_heads(array):
    heads_dev, tok_dev, depth = array.shape
    return array.transpose(1, 0, 2).reshape(tok_dev, heads_dev * depth)


def per_tile(array, qt_dev):
    heads_dev, tok_dev, depth = array.shape
    return array.reshape(heads_dev, qt_dev, TILE, depth).transpose(1, 0, 2, 3)


def from_tiles(array):
    qt_dev, heads_dev, rows_tile, depth = array.shape
    return array.transpose(1, 0, 2, 3).reshape(heads_dev, qt_dev * rows_tile, depth)


def table_sum(taken, pieces, heads_dev, qt_dev):
    flat_pieces = pieces.reshape(pieces.shape[0], -1)
    summed = jnp.dot(
        taken, flat_pieces, precision=lax.Precision.HIGHEST, preferred_element_type=jnp.float32
    )
    summed = summed.reshape(heads_dev, qt_dev, 2, TILE, HD).transpose(2, 0, 1, 3, 4)
    return summed.reshape(2, heads_dev, qt_dev * TILE, HD)


def rounded(array):
    return array.astype(jnp.bfloat16)


def finish_norm(wide, scale, gain, grad, dot_sum, width_all):
    return (scale * gain * grad - wide * scale**3 * (dot_sum / width_all)[:, None]).astype(
        jnp.bfloat16
    )


def tiles_to_queries(q_pre, k_pre, values, out_grad, q_gain, k_gain, selected):
    n_ctx = lax.axis_size("ctx")
    tok_dev, width_dev = q_pre.shape
    width_all = width_dev * lax.axis_size("head")
    heads_dev = width_dev // HD
    qt_dev = tok_dev // TILE
    remote_count = selected.shape[2]
    factor = 1.0 / math.sqrt(HD)
    q_wide = q_pre.astype(jnp.float32)
    k_wide = k_pre.astype(jnp.float32)
    q_square, k_square = lax.psum(
        (jnp.sum(q_wide * q_wide, axis=1), jnp.sum(k_wide * k_wide, axis=1)), "head"
    )
    q_scale = lax.rsqrt(q_square / width_all + epsilon)[:, None]
    k_scale = lax.rsqrt(k_square / width_all + epsilon)[:, None]
    q_heads = split_heads(rounded(q_wide * q_scale * q_gain), heads_dev)
    k_heads = split_heads(rounded(k_wide * k_scale * k_gain), heads_dev)
    v_heads = split_heads(values, heads_dev)
    g_heads = split_heads(out_grad, heads_dev)
    q_tiles = per_tile(q_heads, qt_dev)
    g_tiles = per_tile(g_heads, qt_dev)
    k_table = k_heads.reshape(heads_dev * qt_dev, TILE, HD)
    v_table = v_heads.reshape(heads_dev * qt_dev, TILE, HD)
    flat_sel = selected[0].reshape(-1)
    n_slot = flat_sel.shape[0]
    capacity = -(-n_slot // (n_ctx - 1))
    n_buffer = n_ctx * capacity
    owners = flat_sel // qt_dev
    head_of = jnp.arange(n_slot, dtype=jnp.int32) // remote_count
    codes = head_of * qt_dev + flat_sel % qt_dev
    matches = (owners[:, None] == jnp.arange(n_ctx, dtype=jnp.int32)[None, :]).astype(jnp.int32)
    ranks = jnp.sum((jnp.cumsum(matches, axis=0) - matches) * matches, axis=1)
    position = owners * capacity + ranks
    placed = position[None, :] == jnp.arange(n_buffer, dtype=jnp.int32)[:, None]
    request = jnp.sum(jnp.where(placed, codes[None, :] + 1, 0), axis=1) - 1
    asked = lax.all_to_all(
        request.reshape(n_ctx, capacity), "ctx", split_axis=0, concat_axis=0, tiled=True
    ).reshape(n_buffer)
    clipped = jnp.maximum(asked, 0)
    taken = (asked[None, :] == jnp.arange(heads_dev * qt_dev, dtype=jnp.int32)[:, None]).astype(
        jnp.float32
    )
    s_near = (
        jnp.einsum("rhqd,hkd->rhqk", q_tiles, k_heads, preferred_element_type=jnp.float32) * factor
    )
    dp_near = jnp.einsum("rhqd,hkd->rhqk", g_tiles, v_heads, preferred_element_type=jnp.float32)
    near_top = jnp.max(s_near, axis=-1)
    outgoing = jnp.stack((k_table[clipped], v_table[clipped]), axis=1).reshape(
        n_ctx, capacity, 2, TILE, HD
    )
    incoming = lax.all_to_all(outgoing, "ctx", split_axis=0, concat_axis=0, tiled=True).reshape(
        n_buffer, 2, TILE, HD
    )
    slot_kv = incoming[position].reshape(heads_dev, remote_count, 2, TILE, HD)
    far_k = slot_kv[:, :, 0]
    far_v = slot_kv[:, :, 1]
    s_far = (
        jnp.einsum("rhqd,hckd->rhqck", q_tiles, far_k, preferred_element_type=jnp.float32) * factor
    )
    dp_far = jnp.einsum("rhqd,hckd->rhqck", g_tiles, far_v, preferred_element_type=jnp.float32)
    row_top = jnp.maximum(near_top, jnp.max(s_far, axis=(-2, -1)))
    totals = jnp.sum(jnp.exp(s_near - row_top[..., None]), axis=-1) + jnp.sum(
        jnp.exp(s_far - row_top[..., None, None]), axis=(-2, -1)
    )
    lse = row_top + jnp.log(totals)
    p_near = jnp.exp(s_near - lse[..., None])
    p_far = jnp.exp(s_far - lse[..., None, None])
    delta = jnp.sum(p_near * dp_near, axis=-1) + jnp.sum(p_far * dp_far, axis=(-2, -1))
    ds_near = rounded(p_near * (dp_near - delta[..., None]) * factor)
    pb_near = rounded(p_near)
    dq_near = jnp.einsum("rhqk,hkd->rhqd", ds_near, k_heads, preferred_element_type=jnp.float32)
    dk_near = jnp.einsum("rhqk,rhqd->hkd", ds_near, q_tiles, preferred_element_type=jnp.float32)
    dv_near = jnp.einsum("rhqk,rhqd->hkd", pb_near, g_tiles, preferred_element_type=jnp.float32)
    dq_near, dk_near, dv_near = (dq_near, dk_near, dv_near)
    ds_far = rounded(p_far * (dp_far - delta[..., None, None]) * factor)
    pb_far = rounded(p_far)
    dq_far = jnp.einsum("rhqck,hckd->rhqd", ds_far, far_k, preferred_element_type=jnp.float32)
    dq_wide = merge_heads(from_tiles(dq_near + dq_far))
    q_dot = jnp.sum(q_gain * dq_wide * q_wide, axis=1)
    dq_wide, q_dot = (dq_wide, q_dot)
    dk_far = jnp.einsum("rhqck,rhqd->hckd", ds_far, q_tiles, preferred_element_type=jnp.float32)
    dv_far = jnp.einsum("rhqck,rhqd->hckd", pb_far, g_tiles, preferred_element_type=jnp.float32)
    grads = jnp.stack((dk_far, dv_far), axis=2).reshape(n_slot, 2, TILE, HD)
    sending = jnp.zeros((n_buffer, 2, TILE, HD), jnp.float32).at[position].set(grads)
    returned = lax.all_to_all(
        sending.reshape(n_ctx, capacity, 2, TILE, HD),
        "ctx",
        split_axis=0,
        concat_axis=0,
        tiled=True,
    ).reshape(n_buffer, 2, TILE, HD)
    far_sums = table_sum(taken, returned, heads_dev, qt_dev)
    dk_wide = merge_heads(dk_near + far_sums[0])
    dv_heads = dv_near + far_sums[1]
    k_dot = jnp.sum(k_gain * dk_wide * k_wide, axis=1)
    q_dot, k_dot = lax.psum((q_dot, k_dot), "head")
    dq_result = finish_norm(q_wide, q_scale, q_gain, dq_wide, q_dot, width_all)
    dk_result = finish_norm(k_wide, k_scale, k_gain, dk_wide, k_dot, width_all)
    return (dq_result, dk_result, merge_heads(dv_heads).astype(jnp.bfloat16))


VMEM_BYTES = 48 * 2**20
NT = (((1,), (1,)), ((), ()))
IN_VMEM = pl.BlockSpec(memory_space=pltpu.VMEM)
IN_SMEM = pl.BlockSpec(memory_space=pltpu.SMEM)


def owners_of(group, n_ctx, heads_dev):
    places = [(4 * head + 1) * n_ctx // (4 * heads_dev) for head in range(heads_dev)]
    return [n_ctx - 1 - place if group % 2 else place for place in places]


def routing_table(n_ctx, n_head, heads_dev):
    rows = []
    for block in range(n_ctx):
        for group in range(n_head):
            owners = owners_of(group, n_ctx, heads_dev)
            owned = [owners.index(c) if c in owners else -1 for c in range(n_ctx)]
            row = [owned[(block + shift) % n_ctx] for shift in range(n_ctx)]
            rows.append(row + [owned[block], block])
    return np.array(rows, np.int32)


def pairs_to_owner(shift, n_ctx, n_head, heads_dev):
    pairs = []
    for group in range(n_head):
        owners = owners_of(group, n_ctx, heads_dev)
        for block in range(n_ctx):
            target = (block + shift) % n_ctx
            if target in owners:
                pairs.append((block * n_head + group, target * n_head + group))
    return pairs


def to_owners(arrays, n_ctx, n_head, heads_dev):
    return [arrays[0]] + [
        lax.ppermute(
            arrays[shift], ("ctx", "head"), pairs_to_owner(shift, n_ctx, n_head, heads_dev)
        )
        for shift in range(1, n_ctx)
    ]


def from_owners(arrays, n_ctx, n_head, heads_dev):
    return [arrays[0]] + [
        lax.ppermute(
            arrays[shift],
            ("ctx", "head"),
            [(b, a) for a, b in pairs_to_owner(shift, n_ctx, n_head, heads_dev)],
        )
        for shift in range(1, n_ctx)
    ]


def column(row, width):
    return jnp.broadcast_to(row, (width, row.shape[1])).T


def row_sums(wide):
    total = wide[:, :HD]
    for at in range(HD, wide.shape[1], HD):
        total = total + wide[:, at : at + HD]
    return jnp.sum(total.T, axis=0, keepdims=True)


def pack_kernel(n_ctx, route, normed_ref, plain_ref, square_ref, *outs):
    wide = normed_ref[...].astype(jnp.float32)
    square_ref[...] = row_sums(wide * wide)
    for shift in range(n_ctx):
        head = jnp.maximum(route[0, shift], 0)
        place = pl.ds(pl.multiple_of(head * HD, HD), HD)
        outs[shift][0] = normed_ref[:, place]
        outs[shift][1] = plain_ref[:, place]


def pack(route, normed, plain, n_ctx):
    rows = normed.shape[0]
    result = pl.pallas_call(
        functools.partial(pack_kernel, n_ctx),
        out_shape=[jax.ShapeDtypeStruct((1, rows), jnp.float32)]
        + [jax.ShapeDtypeStruct((2, rows, HD), jnp.bfloat16)] * n_ctx,
        in_specs=[IN_SMEM, IN_VMEM, IN_VMEM],
        out_specs=[IN_VMEM] * (n_ctx + 1),
        compiler_params=pltpu.CompilerParams(vmem_limit_bytes=VMEM_BYTES),
    )(route, normed, plain)
    return result[0], result[1:]


def block_of(route, n_ctx, shift):
    back = route[0, n_ctx + 1] - shift
    return jnp.where(back < 0, back + n_ctx, back)


def keys_kernel(n_ctx, route, scale_ref, gain_ref, *refs):
    messages = refs[:n_ctx]
    k_ref, kt_ref, v_ref = refs[n_ctx:]
    rows = messages[0].shape[1]

    @pl.when(route[0, n_ctx] >= 0)
    def _():
        gain = gain_ref[pl.ds(route[0, n_ctx], 1), :]
        for shift in range(n_ctx):
            block = block_of(route, n_ctx, shift)
            place = pl.ds(pl.multiple_of(block * rows, rows), rows)
            scale = column(scale_ref[block, 1:2, :], HD)
            normed = messages[shift][0].astype(jnp.float32) * scale * gain
            k_ref[place, :] = normed.astype(jnp.bfloat16)
            kt_ref[:, place] = normed.T.astype(jnp.bfloat16)
            v_ref[place, :] = messages[shift][1]


def prepare_keys(route, scales, gain, messages, n_ctx):
    tokens = n_ctx * messages[0].shape[1]
    return pl.pallas_call(
        functools.partial(keys_kernel, n_ctx),
        out_shape=[
            jax.ShapeDtypeStruct((tokens, HD), jnp.bfloat16),
            jax.ShapeDtypeStruct((HD, tokens), jnp.bfloat16),
            jax.ShapeDtypeStruct((tokens, HD), jnp.bfloat16),
        ],
        in_specs=[IN_SMEM] + [IN_VMEM] * (2 + n_ctx),
        out_specs=[IN_VMEM] * 3,
        compiler_params=pltpu.CompilerParams(vmem_limit_bytes=VMEM_BYTES),
    )(route, scales, gain, *messages)


def attend_kernel(n_ctx, shifts, last, has_sums, route, picks, scale_ref, gain_ref, *refs):
    count = len(shifts)
    refs = list(refs)
    k_ref, kt_ref, v_ref = refs[:3]
    messages = refs[3 : 3 + count]
    at = 3 + count + (2 if has_sums else 0)
    sums_in = refs[3 + count : at]
    dq_refs = refs[at : at + count]
    at += count
    if last:
        dk_outs = refs[at : at + n_ctx]
        dv_outs = refs[at + n_ctx : at + 2 * n_ctx]
        at += 2 * n_ctx
    else:
        dk_out, dv_out = refs[at : at + 2]
        at += 2
    q_ref, g_ref, dq_ref, dk_ref, dv_ref, s_ref, dp_ref, p_ref, ds_ref, kt_picked = refs[at:]
    rows = messages[0].shape[1]
    remote_count = picks.shape[1]
    near = rows // TILE
    n_keys = near + remote_count
    factor = 1.0 / math.sqrt(HD)
    to_base2 = factor * math.log2(math.e)

    @pl.when(route[0, n_ctx] >= 0)
    def _():
        gain = gain_ref[pl.ds(route[0, n_ctx], 1), :]
        for index, shift in enumerate(shifts):
            scale = column(scale_ref[block_of(route, n_ctx, shift), 0:1, :], HD)
            normed = messages[index][0].astype(jnp.float32) * scale * gain
            q_ref[index] = normed.astype(jnp.bfloat16)
            g_ref[index] = messages[index][1]
        if has_sums:
            dk_ref[...] = sums_in[0][...]
            dv_ref[...] = sums_in[1][...]
        else:
            dk_ref[...] = jnp.zeros_like(dk_ref)
            dv_ref[...] = jnp.zeros_like(dv_ref)

        def visit(index, carry):
            back = route[0, n_ctx + 1] - (shifts[0] + index)
            block = jnp.where(back < 0, back + n_ctx, back)
            query = q_ref[index]
            grad = g_ref[index]
            places = [
                pl.ds(pl.multiple_of(block * rows + tile * TILE, TILE), TILE)
                for tile in range(near)
            ] + [
                pl.ds(pl.multiple_of(picks[block, slot] * TILE, TILE), TILE)
                for slot in range(remote_count)
            ]
            top = None
            for slot, place in enumerate(places):
                score = lax.dot_general(
                    k_ref[place, :], query, NT, preferred_element_type=jnp.float32
                )
                s_ref[slot] = score
                highest = jnp.max(score, axis=0, keepdims=True)
                top = highest if top is None else jnp.maximum(top, highest)
                kt_picked[:, slot * TILE : (slot + 1) * TILE] = kt_ref[:, place]
            top = top * to_base2
            total = jnp.zeros((1, rows), jnp.float32)
            mixed = jnp.zeros((1, rows), jnp.float32)
            for slot, place in enumerate(places):
                dprob = lax.dot_general(
                    v_ref[place, :], grad, NT, preferred_element_type=jnp.float32
                )
                weight = jnp.exp2(s_ref[slot] * to_base2 - top)
                s_ref[slot] = weight
                dp_ref[slot] = dprob
                total += jnp.sum(weight, axis=0, keepdims=True)
                mixed += jnp.sum(weight * dprob, axis=0, keepdims=True)
            inverse = 1.0 / total
            delta = mixed * inverse
            for slot, place in enumerate(places):
                prob = s_ref[slot] * inverse
                dscore = (prob * (dp_ref[slot] - delta)).astype(jnp.bfloat16)
                ds_ref[slot * TILE : (slot + 1) * TILE, :] = dscore
                dk_ref[place, :] += jnp.dot(dscore, query, preferred_element_type=jnp.float32)
                dv_ref[place, :] += jnp.dot(
                    prob.astype(jnp.bfloat16), grad, preferred_element_type=jnp.float32
                )
            dq_t = jnp.dot(kt_picked[...], ds_ref[...], preferred_element_type=jnp.float32)
            dq_ref[index] = (dq_t * factor).T.astype(jnp.bfloat16)
            return carry

        lax.fori_loop(0, count, visit, 0)
        for index in range(count):
            dq_refs[index][...] = dq_ref[index]
        if last:
            for shift in range(n_ctx):
                block = block_of(route, n_ctx, shift)
                place = pl.ds(pl.multiple_of(block * rows, rows), rows)
                dk_outs[shift][...] = (dk_ref[place, :] * factor).astype(jnp.bfloat16)
                dv_outs[shift][...] = dv_ref[place, :].astype(jnp.bfloat16)
        else:
            dk_out[...] = dk_ref[...]
            dv_out[...] = dv_ref[...]


def attend(route, picks, scales, gain, keys, messages, shifts, sums, last, n_ctx):
    count = len(shifts)
    rows = messages[0].shape[1]
    tokens = n_ctx * rows
    n_keys = rows // TILE + picks.shape[1]
    piece = jax.ShapeDtypeStruct((rows, HD), jnp.bfloat16)
    whole_sum = jax.ShapeDtypeStruct((tokens, HD), jnp.float32)
    sums = list(sums)
    outs = [piece] * count + ([piece] * (2 * n_ctx) if last else [whole_sum] * 2)
    return pl.pallas_call(
        functools.partial(attend_kernel, n_ctx, shifts, last, bool(sums)),
        out_shape=outs,
        in_specs=[IN_SMEM, IN_SMEM] + [IN_VMEM] * (2 + 3 + count + len(sums)),
        out_specs=[IN_VMEM] * len(outs),
        scratch_shapes=[
            pltpu.VMEM((count, rows, HD), jnp.bfloat16),
            pltpu.VMEM((count, rows, HD), jnp.bfloat16),
            pltpu.VMEM((count, rows, HD), jnp.bfloat16),
            pltpu.VMEM((tokens, HD), jnp.float32),
            pltpu.VMEM((tokens, HD), jnp.float32),
            pltpu.VMEM((n_keys, TILE, rows), jnp.float32),
            pltpu.VMEM((n_keys, TILE, rows), jnp.float32),
            pltpu.VMEM((8, 128), jnp.float32),
            pltpu.VMEM((n_keys * TILE, rows), jnp.bfloat16),
            pltpu.VMEM((HD, n_keys * TILE), jnp.bfloat16),
        ],
        compiler_params=pltpu.CompilerParams(vmem_limit_bytes=VMEM_BYTES),
    )(route, picks, scales, gain, *keys, *messages, *sums)


def spread(route, n_ctx, slots, wide_ref):
    for shift in range(n_ctx):

        @pl.when(route[0, shift] >= 0)
        def _(shift=shift):
            place = pl.ds(pl.multiple_of(route[0, shift] * HD, HD), HD)
            wide_ref[:, place] = slots[shift][...]


def dots_kernel(n_ctx, route, q_ref, k_ref, q_gain, k_gain, *refs):
    dq_slots, dk_slots = refs[:n_ctx], refs[n_ctx : 2 * n_ctx]
    dot_ref, dq_ref, dk_ref = refs[2 * n_ctx :]
    for at, (slots, wide_ref, pre_ref, gain) in enumerate(
        ((dq_slots, dq_ref, q_ref, q_gain), (dk_slots, dk_ref, k_ref, k_gain))
    ):
        spread(route, n_ctx, slots, wide_ref)
        terms = gain[...] * wide_ref[...].astype(jnp.float32) * pre_ref[...].astype(jnp.float32)
        dot_ref[at : at + 1, :] = row_sums(terms)


def finish_kernel(n_ctx, width_all, route, q_ref, k_ref, q_gain, k_gain, scale_ref, dot_ref, *refs):
    dq_ref, dk_ref = refs[:2]
    dv_slots = refs[2 : 2 + n_ctx]
    dq_out, dk_out, dv_out = refs[2 + n_ctx :]
    block = route[0, n_ctx + 1]
    for at, (pre_ref, gain, grad_ref, out) in enumerate(
        ((q_ref, q_gain, dq_ref, dq_out), (k_ref, k_gain, dk_ref, dk_out))
    ):
        scale_row = scale_ref[block, at : at + 1, :]
        scale = column(scale_row, HD)
        back = column(scale_row**3 * (dot_ref[at : at + 1, :] / width_all), HD)
        for first in range(0, pre_ref.shape[1], HD):
            place = slice(first, first + HD)
            wide = pre_ref[:, place].astype(jnp.float32)
            grad = grad_ref[:, place].astype(jnp.float32)
            out[:, place] = (scale * gain[:, place] * grad - wide * back).astype(jnp.bfloat16)
    spread(route, n_ctx, dv_slots, dv_out)


def heads_to_owners(q_pre, k_pre, values, out_grad, q_gain, k_gain, selected):
    n_ctx = lax.axis_size("ctx")
    n_head = lax.axis_size("head")
    rows, width_dev = q_pre.shape
    width_all = width_dev * n_head
    heads_dev = width_dev // HD
    remote_count = selected.shape[2]
    sizes = (n_ctx, n_head, heads_dev)
    me = lax.axis_index("ctx") * n_head + lax.axis_index("head")
    route = lax.dynamic_slice_in_dim(jnp.asarray(routing_table(*sizes)), me, 1, 0)
    params = pltpu.CompilerParams(vmem_limit_bytes=VMEM_BYTES)

    k_square, kv_sent = pack(route, k_pre, values, n_ctx)
    kv_here = to_owners(kv_sent, *sizes)
    q_square, qg_sent = pack(route, q_pre, out_grad, n_ctx)
    qg_here = to_owners(qg_sent, *sizes)

    wishes = selected[0].reshape(1, -1).astype(jnp.float32)
    wishes = jnp.pad(wishes, ((0, 0), (0, rows - wishes.shape[1])))
    small = jnp.concatenate((q_square, k_square, wishes), axis=0)
    small = lax.all_gather(small, ("ctx", "head"))
    squares = jnp.sum(small[:, :2].reshape(n_ctx, n_head, 2, rows), axis=1)
    scales = lax.rsqrt(squares / width_all + epsilon)
    mine = small[:, 2].reshape(n_ctx, n_head, rows)
    mine = lax.dynamic_index_in_dim(mine, lax.axis_index("head"), 1, keepdims=False)
    own_head = jnp.maximum(route[0, n_ctx], 0)
    picks = lax.dynamic_slice_in_dim(mine, own_head * remote_count, remote_count, 1)
    picks = picks.astype(jnp.int32)

    q_gains = q_gain.reshape(heads_dev, HD)
    k_gains = k_gain.reshape(heads_dev, HD)
    keys = prepare_keys(route, scales, k_gains, kv_here, n_ctx)
    all_shifts = tuple(range(n_ctx))
    groups = (all_shifts,)
    sums = ()
    dq_there = []
    for at, shifts in enumerate(groups):
        last = at == len(groups) - 1
        results = attend(
            route,
            picks,
            scales,
            q_gains,
            keys,
            [qg_here[shift] for shift in shifts],
            shifts,
            sums,
            last,
            n_ctx,
        )
        dq_there += results[: len(shifts)]
        sums = results[len(shifts) :]
    dk_there, dv_there = sums[:n_ctx], sums[n_ctx:]
    dq_slots = from_owners(dq_there, *sizes)
    dk_slots = from_owners(dk_there, *sizes)
    dv_slots = from_owners(dv_there, *sizes)

    wide = jax.ShapeDtypeStruct((rows, width_dev), jnp.bfloat16)
    q_gain = q_gain[None]
    k_gain = k_gain[None]
    dots, dq_wide, dk_wide = pl.pallas_call(
        functools.partial(dots_kernel, n_ctx),
        out_shape=[jax.ShapeDtypeStruct((2, rows), jnp.float32), wide, wide],
        in_specs=[IN_SMEM] + [IN_VMEM] * (4 + 2 * n_ctx),
        out_specs=[IN_VMEM] * 3,
        compiler_params=params,
    )(route, q_pre, k_pre, q_gain, k_gain, *dq_slots, *dk_slots)
    dots = lax.psum(dots, "head")
    return pl.pallas_call(
        functools.partial(finish_kernel, n_ctx, width_all),
        out_shape=[wide] * 3,
        in_specs=[IN_SMEM] + [IN_VMEM] * (8 + n_ctx),
        out_specs=[IN_VMEM] * 3,
        compiler_params=params,
    )(route, q_pre, k_pre, q_gain, k_gain, scales, dots, dq_wide, dk_wide, *dv_slots)


def on_device(q_pre, k_pre, values, out_grad, q_gain, k_gain, selected):
    n_ctx = lax.axis_size("ctx")
    tiles_dev, heads_dev, remote_count = selected.shape
    capacity = -(-heads_dev * remote_count // (n_ctx - 1))
    by_head = (n_ctx - 1) * tiles_dev * 7
    by_tile = (n_ctx - 1) * capacity * 6
    plan = heads_to_owners if by_head <= by_tile and n_ctx >= heads_dev else tiles_to_queries
    return plan(q_pre, k_pre, values, out_grad, q_gain, k_gain, selected)


def solution(mesh):
    placed = (
        P("ctx", "head"),
        P("ctx", "head"),
        P("ctx", "head"),
        P("ctx", "head"),
        P("head"),
        P("head"),
        P("ctx", "head", None),
    )
    return jax.shard_map(
        on_device,
        mesh=mesh,
        in_specs=placed,
        out_specs=(P("ctx", "head"), P("ctx", "head"), P("ctx", "head")),
        check_vma=False,
    )
```

```python
import functools
import math

import jax
import jax.numpy as jnp
import numpy as np
from jax import lax
from jax.experimental import pallas as pl
from jax.experimental.pallas import tpu as pltpu
from jax.sharding import PartitionSpec as P

HD = 128
TILE = 128


epsilon = 1e-06


def split_heads(array, heads_dev):
    return array.reshape(array.shape[0], heads_dev, HD).transpose(1, 0, 2)


def merge_heads(array):
    heads_dev, tok_dev, depth = array.shape
    return array.transpose(1, 0, 2).reshape(tok_dev, heads_dev * depth)


def per_tile(array, qt_dev):
    heads_dev, tok_dev, depth = array.shape
    return array.reshape(heads_dev, qt_dev, TILE, depth).transpose(1, 0, 2, 3)


def from_tiles(array):
    qt_dev, heads_dev, rows_tile, depth = array.shape
    return array.transpose(1, 0, 2, 3).reshape(heads_dev, qt_dev * rows_tile, depth)


def table_sum(taken, pieces, heads_dev, qt_dev):
    flat_pieces = pieces.reshape(pieces.shape[0], -1)
    summed = jnp.dot(
        taken, flat_pieces, precision=lax.Precision.HIGHEST, preferred_element_type=jnp.float32
    )
    summed = summed.reshape(heads_dev, qt_dev, 2, TILE, HD).transpose(2, 0, 1, 3, 4)
    return summed.reshape(2, heads_dev, qt_dev * TILE, HD)


def rounded(array):
    return array.astype(jnp.bfloat16)


def finish_norm(wide, scale, gain, grad, dot_sum, width_all):
    return (scale * gain * grad - wide * scale**3 * (dot_sum / width_all)[:, None]).astype(
        jnp.bfloat16
    )


def tiles_to_queries(q_pre, k_pre, values, out_grad, q_gain, k_gain, selected):
    n_ctx = lax.axis_size("ctx")
    tok_dev, width_dev = q_pre.shape
    width_all = width_dev * lax.axis_size("head")
    heads_dev = width_dev // HD
    qt_dev = tok_dev // TILE
    remote_count = selected.shape[2]
    factor = 1.0 / math.sqrt(HD)
    q_wide = q_pre.astype(jnp.float32)
    k_wide = k_pre.astype(jnp.float32)
    q_square, k_square = lax.psum(
        (jnp.sum(q_wide * q_wide, axis=1), jnp.sum(k_wide * k_wide, axis=1)), "head"
    )
    q_scale = lax.rsqrt(q_square / width_all + epsilon)[:, None]
    k_scale = lax.rsqrt(k_square / width_all + epsilon)[:, None]
    q_heads = split_heads(rounded(q_wide * q_scale * q_gain), heads_dev)
    k_heads = split_heads(rounded(k_wide * k_scale * k_gain), heads_dev)
    v_heads = split_heads(values, heads_dev)
    g_heads = split_heads(out_grad, heads_dev)
    q_tiles = per_tile(q_heads, qt_dev)
    g_tiles = per_tile(g_heads, qt_dev)
    k_table = k_heads.reshape(heads_dev * qt_dev, TILE, HD)
    v_table = v_heads.reshape(heads_dev * qt_dev, TILE, HD)
    flat_sel = selected[0].reshape(-1)
    n_slot = flat_sel.shape[0]
    capacity = -(-n_slot // (n_ctx - 1))
    n_buffer = n_ctx * capacity
    owners = flat_sel // qt_dev
    head_of = jnp.arange(n_slot, dtype=jnp.int32) // remote_count
    codes = head_of * qt_dev + flat_sel % qt_dev
    matches = (owners[:, None] == jnp.arange(n_ctx, dtype=jnp.int32)[None, :]).astype(jnp.int32)
    ranks = jnp.sum((jnp.cumsum(matches, axis=0) - matches) * matches, axis=1)
    position = owners * capacity + ranks
    placed = position[None, :] == jnp.arange(n_buffer, dtype=jnp.int32)[:, None]
    request = jnp.sum(jnp.where(placed, codes[None, :] + 1, 0), axis=1) - 1
    asked = lax.all_to_all(
        request.reshape(n_ctx, capacity), "ctx", split_axis=0, concat_axis=0, tiled=True
    ).reshape(n_buffer)
    clipped = jnp.maximum(asked, 0)
    taken = (asked[None, :] == jnp.arange(heads_dev * qt_dev, dtype=jnp.int32)[:, None]).astype(
        jnp.float32
    )
    s_near = (
        jnp.einsum("rhqd,hkd->rhqk", q_tiles, k_heads, preferred_element_type=jnp.float32) * factor
    )
    dp_near = jnp.einsum("rhqd,hkd->rhqk", g_tiles, v_heads, preferred_element_type=jnp.float32)
    near_top = jnp.max(s_near, axis=-1)
    outgoing = jnp.stack((k_table[clipped], v_table[clipped]), axis=1).reshape(
        n_ctx, capacity, 2, TILE, HD
    )
    incoming = lax.all_to_all(outgoing, "ctx", split_axis=0, concat_axis=0, tiled=True).reshape(
        n_buffer, 2, TILE, HD
    )
    slot_kv = incoming[position].reshape(heads_dev, remote_count, 2, TILE, HD)
    far_k = slot_kv[:, :, 0]
    far_v = slot_kv[:, :, 1]
    s_far = (
        jnp.einsum("rhqd,hckd->rhqck", q_tiles, far_k, preferred_element_type=jnp.float32) * factor
    )
    dp_far = jnp.einsum("rhqd,hckd->rhqck", g_tiles, far_v, preferred_element_type=jnp.float32)
    row_top = jnp.maximum(near_top, jnp.max(s_far, axis=(-2, -1)))
    totals = jnp.sum(jnp.exp(s_near - row_top[..., None]), axis=-1) + jnp.sum(
        jnp.exp(s_far - row_top[..., None, None]), axis=(-2, -1)
    )
    lse = row_top + jnp.log(totals)
    p_near = jnp.exp(s_near - lse[..., None])
    p_far = jnp.exp(s_far - lse[..., None, None])
    delta = jnp.sum(p_near * dp_near, axis=-1) + jnp.sum(p_far * dp_far, axis=(-2, -1))
    ds_near = rounded(p_near * (dp_near - delta[..., None]) * factor)
    pb_near = rounded(p_near)
    dq_near = jnp.einsum("rhqk,hkd->rhqd", ds_near, k_heads, preferred_element_type=jnp.float32)
    dk_near = jnp.einsum("rhqk,rhqd->hkd", ds_near, q_tiles, preferred_element_type=jnp.float32)
    dv_near = jnp.einsum("rhqk,rhqd->hkd", pb_near, g_tiles, preferred_element_type=jnp.float32)
    dq_near, dk_near, dv_near = (dq_near, dk_near, dv_near)
    ds_far = rounded(p_far * (dp_far - delta[..., None, None]) * factor)
    pb_far = rounded(p_far)
    dq_far = jnp.einsum("rhqck,hckd->rhqd", ds_far, far_k, preferred_element_type=jnp.float32)
    dq_wide = merge_heads(from_tiles(dq_near + dq_far))
    q_dot = jnp.sum(q_gain * dq_wide * q_wide, axis=1)
    dq_wide, q_dot = (dq_wide, q_dot)
    dk_far = jnp.einsum("rhqck,rhqd->hckd", ds_far, q_tiles, preferred_element_type=jnp.float32)
    dv_far = jnp.einsum("rhqck,rhqd->hckd", pb_far, g_tiles, preferred_element_type=jnp.float32)
    grads = jnp.stack((dk_far, dv_far), axis=2).reshape(n_slot, 2, TILE, HD)
    sending = jnp.zeros((n_buffer, 2, TILE, HD), jnp.float32).at[position].set(grads)
    returned = lax.all_to_all(
        sending.reshape(n_ctx, capacity, 2, TILE, HD),
        "ctx",
        split_axis=0,
        concat_axis=0,
        tiled=True,
    ).reshape(n_buffer, 2, TILE, HD)
    far_sums = table_sum(taken, returned, heads_dev, qt_dev)
    dk_wide = merge_heads(dk_near + far_sums[0])
    dv_heads = dv_near + far_sums[1]
    k_dot = jnp.sum(k_gain * dk_wide * k_wide, axis=1)
    q_dot, k_dot = lax.psum((q_dot, k_dot), "head")
    dq_result = finish_norm(q_wide, q_scale, q_gain, dq_wide, q_dot, width_all)
    dk_result = finish_norm(k_wide, k_scale, k_gain, dk_wide, k_dot, width_all)
    return (dq_result, dk_result, merge_heads(dv_heads).astype(jnp.bfloat16))


VMEM_BYTES = 48 * 2**20
NT = (((1,), (1,)), ((), ()))
IN_VMEM = pl.BlockSpec(memory_space=pltpu.VMEM)
IN_SMEM = pl.BlockSpec(memory_space=pltpu.SMEM)


def owners_of(group, n_ctx, heads_dev):
    places = [(4 * head + 1) * n_ctx // (4 * heads_dev) for head in range(heads_dev)]
    return [n_ctx - 1 - place if group % 2 else place for place in places]


def routing_table(n_ctx, n_head, heads_dev):
    rows = []
    for block in range(n_ctx):
        for group in range(n_head):
            owners = owners_of(group, n_ctx, heads_dev)
            owned = [owners.index(c) if c in owners else -1 for c in range(n_ctx)]
            rows.append([owned[block ^ mask] for mask in range(n_ctx)] + [block])
    return np.array(rows, np.int32)


def pairs_to_owner(mask, n_ctx, n_head, heads_dev):
    pairs = []
    for group in range(n_head):
        owners = owners_of(group, n_ctx, heads_dev)
        for block in range(n_ctx):
            if block ^ mask in owners:
                pairs.append((block * n_head + group, (block ^ mask) * n_head + group))
    return pairs


def to_owners(arrays, n_ctx, n_head, heads_dev):
    moved = list(arrays)
    for mask in range(n_ctx - 1, 0, -1):
        pairs = pairs_to_owner(mask, n_ctx, n_head, heads_dev)
        moved[mask] = lax.ppermute(arrays[mask], ("ctx", "head"), pairs)
    return moved


def from_owners(arrays, n_ctx, n_head, heads_dev):
    moved = list(arrays)
    for mask in range(n_ctx - 1, 0, -1):
        pairs = [(b, a) for a, b in pairs_to_owner(mask, n_ctx, n_head, heads_dev)]
        moved[mask] = lax.ppermute(arrays[mask], ("ctx", "head"), pairs)
    return moved


def column(row, width):
    return jnp.broadcast_to(row, (width, row.shape[1])).T


def row_sums(wide):
    total = wide[:, :HD]
    for at in range(HD, wide.shape[1], HD):
        total = total + wide[:, at : at + HD]
    return jnp.sum(total.T, axis=0, keepdims=True)


def pack_kernel(n_ctx, route, q_ref, k_ref, v_ref, g_ref, square_ref, *outs):
    for mask in range(n_ctx - 1, -1, -1):
        head = jnp.maximum(route[0, mask], 0)
        place = pl.ds(pl.multiple_of(head * HD, HD), HD)
        for at, ref in enumerate((q_ref, k_ref, v_ref, g_ref)):
            outs[mask][at] = ref[:, place]
    for at, ref in enumerate((q_ref, k_ref)):
        wide = ref[...].astype(jnp.float32)
        square_ref[at : at + 1, :] = row_sums(wide * wide)


def pack(route, arrays, n_ctx):
    rows = arrays[0].shape[0]
    result = pl.pallas_call(
        functools.partial(pack_kernel, n_ctx),
        out_shape=[jax.ShapeDtypeStruct((2, rows), jnp.float32)]
        + [jax.ShapeDtypeStruct((4, rows, HD), jnp.bfloat16)] * n_ctx,
        in_specs=[IN_SMEM] + [IN_VMEM] * 4,
        out_specs=[IN_VMEM] * (n_ctx + 1),
        compiler_params=pltpu.CompilerParams(vmem_limit_bytes=VMEM_BYTES),
    )(route, *arrays)
    return result[0], result[1:]


def attend_kernel(n_ctx, route, picks, scale_ref, q_gain, k_gain, *refs):
    messages, outs, scratch = refs[:n_ctx], refs[n_ctx : 2 * n_ctx], refs[2 * n_ctx :]
    q_ref, g_ref, k_ref, kt_ref, v_ref, dq_ref, dk_ref, dv_ref, ds_ref, kt_picked = scratch[:10]
    buffers = (scratch[10:13], scratch[13:16])
    rows = messages[0].shape[1]
    remote_count = picks.shape[1]
    near = rows // TILE
    n_keys = near + remote_count
    factor = 1.0 / math.sqrt(HD)
    to_base2 = factor * math.log2(math.e)
    own_block = route[0, n_ctx]

    def rows_of(block):
        return pl.ds(pl.multiple_of(block * rows, rows), rows)

    def places_of(block):
        return [
            pl.ds(pl.multiple_of(block * rows + tile * TILE, TILE), TILE) for tile in range(near)
        ] + [
            pl.ds(pl.multiple_of(picks[block, slot] * TILE, TILE), TILE)
            for slot in range(remote_count)
        ]

    def prepare(mask):
        block = own_block ^ mask
        place = rows_of(block)
        q_scale = column(scale_ref[block, 0:1, :], HD)
        k_scale = column(scale_ref[block, 1:2, :], HD)
        own = route[0, 0]
        q_normed = messages[mask][0].astype(jnp.float32) * q_scale * q_gain[pl.ds(own, 1), :]
        k_normed = messages[mask][1].astype(jnp.float32) * k_scale * k_gain[pl.ds(own, 1), :]
        q_ref[mask] = q_normed.astype(jnp.bfloat16)
        k_ref[place, :] = k_normed.astype(jnp.bfloat16)
        kt_ref[:, place] = k_normed.T.astype(jnp.bfloat16)
        v_ref[place, :] = messages[mask][2]
        g_ref[mask] = messages[mask][3]

    def scores(mask, slot, place, buffer):
        weight_ref, dprob_ref, stat_ref = buffer
        score = lax.dot_general(
            k_ref[place, :], q_ref[mask], NT, preferred_element_type=jnp.float32
        )
        dprob = lax.dot_general(
            v_ref[place, :], g_ref[mask], NT, preferred_element_type=jnp.float32
        )
        top = jnp.max(score, axis=0, keepdims=True)
        weight = jnp.exp2((score - top) * to_base2)
        weight_ref[slot] = weight
        dprob_ref[slot] = dprob
        stat_ref[0, slot : slot + 1, :] = top * to_base2
        stat_ref[1, slot : slot + 1, :] = jnp.sum(weight, axis=0, keepdims=True)
        stat_ref[2, slot : slot + 1, :] = jnp.sum(weight * dprob, axis=0, keepdims=True)

    def settle(buffer):
        stat_ref = buffer[2]
        tops = stat_ref[0, :n_keys, :]
        shares = jnp.exp2(tops - jnp.max(tops, axis=0, keepdims=True))
        total = jnp.sum(shares * stat_ref[1, :n_keys, :], axis=0, keepdims=True)
        mixed = jnp.sum(shares * stat_ref[2, :n_keys, :], axis=0, keepdims=True)
        inverse = 1.0 / total
        return shares * inverse, mixed * inverse

    def gradients(mask, slot, place, buffer, shares, delta):
        weight_ref, dprob_ref, _ = buffer
        prob = weight_ref[slot] * shares[slot : slot + 1, :]
        dscore = (prob * (dprob_ref[slot] - delta)).astype(jnp.bfloat16)
        ds_ref[slot * TILE : (slot + 1) * TILE, :] = dscore
        kt_picked[:, slot * TILE : (slot + 1) * TILE] = kt_ref[:, place]
        dk_ref[place, :] += jnp.dot(dscore, q_ref[mask], preferred_element_type=jnp.float32)
        dv_ref[place, :] += jnp.dot(
            prob.astype(jnp.bfloat16), g_ref[mask], preferred_element_type=jnp.float32
        )

    def query_gradient(mask):
        dq_t = jnp.dot(kt_picked[...], ds_ref[...], preferred_element_type=jnp.float32)
        dq_ref[mask] = (dq_t * factor).T.astype(jnp.bfloat16)

    def step(mask, buffer, later, later_buffer):
        places = places_of(own_block ^ mask)
        shares, delta = settle(buffer)
        later_places = None if later is None else places_of(own_block ^ later)
        for slot in range(n_keys):
            gradients(mask, slot, places[slot], buffer, shares, delta)
            if later is not None:
                scores(later, slot, later_places[slot], later_buffer)
        query_gradient(mask)

    @pl.when(route[0, 0] >= 0)
    def _():
        for mask in range(n_ctx):
            prepare(mask)
        dk_ref[...] = jnp.zeros_like(dk_ref)
        dv_ref[...] = jnp.zeros_like(dv_ref)
        for slot, place in enumerate(places_of(own_block)):
            scores(0, slot, place, buffers[0])

        def two(pair, carry):
            step(2 * pair, buffers[0], 2 * pair + 1, buffers[1])
            step(2 * pair + 1, buffers[1], 2 * pair + 2, buffers[0])
            return carry

        lax.fori_loop(0, n_ctx // 2 - 1, two, 0)
        step(n_ctx - 2, buffers[0], n_ctx - 1, buffers[1])
        step(n_ctx - 1, buffers[1], None, None)
        for mask in range(n_ctx):
            place = rows_of(own_block ^ mask)
            outs[mask][0] = dq_ref[mask]
            outs[mask][1] = (dk_ref[place, :] * factor).astype(jnp.bfloat16)
            outs[mask][2] = dv_ref[place, :].astype(jnp.bfloat16)


def attend(route, picks, scales, q_gain, k_gain, messages, n_ctx):
    rows = messages[0].shape[1]
    tokens = n_ctx * rows
    n_keys = rows // TILE + picks.shape[1]
    by_block = pltpu.VMEM((n_ctx, rows, HD), jnp.bfloat16)
    buffer = [
        pltpu.VMEM((n_keys, TILE, rows), jnp.float32),
        pltpu.VMEM((n_keys, TILE, rows), jnp.float32),
        pltpu.VMEM((3, -(-n_keys // 8) * 8, rows), jnp.float32),
    ]
    return pl.pallas_call(
        functools.partial(attend_kernel, n_ctx),
        out_shape=[jax.ShapeDtypeStruct((3, rows, HD), jnp.bfloat16)] * n_ctx,
        in_specs=[IN_SMEM, IN_SMEM] + [IN_VMEM] * (3 + n_ctx),
        out_specs=[IN_VMEM] * n_ctx,
        scratch_shapes=[
            by_block,
            by_block,
            pltpu.VMEM((tokens, HD), jnp.bfloat16),
            pltpu.VMEM((HD, tokens), jnp.bfloat16),
            pltpu.VMEM((tokens, HD), jnp.bfloat16),
            by_block,
            pltpu.VMEM((tokens, HD), jnp.float32),
            pltpu.VMEM((tokens, HD), jnp.float32),
            pltpu.VMEM((n_keys * TILE, rows), jnp.bfloat16),
            pltpu.VMEM((HD, n_keys * TILE), jnp.bfloat16),
        ]
        + buffer
        + buffer,
        compiler_params=pltpu.CompilerParams(vmem_limit_bytes=VMEM_BYTES),
    )(route, picks, scales, q_gain, k_gain, *messages)


def spread(route, n_ctx, slots, at, wide_ref):
    for mask in range(n_ctx):

        @pl.when(route[0, mask] >= 0)
        def _(mask=mask):
            place = pl.ds(pl.multiple_of(route[0, mask] * HD, HD), HD)
            wide_ref[:, place] = slots[mask][at]


def dots_kernel(n_ctx, route, q_ref, k_ref, q_gain, k_gain, *refs):
    slots = refs[:n_ctx]
    dot_ref, dq_ref, dk_ref = refs[n_ctx:]
    for at, (wide_ref, pre_ref, gain) in enumerate(
        ((dq_ref, q_ref, q_gain), (dk_ref, k_ref, k_gain))
    ):
        spread(route, n_ctx, slots, at, wide_ref)
        terms = gain[...] * wide_ref[...].astype(jnp.float32) * pre_ref[...].astype(jnp.float32)
        dot_ref[at : at + 1, :] = row_sums(terms)


def finish_kernel(n_ctx, width_all, route, q_ref, k_ref, q_gain, k_gain, scale_ref, dot_ref, *refs):
    dq_ref, dk_ref = refs[:2]
    slots = refs[2 : 2 + n_ctx]
    dq_out, dk_out, dv_out = refs[2 + n_ctx :]
    block = route[0, n_ctx]
    for at, (pre_ref, gain, grad_ref, out) in enumerate(
        ((q_ref, q_gain, dq_ref, dq_out), (k_ref, k_gain, dk_ref, dk_out))
    ):
        scale_row = scale_ref[block, at : at + 1, :]
        scale = column(scale_row, HD)
        back = column(scale_row**3 * (dot_ref[at : at + 1, :] / width_all), HD)
        for first in range(0, pre_ref.shape[1], HD):
            place = slice(first, first + HD)
            wide = pre_ref[:, place].astype(jnp.float32)
            grad = grad_ref[:, place].astype(jnp.float32)
            out[:, place] = (scale * gain[:, place] * grad - wide * back).astype(jnp.bfloat16)
    spread(route, n_ctx, slots, 2, dv_out)


def heads_to_owners(q_pre, k_pre, values, out_grad, q_gain, k_gain, selected):
    n_ctx = lax.axis_size("ctx")
    n_head = lax.axis_size("head")
    rows, width_dev = q_pre.shape
    width_all = width_dev * n_head
    heads_dev = width_dev // HD
    remote_count = selected.shape[2]
    sizes = (n_ctx, n_head, heads_dev)
    me = lax.axis_index("ctx") * n_head + lax.axis_index("head")
    route = lax.dynamic_slice_in_dim(jnp.asarray(routing_table(*sizes)), me, 1, 0)
    params = pltpu.CompilerParams(vmem_limit_bytes=VMEM_BYTES)

    squares, sent = pack(route, (q_pre, k_pre, values, out_grad), n_ctx)
    messages = to_owners(sent, *sizes)

    wishes = selected[0].reshape(1, -1).astype(jnp.float32)
    wishes = jnp.pad(wishes, ((0, 0), (0, rows - wishes.shape[1])))
    small = jnp.concatenate((lax.psum(squares, "head"), wishes), axis=0)
    small = lax.all_gather(small, "ctx")
    scales = lax.rsqrt(small[:, :2] / width_all + epsilon)
    own_head = jnp.maximum(route[0, 0], 0)
    picks = lax.dynamic_slice_in_dim(small[:, 2], own_head * remote_count, remote_count, 1)
    picks = picks.astype(jnp.int32)

    results = attend(
        route,
        picks,
        scales,
        q_gain.reshape(heads_dev, HD),
        k_gain.reshape(heads_dev, HD),
        messages,
        n_ctx,
    )
    slots = from_owners(results, *sizes)

    wide = jax.ShapeDtypeStruct((rows, width_dev), jnp.bfloat16)
    q_gain = q_gain[None]
    k_gain = k_gain[None]
    dots, dq_wide, dk_wide = pl.pallas_call(
        functools.partial(dots_kernel, n_ctx),
        out_shape=[jax.ShapeDtypeStruct((2, rows), jnp.float32), wide, wide],
        in_specs=[IN_SMEM] + [IN_VMEM] * (4 + n_ctx),
        out_specs=[IN_VMEM] * 3,
        compiler_params=params,
    )(route, q_pre, k_pre, q_gain, k_gain, *slots)
    dots = lax.psum(dots, "head")
    return pl.pallas_call(
        functools.partial(finish_kernel, n_ctx, width_all),
        out_shape=[wide] * 3,
        in_specs=[IN_SMEM] + [IN_VMEM] * (8 + n_ctx),
        out_specs=[IN_VMEM] * 3,
        compiler_params=params,
    )(route, q_pre, k_pre, q_gain, k_gain, scales, dots, dq_wide, dk_wide, *slots)


def on_device(q_pre, k_pre, values, out_grad, q_gain, k_gain, selected):
    n_ctx = lax.axis_size("ctx")
    tiles_dev, heads_dev, remote_count = selected.shape
    capacity = -(-heads_dev * remote_count // (n_ctx - 1))
    by_head = (n_ctx - 1) * tiles_dev * 7
    by_tile = (n_ctx - 1) * capacity * 6
    paired = n_ctx & (n_ctx - 1) == 0 and n_ctx >= max(heads_dev, 4)
    plan = heads_to_owners if paired and by_head <= by_tile else tiles_to_queries
    return plan(q_pre, k_pre, values, out_grad, q_gain, k_gain, selected)


def solution(mesh):
    placed = (
        P("ctx", "head"),
        P("ctx", "head"),
        P("ctx", "head"),
        P("ctx", "head"),
        P("head"),
        P("head"),
        P("ctx", "head", None),
    )
    return jax.shard_map(
        on_device,
        mesh=mesh,
        in_specs=placed,
        out_specs=(P("ctx", "head"), P("ctx", "head"), P("ctx", "head")),
        check_vma=False,
    )
```

```python
import functools
import math

import jax
import jax.numpy as jnp
from jax import lax
from jax.experimental import pallas as pl
from jax.experimental.pallas import tpu as pltpu
from jax.sharding import PartitionSpec as P

HD = 128
TILE = 128


epsilon = 1e-06


def split_heads(array, heads_dev):
    return array.reshape(array.shape[0], heads_dev, HD).transpose(1, 0, 2)


def merge_heads(array):
    heads_dev, tok_dev, depth = array.shape
    return array.transpose(1, 0, 2).reshape(tok_dev, heads_dev * depth)


def per_tile(array, qt_dev):
    heads_dev, tok_dev, depth = array.shape
    return array.reshape(heads_dev, qt_dev, TILE, depth).transpose(1, 0, 2, 3)


def from_tiles(array):
    qt_dev, heads_dev, rows_tile, depth = array.shape
    return array.transpose(1, 0, 2, 3).reshape(heads_dev, qt_dev * rows_tile, depth)


def table_sum(taken, pieces, heads_dev, qt_dev):
    flat_pieces = pieces.reshape(pieces.shape[0], -1)
    summed = jnp.dot(
        taken, flat_pieces, precision=lax.Precision.HIGHEST, preferred_element_type=jnp.float32
    )
    summed = summed.reshape(heads_dev, qt_dev, 2, TILE, HD).transpose(2, 0, 1, 3, 4)
    return summed.reshape(2, heads_dev, qt_dev * TILE, HD)


def rounded(array):
    return array.astype(jnp.bfloat16)


def finish_norm(wide, scale, gain, grad, dot_sum, width_all):
    return (scale * gain * grad - wide * scale**3 * (dot_sum / width_all)[:, None]).astype(
        jnp.bfloat16
    )


def tiles_to_queries(q_pre, k_pre, values, out_grad, q_gain, k_gain, selected):
    n_ctx = lax.axis_size("ctx")
    tok_dev, width_dev = q_pre.shape
    width_all = width_dev * lax.axis_size("head")
    heads_dev = width_dev // HD
    qt_dev = tok_dev // TILE
    remote_count = selected.shape[2]
    factor = 1.0 / math.sqrt(HD)
    q_wide = q_pre.astype(jnp.float32)
    k_wide = k_pre.astype(jnp.float32)
    q_square, k_square = lax.psum(
        (jnp.sum(q_wide * q_wide, axis=1), jnp.sum(k_wide * k_wide, axis=1)), "head"
    )
    q_scale = lax.rsqrt(q_square / width_all + epsilon)[:, None]
    k_scale = lax.rsqrt(k_square / width_all + epsilon)[:, None]
    q_heads = split_heads(rounded(q_wide * q_scale * q_gain), heads_dev)
    k_heads = split_heads(rounded(k_wide * k_scale * k_gain), heads_dev)
    v_heads = split_heads(values, heads_dev)
    g_heads = split_heads(out_grad, heads_dev)
    q_tiles = per_tile(q_heads, qt_dev)
    g_tiles = per_tile(g_heads, qt_dev)
    k_table = k_heads.reshape(heads_dev * qt_dev, TILE, HD)
    v_table = v_heads.reshape(heads_dev * qt_dev, TILE, HD)
    flat_sel = selected[0].reshape(-1)
    n_slot = flat_sel.shape[0]
    capacity = -(-n_slot // (n_ctx - 1))
    n_buffer = n_ctx * capacity
    owners = flat_sel // qt_dev
    head_of = jnp.arange(n_slot, dtype=jnp.int32) // remote_count
    codes = head_of * qt_dev + flat_sel % qt_dev
    matches = (owners[:, None] == jnp.arange(n_ctx, dtype=jnp.int32)[None, :]).astype(jnp.int32)
    ranks = jnp.sum((jnp.cumsum(matches, axis=0) - matches) * matches, axis=1)
    position = owners * capacity + ranks
    placed = position[None, :] == jnp.arange(n_buffer, dtype=jnp.int32)[:, None]
    request = jnp.sum(jnp.where(placed, codes[None, :] + 1, 0), axis=1) - 1
    asked = lax.all_to_all(
        request.reshape(n_ctx, capacity), "ctx", split_axis=0, concat_axis=0, tiled=True
    ).reshape(n_buffer)
    clipped = jnp.maximum(asked, 0)
    taken = (asked[None, :] == jnp.arange(heads_dev * qt_dev, dtype=jnp.int32)[:, None]).astype(
        jnp.float32
    )
    s_near = (
        jnp.einsum("rhqd,hkd->rhqk", q_tiles, k_heads, preferred_element_type=jnp.float32) * factor
    )
    dp_near = jnp.einsum("rhqd,hkd->rhqk", g_tiles, v_heads, preferred_element_type=jnp.float32)
    near_top = jnp.max(s_near, axis=-1)
    outgoing = jnp.stack((k_table[clipped], v_table[clipped]), axis=1).reshape(
        n_ctx, capacity, 2, TILE, HD
    )
    incoming = lax.all_to_all(outgoing, "ctx", split_axis=0, concat_axis=0, tiled=True).reshape(
        n_buffer, 2, TILE, HD
    )
    slot_kv = incoming[position].reshape(heads_dev, remote_count, 2, TILE, HD)
    far_k = slot_kv[:, :, 0]
    far_v = slot_kv[:, :, 1]
    s_far = (
        jnp.einsum("rhqd,hckd->rhqck", q_tiles, far_k, preferred_element_type=jnp.float32) * factor
    )
    dp_far = jnp.einsum("rhqd,hckd->rhqck", g_tiles, far_v, preferred_element_type=jnp.float32)
    row_top = jnp.maximum(near_top, jnp.max(s_far, axis=(-2, -1)))
    totals = jnp.sum(jnp.exp(s_near - row_top[..., None]), axis=-1) + jnp.sum(
        jnp.exp(s_far - row_top[..., None, None]), axis=(-2, -1)
    )
    lse = row_top + jnp.log(totals)
    p_near = jnp.exp(s_near - lse[..., None])
    p_far = jnp.exp(s_far - lse[..., None, None])
    delta = jnp.sum(p_near * dp_near, axis=-1) + jnp.sum(p_far * dp_far, axis=(-2, -1))
    ds_near = rounded(p_near * (dp_near - delta[..., None]) * factor)
    pb_near = rounded(p_near)
    dq_near = jnp.einsum("rhqk,hkd->rhqd", ds_near, k_heads, preferred_element_type=jnp.float32)
    dk_near = jnp.einsum("rhqk,rhqd->hkd", ds_near, q_tiles, preferred_element_type=jnp.float32)
    dv_near = jnp.einsum("rhqk,rhqd->hkd", pb_near, g_tiles, preferred_element_type=jnp.float32)
    dq_near, dk_near, dv_near = (dq_near, dk_near, dv_near)
    ds_far = rounded(p_far * (dp_far - delta[..., None, None]) * factor)
    pb_far = rounded(p_far)
    dq_far = jnp.einsum("rhqck,hckd->rhqd", ds_far, far_k, preferred_element_type=jnp.float32)
    dq_wide = merge_heads(from_tiles(dq_near + dq_far))
    q_dot = jnp.sum(q_gain * dq_wide * q_wide, axis=1)
    dq_wide, q_dot = (dq_wide, q_dot)
    dk_far = jnp.einsum("rhqck,rhqd->hckd", ds_far, q_tiles, preferred_element_type=jnp.float32)
    dv_far = jnp.einsum("rhqck,rhqd->hckd", pb_far, g_tiles, preferred_element_type=jnp.float32)
    grads = jnp.stack((dk_far, dv_far), axis=2).reshape(n_slot, 2, TILE, HD)
    sending = jnp.zeros((n_buffer, 2, TILE, HD), jnp.float32).at[position].set(grads)
    returned = lax.all_to_all(
        sending.reshape(n_ctx, capacity, 2, TILE, HD),
        "ctx",
        split_axis=0,
        concat_axis=0,
        tiled=True,
    ).reshape(n_buffer, 2, TILE, HD)
    far_sums = table_sum(taken, returned, heads_dev, qt_dev)
    dk_wide = merge_heads(dk_near + far_sums[0])
    dv_heads = dv_near + far_sums[1]
    k_dot = jnp.sum(k_gain * dk_wide * k_wide, axis=1)
    q_dot, k_dot = lax.psum((q_dot, k_dot), "head")
    dq_result = finish_norm(q_wide, q_scale, q_gain, dq_wide, q_dot, width_all)
    dk_result = finish_norm(k_wide, k_scale, k_gain, dk_wide, k_dot, width_all)
    return (dq_result, dk_result, merge_heads(dv_heads).astype(jnp.bfloat16))


VMEM_BYTES = 48 * 2**20
NT = (((1,), (1,)), ((), ()))
IN_VMEM = pl.BlockSpec(memory_space=pltpu.VMEM)
IN_SMEM = pl.BlockSpec(memory_space=pltpu.SMEM)


def owners_of(group, n_ctx, heads_dev):
    places = [(4 * head + 1) * n_ctx // (4 * heads_dev) for head in range(heads_dev)]
    return [n_ctx - 1 - place if group % 2 else place for place in places]


def head_at(place, group, n_ctx, heads_dev):
    even = jnp.where(group % 2 == 1, n_ctx - 1 - place, place)
    head = -1
    for index, owner in enumerate(owners_of(0, n_ctx, heads_dev)):
        head = jnp.where(even == owner, index, head)
    return head


def pairs_to_owner(mask, n_ctx, n_head, heads_dev):
    pairs = []
    for group in range(n_head):
        owners = owners_of(group, n_ctx, heads_dev)
        for block in range(n_ctx):
            if block ^ mask in owners:
                pairs.append((block * n_head + group, (block ^ mask) * n_head + group))
    return pairs


def to_owners(arrays, n_ctx, n_head, heads_dev):
    moved = list(arrays)
    for mask in range(n_ctx - 1, 0, -1):
        pairs = pairs_to_owner(mask, n_ctx, n_head, heads_dev)
        moved[mask] = lax.ppermute(arrays[mask], ("ctx", "head"), pairs)
    return moved


def from_owners(arrays, n_ctx, n_head, heads_dev):
    moved = list(arrays)
    for mask in range(n_ctx - 1, 0, -1):
        pairs = [(b, a) for a, b in pairs_to_owner(mask, n_ctx, n_head, heads_dev)]
        moved[mask] = lax.ppermute(arrays[mask], ("ctx", "head"), pairs)
    return moved


def column(row, width):
    return jnp.broadcast_to(row, (width, row.shape[1])).T


def row_sums(wide):
    total = wide[:, :HD]
    for at in range(HD, wide.shape[1], HD):
        total = total + wide[:, at : at + HD]
    return jnp.sum(total.T, axis=0, keepdims=True)


def pack_kernel(n_ctx, heads_dev, *refs):
    inputs, outs, sems = refs[:4], refs[4:-1], refs[-1]
    block, group = lax.axis_index("ctx"), lax.axis_index("head")
    heads = [head_at(block ^ mask, group, n_ctx, heads_dev) for mask in range(n_ctx)]

    def copies(mask):
        place = pl.ds(pl.multiple_of(heads[mask] * HD, HD), HD)
        return [
            pltpu.make_async_copy(ref.at[:, place], outs[mask].at[at], sems.at[mask, at])
            for at, ref in enumerate(inputs)
        ]

    for mask in range(n_ctx - 1, -1, -1):

        @pl.when(heads[mask] >= 0)
        def _(mask=mask):
            for copy in copies(mask):
                copy.start()

    for mask in range(n_ctx - 1, -1, -1):

        @pl.when(heads[mask] >= 0)
        def _(mask=mask):
            for copy in copies(mask):
                copy.wait()


def pack(arrays, n_ctx):
    rows, width_dev = arrays[0].shape
    return pl.pallas_call(
        functools.partial(pack_kernel, n_ctx, width_dev // HD),
        out_shape=[jax.ShapeDtypeStruct((4, rows, HD), jnp.bfloat16)] * n_ctx,
        in_specs=[pl.BlockSpec(memory_space=pl.ANY)] * 4,
        out_specs=[IN_VMEM] * n_ctx,
        scratch_shapes=[pltpu.SemaphoreType.DMA((n_ctx, 4))],
        compiler_params=pltpu.CompilerParams(vmem_limit_bytes=VMEM_BYTES),
    )(*arrays)


def squares_kernel(q_ref, k_ref, square_ref):
    for at, ref in enumerate((q_ref, k_ref)):
        wide = ref[...].astype(jnp.float32)
        square_ref[at : at + 1, :] = row_sums(wide * wide)


def attend_kernel(n_ctx, heads_dev, picks, scale_ref, q_gain, k_gain, *refs):
    messages, outs, scratch = refs[:n_ctx][::-1], refs[n_ctx : 2 * n_ctx], refs[2 * n_ctx :]
    q_ref, g_ref, k_ref, kt_ref, v_ref, dq_ref, dk_ref, dv_ref, ds_ref, kt_picked = scratch[:10]
    buffers = (scratch[10:13], scratch[13:16])
    rows = messages[0].shape[1]
    remote_count = picks.shape[1]
    near = rows // TILE
    n_keys = near + remote_count
    factor = 1.0 / math.sqrt(HD)
    to_base2 = factor * math.log2(math.e)
    own_block = lax.axis_index("ctx")
    own_head = head_at(own_block, lax.axis_index("head"), n_ctx, heads_dev)

    def rows_of(block):
        return pl.ds(pl.multiple_of(block * rows, rows), rows)

    def places_of(block):
        return [
            pl.ds(pl.multiple_of(block * rows + tile * TILE, TILE), TILE) for tile in range(near)
        ] + [
            pl.ds(pl.multiple_of(picks[block, slot] * TILE, TILE), TILE)
            for slot in range(remote_count)
        ]

    def prepare(mask):
        block = own_block ^ mask
        place = rows_of(block)
        q_scale = column(scale_ref[block, 0:1, :], HD)
        k_scale = column(scale_ref[block, 1:2, :], HD)
        q_normed = messages[mask][0].astype(jnp.float32) * q_scale * q_gain[pl.ds(own_head, 1), :]
        k_normed = messages[mask][1].astype(jnp.float32) * k_scale * k_gain[pl.ds(own_head, 1), :]
        q_ref[mask] = q_normed.astype(jnp.bfloat16)
        k_ref[place, :] = k_normed.astype(jnp.bfloat16)
        kt_ref[:, place] = k_normed.T.astype(jnp.bfloat16)
        v_ref[place, :] = messages[mask][2]
        g_ref[mask] = messages[mask][3]

    def scores(mask, slot, place, buffer):
        weight_ref, dprob_ref, stat_ref = buffer
        score = lax.dot_general(
            k_ref[place, :], q_ref[mask], NT, preferred_element_type=jnp.float32
        )
        dprob = lax.dot_general(
            v_ref[place, :], g_ref[mask], NT, preferred_element_type=jnp.float32
        )
        top = jnp.max(score, axis=0, keepdims=True)
        weight = jnp.exp2((score - top) * to_base2)
        weight_ref[slot] = weight
        dprob_ref[slot] = dprob
        stat_ref[0, slot : slot + 1, :] = top * to_base2
        stat_ref[1, slot : slot + 1, :] = jnp.sum(weight, axis=0, keepdims=True)
        stat_ref[2, slot : slot + 1, :] = jnp.sum(weight * dprob, axis=0, keepdims=True)

    def settle(buffer):
        stat_ref = buffer[2]
        tops = stat_ref[0, :n_keys, :]
        shares = jnp.exp2(tops - jnp.max(tops, axis=0, keepdims=True))
        total = jnp.sum(shares * stat_ref[1, :n_keys, :], axis=0, keepdims=True)
        mixed = jnp.sum(shares * stat_ref[2, :n_keys, :], axis=0, keepdims=True)
        inverse = 1.0 / total
        return shares * inverse, mixed * inverse

    def gradients(mask, slot, place, buffer, shares, delta):
        weight_ref, dprob_ref, _ = buffer
        prob = weight_ref[slot] * shares[slot : slot + 1, :]
        dscore = (prob * (dprob_ref[slot] - delta)).astype(jnp.bfloat16)
        ds_ref[slot * TILE : (slot + 1) * TILE, :] = dscore
        kt_picked[:, slot * TILE : (slot + 1) * TILE] = kt_ref[:, place]
        dk_ref[place, :] += jnp.dot(dscore, q_ref[mask], preferred_element_type=jnp.float32)
        dv_ref[place, :] += jnp.dot(
            prob.astype(jnp.bfloat16), g_ref[mask], preferred_element_type=jnp.float32
        )

    def query_gradient(mask):
        dq_t = jnp.dot(kt_picked[...], ds_ref[...], preferred_element_type=jnp.float32)
        dq_ref[mask] = (dq_t * factor).T.astype(jnp.bfloat16)

    def step(mask, buffer, later, later_buffer):
        places = places_of(own_block ^ mask)
        shares, delta = settle(buffer)
        later_places = None if later is None else places_of(own_block ^ later)
        for slot in range(n_keys):
            gradients(mask, slot, places[slot], buffer, shares, delta)
            if later is not None:
                scores(later, slot, later_places[slot], later_buffer)
        query_gradient(mask)

    @pl.when(own_head >= 0)
    def _():
        for mask in range(n_ctx):
            prepare(mask)
        dk_ref[...] = jnp.zeros_like(dk_ref)
        dv_ref[...] = jnp.zeros_like(dv_ref)
        for slot, place in enumerate(places_of(own_block)):
            scores(0, slot, place, buffers[0])

        def two(pair, carry):
            step(2 * pair, buffers[0], 2 * pair + 1, buffers[1])
            step(2 * pair + 1, buffers[1], 2 * pair + 2, buffers[0])
            return carry

        lax.fori_loop(0, n_ctx // 2 - 1, two, 0)
        step(n_ctx - 2, buffers[0], n_ctx - 1, buffers[1])
        step(n_ctx - 1, buffers[1], None, None)
        for mask in range(n_ctx):
            place = rows_of(own_block ^ mask)
            outs[mask][0] = dq_ref[mask]
            outs[mask][1] = (dk_ref[place, :] * factor).astype(jnp.bfloat16)
            outs[mask][2] = dv_ref[place, :].astype(jnp.bfloat16)


def attend(picks, scales, q_gain, k_gain, messages, n_ctx):
    rows = messages[0].shape[1]
    tokens = n_ctx * rows
    n_keys = rows // TILE + picks.shape[1]
    by_block = pltpu.VMEM((n_ctx, rows, HD), jnp.bfloat16)
    buffer = [
        pltpu.VMEM((n_keys, TILE, rows), jnp.float32),
        pltpu.VMEM((n_keys, TILE, rows), jnp.float32),
        pltpu.VMEM((3, -(-n_keys // 8) * 8, rows), jnp.float32),
    ]
    return pl.pallas_call(
        functools.partial(attend_kernel, n_ctx, q_gain.shape[0]),
        out_shape=[jax.ShapeDtypeStruct((3, rows, HD), jnp.bfloat16)] * n_ctx,
        in_specs=[IN_SMEM] + [IN_VMEM] * (3 + n_ctx),
        out_specs=[IN_VMEM] * n_ctx,
        scratch_shapes=[
            by_block,
            by_block,
            pltpu.VMEM((tokens, HD), jnp.bfloat16),
            pltpu.VMEM((HD, tokens), jnp.bfloat16),
            pltpu.VMEM((tokens, HD), jnp.bfloat16),
            by_block,
            pltpu.VMEM((tokens, HD), jnp.float32),
            pltpu.VMEM((tokens, HD), jnp.float32),
            pltpu.VMEM((n_keys * TILE, rows), jnp.bfloat16),
            pltpu.VMEM((HD, n_keys * TILE), jnp.bfloat16),
        ]
        + buffer
        + buffer,
        compiler_params=pltpu.CompilerParams(vmem_limit_bytes=VMEM_BYTES),
    )(picks, scales, q_gain, k_gain, *messages[::-1])


def spread(n_ctx, heads_dev, slots, at, wide_ref):
    block, group = lax.axis_index("ctx"), lax.axis_index("head")
    for mask in range(n_ctx):
        head = head_at(block ^ mask, group, n_ctx, heads_dev)

        @pl.when(head >= 0)
        def _(mask=mask, head=head):
            place = pl.ds(pl.multiple_of(head * HD, HD), HD)
            wide_ref[:, place] = slots[mask][at]


def dots_kernel(n_ctx, heads_dev, q_ref, k_ref, q_gain, k_gain, *refs):
    slots = refs[:n_ctx]
    dot_ref, dq_ref, dk_ref = refs[n_ctx:]
    for at, (wide_ref, pre_ref, gain) in enumerate(
        ((dq_ref, q_ref, q_gain), (dk_ref, k_ref, k_gain))
    ):
        spread(n_ctx, heads_dev, slots, at, wide_ref)
        terms = gain[...] * wide_ref[...].astype(jnp.float32) * pre_ref[...].astype(jnp.float32)
        dot_ref[at : at + 1, :] = row_sums(terms)


def finish_kernel(n_ctx, heads_dev, width_all, q_ref, k_ref, q_gain, k_gain, *refs):
    scale_ref, dot_ref, dq_ref, dk_ref = refs[:4]
    slots = refs[4 : 4 + n_ctx]
    dq_out, dk_out, dv_out = refs[4 + n_ctx :]
    block = lax.axis_index("ctx")
    for at, (pre_ref, gain, grad_ref, out) in enumerate(
        ((q_ref, q_gain, dq_ref, dq_out), (k_ref, k_gain, dk_ref, dk_out))
    ):
        scale_row = scale_ref[block, at : at + 1, :]
        scale = column(scale_row, HD)
        back = column(scale_row**3 * (dot_ref[at : at + 1, :] / width_all), HD)
        for first in range(0, pre_ref.shape[1], HD):
            place = slice(first, first + HD)
            wide = pre_ref[:, place].astype(jnp.float32)
            grad = grad_ref[:, place].astype(jnp.float32)
            out[:, place] = (scale * gain[:, place] * grad - wide * back).astype(jnp.bfloat16)
    spread(n_ctx, heads_dev, slots, 2, dv_out)


def heads_to_owners(q_pre, k_pre, values, out_grad, q_gain, k_gain, selected):
    n_ctx = lax.axis_size("ctx")
    n_head = lax.axis_size("head")
    rows, width_dev = q_pre.shape
    width_all = width_dev * n_head
    heads_dev = width_dev // HD
    remote_count = selected.shape[2]
    sizes = (n_ctx, n_head, heads_dev)
    params = pltpu.CompilerParams(vmem_limit_bytes=VMEM_BYTES)

    sent = pack((q_pre, k_pre, values, out_grad), n_ctx)
    messages = to_owners(sent, *sizes)

    squares = pl.pallas_call(
        squares_kernel,
        out_shape=jax.ShapeDtypeStruct((2, rows), jnp.float32),
        in_specs=[IN_VMEM] * 2,
        out_specs=IN_VMEM,
        compiler_params=params,
    )(q_pre, k_pre)
    wishes = selected[0].reshape(1, -1).astype(jnp.float32)
    wishes = jnp.pad(wishes, ((0, 0), (0, rows - wishes.shape[1])))
    small = jnp.concatenate((lax.psum(squares, "head"), wishes), axis=0)
    small = jnp.broadcast_to(small[None], (n_ctx,) + small.shape)
    small = lax.all_to_all(small, "ctx", split_axis=0, concat_axis=0, tiled=True)
    scales = lax.rsqrt(small[:, :2] / width_all + epsilon)
    own_head = head_at(lax.axis_index("ctx"), lax.axis_index("head"), n_ctx, heads_dev)
    first = jnp.maximum(own_head, 0) * remote_count
    picks = lax.dynamic_slice_in_dim(small[:, 2], first, remote_count, 1).astype(jnp.int32)

    q_gains = q_gain.reshape(heads_dev, HD)
    k_gains = k_gain.reshape(heads_dev, HD)
    results = attend(picks, scales, q_gains, k_gains, messages, n_ctx)
    slots = from_owners(results, *sizes)

    wide = jax.ShapeDtypeStruct((rows, width_dev), jnp.bfloat16)
    q_gain = q_gain[None]
    k_gain = k_gain[None]
    dots, dq_wide, dk_wide = pl.pallas_call(
        functools.partial(dots_kernel, n_ctx, heads_dev),
        out_shape=[jax.ShapeDtypeStruct((2, rows), jnp.float32), wide, wide],
        in_specs=[IN_VMEM] * (4 + n_ctx),
        out_specs=[IN_VMEM] * 3,
        compiler_params=params,
    )(q_pre, k_pre, q_gain, k_gain, *slots)
    dots = lax.psum(dots, "head")
    return pl.pallas_call(
        functools.partial(finish_kernel, n_ctx, heads_dev, width_all),
        out_shape=[wide] * 3,
        in_specs=[IN_VMEM] * (8 + n_ctx),
        out_specs=[IN_VMEM] * 3,
        compiler_params=params,
    )(q_pre, k_pre, q_gain, k_gain, scales, dots, dq_wide, dk_wide, *slots)


def on_device(q_pre, k_pre, values, out_grad, q_gain, k_gain, selected):
    n_ctx = lax.axis_size("ctx")
    tiles_dev, heads_dev, remote_count = selected.shape
    capacity = -(-heads_dev * remote_count // (n_ctx - 1))
    by_head = (n_ctx - 1) * tiles_dev * 7
    by_tile = (n_ctx - 1) * capacity * 6
    paired = n_ctx & (n_ctx - 1) == 0 and n_ctx >= max(heads_dev, 4)
    plan = heads_to_owners if paired and by_head <= by_tile else tiles_to_queries
    return plan(q_pre, k_pre, values, out_grad, q_gain, k_gain, selected)


def solution(mesh):
    placed = (
        P("ctx", "head"),
        P("ctx", "head"),
        P("ctx", "head"),
        P("ctx", "head"),
        P("head"),
        P("head"),
        P("ctx", "head", None),
    )
    return jax.shard_map(
        on_device,
        mesh=mesh,
        in_specs=placed,
        out_specs=(P("ctx", "head"), P("ctx", "head"), P("ctx", "head")),
        check_vma=False,
    )
```

```python
import functools
import math

import jax
import jax.numpy as jnp
from jax import lax
from jax.experimental import pallas as pl
from jax.experimental.pallas import tpu as pltpu
from jax.sharding import PartitionSpec as P

HD = 128
TILE = 128


epsilon = 1e-06


def split_heads(array, heads_dev):
    return array.reshape(array.shape[0], heads_dev, HD).transpose(1, 0, 2)


def merge_heads(array):
    heads_dev, tok_dev, depth = array.shape
    return array.transpose(1, 0, 2).reshape(tok_dev, heads_dev * depth)


def per_tile(array, qt_dev):
    heads_dev, tok_dev, depth = array.shape
    return array.reshape(heads_dev, qt_dev, TILE, depth).transpose(1, 0, 2, 3)


def from_tiles(array):
    qt_dev, heads_dev, rows_tile, depth = array.shape
    return array.transpose(1, 0, 2, 3).reshape(heads_dev, qt_dev * rows_tile, depth)


def table_sum(taken, pieces, heads_dev, qt_dev):
    flat_pieces = pieces.reshape(pieces.shape[0], -1)
    summed = jnp.dot(
        taken, flat_pieces, precision=lax.Precision.HIGHEST, preferred_element_type=jnp.float32
    )
    summed = summed.reshape(heads_dev, qt_dev, 2, TILE, HD).transpose(2, 0, 1, 3, 4)
    return summed.reshape(2, heads_dev, qt_dev * TILE, HD)


def rounded(array):
    return array.astype(jnp.bfloat16)


def finish_norm(wide, scale, gain, grad, dot_sum, width_all):
    return (scale * gain * grad - wide * scale**3 * (dot_sum / width_all)[:, None]).astype(
        jnp.bfloat16
    )


def tiles_to_queries(q_pre, k_pre, values, out_grad, q_gain, k_gain, selected):
    n_ctx = lax.axis_size("ctx")
    tok_dev, width_dev = q_pre.shape
    width_all = width_dev * lax.axis_size("head")
    heads_dev = width_dev // HD
    qt_dev = tok_dev // TILE
    remote_count = selected.shape[2]
    factor = 1.0 / math.sqrt(HD)
    q_wide = q_pre.astype(jnp.float32)
    k_wide = k_pre.astype(jnp.float32)
    q_square, k_square = lax.psum(
        (jnp.sum(q_wide * q_wide, axis=1), jnp.sum(k_wide * k_wide, axis=1)), "head"
    )
    q_scale = lax.rsqrt(q_square / width_all + epsilon)[:, None]
    k_scale = lax.rsqrt(k_square / width_all + epsilon)[:, None]
    q_heads = split_heads(rounded(q_wide * q_scale * q_gain), heads_dev)
    k_heads = split_heads(rounded(k_wide * k_scale * k_gain), heads_dev)
    v_heads = split_heads(values, heads_dev)
    g_heads = split_heads(out_grad, heads_dev)
    q_tiles = per_tile(q_heads, qt_dev)
    g_tiles = per_tile(g_heads, qt_dev)
    k_table = k_heads.reshape(heads_dev * qt_dev, TILE, HD)
    v_table = v_heads.reshape(heads_dev * qt_dev, TILE, HD)
    flat_sel = selected[0].reshape(-1)
    n_slot = flat_sel.shape[0]
    capacity = -(-n_slot // (n_ctx - 1))
    n_buffer = n_ctx * capacity
    owners = flat_sel // qt_dev
    head_of = jnp.arange(n_slot, dtype=jnp.int32) // remote_count
    codes = head_of * qt_dev + flat_sel % qt_dev
    matches = (owners[:, None] == jnp.arange(n_ctx, dtype=jnp.int32)[None, :]).astype(jnp.int32)
    ranks = jnp.sum((jnp.cumsum(matches, axis=0) - matches) * matches, axis=1)
    position = owners * capacity + ranks
    placed = position[None, :] == jnp.arange(n_buffer, dtype=jnp.int32)[:, None]
    request = jnp.sum(jnp.where(placed, codes[None, :] + 1, 0), axis=1) - 1
    asked = lax.all_to_all(
        request.reshape(n_ctx, capacity), "ctx", split_axis=0, concat_axis=0, tiled=True
    ).reshape(n_buffer)
    clipped = jnp.maximum(asked, 0)
    taken = (asked[None, :] == jnp.arange(heads_dev * qt_dev, dtype=jnp.int32)[:, None]).astype(
        jnp.float32
    )
    s_near = (
        jnp.einsum("rhqd,hkd->rhqk", q_tiles, k_heads, preferred_element_type=jnp.float32) * factor
    )
    dp_near = jnp.einsum("rhqd,hkd->rhqk", g_tiles, v_heads, preferred_element_type=jnp.float32)
    near_top = jnp.max(s_near, axis=-1)
    outgoing = jnp.stack((k_table[clipped], v_table[clipped]), axis=1).reshape(
        n_ctx, capacity, 2, TILE, HD
    )
    incoming = lax.all_to_all(outgoing, "ctx", split_axis=0, concat_axis=0, tiled=True).reshape(
        n_buffer, 2, TILE, HD
    )
    slot_kv = incoming[position].reshape(heads_dev, remote_count, 2, TILE, HD)
    far_k = slot_kv[:, :, 0]
    far_v = slot_kv[:, :, 1]
    s_far = (
        jnp.einsum("rhqd,hckd->rhqck", q_tiles, far_k, preferred_element_type=jnp.float32) * factor
    )
    dp_far = jnp.einsum("rhqd,hckd->rhqck", g_tiles, far_v, preferred_element_type=jnp.float32)
    row_top = jnp.maximum(near_top, jnp.max(s_far, axis=(-2, -1)))
    totals = jnp.sum(jnp.exp(s_near - row_top[..., None]), axis=-1) + jnp.sum(
        jnp.exp(s_far - row_top[..., None, None]), axis=(-2, -1)
    )
    lse = row_top + jnp.log(totals)
    p_near = jnp.exp(s_near - lse[..., None])
    p_far = jnp.exp(s_far - lse[..., None, None])
    delta = jnp.sum(p_near * dp_near, axis=-1) + jnp.sum(p_far * dp_far, axis=(-2, -1))
    ds_near = rounded(p_near * (dp_near - delta[..., None]) * factor)
    pb_near = rounded(p_near)
    dq_near = jnp.einsum("rhqk,hkd->rhqd", ds_near, k_heads, preferred_element_type=jnp.float32)
    dk_near = jnp.einsum("rhqk,rhqd->hkd", ds_near, q_tiles, preferred_element_type=jnp.float32)
    dv_near = jnp.einsum("rhqk,rhqd->hkd", pb_near, g_tiles, preferred_element_type=jnp.float32)
    dq_near, dk_near, dv_near = (dq_near, dk_near, dv_near)
    ds_far = rounded(p_far * (dp_far - delta[..., None, None]) * factor)
    pb_far = rounded(p_far)
    dq_far = jnp.einsum("rhqck,hckd->rhqd", ds_far, far_k, preferred_element_type=jnp.float32)
    dq_wide = merge_heads(from_tiles(dq_near + dq_far))
    q_dot = jnp.sum(q_gain * dq_wide * q_wide, axis=1)
    dq_wide, q_dot = (dq_wide, q_dot)
    dk_far = jnp.einsum("rhqck,rhqd->hckd", ds_far, q_tiles, preferred_element_type=jnp.float32)
    dv_far = jnp.einsum("rhqck,rhqd->hckd", pb_far, g_tiles, preferred_element_type=jnp.float32)
    grads = jnp.stack((dk_far, dv_far), axis=2).reshape(n_slot, 2, TILE, HD)
    sending = jnp.zeros((n_buffer, 2, TILE, HD), jnp.float32).at[position].set(grads)
    returned = lax.all_to_all(
        sending.reshape(n_ctx, capacity, 2, TILE, HD),
        "ctx",
        split_axis=0,
        concat_axis=0,
        tiled=True,
    ).reshape(n_buffer, 2, TILE, HD)
    far_sums = table_sum(taken, returned, heads_dev, qt_dev)
    dk_wide = merge_heads(dk_near + far_sums[0])
    dv_heads = dv_near + far_sums[1]
    k_dot = jnp.sum(k_gain * dk_wide * k_wide, axis=1)
    q_dot, k_dot = lax.psum((q_dot, k_dot), "head")
    dq_result = finish_norm(q_wide, q_scale, q_gain, dq_wide, q_dot, width_all)
    dk_result = finish_norm(k_wide, k_scale, k_gain, dk_wide, k_dot, width_all)
    return (dq_result, dk_result, merge_heads(dv_heads).astype(jnp.bfloat16))


VMEM_BYTES = 48 * 2**20
NT = (((1,), (1,)), ((), ()))
IN_VMEM = pl.BlockSpec(memory_space=pltpu.VMEM)
IN_SMEM = pl.BlockSpec(memory_space=pltpu.SMEM)


def owners_of(group, n_ctx, heads_dev):
    places = [(4 * head + 1) * n_ctx // (4 * heads_dev) for head in range(heads_dev)]
    return [n_ctx - 1 - place if group % 2 else place for place in places]


def head_at(place, group, n_ctx, heads_dev):
    even = jnp.where(group % 2 == 1, n_ctx - 1 - place, place)
    head = -1
    for index, owner in enumerate(owners_of(0, n_ctx, heads_dev)):
        head = jnp.where(even == owner, index, head)
    return head


def pairs_to_owner(mask, n_ctx, n_head, heads_dev):
    pairs = []
    for group in range(n_head):
        owners = owners_of(group, n_ctx, heads_dev)
        for block in range(n_ctx):
            if block ^ mask in owners:
                pairs.append((block * n_head + group, (block ^ mask) * n_head + group))
    return pairs


def to_owners(arrays, n_ctx, n_head, heads_dev):
    moved = list(arrays)
    for mask in range(n_ctx - 1, 0, -1):
        pairs = pairs_to_owner(mask, n_ctx, n_head, heads_dev)
        moved[mask] = lax.ppermute(arrays[mask], ("ctx", "head"), pairs)
    return moved


def from_owners(arrays, n_ctx, n_head, heads_dev):
    moved = list(arrays)
    for mask in range(n_ctx - 1, 0, -1):
        pairs = [(b, a) for a, b in pairs_to_owner(mask, n_ctx, n_head, heads_dev)]
        moved[mask] = lax.ppermute(arrays[mask], ("ctx", "head"), pairs)
    return moved


def column(row, width):
    return jnp.broadcast_to(row, (width, row.shape[1])).T


def row_sums(wide):
    total = wide[:, :HD]
    for at in range(HD, wide.shape[1], HD):
        total = total + wide[:, at : at + HD]
    return jnp.sum(total.T, axis=0, keepdims=True)


def pack_kernel(n_ctx, heads_dev, *refs):
    inputs, outs, sems = refs[:4], refs[4:-1], refs[-1]
    block, group = lax.axis_index("ctx"), lax.axis_index("head")
    heads = [head_at(block ^ mask, group, n_ctx, heads_dev) for mask in range(n_ctx)]

    def copies(mask):
        place = pl.ds(pl.multiple_of(heads[mask] * HD, HD), HD)
        return [
            pltpu.make_async_copy(ref.at[:, place], outs[mask].at[at], sems.at[mask, at])
            for at, ref in enumerate(inputs)
        ]

    for mask in range(n_ctx - 1, -1, -1):

        @pl.when(heads[mask] >= 0)
        def _(mask=mask):
            for copy in copies(mask):
                copy.start()

    for mask in range(n_ctx - 1, -1, -1):

        @pl.when(heads[mask] >= 0)
        def _(mask=mask):
            for copy in copies(mask):
                copy.wait()


def pack(arrays, n_ctx):
    rows, width_dev = arrays[0].shape
    return pl.pallas_call(
        functools.partial(pack_kernel, n_ctx, width_dev // HD),
        out_shape=[jax.ShapeDtypeStruct((4, rows, HD), jnp.bfloat16)] * n_ctx,
        in_specs=[pl.BlockSpec(memory_space=pltpu.HBM)] * 4,
        out_specs=[pl.BlockSpec(memory_space=pltpu.HBM)] * n_ctx,
        scratch_shapes=[pltpu.SemaphoreType.DMA((n_ctx, 4))],
        compiler_params=pltpu.CompilerParams(vmem_limit_bytes=62 * 2**20),
    )(*arrays)


def squares_kernel(q_ref, k_ref, square_ref):
    for at, ref in enumerate((q_ref, k_ref)):
        wide = ref[...].astype(jnp.float32)
        square_ref[at : at + 1, :] = row_sums(wide * wide)


def attend_kernel(n_ctx, heads_dev, picks, scale_ref, q_gain, k_gain, *refs):
    messages, outs = refs[:n_ctx][::-1], refs[n_ctx : 2 * n_ctx]
    dot_ref, scratch = refs[2 * n_ctx], refs[2 * n_ctx + 1 :]
    q_ref, g_ref, k_ref, kt_ref, v_ref, dq_ref, dk_ref, dv_ref, ds_ref, kt_picked = scratch[:10]
    buffers = (scratch[10:13], scratch[13:16])
    rows = messages[0].shape[1]
    remote_count = picks.shape[1]
    near = rows // TILE
    n_keys = near + remote_count
    factor = 1.0 / math.sqrt(HD)
    to_base2 = factor * math.log2(math.e)
    own_block = lax.axis_index("ctx")
    own_head = head_at(own_block, lax.axis_index("head"), n_ctx, heads_dev)

    def rows_of(block):
        return pl.ds(pl.multiple_of(block * rows, rows), rows)

    def places_of(block):
        return [
            pl.ds(pl.multiple_of(block * rows + tile * TILE, TILE), TILE) for tile in range(near)
        ] + [
            pl.ds(pl.multiple_of(picks[block, slot] * TILE, TILE), TILE)
            for slot in range(remote_count)
        ]

    def prepare(mask):
        block = own_block ^ mask
        place = rows_of(block)
        q_scale = column(scale_ref[block, 0:1, :], HD)
        k_scale = column(scale_ref[block, 1:2, :], HD)
        q_normed = messages[mask][0].astype(jnp.float32) * q_scale * q_gain[pl.ds(own_head, 1), :]
        k_normed = messages[mask][1].astype(jnp.float32) * k_scale * k_gain[pl.ds(own_head, 1), :]
        q_ref[mask] = q_normed.astype(jnp.bfloat16)
        k_ref[place, :] = k_normed.astype(jnp.bfloat16)
        kt_ref[:, place] = k_normed.T.astype(jnp.bfloat16)
        v_ref[place, :] = messages[mask][2]
        g_ref[mask] = messages[mask][3]

    def scores(mask, slot, place, buffer):
        weight_ref, dprob_ref, stat_ref = buffer
        score = lax.dot_general(
            k_ref[place, :], q_ref[mask], NT, preferred_element_type=jnp.float32
        )
        dprob = lax.dot_general(
            v_ref[place, :], g_ref[mask], NT, preferred_element_type=jnp.float32
        )
        top = jnp.max(score, axis=0, keepdims=True)
        weight = jnp.exp2((score - top) * to_base2)
        weight_ref[slot] = weight
        dprob_ref[slot] = dprob
        stat_ref[0, slot : slot + 1, :] = top * to_base2
        stat_ref[1, slot : slot + 1, :] = jnp.sum(weight, axis=0, keepdims=True)
        stat_ref[2, slot : slot + 1, :] = jnp.sum(weight * dprob, axis=0, keepdims=True)

    def settle(buffer):
        stat_ref = buffer[2]
        tops = stat_ref[0, :n_keys, :]
        shares = jnp.exp2(tops - jnp.max(tops, axis=0, keepdims=True))
        total = jnp.sum(shares * stat_ref[1, :n_keys, :], axis=0, keepdims=True)
        mixed = jnp.sum(shares * stat_ref[2, :n_keys, :], axis=0, keepdims=True)
        inverse = 1.0 / total
        return shares * inverse, mixed * inverse

    def gradients(mask, slot, place, buffer, shares, delta):
        weight_ref, dprob_ref, _ = buffer
        prob = weight_ref[slot] * shares[slot : slot + 1, :]
        dscore = (prob * (dprob_ref[slot] - delta)).astype(jnp.bfloat16)
        ds_ref[slot * TILE : (slot + 1) * TILE, :] = dscore
        kt_picked[:, slot * TILE : (slot + 1) * TILE] = kt_ref[:, place]
        dk_ref[place, :] += jnp.dot(dscore, q_ref[mask], preferred_element_type=jnp.float32)
        dv_ref[place, :] += jnp.dot(
            prob.astype(jnp.bfloat16), g_ref[mask], preferred_element_type=jnp.float32
        )

    def query_gradient(mask):
        dq_t = jnp.dot(kt_picked[...], ds_ref[...], preferred_element_type=jnp.float32)
        dq_ref[mask] = (dq_t * factor).T

    def step(mask, buffer, later, later_buffer):
        places = places_of(own_block ^ mask)
        shares, delta = settle(buffer)
        later_places = None if later is None else places_of(own_block ^ later)
        for slot in range(n_keys):
            gradients(mask, slot, places[slot], buffer, shares, delta)
            if later is not None:
                scores(later, slot, later_places[slot], later_buffer)
        query_gradient(mask)

    def send(mask):
        block = own_block ^ mask
        place = rows_of(block)
        dq = dq_ref[mask]
        dk = dk_ref[place, :] * factor
        outs[mask][0] = dq.astype(jnp.bfloat16)
        outs[mask][1] = dk.astype(jnp.bfloat16)
        outs[mask][2] = dv_ref[place, :].astype(jnp.bfloat16)
        for at, (grad, gain) in enumerate(((dq, q_gain), (dk, k_gain))):
            pre = messages[mask][at].astype(jnp.float32)
            dot_ref[block, at : at + 1, :] = row_sums(gain[pl.ds(own_head, 1), :] * grad * pre)

    @pl.when(own_head < 0)
    def _():
        dot_ref[...] = jnp.zeros_like(dot_ref)

    @pl.when(own_head >= 0)
    def _():
        for mask in range(n_ctx):
            prepare(mask)
        dk_ref[...] = jnp.zeros_like(dk_ref)
        dv_ref[...] = jnp.zeros_like(dv_ref)
        for slot, place in enumerate(places_of(own_block)):
            scores(0, slot, place, buffers[0])

        def two(pair, carry):
            step(2 * pair, buffers[0], 2 * pair + 1, buffers[1])
            step(2 * pair + 1, buffers[1], 2 * pair + 2, buffers[0])
            return carry

        lax.fori_loop(0, n_ctx // 2 - 1, two, 0)
        step(n_ctx - 2, buffers[0], n_ctx - 1, buffers[1])
        step(n_ctx - 1, buffers[1], None, None)
        for mask in range(n_ctx):
            send(mask)


def attend(picks, scales, q_gain, k_gain, messages, n_ctx):
    rows = messages[0].shape[1]
    tokens = n_ctx * rows
    n_keys = rows // TILE + picks.shape[1]
    by_block = pltpu.VMEM((n_ctx, rows, HD), jnp.bfloat16)
    buffer = [
        pltpu.VMEM((n_keys, TILE, rows), jnp.float32),
        pltpu.VMEM((n_keys, TILE, rows), jnp.float32),
        pltpu.VMEM((3, -(-n_keys // 8) * 8, rows), jnp.float32),
    ]
    return pl.pallas_call(
        functools.partial(attend_kernel, n_ctx, q_gain.shape[0]),
        out_shape=[jax.ShapeDtypeStruct((3, rows, HD), jnp.bfloat16)] * n_ctx
        + [jax.ShapeDtypeStruct((n_ctx, 2, rows), jnp.float32)],
        in_specs=[IN_SMEM] + [IN_VMEM] * (3 + n_ctx),
        out_specs=[IN_VMEM] * (n_ctx + 1),
        scratch_shapes=[
            by_block,
            by_block,
            pltpu.VMEM((tokens, HD), jnp.bfloat16),
            pltpu.VMEM((HD, tokens), jnp.bfloat16),
            pltpu.VMEM((tokens, HD), jnp.bfloat16),
            pltpu.VMEM((n_ctx, rows, HD), jnp.float32),
            pltpu.VMEM((tokens, HD), jnp.float32),
            pltpu.VMEM((tokens, HD), jnp.float32),
            pltpu.VMEM((n_keys * TILE, rows), jnp.bfloat16),
            pltpu.VMEM((HD, n_keys * TILE), jnp.bfloat16),
        ]
        + buffer
        + buffer,
        compiler_params=pltpu.CompilerParams(vmem_limit_bytes=VMEM_BYTES),
    )(picks, scales, q_gain, k_gain, *messages[::-1])


def finish_kernel(n_ctx, heads_dev, width_all, q_ref, k_ref, q_gain, k_gain, *refs):
    scale_ref, dot_ref = refs[:2]
    slots = refs[2 : 2 + n_ctx][::-1]
    dq_out, dk_out, dv_out = refs[2 + n_ctx :]
    block, group = lax.axis_index("ctx"), lax.axis_index("head")
    scales, backs = [], []
    for at in range(2):
        scale_row = scale_ref[block, at : at + 1, :]
        scales.append(column(scale_row, HD))
        backs.append(column(scale_row**3 * (dot_ref[at : at + 1, :] / width_all), HD))
    for mask in range(n_ctx):
        head = head_at(block ^ mask, group, n_ctx, heads_dev)

        @pl.when(head >= 0)
        def _(mask=mask, head=head):
            place = pl.ds(pl.multiple_of(head * HD, HD), HD)
            for at, (pre_ref, gain, out) in enumerate(
                ((q_ref, q_gain, dq_out), (k_ref, k_gain, dk_out))
            ):
                wide = pre_ref[:, place].astype(jnp.float32)
                grad = slots[mask][at].astype(jnp.float32)
                scaled = scales[at] * gain[pl.ds(head, 1), :] * grad
                out[:, place] = (scaled - wide * backs[at]).astype(jnp.bfloat16)
            dv_out[:, place] = slots[mask][2]


def heads_to_owners(q_pre, k_pre, values, out_grad, q_gain, k_gain, selected):
    n_ctx = lax.axis_size("ctx")
    n_head = lax.axis_size("head")
    rows, width_dev = q_pre.shape
    width_all = width_dev * n_head
    heads_dev = width_dev // HD
    remote_count = selected.shape[2]
    sizes = (n_ctx, n_head, heads_dev)
    params = pltpu.CompilerParams(vmem_limit_bytes=VMEM_BYTES)

    sent = pack((q_pre, k_pre, values, out_grad), n_ctx)
    messages = to_owners(sent, *sizes)

    squares = pl.pallas_call(
        squares_kernel,
        out_shape=jax.ShapeDtypeStruct((2, rows), jnp.float32),
        in_specs=[IN_VMEM] * 2,
        out_specs=IN_VMEM,
        compiler_params=params,
    )(q_pre, k_pre)
    squares, messages[1] = lax.optimization_barrier((squares, messages[1]))
    wishes = selected[0].reshape(1, -1).astype(jnp.float32)
    wishes = jnp.pad(wishes, ((0, 0), (0, rows - wishes.shape[1])))
    small = jnp.concatenate((lax.psum(squares, "head"), wishes), axis=0)
    small = jnp.broadcast_to(small[None], (n_ctx,) + small.shape)
    small = lax.all_to_all(small, "ctx", split_axis=0, concat_axis=0, tiled=True)
    scales = lax.rsqrt(small[:, :2] / width_all + epsilon)
    own_head = head_at(lax.axis_index("ctx"), lax.axis_index("head"), n_ctx, heads_dev)
    first = jnp.maximum(own_head, 0) * remote_count
    picks = lax.dynamic_slice_in_dim(small[:, 2], first, remote_count, 1).astype(jnp.int32)

    q_gains = q_gain.reshape(heads_dev, HD)
    k_gains = k_gain.reshape(heads_dev, HD)
    *results, dots = attend(picks, scales, q_gains, k_gains, messages, n_ctx)
    slots = from_owners(results, *sizes)

    dots = lax.all_to_all(dots, "ctx", split_axis=0, concat_axis=0, tiled=True)
    dots = lax.psum(jnp.sum(dots, axis=0), "head")

    return pl.pallas_call(
        functools.partial(finish_kernel, n_ctx, heads_dev, width_all),
        out_shape=[jax.ShapeDtypeStruct((rows, width_dev), jnp.bfloat16)] * 3,
        in_specs=[IN_VMEM] * (6 + n_ctx),
        out_specs=[IN_VMEM] * 3,
        compiler_params=params,
    )(q_pre, k_pre, q_gains, k_gains, scales, dots, *slots[::-1])


def on_device(q_pre, k_pre, values, out_grad, q_gain, k_gain, selected):
    n_ctx = lax.axis_size("ctx")
    tiles_dev, heads_dev, remote_count = selected.shape
    capacity = -(-heads_dev * remote_count // (n_ctx - 1))
    by_head = (n_ctx - 1) * tiles_dev * 7
    by_tile = (n_ctx - 1) * capacity * 6
    paired = n_ctx & (n_ctx - 1) == 0 and n_ctx >= max(heads_dev, 4)
    plan = heads_to_owners if paired and by_head <= by_tile else tiles_to_queries
    return plan(q_pre, k_pre, values, out_grad, q_gain, k_gain, selected)


def solution(mesh):
    placed = (
        P("ctx", "head"),
        P("ctx", "head"),
        P("ctx", "head"),
        P("ctx", "head"),
        P("head"),
        P("head"),
        P("ctx", "head", None),
    )
    return jax.shard_map(
        on_device,
        mesh=mesh,
        in_specs=placed,
        out_specs=(P("ctx", "head"), P("ctx", "head"), P("ctx", "head")),
        check_vma=False,
    )
```

```python
import functools
import math

import jax
import jax.numpy as jnp
from jax import lax
from jax.experimental import pallas as pl
from jax.experimental.pallas import tpu as pltpu
from jax.sharding import PartitionSpec as P

HD = 128
TILE = 128


epsilon = 1e-06


def split_heads(array, heads_dev):
    return array.reshape(array.shape[0], heads_dev, HD).transpose(1, 0, 2)


def merge_heads(array):
    heads_dev, tok_dev, depth = array.shape
    return array.transpose(1, 0, 2).reshape(tok_dev, heads_dev * depth)


def per_tile(array, qt_dev):
    heads_dev, tok_dev, depth = array.shape
    return array.reshape(heads_dev, qt_dev, TILE, depth).transpose(1, 0, 2, 3)


def from_tiles(array):
    qt_dev, heads_dev, rows_tile, depth = array.shape
    return array.transpose(1, 0, 2, 3).reshape(heads_dev, qt_dev * rows_tile, depth)


def table_sum(taken, pieces, heads_dev, qt_dev):
    flat_pieces = pieces.reshape(pieces.shape[0], -1)
    summed = jnp.dot(
        taken, flat_pieces, precision=lax.Precision.HIGHEST, preferred_element_type=jnp.float32
    )
    summed = summed.reshape(heads_dev, qt_dev, 2, TILE, HD).transpose(2, 0, 1, 3, 4)
    return summed.reshape(2, heads_dev, qt_dev * TILE, HD)


def rounded(array):
    return array.astype(jnp.bfloat16)


def finish_norm(wide, scale, gain, grad, dot_sum, width_all):
    return (scale * gain * grad - wide * scale**3 * (dot_sum / width_all)[:, None]).astype(
        jnp.bfloat16
    )


def tiles_to_queries(q_pre, k_pre, values, out_grad, q_gain, k_gain, selected):
    n_ctx = lax.axis_size("ctx")
    tok_dev, width_dev = q_pre.shape
    width_all = width_dev * lax.axis_size("head")
    heads_dev = width_dev // HD
    qt_dev = tok_dev // TILE
    remote_count = selected.shape[2]
    factor = 1.0 / math.sqrt(HD)
    q_wide = q_pre.astype(jnp.float32)
    k_wide = k_pre.astype(jnp.float32)
    q_square, k_square = lax.psum(
        (jnp.sum(q_wide * q_wide, axis=1), jnp.sum(k_wide * k_wide, axis=1)), "head"
    )
    q_scale = lax.rsqrt(q_square / width_all + epsilon)[:, None]
    k_scale = lax.rsqrt(k_square / width_all + epsilon)[:, None]
    q_heads = split_heads(rounded(q_wide * q_scale * q_gain), heads_dev)
    k_heads = split_heads(rounded(k_wide * k_scale * k_gain), heads_dev)
    v_heads = split_heads(values, heads_dev)
    g_heads = split_heads(out_grad, heads_dev)
    q_tiles = per_tile(q_heads, qt_dev)
    g_tiles = per_tile(g_heads, qt_dev)
    k_table = k_heads.reshape(heads_dev * qt_dev, TILE, HD)
    v_table = v_heads.reshape(heads_dev * qt_dev, TILE, HD)
    flat_sel = selected[0].reshape(-1)
    n_slot = flat_sel.shape[0]
    capacity = -(-n_slot // (n_ctx - 1))
    n_buffer = n_ctx * capacity
    owners = flat_sel // qt_dev
    head_of = jnp.arange(n_slot, dtype=jnp.int32) // remote_count
    codes = head_of * qt_dev + flat_sel % qt_dev
    matches = (owners[:, None] == jnp.arange(n_ctx, dtype=jnp.int32)[None, :]).astype(jnp.int32)
    ranks = jnp.sum((jnp.cumsum(matches, axis=0) - matches) * matches, axis=1)
    position = owners * capacity + ranks
    placed = position[None, :] == jnp.arange(n_buffer, dtype=jnp.int32)[:, None]
    request = jnp.sum(jnp.where(placed, codes[None, :] + 1, 0), axis=1) - 1
    asked = lax.all_to_all(
        request.reshape(n_ctx, capacity), "ctx", split_axis=0, concat_axis=0, tiled=True
    ).reshape(n_buffer)
    clipped = jnp.maximum(asked, 0)
    taken = (asked[None, :] == jnp.arange(heads_dev * qt_dev, dtype=jnp.int32)[:, None]).astype(
        jnp.float32
    )
    s_near = (
        jnp.einsum("rhqd,hkd->rhqk", q_tiles, k_heads, preferred_element_type=jnp.float32) * factor
    )
    dp_near = jnp.einsum("rhqd,hkd->rhqk", g_tiles, v_heads, preferred_element_type=jnp.float32)
    near_top = jnp.max(s_near, axis=-1)
    outgoing = jnp.stack((k_table[clipped], v_table[clipped]), axis=1).reshape(
        n_ctx, capacity, 2, TILE, HD
    )
    incoming = lax.all_to_all(outgoing, "ctx", split_axis=0, concat_axis=0, tiled=True).reshape(
        n_buffer, 2, TILE, HD
    )
    slot_kv = incoming[position].reshape(heads_dev, remote_count, 2, TILE, HD)
    far_k = slot_kv[:, :, 0]
    far_v = slot_kv[:, :, 1]
    s_far = (
        jnp.einsum("rhqd,hckd->rhqck", q_tiles, far_k, preferred_element_type=jnp.float32) * factor
    )
    dp_far = jnp.einsum("rhqd,hckd->rhqck", g_tiles, far_v, preferred_element_type=jnp.float32)
    row_top = jnp.maximum(near_top, jnp.max(s_far, axis=(-2, -1)))
    totals = jnp.sum(jnp.exp(s_near - row_top[..., None]), axis=-1) + jnp.sum(
        jnp.exp(s_far - row_top[..., None, None]), axis=(-2, -1)
    )
    lse = row_top + jnp.log(totals)
    p_near = jnp.exp(s_near - lse[..., None])
    p_far = jnp.exp(s_far - lse[..., None, None])
    delta = jnp.sum(p_near * dp_near, axis=-1) + jnp.sum(p_far * dp_far, axis=(-2, -1))
    ds_near = rounded(p_near * (dp_near - delta[..., None]) * factor)
    pb_near = rounded(p_near)
    dq_near = jnp.einsum("rhqk,hkd->rhqd", ds_near, k_heads, preferred_element_type=jnp.float32)
    dk_near = jnp.einsum("rhqk,rhqd->hkd", ds_near, q_tiles, preferred_element_type=jnp.float32)
    dv_near = jnp.einsum("rhqk,rhqd->hkd", pb_near, g_tiles, preferred_element_type=jnp.float32)
    dq_near, dk_near, dv_near = (dq_near, dk_near, dv_near)
    ds_far = rounded(p_far * (dp_far - delta[..., None, None]) * factor)
    pb_far = rounded(p_far)
    dq_far = jnp.einsum("rhqck,hckd->rhqd", ds_far, far_k, preferred_element_type=jnp.float32)
    dq_wide = merge_heads(from_tiles(dq_near + dq_far))
    q_dot = jnp.sum(q_gain * dq_wide * q_wide, axis=1)
    dq_wide, q_dot = (dq_wide, q_dot)
    dk_far = jnp.einsum("rhqck,rhqd->hckd", ds_far, q_tiles, preferred_element_type=jnp.float32)
    dv_far = jnp.einsum("rhqck,rhqd->hckd", pb_far, g_tiles, preferred_element_type=jnp.float32)
    grads = jnp.stack((dk_far, dv_far), axis=2).reshape(n_slot, 2, TILE, HD)
    sending = jnp.zeros((n_buffer, 2, TILE, HD), jnp.float32).at[position].set(grads)
    returned = lax.all_to_all(
        sending.reshape(n_ctx, capacity, 2, TILE, HD),
        "ctx",
        split_axis=0,
        concat_axis=0,
        tiled=True,
    ).reshape(n_buffer, 2, TILE, HD)
    far_sums = table_sum(taken, returned, heads_dev, qt_dev)
    dk_wide = merge_heads(dk_near + far_sums[0])
    dv_heads = dv_near + far_sums[1]
    k_dot = jnp.sum(k_gain * dk_wide * k_wide, axis=1)
    q_dot, k_dot = lax.psum((q_dot, k_dot), "head")
    dq_result = finish_norm(q_wide, q_scale, q_gain, dq_wide, q_dot, width_all)
    dk_result = finish_norm(k_wide, k_scale, k_gain, dk_wide, k_dot, width_all)
    return (dq_result, dk_result, merge_heads(dv_heads).astype(jnp.bfloat16))


VMEM_BYTES = 48 * 2**20
PICK_ROWS = 16
NT = (((1,), (1,)), ((), ()))
IN_VMEM = pl.BlockSpec(memory_space=pltpu.VMEM)
IN_SMEM = pl.BlockSpec(memory_space=pltpu.SMEM)


def owners_of(group, n_ctx, heads_dev):
    places = [(4 * head + 1) * n_ctx // (4 * heads_dev) for head in range(heads_dev)]
    return [n_ctx - 1 - place if group % 2 else place for place in places]


def head_at(place, group, n_ctx, heads_dev):
    even = jnp.where(group % 2 == 1, n_ctx - 1 - place, place)
    head = -1
    for index, owner in enumerate(owners_of(0, n_ctx, heads_dev)):
        head = jnp.where(even == owner, index, head)
    return head


def pairs_to_owner(mask, n_ctx, n_head, heads_dev):
    pairs = []
    for group in range(n_head):
        owners = owners_of(group, n_ctx, heads_dev)
        for block in range(n_ctx):
            if block ^ mask in owners:
                pairs.append((block * n_head + group, (block ^ mask) * n_head + group))
    return pairs


def mask_order(n_ctx):
    half = n_ctx // 2
    masks = [1, 3] + list(range(n_ctx - 1, half - 1, -1)) + list(range(half - 1, 0, -1)) + [0]
    return list(dict.fromkeys(masks))


def move(arrays, back, n_ctx, n_head, heads_dev):
    moved = []
    for mask, array in zip(mask_order(n_ctx), arrays):
        pairs = pairs_to_owner(mask, n_ctx, n_head, heads_dev)
        if back:
            pairs = [(b, a) for a, b in pairs]
        moved.append(lax.ppermute(array, ("ctx", "head"), pairs) if mask else array)
    return moved


def column(row, width):
    return jnp.broadcast_to(row, (width, row.shape[1])).T


def row_sums(wide):
    total = wide[:, :HD]
    for at in range(HD, wide.shape[1], HD):
        total = total + wide[:, at : at + HD]
    return jnp.sum(total.T, axis=0, keepdims=True)


def squares_kernel(q_ref, k_ref, square_ref):
    for at, ref in enumerate((q_ref, k_ref)):
        wide = ref[...].astype(jnp.float32)
        square_ref[at : at + 1, :] = row_sums(wide * wide)


def row_scales(square_ref, width_all):
    return lax.rsqrt(square_ref[...] / width_all + epsilon)


def pack_kernel(n_ctx, width_all, sel, square_ref, q_gain, k_gain, q_ref, k_ref, v_ref, g_ref, *outs):
    heads_dev, remote_count = sel.shape[1:]
    rows = q_ref.shape[0]
    block, group = lax.axis_index("ctx"), lax.axis_index("head")
    scale_rows = row_scales(square_ref, width_all)
    scales = [column(scale_rows[at : at + 1, :], HD) for at in range(2)]
    lane = lax.broadcasted_iota(jnp.int32, (PICK_ROWS, HD), 1)
    for mask, out in zip(mask_order(n_ctx), outs):
        head = head_at(block ^ mask, group, n_ctx, heads_dev)

        @pl.when(head >= 0)
        def _(head=head, out=out):
            place = pl.ds(pl.multiple_of(head * HD, HD), HD)
            for at, (ref, gain) in enumerate(((q_ref, q_gain), (k_ref, k_gain))):
                normed = ref[:, place].astype(jnp.float32) * scales[at] * gain[pl.ds(head, 1), :]
                out[at * rows : (at + 1) * rows, :] = normed.astype(jnp.bfloat16)
            out[2 * rows : 3 * rows, :] = v_ref[:, place]
            out[3 * rows : 4 * rows, :] = g_ref[:, place]
            picks = jnp.zeros((PICK_ROWS, HD), jnp.float32)
            for slot in range(remote_count):
                picks = jnp.where(lane == slot, sel[0, head, slot].astype(jnp.float32), picks)
            out[4 * rows :, :] = picks.astype(jnp.bfloat16)


def attend_kernel(n_ctx, heads_dev, remote_count, *refs):
    order = mask_order(n_ctx)
    messages = dict(zip(order, refs[:n_ctx]))
    outs = dict(zip(order, refs[n_ctx : 2 * n_ctx]))
    scratch = refs[2 * n_ctx :]
    q_ref, g_ref, k_ref, kt_ref, v_ref, dq_ref, dk_ref, dv_ref = scratch[:8]
    ds_ref, pb_ref, kt_picked, k_picked, v_picked = scratch[8:13]
    picks_ref, picks, sem = scratch[13:16]
    buffers = (scratch[16:19], scratch[19:22])
    rows = q_ref.shape[1]
    near = rows // TILE
    n_keys = near + remote_count
    factor = 1.0 / math.sqrt(HD)
    to_base2 = factor * math.log2(math.e)
    own_block = lax.axis_index("ctx")
    own_head = head_at(own_block, lax.axis_index("head"), n_ctx, heads_dev)

    def rows_of(block):
        return pl.ds(pl.multiple_of(block * rows, rows), rows)

    def places_of(mask):
        block = own_block ^ mask
        return [
            pl.ds(pl.multiple_of(block * rows + tile * TILE, TILE), TILE) for tile in range(near)
        ] + [
            pl.ds(pl.multiple_of(picks[mask, slot] * TILE, TILE), TILE)
            for slot in range(remote_count)
        ]

    def tile(slot):
        return slice(slot * TILE, (slot + 1) * TILE)

    def prepare(mask):
        message = messages[mask]
        place = rows_of(own_block ^ mask)
        q_ref[mask] = message[:rows, :]
        keys = message[rows : 2 * rows, :]
        k_ref[place, :] = keys
        kt_ref[:, place] = keys.T
        v_ref[place, :] = message[2 * rows : 3 * rows, :]
        g_ref[mask] = message[3 * rows : 4 * rows, :]

    def scores(mask, buffer):
        weight_ref, dprob_ref, stat_ref = buffer
        for slot, place in enumerate(places_of(mask)):
            k_picked[tile(slot), :] = k_ref[place, :]
            v_picked[tile(slot), :] = v_ref[place, :]
        score_all = lax.dot_general(
            k_picked[...], q_ref[mask], NT, preferred_element_type=jnp.float32
        )
        dprob_all = lax.dot_general(
            v_picked[...], g_ref[mask], NT, preferred_element_type=jnp.float32
        )
        for slot in range(n_keys):
            score = score_all[tile(slot), :]
            dprob = dprob_all[tile(slot), :]
            top = jnp.max(score, axis=0, keepdims=True)
            weight = jnp.exp2((score - top) * to_base2)
            weight_ref[slot] = weight
            dprob_ref[slot] = dprob
            stat_ref[0, slot : slot + 1, :] = top * to_base2
            stat_ref[1, slot : slot + 1, :] = jnp.sum(weight, axis=0, keepdims=True)
            stat_ref[2, slot : slot + 1, :] = jnp.sum(weight * dprob, axis=0, keepdims=True)

    def settle(buffer):
        stat_ref = buffer[2]
        tops = stat_ref[0, :n_keys, :]
        shares = jnp.exp2(tops - jnp.max(tops, axis=0, keepdims=True))
        total = jnp.sum(shares * stat_ref[1, :n_keys, :], axis=0, keepdims=True)
        mixed = jnp.sum(shares * stat_ref[2, :n_keys, :], axis=0, keepdims=True)
        inverse = 1.0 / total
        return shares * inverse, mixed * inverse

    def score_gradients(mask, buffer):
        weight_ref, dprob_ref, _ = buffer
        shares, delta = settle(buffer)
        for slot, place in enumerate(places_of(mask)):
            prob = weight_ref[slot] * shares[slot : slot + 1, :]
            pb_ref[tile(slot), :] = prob.astype(jnp.bfloat16)
            ds_ref[tile(slot), :] = (prob * (dprob_ref[slot] - delta)).astype(jnp.bfloat16)
            kt_picked[:, tile(slot)] = kt_ref[:, place]

    def products(mask):
        places = places_of(mask)
        dk = jnp.dot(ds_ref[...], q_ref[mask], preferred_element_type=jnp.float32)
        for slot, place in enumerate(places):
            dk_ref[place, :] += dk[tile(slot), :]
        dv = jnp.dot(pb_ref[...], g_ref[mask], preferred_element_type=jnp.float32)
        for slot, place in enumerate(places):
            dv_ref[place, :] += dv[tile(slot), :]
        dq_t = jnp.dot(kt_picked[...], ds_ref[...], preferred_element_type=jnp.float32)
        dq_ref[mask] = (dq_t * factor).T.astype(jnp.bfloat16)

    @pl.when(own_head >= 0)
    def _():
        for mask in range(n_ctx):
            picked = messages[mask][4 * rows :, :].astype(jnp.float32).astype(jnp.int32)
            picks_ref[mask : mask + 1, :] = picked[:1, :]
        copy = pltpu.make_async_copy(picks_ref, picks, sem)
        copy.start()
        for mask in range(n_ctx):
            prepare(mask)
        dk_ref[...] = jnp.zeros_like(dk_ref)
        dv_ref[...] = jnp.zeros_like(dv_ref)
        copy.wait()
        scores(0, buffers[0])

        def two(pair, carry):
            for half in range(2):
                mask = 2 * pair + half
                score_gradients(mask, buffers[half])
                scores(mask + 1, buffers[1 - half])
                products(mask)
            return carry

        lax.fori_loop(0, n_ctx // 2 - 1, two, 0)
        score_gradients(n_ctx - 2, buffers[0])
        scores(n_ctx - 1, buffers[1])
        products(n_ctx - 2)
        score_gradients(n_ctx - 1, buffers[1])
        products(n_ctx - 1)
        for mask in range(n_ctx):
            place = rows_of(own_block ^ mask)
            outs[mask][0] = dq_ref[mask]
            outs[mask][1] = (dk_ref[place, :] * factor).astype(jnp.bfloat16)
            outs[mask][2] = dv_ref[place, :].astype(jnp.bfloat16)


def attend(messages, heads_dev, remote_count):
    n_ctx = len(messages)
    rows = (messages[0].shape[0] - PICK_ROWS) // 4
    tokens = n_ctx * rows
    n_keys = rows // TILE + remote_count
    by_block = pltpu.VMEM((n_ctx, rows, HD), jnp.bfloat16)
    picked = pltpu.VMEM((n_keys * TILE, HD), jnp.bfloat16)
    scored = pltpu.VMEM((n_keys * TILE, rows), jnp.bfloat16)
    buffer = [
        pltpu.VMEM((n_keys, TILE, rows), jnp.float32),
        pltpu.VMEM((n_keys, TILE, rows), jnp.float32),
        pltpu.VMEM((3, -(-n_keys // 8) * 8, rows), jnp.float32),
    ]
    return pl.pallas_call(
        functools.partial(attend_kernel, n_ctx, heads_dev, remote_count),
        out_shape=[jax.ShapeDtypeStruct((3, rows, HD), jnp.bfloat16)] * n_ctx,
        in_specs=[IN_VMEM] * n_ctx,
        out_specs=[IN_VMEM] * n_ctx,
        scratch_shapes=[
            by_block,
            by_block,
            pltpu.VMEM((tokens, HD), jnp.bfloat16),
            pltpu.VMEM((HD, tokens), jnp.bfloat16),
            pltpu.VMEM((tokens, HD), jnp.bfloat16),
            by_block,
            pltpu.VMEM((tokens, HD), jnp.float32),
            pltpu.VMEM((tokens, HD), jnp.float32),
            scored,
            scored,
            pltpu.VMEM((HD, n_keys * TILE), jnp.bfloat16),
            picked,
            picked,
            pltpu.VMEM((n_ctx, HD), jnp.int32),
            pltpu.SMEM((n_ctx, HD), jnp.int32),
            pltpu.SemaphoreType.DMA,
        ]
        + buffer
        + buffer,
        compiler_params=pltpu.CompilerParams(vmem_limit_bytes=VMEM_BYTES),
    )(*messages)


def gather_kernel(n_ctx, heads_dev, q_ref, k_ref, q_gain, k_gain, *refs):
    slots = refs[:n_ctx]
    dot_ref, dq_ref, dk_ref, dv_ref = refs[n_ctx:]
    block, group = lax.axis_index("ctx"), lax.axis_index("head")
    for mask, slot in zip(mask_order(n_ctx), slots):
        head = head_at(block ^ mask, group, n_ctx, heads_dev)

        @pl.when(head >= 0)
        def _(head=head, slot=slot):
            place = pl.ds(pl.multiple_of(head * HD, HD), HD)
            for at, out in enumerate((dq_ref, dk_ref, dv_ref)):
                out[:, place] = slot[at]

    for at, (wide_ref, pre_ref, gain) in enumerate(
        ((dq_ref, q_ref, q_gain), (dk_ref, k_ref, k_gain))
    ):
        terms = gain[...] * wide_ref[...].astype(jnp.float32) * pre_ref[...].astype(jnp.float32)
        dot_ref[at : at + 1, :] = row_sums(terms)


def finish_kernel(width_all, q_ref, k_ref, q_gain, k_gain, square_ref, dot_ref, *refs):
    dq_ref, dk_ref, dq_out, dk_out = refs
    scales = row_scales(square_ref, width_all)
    backs = scales**3 * (dot_ref[...] / width_all)
    for at, (pre_ref, gain, grad_ref, out) in enumerate(
        ((q_ref, q_gain, dq_ref, dq_out), (k_ref, k_gain, dk_ref, dk_out))
    ):
        scale = column(scales[at : at + 1, :], HD)
        back = column(backs[at : at + 1, :], HD)
        for first in range(0, pre_ref.shape[1], HD):
            place = slice(first, first + HD)
            wide = pre_ref[:, place].astype(jnp.float32)
            grad = grad_ref[:, place].astype(jnp.float32)
            out[:, place] = (scale * gain[:, place] * grad - wide * back).astype(jnp.bfloat16)


def heads_to_owners(q_pre, k_pre, values, out_grad, q_gain, k_gain, selected):
    n_ctx = lax.axis_size("ctx")
    n_head = lax.axis_size("head")
    rows, width_dev = q_pre.shape
    width_all = width_dev * n_head
    heads_dev = width_dev // HD
    remote_count = selected.shape[2]
    sizes = (n_ctx, n_head, heads_dev)
    params = pltpu.CompilerParams(vmem_limit_bytes=VMEM_BYTES)
    by_row = jax.ShapeDtypeStruct((2, rows), jnp.float32)
    wide = jax.ShapeDtypeStruct((rows, width_dev), jnp.bfloat16)

    squares = pl.pallas_call(
        squares_kernel,
        out_shape=by_row,
        in_specs=[IN_VMEM] * 2,
        out_specs=IN_VMEM,
        compiler_params=params,
    )(q_pre, k_pre)
    squares = lax.psum(squares, "head")
    sent = pl.pallas_call(
        functools.partial(pack_kernel, n_ctx, width_all),
        out_shape=[jax.ShapeDtypeStruct((4 * rows + PICK_ROWS, HD), jnp.bfloat16)] * n_ctx,
        in_specs=[IN_SMEM] + [IN_VMEM] * 7,
        out_specs=[IN_VMEM] * n_ctx,
        compiler_params=params,
    )(
        selected,
        squares,
        q_gain.reshape(heads_dev, HD),
        k_gain.reshape(heads_dev, HD),
        q_pre,
        k_pre,
        values,
        out_grad,
    )
    messages = move(sent, False, *sizes)
    results = attend(messages, heads_dev, remote_count)
    slots = move(results, True, *sizes)

    pres = (q_pre, k_pre, q_gain[None], k_gain[None])
    dots, dq_wide, dk_wide, dv = pl.pallas_call(
        functools.partial(gather_kernel, n_ctx, heads_dev),
        out_shape=[by_row, wide, wide, wide],
        in_specs=[IN_VMEM] * (4 + n_ctx),
        out_specs=[IN_VMEM] * 4,
        compiler_params=params,
    )(*pres, *slots)
    dots = lax.psum(dots, "head")
    dq, dk = pl.pallas_call(
        functools.partial(finish_kernel, width_all),
        out_shape=[wide, wide],
        in_specs=[IN_VMEM] * 8,
        out_specs=[IN_VMEM] * 2,
        compiler_params=params,
    )(*pres, squares, dots, dq_wide, dk_wide)
    return dq, dk, dv


def on_device(q_pre, k_pre, values, out_grad, q_gain, k_gain, selected):
    n_ctx = lax.axis_size("ctx")
    tiles_dev, heads_dev, remote_count = selected.shape
    capacity = -(-heads_dev * remote_count // (n_ctx - 1))
    by_head = (n_ctx - 1) * tiles_dev * 7
    by_tile = (n_ctx - 1) * capacity * 6
    paired = n_ctx & (n_ctx - 1) == 0 and n_ctx >= max(heads_dev, 4) and n_ctx * tiles_dev <= 256
    plan = heads_to_owners if paired and by_head <= by_tile else tiles_to_queries
    return plan(q_pre, k_pre, values, out_grad, q_gain, k_gain, selected)


def solution(mesh):
    placed = (
        P("ctx", "head"),
        P("ctx", "head"),
        P("ctx", "head"),
        P("ctx", "head"),
        P("head"),
        P("head"),
        P("ctx", "head", None),
    )
    return jax.shard_map(
        on_device,
        mesh=mesh,
        in_specs=placed,
        out_specs=(P("ctx", "head"), P("ctx", "head"), P("ctx", "head")),
        check_vma=False,
    )
```

```python
import functools
import math

import jax
import jax.numpy as jnp
from jax import lax
from jax.experimental import pallas as pl
from jax.experimental.pallas import tpu as pltpu
from jax.sharding import PartitionSpec as P

HD = 128
TILE = 128


epsilon = 1e-06


def split_heads(array, heads_dev):
    return array.reshape(array.shape[0], heads_dev, HD).transpose(1, 0, 2)


def merge_heads(array):
    heads_dev, tok_dev, depth = array.shape
    return array.transpose(1, 0, 2).reshape(tok_dev, heads_dev * depth)


def per_tile(array, qt_dev):
    heads_dev, tok_dev, depth = array.shape
    return array.reshape(heads_dev, qt_dev, TILE, depth).transpose(1, 0, 2, 3)


def from_tiles(array):
    qt_dev, heads_dev, rows_tile, depth = array.shape
    return array.transpose(1, 0, 2, 3).reshape(heads_dev, qt_dev * rows_tile, depth)


def table_sum(taken, pieces, heads_dev, qt_dev):
    flat_pieces = pieces.reshape(pieces.shape[0], -1)
    summed = jnp.dot(
        taken, flat_pieces, precision=lax.Precision.HIGHEST, preferred_element_type=jnp.float32
    )
    summed = summed.reshape(heads_dev, qt_dev, 2, TILE, HD).transpose(2, 0, 1, 3, 4)
    return summed.reshape(2, heads_dev, qt_dev * TILE, HD)


def rounded(array):
    return array.astype(jnp.bfloat16)


def finish_norm(wide, scale, gain, grad, dot_sum, width_all):
    return (scale * gain * grad - wide * scale**3 * (dot_sum / width_all)[:, None]).astype(
        jnp.bfloat16
    )


def tiles_to_queries(q_pre, k_pre, values, out_grad, q_gain, k_gain, selected):
    n_ctx = lax.axis_size("ctx")
    tok_dev, width_dev = q_pre.shape
    width_all = width_dev * lax.axis_size("head")
    heads_dev = width_dev // HD
    qt_dev = tok_dev // TILE
    remote_count = selected.shape[2]
    factor = 1.0 / math.sqrt(HD)
    q_wide = q_pre.astype(jnp.float32)
    k_wide = k_pre.astype(jnp.float32)
    q_square, k_square = lax.psum(
        (jnp.sum(q_wide * q_wide, axis=1), jnp.sum(k_wide * k_wide, axis=1)), "head"
    )
    q_scale = lax.rsqrt(q_square / width_all + epsilon)[:, None]
    k_scale = lax.rsqrt(k_square / width_all + epsilon)[:, None]
    q_heads = split_heads(rounded(q_wide * q_scale * q_gain), heads_dev)
    k_heads = split_heads(rounded(k_wide * k_scale * k_gain), heads_dev)
    v_heads = split_heads(values, heads_dev)
    g_heads = split_heads(out_grad, heads_dev)
    q_tiles = per_tile(q_heads, qt_dev)
    g_tiles = per_tile(g_heads, qt_dev)
    k_table = k_heads.reshape(heads_dev * qt_dev, TILE, HD)
    v_table = v_heads.reshape(heads_dev * qt_dev, TILE, HD)
    flat_sel = selected[0].reshape(-1)
    n_slot = flat_sel.shape[0]
    capacity = -(-n_slot // (n_ctx - 1))
    n_buffer = n_ctx * capacity
    owners = flat_sel // qt_dev
    head_of = jnp.arange(n_slot, dtype=jnp.int32) // remote_count
    codes = head_of * qt_dev + flat_sel % qt_dev
    matches = (owners[:, None] == jnp.arange(n_ctx, dtype=jnp.int32)[None, :]).astype(jnp.int32)
    ranks = jnp.sum((jnp.cumsum(matches, axis=0) - matches) * matches, axis=1)
    position = owners * capacity + ranks
    placed = position[None, :] == jnp.arange(n_buffer, dtype=jnp.int32)[:, None]
    request = jnp.sum(jnp.where(placed, codes[None, :] + 1, 0), axis=1) - 1
    asked = lax.all_to_all(
        request.reshape(n_ctx, capacity), "ctx", split_axis=0, concat_axis=0, tiled=True
    ).reshape(n_buffer)
    clipped = jnp.maximum(asked, 0)
    taken = (asked[None, :] == jnp.arange(heads_dev * qt_dev, dtype=jnp.int32)[:, None]).astype(
        jnp.float32
    )
    s_near = (
        jnp.einsum("rhqd,hkd->rhqk", q_tiles, k_heads, preferred_element_type=jnp.float32) * factor
    )
    dp_near = jnp.einsum("rhqd,hkd->rhqk", g_tiles, v_heads, preferred_element_type=jnp.float32)
    near_top = jnp.max(s_near, axis=-1)
    outgoing = jnp.stack((k_table[clipped], v_table[clipped]), axis=1).reshape(
        n_ctx, capacity, 2, TILE, HD
    )
    incoming = lax.all_to_all(outgoing, "ctx", split_axis=0, concat_axis=0, tiled=True).reshape(
        n_buffer, 2, TILE, HD
    )
    slot_kv = incoming[position].reshape(heads_dev, remote_count, 2, TILE, HD)
    far_k = slot_kv[:, :, 0]
    far_v = slot_kv[:, :, 1]
    s_far = (
        jnp.einsum("rhqd,hckd->rhqck", q_tiles, far_k, preferred_element_type=jnp.float32) * factor
    )
    dp_far = jnp.einsum("rhqd,hckd->rhqck", g_tiles, far_v, preferred_element_type=jnp.float32)
    row_top = jnp.maximum(near_top, jnp.max(s_far, axis=(-2, -1)))
    totals = jnp.sum(jnp.exp(s_near - row_top[..., None]), axis=-1) + jnp.sum(
        jnp.exp(s_far - row_top[..., None, None]), axis=(-2, -1)
    )
    lse = row_top + jnp.log(totals)
    p_near = jnp.exp(s_near - lse[..., None])
    p_far = jnp.exp(s_far - lse[..., None, None])
    delta = jnp.sum(p_near * dp_near, axis=-1) + jnp.sum(p_far * dp_far, axis=(-2, -1))
    ds_near = rounded(p_near * (dp_near - delta[..., None]) * factor)
    pb_near = rounded(p_near)
    dq_near = jnp.einsum("rhqk,hkd->rhqd", ds_near, k_heads, preferred_element_type=jnp.float32)
    dk_near = jnp.einsum("rhqk,rhqd->hkd", ds_near, q_tiles, preferred_element_type=jnp.float32)
    dv_near = jnp.einsum("rhqk,rhqd->hkd", pb_near, g_tiles, preferred_element_type=jnp.float32)
    dq_near, dk_near, dv_near = (dq_near, dk_near, dv_near)
    ds_far = rounded(p_far * (dp_far - delta[..., None, None]) * factor)
    pb_far = rounded(p_far)
    dq_far = jnp.einsum("rhqck,hckd->rhqd", ds_far, far_k, preferred_element_type=jnp.float32)
    dq_wide = merge_heads(from_tiles(dq_near + dq_far))
    q_dot = jnp.sum(q_gain * dq_wide * q_wide, axis=1)
    dq_wide, q_dot = (dq_wide, q_dot)
    dk_far = jnp.einsum("rhqck,rhqd->hckd", ds_far, q_tiles, preferred_element_type=jnp.float32)
    dv_far = jnp.einsum("rhqck,rhqd->hckd", pb_far, g_tiles, preferred_element_type=jnp.float32)
    grads = jnp.stack((dk_far, dv_far), axis=2).reshape(n_slot, 2, TILE, HD)
    sending = jnp.zeros((n_buffer, 2, TILE, HD), jnp.float32).at[position].set(grads)
    returned = lax.all_to_all(
        sending.reshape(n_ctx, capacity, 2, TILE, HD),
        "ctx",
        split_axis=0,
        concat_axis=0,
        tiled=True,
    ).reshape(n_buffer, 2, TILE, HD)
    far_sums = table_sum(taken, returned, heads_dev, qt_dev)
    dk_wide = merge_heads(dk_near + far_sums[0])
    dv_heads = dv_near + far_sums[1]
    k_dot = jnp.sum(k_gain * dk_wide * k_wide, axis=1)
    q_dot, k_dot = lax.psum((q_dot, k_dot), "head")
    dq_result = finish_norm(q_wide, q_scale, q_gain, dq_wide, q_dot, width_all)
    dk_result = finish_norm(k_wide, k_scale, k_gain, dk_wide, k_dot, width_all)
    return (dq_result, dk_result, merge_heads(dv_heads).astype(jnp.bfloat16))


VMEM_BYTES = 48 * 2**20
NT = (((1,), (1,)), ((), ()))
IN_VMEM = pl.BlockSpec(memory_space=pltpu.VMEM)
IN_SMEM = pl.BlockSpec(memory_space=pltpu.SMEM)


def owners_of(group, n_ctx, heads_dev):
    places = [(4 * head + 1) * n_ctx // (4 * heads_dev) for head in range(heads_dev)]
    return [n_ctx - 1 - place if group % 2 else place for place in places]


def head_at(place, group, n_ctx, heads_dev):
    even = jnp.where(group % 2 == 1, n_ctx - 1 - place, place)
    head = -1
    for index, owner in enumerate(owners_of(0, n_ctx, heads_dev)):
        head = jnp.where(even == owner, index, head)
    return head


def pairs_to_owner(mask, n_ctx, n_head, heads_dev):
    pairs = []
    for group in range(n_head):
        owners = owners_of(group, n_ctx, heads_dev)
        for block in range(n_ctx):
            if block ^ mask in owners:
                pairs.append((block * n_head + group, (block ^ mask) * n_head + group))
    return pairs


def far_masks(n_ctx):
    return range(n_ctx - 1, n_ctx // 2 - 1, -1)


def move(far, near, back, n_ctx, n_head, heads_dev):
    half = n_ctx // 2
    moved = []
    for mask, array in zip(far_masks(n_ctx), far):
        pairs = pairs_to_owner(mask, n_ctx, n_head, heads_dev)
        if back:
            pairs = [(b, a) for a, b in pairs]
        moved.append(lax.ppermute(array, ("ctx", "head"), pairs))
    halves = [list(range(half)), list(range(half, n_ctx))]
    near = lax.all_to_all(
        near, "ctx", split_axis=0, concat_axis=0, axis_index_groups=halves, tiled=True
    )
    return moved, near


def message_of(far, near, mask, own_block):
    half = len(far)
    if mask >= half:
        return far[2 * half - 1 - mask]
    return near.at[(own_block ^ mask) & (half - 1)]


def column(row, width):
    return jnp.broadcast_to(row, (width, row.shape[1])).T


def row_sums(wide):
    total = wide[:, :HD]
    for at in range(HD, wide.shape[1], HD):
        total = total + wide[:, at : at + HD]
    return jnp.sum(total.T, axis=0, keepdims=True)


def pack_kernel(n_ctx, heads_dev, *refs):
    inputs, far, near, sems = refs[:4], refs[4:-2], refs[-2], refs[-1]
    block, group = lax.axis_index("ctx"), lax.axis_index("head")
    heads = [head_at(block ^ mask, group, n_ctx, heads_dev) for mask in range(n_ctx)]

    def copies(mask):
        place = pl.ds(pl.multiple_of(heads[mask] * HD, HD), HD)
        message = message_of(far, near, mask, block)
        return [
            pltpu.make_async_copy(ref.at[:, place], message.at[at], sems.at[mask, at])
            for at, ref in enumerate(inputs)
        ]

    for mask in range(n_ctx - 1, -1, -1):

        @pl.when(heads[mask] >= 0)
        def _(mask=mask):
            for copy in copies(mask):
                copy.start()

    for mask in range(n_ctx - 1, -1, -1):

        @pl.when(heads[mask] >= 0)
        def _(mask=mask):
            for copy in copies(mask):
                copy.wait()


def pack(arrays, n_ctx):
    rows, width_dev = arrays[0].shape
    half = n_ctx // 2
    result = pl.pallas_call(
        functools.partial(pack_kernel, n_ctx, width_dev // HD),
        out_shape=[jax.ShapeDtypeStruct((4, rows, HD), jnp.bfloat16)] * half
        + [jax.ShapeDtypeStruct((half, 4, rows, HD), jnp.bfloat16)],
        in_specs=[IN_VMEM] * 4,
        out_specs=[IN_VMEM] * (half + 1),
        scratch_shapes=[pltpu.SemaphoreType.DMA((n_ctx, 4))],
        compiler_params=pltpu.CompilerParams(vmem_limit_bytes=VMEM_BYTES),
    )(*arrays)
    return result[:half], result[half]


def squares_kernel(q_ref, k_ref, square_ref):
    for at, ref in enumerate((q_ref, k_ref)):
        wide = ref[...].astype(jnp.float32)
        square_ref[at : at + 1, :] = row_sums(wide * wide)


def attend_kernel(n_ctx, heads_dev, picks, scale_ref, q_gain, k_gain, *refs):
    half = n_ctx // 2
    far_in, near_in, far_out, near_out = (
        refs[:half],
        refs[half],
        refs[half + 1 : n_ctx + 1],
        refs[n_ctx + 1],
    )
    scratch = refs[n_ctx + 2 :]
    q_ref, g_ref, k_ref, kt_ref, v_ref, dq_ref, dk_ref, dv_ref, ds_ref, kt_picked = scratch[:10]
    buffers = (scratch[10:13], scratch[13:16])
    rows = far_in[0].shape[1]
    remote_count = picks.shape[1]
    near = rows // TILE
    n_keys = near + remote_count
    factor = 1.0 / math.sqrt(HD)
    to_base2 = factor * math.log2(math.e)
    own_block = lax.axis_index("ctx")
    own_head = head_at(own_block, lax.axis_index("head"), n_ctx, heads_dev)

    def rows_of(block):
        return pl.ds(pl.multiple_of(block * rows, rows), rows)

    def places_of(block):
        return [
            pl.ds(pl.multiple_of(block * rows + tile * TILE, TILE), TILE) for tile in range(near)
        ] + [
            pl.ds(pl.multiple_of(picks[block, slot] * TILE, TILE), TILE)
            for slot in range(remote_count)
        ]

    def prepare(mask):
        block = own_block ^ mask
        message = message_of(far_in, near_in, mask, own_block)
        place = rows_of(block)
        q_scale = column(scale_ref[block, 0:1, :], HD)
        k_scale = column(scale_ref[block, 1:2, :], HD)
        q_normed = message[0].astype(jnp.float32) * q_scale * q_gain[pl.ds(own_head, 1), :]
        k_normed = message[1].astype(jnp.float32) * k_scale * k_gain[pl.ds(own_head, 1), :]
        q_ref[mask] = q_normed.astype(jnp.bfloat16)
        k_ref[place, :] = k_normed.astype(jnp.bfloat16)
        kt_ref[:, place] = k_normed.T.astype(jnp.bfloat16)
        v_ref[place, :] = message[2]
        g_ref[mask] = message[3]

    def scores(mask, slot, place, buffer):
        weight_ref, dprob_ref, stat_ref = buffer
        score = lax.dot_general(
            k_ref[place, :], q_ref[mask], NT, preferred_element_type=jnp.float32
        )
        dprob = lax.dot_general(
            v_ref[place, :], g_ref[mask], NT, preferred_element_type=jnp.float32
        )
        top = jnp.max(score, axis=0, keepdims=True)
        weight = jnp.exp2((score - top) * to_base2)
        weight_ref[slot] = weight
        dprob_ref[slot] = dprob
        stat_ref[0, slot : slot + 1, :] = top * to_base2
        stat_ref[1, slot : slot + 1, :] = jnp.sum(weight, axis=0, keepdims=True)
        stat_ref[2, slot : slot + 1, :] = jnp.sum(weight * dprob, axis=0, keepdims=True)

    def settle(buffer):
        stat_ref = buffer[2]
        tops = stat_ref[0, :n_keys, :]
        shares = jnp.exp2(tops - jnp.max(tops, axis=0, keepdims=True))
        total = jnp.sum(shares * stat_ref[1, :n_keys, :], axis=0, keepdims=True)
        mixed = jnp.sum(shares * stat_ref[2, :n_keys, :], axis=0, keepdims=True)
        inverse = 1.0 / total
        return shares * inverse, mixed * inverse

    def gradients(mask, slot, place, buffer, shares, delta):
        weight_ref, dprob_ref, _ = buffer
        prob = weight_ref[slot] * shares[slot : slot + 1, :]
        dscore = (prob * (dprob_ref[slot] - delta)).astype(jnp.bfloat16)
        ds_ref[slot * TILE : (slot + 1) * TILE, :] = dscore
        kt_picked[:, slot * TILE : (slot + 1) * TILE] = kt_ref[:, place]
        dk_ref[place, :] += jnp.dot(dscore, q_ref[mask], preferred_element_type=jnp.float32)
        dv_ref[place, :] += jnp.dot(
            prob.astype(jnp.bfloat16), g_ref[mask], preferred_element_type=jnp.float32
        )

    def query_gradient(mask):
        dq_t = jnp.dot(kt_picked[...], ds_ref[...], preferred_element_type=jnp.float32)
        dq_ref[mask] = (dq_t * factor).T.astype(jnp.bfloat16)

    def step(mask, buffer, later, later_buffer):
        places = places_of(own_block ^ mask)
        shares, delta = settle(buffer)
        later_places = None if later is None else places_of(own_block ^ later)
        for slot in range(n_keys):
            gradients(mask, slot, places[slot], buffer, shares, delta)
            if later is not None:
                scores(later, slot, later_places[slot], later_buffer)
        query_gradient(mask)

    @pl.when(own_head >= 0)
    def _():
        for mask in range(n_ctx):
            prepare(mask)
        dk_ref[...] = jnp.zeros_like(dk_ref)
        dv_ref[...] = jnp.zeros_like(dv_ref)
        for slot, place in enumerate(places_of(own_block)):
            scores(0, slot, place, buffers[0])

        def two(pair, carry):
            step(2 * pair, buffers[0], 2 * pair + 1, buffers[1])
            step(2 * pair + 1, buffers[1], 2 * pair + 2, buffers[0])
            return carry

        lax.fori_loop(0, n_ctx // 2 - 1, two, 0)
        step(n_ctx - 2, buffers[0], n_ctx - 1, buffers[1])
        step(n_ctx - 1, buffers[1], None, None)
        for mask in range(n_ctx):
            place = rows_of(own_block ^ mask)
            message = message_of(far_out, near_out, mask, own_block)
            message[0] = dq_ref[mask]
            message[1] = (dk_ref[place, :] * factor).astype(jnp.bfloat16)
            message[2] = dv_ref[place, :].astype(jnp.bfloat16)


def attend(picks, scales, q_gain, k_gain, far, near):
    half, rows = len(far), far[0].shape[1]
    n_ctx = 2 * half
    tokens = n_ctx * rows
    n_keys = rows // TILE + picks.shape[1]
    by_block = pltpu.VMEM((n_ctx, rows, HD), jnp.bfloat16)
    buffer = [
        pltpu.VMEM((n_keys, TILE, rows), jnp.float32),
        pltpu.VMEM((n_keys, TILE, rows), jnp.float32),
        pltpu.VMEM((3, -(-n_keys // 8) * 8, rows), jnp.float32),
    ]
    return pl.pallas_call(
        functools.partial(attend_kernel, n_ctx, q_gain.shape[0]),
        out_shape=[jax.ShapeDtypeStruct((3, rows, HD), jnp.bfloat16)] * half
        + [jax.ShapeDtypeStruct((half, 3, rows, HD), jnp.bfloat16)],
        in_specs=[IN_SMEM] + [IN_VMEM] * (4 + half),
        out_specs=[IN_VMEM] * (half + 1),
        scratch_shapes=[
            by_block,
            by_block,
            pltpu.VMEM((tokens, HD), jnp.bfloat16),
            pltpu.VMEM((HD, tokens), jnp.bfloat16),
            pltpu.VMEM((tokens, HD), jnp.bfloat16),
            by_block,
            pltpu.VMEM((tokens, HD), jnp.float32),
            pltpu.VMEM((tokens, HD), jnp.float32),
            pltpu.VMEM((n_keys * TILE, rows), jnp.bfloat16),
            pltpu.VMEM((HD, n_keys * TILE), jnp.bfloat16),
        ]
        + buffer
        + buffer,
        compiler_params=pltpu.CompilerParams(vmem_limit_bytes=VMEM_BYTES),
    )(picks, scales, q_gain, k_gain, *far, near)


def row_scales(square_ref, width_all):
    return lax.rsqrt(square_ref[...] / width_all + epsilon)


def gather_kernel(n_ctx, heads_dev, q_ref, k_ref, q_gain, k_gain, *refs):
    half = n_ctx // 2
    far, near = refs[:half], refs[half]
    dot_ref, dq_ref, dk_ref, dv_ref = refs[half + 1 :]
    block, group = lax.axis_index("ctx"), lax.axis_index("head")
    for mask in range(n_ctx):
        head = head_at(block ^ mask, group, n_ctx, heads_dev)

        @pl.when(head >= 0)
        def _(mask=mask, head=head):
            place = pl.ds(pl.multiple_of(head * HD, HD), HD)
            message = message_of(far, near, mask, block)
            for at, out in enumerate((dq_ref, dk_ref, dv_ref)):
                out[:, place] = message[at]

    for at, (wide_ref, pre_ref, gain) in enumerate(
        ((dq_ref, q_ref, q_gain), (dk_ref, k_ref, k_gain))
    ):
        terms = gain[...] * wide_ref[...].astype(jnp.float32) * pre_ref[...].astype(jnp.float32)
        dot_ref[at : at + 1, :] = row_sums(terms)


def finish_kernel(width_all, q_ref, k_ref, q_gain, k_gain, square_ref, dot_ref, *refs):
    dq_ref, dk_ref, dq_out, dk_out = refs
    scales = row_scales(square_ref, width_all)
    backs = scales**3 * (dot_ref[...] / width_all)
    for at, (pre_ref, gain, grad_ref, out) in enumerate(
        ((q_ref, q_gain, dq_ref, dq_out), (k_ref, k_gain, dk_ref, dk_out))
    ):
        scale = column(scales[at : at + 1, :], HD)
        back = column(backs[at : at + 1, :], HD)
        for first in range(0, pre_ref.shape[1], HD):
            place = slice(first, first + HD)
            wide = pre_ref[:, place].astype(jnp.float32)
            grad = grad_ref[:, place].astype(jnp.float32)
            out[:, place] = (scale * gain[:, place] * grad - wide * back).astype(jnp.bfloat16)


def heads_to_owners(q_pre, k_pre, values, out_grad, q_gain, k_gain, selected):
    n_ctx = lax.axis_size("ctx")
    n_head = lax.axis_size("head")
    rows, width_dev = q_pre.shape
    width_all = width_dev * n_head
    heads_dev = width_dev // HD
    remote_count = selected.shape[2]
    sizes = (n_ctx, n_head, heads_dev)
    params = pltpu.CompilerParams(vmem_limit_bytes=VMEM_BYTES)

    by_row = jax.ShapeDtypeStruct((2, rows), jnp.float32)
    wide = jax.ShapeDtypeStruct((rows, width_dev), jnp.bfloat16)

    sent = pack((q_pre, k_pre, values, out_grad), n_ctx)
    far, near = move(*sent, False, *sizes)

    squares = pl.pallas_call(
        squares_kernel,
        out_shape=by_row,
        in_specs=[IN_VMEM] * 2,
        out_specs=IN_VMEM,
        compiler_params=params,
    )(q_pre, k_pre)
    wishes = selected[0].reshape(1, -1).astype(jnp.float32)
    wishes = jnp.pad(wishes, ((0, 0), (0, rows - wishes.shape[1])))
    squares = lax.psum(squares, "head")
    small = jnp.concatenate((squares, wishes), axis=0)
    small = jnp.broadcast_to(small[None], (n_ctx,) + small.shape)
    small = lax.all_to_all(small, "ctx", split_axis=0, concat_axis=0, tiled=True)
    scales = lax.rsqrt(small[:, :2] / width_all + epsilon)
    own_head = head_at(lax.axis_index("ctx"), lax.axis_index("head"), n_ctx, heads_dev)
    first = jnp.maximum(own_head, 0) * remote_count
    picks = lax.dynamic_slice_in_dim(small[:, 2], first, remote_count, 1).astype(jnp.int32)

    q_gains = q_gain.reshape(heads_dev, HD)
    k_gains = k_gain.reshape(heads_dev, HD)
    *far, near = attend(picks, scales, q_gains, k_gains, far, near)
    far, near = move(far, near, True, *sizes)

    pres = (q_pre, k_pre, q_gain[None], k_gain[None])
    dots, dq_wide, dk_wide, dv = pl.pallas_call(
        functools.partial(gather_kernel, n_ctx, heads_dev),
        out_shape=[by_row, wide, wide, wide],
        in_specs=[IN_VMEM] * (5 + len(far)),
        out_specs=[IN_VMEM] * 4,
        compiler_params=params,
    )(*pres, *far, near)
    dots = lax.psum(dots, "head")
    dq, dk = pl.pallas_call(
        functools.partial(finish_kernel, width_all),
        out_shape=[wide, wide],
        in_specs=[IN_VMEM] * 8,
        out_specs=[IN_VMEM] * 2,
        compiler_params=params,
    )(*pres, squares, dots, dq_wide, dk_wide)
    return dq, dk, dv


def on_device(q_pre, k_pre, values, out_grad, q_gain, k_gain, selected):
    n_ctx = lax.axis_size("ctx")
    tiles_dev, heads_dev, remote_count = selected.shape
    capacity = -(-heads_dev * remote_count // (n_ctx - 1))
    by_head = (n_ctx - 1) * tiles_dev * 7
    by_tile = (n_ctx - 1) * capacity * 6
    paired = n_ctx & (n_ctx - 1) == 0 and n_ctx >= max(heads_dev, 4)
    plan = heads_to_owners if paired and by_head <= by_tile else tiles_to_queries
    return plan(q_pre, k_pre, values, out_grad, q_gain, k_gain, selected)


def solution(mesh):
    placed = (
        P("ctx", "head"),
        P("ctx", "head"),
        P("ctx", "head"),
        P("ctx", "head"),
        P("head"),
        P("head"),
        P("ctx", "head", None),
    )
    return jax.shard_map(
        on_device,
        mesh=mesh,
        in_specs=placed,
        out_specs=(P("ctx", "head"), P("ctx", "head"), P("ctx", "head")),
        check_vma=False,
    )
```

```python
import functools
import math

import jax
import jax.numpy as jnp
from jax import lax
from jax.experimental import pallas as pl
from jax.experimental.pallas import tpu as pltpu
from jax.sharding import PartitionSpec as P

HD = 128
TILE = 128


epsilon = 1e-06


def split_heads(array, heads_dev):
    return array.reshape(array.shape[0], heads_dev, HD).transpose(1, 0, 2)


def merge_heads(array):
    heads_dev, tok_dev, depth = array.shape
    return array.transpose(1, 0, 2).reshape(tok_dev, heads_dev * depth)


def per_tile(array, qt_dev):
    heads_dev, tok_dev, depth = array.shape
    return array.reshape(heads_dev, qt_dev, TILE, depth).transpose(1, 0, 2, 3)


def from_tiles(array):
    qt_dev, heads_dev, rows_tile, depth = array.shape
    return array.transpose(1, 0, 2, 3).reshape(heads_dev, qt_dev * rows_tile, depth)


def table_sum(taken, pieces, heads_dev, qt_dev):
    flat_pieces = pieces.reshape(pieces.shape[0], -1)
    summed = jnp.dot(
        taken, flat_pieces, precision=lax.Precision.HIGHEST, preferred_element_type=jnp.float32
    )
    summed = summed.reshape(heads_dev, qt_dev, 2, TILE, HD).transpose(2, 0, 1, 3, 4)
    return summed.reshape(2, heads_dev, qt_dev * TILE, HD)


def rounded(array):
    return array.astype(jnp.bfloat16)


def finish_norm(wide, scale, gain, grad, dot_sum, width_all):
    return (scale * gain * grad - wide * scale**3 * (dot_sum / width_all)[:, None]).astype(
        jnp.bfloat16
    )


def tiles_to_queries(q_pre, k_pre, values, out_grad, q_gain, k_gain, selected):
    n_ctx = lax.axis_size("ctx")
    tok_dev, width_dev = q_pre.shape
    width_all = width_dev * lax.axis_size("head")
    heads_dev = width_dev // HD
    qt_dev = tok_dev // TILE
    remote_count = selected.shape[2]
    factor = 1.0 / math.sqrt(HD)
    q_wide = q_pre.astype(jnp.float32)
    k_wide = k_pre.astype(jnp.float32)
    q_square, k_square = lax.psum(
        (jnp.sum(q_wide * q_wide, axis=1), jnp.sum(k_wide * k_wide, axis=1)), "head"
    )
    q_scale = lax.rsqrt(q_square / width_all + epsilon)[:, None]
    k_scale = lax.rsqrt(k_square / width_all + epsilon)[:, None]
    q_heads = split_heads(rounded(q_wide * q_scale * q_gain), heads_dev)
    k_heads = split_heads(rounded(k_wide * k_scale * k_gain), heads_dev)
    v_heads = split_heads(values, heads_dev)
    g_heads = split_heads(out_grad, heads_dev)
    q_tiles = per_tile(q_heads, qt_dev)
    g_tiles = per_tile(g_heads, qt_dev)
    k_table = k_heads.reshape(heads_dev * qt_dev, TILE, HD)
    v_table = v_heads.reshape(heads_dev * qt_dev, TILE, HD)
    flat_sel = selected[0].reshape(-1)
    n_slot = flat_sel.shape[0]
    capacity = -(-n_slot // (n_ctx - 1))
    n_buffer = n_ctx * capacity
    owners = flat_sel // qt_dev
    head_of = jnp.arange(n_slot, dtype=jnp.int32) // remote_count
    codes = head_of * qt_dev + flat_sel % qt_dev
    matches = (owners[:, None] == jnp.arange(n_ctx, dtype=jnp.int32)[None, :]).astype(jnp.int32)
    ranks = jnp.sum((jnp.cumsum(matches, axis=0) - matches) * matches, axis=1)
    position = owners * capacity + ranks
    placed = position[None, :] == jnp.arange(n_buffer, dtype=jnp.int32)[:, None]
    request = jnp.sum(jnp.where(placed, codes[None, :] + 1, 0), axis=1) - 1
    asked = lax.all_to_all(
        request.reshape(n_ctx, capacity), "ctx", split_axis=0, concat_axis=0, tiled=True
    ).reshape(n_buffer)
    clipped = jnp.maximum(asked, 0)
    taken = (asked[None, :] == jnp.arange(heads_dev * qt_dev, dtype=jnp.int32)[:, None]).astype(
        jnp.float32
    )
    s_near = (
        jnp.einsum("rhqd,hkd->rhqk", q_tiles, k_heads, preferred_element_type=jnp.float32) * factor
    )
    dp_near = jnp.einsum("rhqd,hkd->rhqk", g_tiles, v_heads, preferred_element_type=jnp.float32)
    near_top = jnp.max(s_near, axis=-1)
    outgoing = jnp.stack((k_table[clipped], v_table[clipped]), axis=1).reshape(
        n_ctx, capacity, 2, TILE, HD
    )
    incoming = lax.all_to_all(outgoing, "ctx", split_axis=0, concat_axis=0, tiled=True).reshape(
        n_buffer, 2, TILE, HD
    )
    slot_kv = incoming[position].reshape(heads_dev, remote_count, 2, TILE, HD)
    far_k = slot_kv[:, :, 0]
    far_v = slot_kv[:, :, 1]
    s_far = (
        jnp.einsum("rhqd,hckd->rhqck", q_tiles, far_k, preferred_element_type=jnp.float32) * factor
    )
    dp_far = jnp.einsum("rhqd,hckd->rhqck", g_tiles, far_v, preferred_element_type=jnp.float32)
    row_top = jnp.maximum(near_top, jnp.max(s_far, axis=(-2, -1)))
    totals = jnp.sum(jnp.exp(s_near - row_top[..., None]), axis=-1) + jnp.sum(
        jnp.exp(s_far - row_top[..., None, None]), axis=(-2, -1)
    )
    lse = row_top + jnp.log(totals)
    p_near = jnp.exp(s_near - lse[..., None])
    p_far = jnp.exp(s_far - lse[..., None, None])
    delta = jnp.sum(p_near * dp_near, axis=-1) + jnp.sum(p_far * dp_far, axis=(-2, -1))
    ds_near = rounded(p_near * (dp_near - delta[..., None]) * factor)
    pb_near = rounded(p_near)
    dq_near = jnp.einsum("rhqk,hkd->rhqd", ds_near, k_heads, preferred_element_type=jnp.float32)
    dk_near = jnp.einsum("rhqk,rhqd->hkd", ds_near, q_tiles, preferred_element_type=jnp.float32)
    dv_near = jnp.einsum("rhqk,rhqd->hkd", pb_near, g_tiles, preferred_element_type=jnp.float32)
    dq_near, dk_near, dv_near = (dq_near, dk_near, dv_near)
    ds_far = rounded(p_far * (dp_far - delta[..., None, None]) * factor)
    pb_far = rounded(p_far)
    dq_far = jnp.einsum("rhqck,hckd->rhqd", ds_far, far_k, preferred_element_type=jnp.float32)
    dq_wide = merge_heads(from_tiles(dq_near + dq_far))
    q_dot = jnp.sum(q_gain * dq_wide * q_wide, axis=1)
    dq_wide, q_dot = (dq_wide, q_dot)
    dk_far = jnp.einsum("rhqck,rhqd->hckd", ds_far, q_tiles, preferred_element_type=jnp.float32)
    dv_far = jnp.einsum("rhqck,rhqd->hckd", pb_far, g_tiles, preferred_element_type=jnp.float32)
    grads = jnp.stack((dk_far, dv_far), axis=2).reshape(n_slot, 2, TILE, HD)
    sending = jnp.zeros((n_buffer, 2, TILE, HD), jnp.float32).at[position].set(grads)
    returned = lax.all_to_all(
        sending.reshape(n_ctx, capacity, 2, TILE, HD),
        "ctx",
        split_axis=0,
        concat_axis=0,
        tiled=True,
    ).reshape(n_buffer, 2, TILE, HD)
    far_sums = table_sum(taken, returned, heads_dev, qt_dev)
    dk_wide = merge_heads(dk_near + far_sums[0])
    dv_heads = dv_near + far_sums[1]
    k_dot = jnp.sum(k_gain * dk_wide * k_wide, axis=1)
    q_dot, k_dot = lax.psum((q_dot, k_dot), "head")
    dq_result = finish_norm(q_wide, q_scale, q_gain, dq_wide, q_dot, width_all)
    dk_result = finish_norm(k_wide, k_scale, k_gain, dk_wide, k_dot, width_all)
    return (dq_result, dk_result, merge_heads(dv_heads).astype(jnp.bfloat16))


VMEM_BYTES = 48 * 2**20
PICK_ROWS = 16
NT = (((1,), (1,)), ((), ()))
IN_VMEM = pl.BlockSpec(memory_space=pltpu.VMEM)
IN_SMEM = pl.BlockSpec(memory_space=pltpu.SMEM)


def owners_of(group, n_ctx, heads_dev):
    places = [(4 * head + 1) * n_ctx // (4 * heads_dev) for head in range(heads_dev)]
    return [n_ctx - 1 - place if group % 2 else place for place in places]


def head_at(place, group, n_ctx, heads_dev):
    even = jnp.where(group % 2 == 1, n_ctx - 1 - place, place)
    head = -1
    for index, owner in enumerate(owners_of(0, n_ctx, heads_dev)):
        head = jnp.where(even == owner, index, head)
    return head


def pairs_to_owner(mask, n_ctx, n_head, heads_dev):
    pairs = []
    for group in range(n_head):
        owners = owners_of(group, n_ctx, heads_dev)
        for block in range(n_ctx):
            if block ^ mask in owners:
                pairs.append((block * n_head + group, (block ^ mask) * n_head + group))
    return pairs


def far_masks(n_ctx):
    return list(range(n_ctx - 1, n_ctx // 2 - 1, -1))


def near_masks(n_ctx):
    return list(range(n_ctx // 2 - 1, -1, -1))


def back_masks(n_ctx):
    return far_masks(n_ctx) + near_masks(n_ctx)


def move(masks, arrays, back, n_ctx, n_head, heads_dev):
    moved = []
    for mask, array in zip(masks, arrays):
        pairs = pairs_to_owner(mask, n_ctx, n_head, heads_dev)
        if back:
            pairs = [(b, a) for a, b in pairs]
        moved.append(lax.ppermute(array, ("ctx", "head"), pairs) if mask else array)
    return moved


def column(row, width):
    return jnp.broadcast_to(row, (width, row.shape[1])).T


def row_sums(wide):
    total = wide[:, :HD]
    for at in range(HD, wide.shape[1], HD):
        total = total + wide[:, at : at + HD]
    return jnp.sum(total.T, axis=0, keepdims=True)


def squares_kernel(q_ref, k_ref, square_ref):
    for at, ref in enumerate((q_ref, k_ref)):
        wide = ref[...].astype(jnp.float32)
        square_ref[at : at + 1, :] = row_sums(wide * wide)


def row_scales(square_ref, width_all):
    return lax.rsqrt(square_ref[...] / width_all + epsilon)


def pack_far_kernel(n_ctx, heads_dev, v_ref, g_ref, *outs):
    rows = v_ref.shape[0]
    block, group = lax.axis_index("ctx"), lax.axis_index("head")
    for mask, out in zip(far_masks(n_ctx), outs):
        head = head_at(block ^ mask, group, n_ctx, heads_dev)

        @pl.when(head >= 0)
        def _(head=head, out=out):
            place = pl.ds(pl.multiple_of(head * HD, HD), HD)
            out[:rows, :] = v_ref[:, place]
            out[rows:, :] = g_ref[:, place]


def pack_kernel(n_ctx, width_all, sel, square_ref, q_gain, k_gain, q_ref, k_ref, v_ref, g_ref, *outs):
    heads_dev, remote_count = sel.shape[1:]
    rows = q_ref.shape[0]
    block, group = lax.axis_index("ctx"), lax.axis_index("head")
    scale_rows = row_scales(square_ref, width_all)
    scales = [column(scale_rows[at : at + 1, :], HD) for at in range(2)]
    lane = lax.broadcasted_iota(jnp.int32, (PICK_ROWS, HD), 1)
    for mask, out in zip(far_masks(n_ctx) + near_masks(n_ctx), outs):
        head = head_at(block ^ mask, group, n_ctx, heads_dev)

        @pl.when(head >= 0)
        def _(mask=mask, head=head, out=out):
            place = pl.ds(pl.multiple_of(head * HD, HD), HD)
            for at, (ref, gain) in enumerate(((q_ref, q_gain), (k_ref, k_gain))):
                normed = ref[:, place].astype(jnp.float32) * scales[at] * gain[pl.ds(head, 1), :]
                out[at * rows : (at + 1) * rows, :] = normed.astype(jnp.bfloat16)
            picks = jnp.zeros((PICK_ROWS, HD), jnp.float32)
            for slot in range(remote_count):
                picks = jnp.where(lane == slot, sel[0, head, slot].astype(jnp.float32), picks)
            after = 2 * rows + PICK_ROWS
            out[2 * rows : after, :] = picks.astype(jnp.bfloat16)
            if mask < n_ctx // 2:
                out[after : after + rows, :] = v_ref[:, place]
                out[after + rows :, :] = g_ref[:, place]


def attend_kernel(n_ctx, heads_dev, remote_count, *refs):
    half = n_ctx // 2
    far, near, back = far_masks(n_ctx), near_masks(n_ctx), back_masks(n_ctx)
    far_vg = dict(zip(far, refs[:half]))
    qk = dict(zip(far + near, refs[half : half + n_ctx]))
    outs = dict(zip(back, refs[half + n_ctx : half + 2 * n_ctx]))
    scratch = refs[half + 2 * n_ctx :]
    q_ref, g_ref, k_ref, kt_ref, v_ref, dq_ref, dk_ref, dv_ref, ds_ref, kt_picked = scratch[:10]
    picks_ref, picks, sem = scratch[10:13]
    buffers = (scratch[13:16], scratch[16:19])
    rows = q_ref.shape[1]
    near_tiles = rows // TILE
    n_keys = near_tiles + remote_count
    factor = 1.0 / math.sqrt(HD)
    to_base2 = factor * math.log2(math.e)
    own_block = lax.axis_index("ctx")
    own_head = head_at(own_block, lax.axis_index("head"), n_ctx, heads_dev)

    def rows_of(block):
        return pl.ds(pl.multiple_of(block * rows, rows), rows)

    def places_of(mask):
        block = own_block ^ mask
        return [
            pl.ds(pl.multiple_of(block * rows + tile * TILE, TILE), TILE)
            for tile in range(near_tiles)
        ] + [
            pl.ds(pl.multiple_of(picks[mask, slot] * TILE, TILE), TILE)
            for slot in range(remote_count)
        ]

    def prepare(mask):
        place = rows_of(own_block ^ mask)
        q_ref[mask] = qk[mask][:rows, :]
        keys = qk[mask][rows : 2 * rows, :]
        k_ref[place, :] = keys
        kt_ref[:, place] = keys.T
        vg, at = (far_vg[mask], 0) if mask >= half else (qk[mask], 2 * rows + PICK_ROWS)
        v_ref[place, :] = vg[at : at + rows, :]
        g_ref[mask] = vg[at + rows : at + 2 * rows, :]

    def scores(mask, slot, place, buffer):
        weight_ref, dprob_ref, stat_ref = buffer
        score = lax.dot_general(
            k_ref[place, :], q_ref[mask], NT, preferred_element_type=jnp.float32
        )
        dprob = lax.dot_general(
            v_ref[place, :], g_ref[mask], NT, preferred_element_type=jnp.float32
        )
        top = jnp.max(score, axis=0, keepdims=True)
        weight = jnp.exp2((score - top) * to_base2)
        weight_ref[slot] = weight
        dprob_ref[slot] = dprob
        stat_ref[0, slot : slot + 1, :] = top * to_base2
        stat_ref[1, slot : slot + 1, :] = jnp.sum(weight, axis=0, keepdims=True)
        stat_ref[2, slot : slot + 1, :] = jnp.sum(weight * dprob, axis=0, keepdims=True)

    def settle(buffer):
        stat_ref = buffer[2]
        tops = stat_ref[0, :n_keys, :]
        shares = jnp.exp2(tops - jnp.max(tops, axis=0, keepdims=True))
        total = jnp.sum(shares * stat_ref[1, :n_keys, :], axis=0, keepdims=True)
        mixed = jnp.sum(shares * stat_ref[2, :n_keys, :], axis=0, keepdims=True)
        inverse = 1.0 / total
        return shares * inverse, mixed * inverse

    def gradients(mask, slot, place, buffer, shares, delta):
        weight_ref, dprob_ref, _ = buffer
        prob = weight_ref[slot] * shares[slot : slot + 1, :]
        dscore = (prob * (dprob_ref[slot] - delta)).astype(jnp.bfloat16)
        ds_ref[slot * TILE : (slot + 1) * TILE, :] = dscore
        kt_picked[:, slot * TILE : (slot + 1) * TILE] = kt_ref[:, place]
        dk_ref[place, :] += jnp.dot(dscore, q_ref[mask], preferred_element_type=jnp.float32)
        dv_ref[place, :] += jnp.dot(
            prob.astype(jnp.bfloat16), g_ref[mask], preferred_element_type=jnp.float32
        )

    def query_gradient(mask):
        dq_t = jnp.dot(kt_picked[...], ds_ref[...], preferred_element_type=jnp.float32)
        dq_ref[mask] = (dq_t * factor).T.astype(jnp.bfloat16)

    def step(mask, buffer, later, later_buffer):
        places = places_of(mask)
        shares, delta = settle(buffer)
        later_places = None if later is None else places_of(later)
        for slot in range(n_keys):
            gradients(mask, slot, places[slot], buffer, shares, delta)
            if later is not None:
                scores(later, slot, later_places[slot], later_buffer)
        query_gradient(mask)

    @pl.when(own_head >= 0)
    def _():
        for mask in range(n_ctx):
            picked = qk[mask][2 * rows : 2 * rows + PICK_ROWS, :].astype(jnp.float32)
            picks_ref[mask : mask + 1, :] = picked.astype(jnp.int32)[:1, :]
        copy = pltpu.make_async_copy(picks_ref, picks, sem)
        copy.start()
        for mask in range(n_ctx):
            prepare(mask)
        dk_ref[...] = jnp.zeros_like(dk_ref)
        dv_ref[...] = jnp.zeros_like(dv_ref)
        copy.wait()
        for slot, place in enumerate(places_of(0)):
            scores(0, slot, place, buffers[0])

        def two(pair, carry):
            step(2 * pair, buffers[0], 2 * pair + 1, buffers[1])
            step(2 * pair + 1, buffers[1], 2 * pair + 2, buffers[0])
            return carry

        lax.fori_loop(0, n_ctx // 2 - 1, two, 0)
        step(n_ctx - 2, buffers[0], n_ctx - 1, buffers[1])
        step(n_ctx - 1, buffers[1], None, None)
        for mask in range(n_ctx):
            place = rows_of(own_block ^ mask)
            outs[mask][0] = dq_ref[mask]
            outs[mask][1] = (dk_ref[place, :] * factor).astype(jnp.bfloat16)
            outs[mask][2] = dv_ref[place, :].astype(jnp.bfloat16)


def attend(far_vg, qk, heads_dev, remote_count):
    n_ctx = len(qk)
    rows = far_vg[0].shape[0] // 2
    tokens = n_ctx * rows
    n_keys = rows // TILE + remote_count
    by_block = pltpu.VMEM((n_ctx, rows, HD), jnp.bfloat16)
    buffer = [
        pltpu.VMEM((n_keys, TILE, rows), jnp.float32),
        pltpu.VMEM((n_keys, TILE, rows), jnp.float32),
        pltpu.VMEM((3, -(-n_keys // 8) * 8, rows), jnp.float32),
    ]
    return pl.pallas_call(
        functools.partial(attend_kernel, n_ctx, heads_dev, remote_count),
        out_shape=[jax.ShapeDtypeStruct((3, rows, HD), jnp.bfloat16)] * n_ctx,
        in_specs=[IN_VMEM] * (len(far_vg) + n_ctx),
        out_specs=[IN_VMEM] * n_ctx,
        scratch_shapes=[
            by_block,
            by_block,
            pltpu.VMEM((tokens, HD), jnp.bfloat16),
            pltpu.VMEM((HD, tokens), jnp.bfloat16),
            pltpu.VMEM((tokens, HD), jnp.bfloat16),
            by_block,
            pltpu.VMEM((tokens, HD), jnp.float32),
            pltpu.VMEM((tokens, HD), jnp.float32),
            pltpu.VMEM((n_keys * TILE, rows), jnp.bfloat16),
            pltpu.VMEM((HD, n_keys * TILE), jnp.bfloat16),
            pltpu.VMEM((n_ctx, HD), jnp.int32),
            pltpu.SMEM((n_ctx, HD), jnp.int32),
            pltpu.SemaphoreType.DMA,
        ]
        + buffer
        + buffer,
        compiler_params=pltpu.CompilerParams(vmem_limit_bytes=VMEM_BYTES),
    )(*far_vg, *qk)


def gather_kernel(n_ctx, heads_dev, q_ref, k_ref, q_gain, k_gain, *refs):
    slots = refs[:n_ctx]
    dot_ref, dq_ref, dk_ref, dv_ref = refs[n_ctx:]
    block, group = lax.axis_index("ctx"), lax.axis_index("head")
    for mask, slot in zip(back_masks(n_ctx), slots):
        head = head_at(block ^ mask, group, n_ctx, heads_dev)

        @pl.when(head >= 0)
        def _(head=head, slot=slot):
            place = pl.ds(pl.multiple_of(head * HD, HD), HD)
            for at, out in enumerate((dq_ref, dk_ref, dv_ref)):
                out[:, place] = slot[at]

    for at, (wide_ref, pre_ref, gain) in enumerate(
        ((dq_ref, q_ref, q_gain), (dk_ref, k_ref, k_gain))
    ):
        terms = gain[...] * wide_ref[...].astype(jnp.float32) * pre_ref[...].astype(jnp.float32)
        dot_ref[at : at + 1, :] = row_sums(terms)


def finish_kernel(width_all, q_ref, k_ref, q_gain, k_gain, square_ref, dot_ref, *refs):
    dq_ref, dk_ref, dq_out, dk_out = refs
    scales = row_scales(square_ref, width_all)
    backs = scales**3 * (dot_ref[...] / width_all)
    for at, (pre_ref, gain, grad_ref, out) in enumerate(
        ((q_ref, q_gain, dq_ref, dq_out), (k_ref, k_gain, dk_ref, dk_out))
    ):
        scale = column(scales[at : at + 1, :], HD)
        back = column(backs[at : at + 1, :], HD)
        for first in range(0, pre_ref.shape[1], HD):
            place = slice(first, first + HD)
            wide = pre_ref[:, place].astype(jnp.float32)
            grad = grad_ref[:, place].astype(jnp.float32)
            out[:, place] = (scale * gain[:, place] * grad - wide * back).astype(jnp.bfloat16)


def heads_to_owners(q_pre, k_pre, values, out_grad, q_gain, k_gain, selected):
    n_ctx = lax.axis_size("ctx")
    n_head = lax.axis_size("head")
    rows, width_dev = q_pre.shape
    width_all = width_dev * n_head
    heads_dev = width_dev // HD
    remote_count = selected.shape[2]
    sizes = (n_ctx, n_head, heads_dev)
    params = pltpu.CompilerParams(vmem_limit_bytes=VMEM_BYTES)
    by_row = jax.ShapeDtypeStruct((2, rows), jnp.float32)
    wide = jax.ShapeDtypeStruct((rows, width_dev), jnp.bfloat16)

    q_gains = q_gain.reshape(heads_dev, HD)
    k_gains = k_gain.reshape(heads_dev, HD)
    far, near = far_masks(n_ctx), near_masks(n_ctx)

    far_vg = pl.pallas_call(
        functools.partial(pack_far_kernel, n_ctx, heads_dev),
        out_shape=[jax.ShapeDtypeStruct((2 * rows, HD), jnp.bfloat16)] * len(far),
        in_specs=[IN_VMEM] * 2,
        out_specs=[IN_VMEM] * len(far),
        compiler_params=params,
    )(values, out_grad)
    far_vg = move(far, far_vg, False, *sizes)
    squares = pl.pallas_call(
        squares_kernel,
        out_shape=by_row,
        in_specs=[IN_VMEM] * 2,
        out_specs=IN_VMEM,
        compiler_params=params,
    )(q_pre, k_pre)
    squares = lax.psum(squares, "head")
    after = 2 * rows + PICK_ROWS
    qk = pl.pallas_call(
        functools.partial(pack_kernel, n_ctx, width_all),
        out_shape=[jax.ShapeDtypeStruct((after, HD), jnp.bfloat16)] * len(far)
        + [jax.ShapeDtypeStruct((after + 2 * rows, HD), jnp.bfloat16)] * len(near),
        in_specs=[IN_SMEM] + [IN_VMEM] * 7,
        out_specs=[IN_VMEM] * n_ctx,
        compiler_params=params,
    )(selected, squares, q_gains, k_gains, q_pre, k_pre, values, out_grad)
    qk = move(far + near, qk, False, *sizes)
    results = attend(far_vg, qk, heads_dev, remote_count)
    slots = move(back_masks(n_ctx), results, True, *sizes)

    pres = (q_pre, k_pre, q_gain[None], k_gain[None])
    dots, dq_wide, dk_wide, dv = pl.pallas_call(
        functools.partial(gather_kernel, n_ctx, heads_dev),
        out_shape=[by_row, wide, wide, wide],
        in_specs=[IN_VMEM] * (4 + n_ctx),
        out_specs=[IN_VMEM] * 4,
        compiler_params=params,
    )(*pres, *slots)
    dots = lax.psum(dots, "head")
    dq, dk = pl.pallas_call(
        functools.partial(finish_kernel, width_all),
        out_shape=[wide, wide],
        in_specs=[IN_VMEM] * 8,
        out_specs=[IN_VMEM] * 2,
        compiler_params=params,
    )(*pres, squares, dots, dq_wide, dk_wide)
    return dq, dk, dv


def on_device(q_pre, k_pre, values, out_grad, q_gain, k_gain, selected):
    n_ctx = lax.axis_size("ctx")
    tiles_dev, heads_dev, remote_count = selected.shape
    capacity = -(-heads_dev * remote_count // (n_ctx - 1))
    by_head = (n_ctx - 1) * tiles_dev * 7
    by_tile = (n_ctx - 1) * capacity * 6
    paired = n_ctx & (n_ctx - 1) == 0 and n_ctx >= max(heads_dev, 4) and n_ctx * tiles_dev <= 256
    plan = heads_to_owners if paired and by_head <= by_tile else tiles_to_queries
    return plan(q_pre, k_pre, values, out_grad, q_gain, k_gain, selected)


def solution(mesh):
    placed = (
        P("ctx", "head"),
        P("ctx", "head"),
        P("ctx", "head"),
        P("ctx", "head"),
        P("head"),
        P("head"),
        P("ctx", "head", None),
    )
    return jax.shard_map(
        on_device,
        mesh=mesh,
        in_specs=placed,
        out_specs=(P("ctx", "head"), P("ctx", "head"), P("ctx", "head")),
        check_vma=False,
    )
```

```python
import functools
import math

import jax
import jax.numpy as jnp
from jax import lax
from jax.experimental import pallas as pl
from jax.experimental.pallas import tpu as pltpu
from jax.sharding import PartitionSpec as P

HD = 128
TILE = 128


epsilon = 1e-06


def split_heads(array, heads_dev):
    return array.reshape(array.shape[0], heads_dev, HD).transpose(1, 0, 2)


def merge_heads(array):
    heads_dev, tok_dev, depth = array.shape
    return array.transpose(1, 0, 2).reshape(tok_dev, heads_dev * depth)


def per_tile(array, qt_dev):
    heads_dev, tok_dev, depth = array.shape
    return array.reshape(heads_dev, qt_dev, TILE, depth).transpose(1, 0, 2, 3)


def from_tiles(array):
    qt_dev, heads_dev, rows_tile, depth = array.shape
    return array.transpose(1, 0, 2, 3).reshape(heads_dev, qt_dev * rows_tile, depth)


def table_sum(taken, pieces, heads_dev, qt_dev):
    flat_pieces = pieces.reshape(pieces.shape[0], -1)
    summed = jnp.dot(
        taken, flat_pieces, precision=lax.Precision.HIGHEST, preferred_element_type=jnp.float32
    )
    summed = summed.reshape(heads_dev, qt_dev, 2, TILE, HD).transpose(2, 0, 1, 3, 4)
    return summed.reshape(2, heads_dev, qt_dev * TILE, HD)


def rounded(array):
    return array.astype(jnp.bfloat16)


def finish_norm(wide, scale, gain, grad, dot_sum, width_all):
    return (scale * gain * grad - wide * scale**3 * (dot_sum / width_all)[:, None]).astype(
        jnp.bfloat16
    )


def tiles_to_queries(q_pre, k_pre, values, out_grad, q_gain, k_gain, selected):
    n_ctx = lax.axis_size("ctx")
    tok_dev, width_dev = q_pre.shape
    width_all = width_dev * lax.axis_size("head")
    heads_dev = width_dev // HD
    qt_dev = tok_dev // TILE
    remote_count = selected.shape[2]
    factor = 1.0 / math.sqrt(HD)
    q_wide = q_pre.astype(jnp.float32)
    k_wide = k_pre.astype(jnp.float32)
    q_square, k_square = lax.psum(
        (jnp.sum(q_wide * q_wide, axis=1), jnp.sum(k_wide * k_wide, axis=1)), "head"
    )
    q_scale = lax.rsqrt(q_square / width_all + epsilon)[:, None]
    k_scale = lax.rsqrt(k_square / width_all + epsilon)[:, None]
    q_heads = split_heads(rounded(q_wide * q_scale * q_gain), heads_dev)
    k_heads = split_heads(rounded(k_wide * k_scale * k_gain), heads_dev)
    v_heads = split_heads(values, heads_dev)
    g_heads = split_heads(out_grad, heads_dev)
    q_tiles = per_tile(q_heads, qt_dev)
    g_tiles = per_tile(g_heads, qt_dev)
    k_table = k_heads.reshape(heads_dev * qt_dev, TILE, HD)
    v_table = v_heads.reshape(heads_dev * qt_dev, TILE, HD)
    flat_sel = selected[0].reshape(-1)
    n_slot = flat_sel.shape[0]
    capacity = -(-n_slot // (n_ctx - 1))
    n_buffer = n_ctx * capacity
    owners = flat_sel // qt_dev
    head_of = jnp.arange(n_slot, dtype=jnp.int32) // remote_count
    codes = head_of * qt_dev + flat_sel % qt_dev
    matches = (owners[:, None] == jnp.arange(n_ctx, dtype=jnp.int32)[None, :]).astype(jnp.int32)
    ranks = jnp.sum((jnp.cumsum(matches, axis=0) - matches) * matches, axis=1)
    position = owners * capacity + ranks
    placed = position[None, :] == jnp.arange(n_buffer, dtype=jnp.int32)[:, None]
    request = jnp.sum(jnp.where(placed, codes[None, :] + 1, 0), axis=1) - 1
    asked = lax.all_to_all(
        request.reshape(n_ctx, capacity), "ctx", split_axis=0, concat_axis=0, tiled=True
    ).reshape(n_buffer)
    clipped = jnp.maximum(asked, 0)
    taken = (asked[None, :] == jnp.arange(heads_dev * qt_dev, dtype=jnp.int32)[:, None]).astype(
        jnp.float32
    )
    s_near = (
        jnp.einsum("rhqd,hkd->rhqk", q_tiles, k_heads, preferred_element_type=jnp.float32) * factor
    )
    dp_near = jnp.einsum("rhqd,hkd->rhqk", g_tiles, v_heads, preferred_element_type=jnp.float32)
    near_top = jnp.max(s_near, axis=-1)
    outgoing = jnp.stack((k_table[clipped], v_table[clipped]), axis=1).reshape(
        n_ctx, capacity, 2, TILE, HD
    )
    incoming = lax.all_to_all(outgoing, "ctx", split_axis=0, concat_axis=0, tiled=True).reshape(
        n_buffer, 2, TILE, HD
    )
    slot_kv = incoming[position].reshape(heads_dev, remote_count, 2, TILE, HD)
    far_k = slot_kv[:, :, 0]
    far_v = slot_kv[:, :, 1]
    s_far = (
        jnp.einsum("rhqd,hckd->rhqck", q_tiles, far_k, preferred_element_type=jnp.float32) * factor
    )
    dp_far = jnp.einsum("rhqd,hckd->rhqck", g_tiles, far_v, preferred_element_type=jnp.float32)
    row_top = jnp.maximum(near_top, jnp.max(s_far, axis=(-2, -1)))
    totals = jnp.sum(jnp.exp(s_near - row_top[..., None]), axis=-1) + jnp.sum(
        jnp.exp(s_far - row_top[..., None, None]), axis=(-2, -1)
    )
    lse = row_top + jnp.log(totals)
    p_near = jnp.exp(s_near - lse[..., None])
    p_far = jnp.exp(s_far - lse[..., None, None])
    delta = jnp.sum(p_near * dp_near, axis=-1) + jnp.sum(p_far * dp_far, axis=(-2, -1))
    ds_near = rounded(p_near * (dp_near - delta[..., None]) * factor)
    pb_near = rounded(p_near)
    dq_near = jnp.einsum("rhqk,hkd->rhqd", ds_near, k_heads, preferred_element_type=jnp.float32)
    dk_near = jnp.einsum("rhqk,rhqd->hkd", ds_near, q_tiles, preferred_element_type=jnp.float32)
    dv_near = jnp.einsum("rhqk,rhqd->hkd", pb_near, g_tiles, preferred_element_type=jnp.float32)
    dq_near, dk_near, dv_near = (dq_near, dk_near, dv_near)
    ds_far = rounded(p_far * (dp_far - delta[..., None, None]) * factor)
    pb_far = rounded(p_far)
    dq_far = jnp.einsum("rhqck,hckd->rhqd", ds_far, far_k, preferred_element_type=jnp.float32)
    dq_wide = merge_heads(from_tiles(dq_near + dq_far))
    q_dot = jnp.sum(q_gain * dq_wide * q_wide, axis=1)
    dq_wide, q_dot = (dq_wide, q_dot)
    dk_far = jnp.einsum("rhqck,rhqd->hckd", ds_far, q_tiles, preferred_element_type=jnp.float32)
    dv_far = jnp.einsum("rhqck,rhqd->hckd", pb_far, g_tiles, preferred_element_type=jnp.float32)
    grads = jnp.stack((dk_far, dv_far), axis=2).reshape(n_slot, 2, TILE, HD)
    sending = jnp.zeros((n_buffer, 2, TILE, HD), jnp.float32).at[position].set(grads)
    returned = lax.all_to_all(
        sending.reshape(n_ctx, capacity, 2, TILE, HD),
        "ctx",
        split_axis=0,
        concat_axis=0,
        tiled=True,
    ).reshape(n_buffer, 2, TILE, HD)
    far_sums = table_sum(taken, returned, heads_dev, qt_dev)
    dk_wide = merge_heads(dk_near + far_sums[0])
    dv_heads = dv_near + far_sums[1]
    k_dot = jnp.sum(k_gain * dk_wide * k_wide, axis=1)
    q_dot, k_dot = lax.psum((q_dot, k_dot), "head")
    dq_result = finish_norm(q_wide, q_scale, q_gain, dq_wide, q_dot, width_all)
    dk_result = finish_norm(k_wide, k_scale, k_gain, dk_wide, k_dot, width_all)
    return (dq_result, dk_result, merge_heads(dv_heads).astype(jnp.bfloat16))


VMEM_BYTES = 48 * 2**20
PIECES = 4
NT = (((1,), (1,)), ((), ()))
IN_VMEM = pl.BlockSpec(memory_space=pltpu.VMEM)
IN_SMEM = pl.BlockSpec(memory_space=pltpu.SMEM)


def owners_of(group, n_ctx, heads_dev):
    places = [(4 * head + 1) * n_ctx // (4 * heads_dev) for head in range(heads_dev)]
    return [n_ctx - 1 - place if group % 2 else place for place in places]


def head_at(place, group, n_ctx, heads_dev):
    even = jnp.where(group % 2 == 1, n_ctx - 1 - place, place)
    head = -1
    for index, owner in enumerate(owners_of(0, n_ctx, heads_dev)):
        head = jnp.where(even == owner, index, head)
    return head


def pairs_to_owner(mask, n_ctx, n_head, heads_dev):
    pairs = []
    for group in range(n_head):
        owners = owners_of(group, n_ctx, heads_dev)
        for block in range(n_ctx):
            if block ^ mask in owners:
                pairs.append((block * n_head + group, (block ^ mask) * n_head + group))
    return pairs


def there_masks(n_ctx):
    return list(range(n_ctx - 1, -1, -1))


def back_masks(n_ctx):
    return list(range(n_ctx // 2 - 1, 0, -1)) + list(range(n_ctx - 1, n_ctx // 2 - 1, -1)) + [0]


def move(masks, arrays, back, n_ctx, n_head, heads_dev):
    moved = []
    for mask, array in zip(masks, arrays):
        pairs = pairs_to_owner(mask, n_ctx, n_head, heads_dev)
        if back:
            pairs = [(b, a) for a, b in pairs]
        moved.append(lax.ppermute(array, ("ctx", "head"), pairs) if mask else array)
    return moved


def column(row, width):
    return jnp.broadcast_to(row, (width, row.shape[1])).T


def row_sums(wide):
    total = wide[:, :HD]
    for at in range(HD, wide.shape[1], HD):
        total = total + wide[:, at : at + HD]
    return jnp.sum(total.T, axis=0, keepdims=True)


def pack_kernel(n_ctx, heads_dev, *refs):
    inputs, square_ref, outs = refs[:4], refs[4], refs[5 : 5 + n_ctx]
    held, sems = refs[5 + n_ctx :]
    rows = held.shape[1]
    piece = rows // PIECES
    block, group = lax.axis_index("ctx"), lax.axis_index("head")

    def copy(at, part):
        place = pl.ds(part * piece, piece)
        return pltpu.make_async_copy(
            inputs[at].at[place, :], held.at[at, place, :], sems.at[at, part]
        )

    for at in range(4):
        for part in range(PIECES):
            copy(at, part).start()
    for at in range(4):
        for part in range(PIECES):
            copy(at, part).wait()
    for mask, out in zip(there_masks(n_ctx), outs):
        head = head_at(block ^ mask, group, n_ctx, heads_dev)

        @pl.when(head >= 0)
        def _(head=head, out=out):
            place = pl.ds(pl.multiple_of(head * HD, HD), HD)
            for at in range(4):
                out[at] = held[at, :, place]

    for at in range(2):
        wide = held[at].astype(jnp.float32)
        square_ref[at : at + 1, :] = row_sums(wide * wide)


def pack(arrays, n_ctx):
    rows, width_dev = arrays[0].shape
    result = pl.pallas_call(
        functools.partial(pack_kernel, n_ctx, width_dev // HD),
        out_shape=[jax.ShapeDtypeStruct((2, rows), jnp.float32)]
        + [jax.ShapeDtypeStruct((4, rows, HD), jnp.bfloat16)] * n_ctx,
        in_specs=[pl.BlockSpec(memory_space=pltpu.HBM)] * 4,
        out_specs=[IN_VMEM] * (n_ctx + 1),
        scratch_shapes=[
            pltpu.VMEM((4, rows, width_dev), jnp.bfloat16),
            pltpu.SemaphoreType.DMA((4, PIECES)),
        ],
        compiler_params=pltpu.CompilerParams(vmem_limit_bytes=VMEM_BYTES),
    )(*[pltpu.with_memory_space_constraint(array, pltpu.HBM) for array in arrays])
    return result[0], result[1:]


def attend_kernel(n_ctx, heads_dev, picks, scale_ref, q_gain, k_gain, *refs):
    messages = dict(zip(there_masks(n_ctx), refs[:n_ctx]))
    outs = dict(zip(back_masks(n_ctx), refs[n_ctx : 2 * n_ctx]))
    scratch = refs[2 * n_ctx :]
    q_ref, g_ref, k_ref, kt_ref, v_ref, dq_ref, dk_ref, dv_ref, ds_ref, kt_picked = scratch[:10]
    buffers = (scratch[10:13], scratch[13:16])
    rows = messages[0].shape[1]
    remote_count = picks.shape[1]
    near = rows // TILE
    n_keys = near + remote_count
    factor = 1.0 / math.sqrt(HD)
    to_base2 = factor * math.log2(math.e)
    own_block = lax.axis_index("ctx")
    own_head = head_at(own_block, lax.axis_index("head"), n_ctx, heads_dev)

    def rows_of(block):
        return pl.ds(pl.multiple_of(block * rows, rows), rows)

    def places_of(block):
        return [
            pl.ds(pl.multiple_of(block * rows + tile * TILE, TILE), TILE) for tile in range(near)
        ] + [
            pl.ds(pl.multiple_of(picks[block, slot] * TILE, TILE), TILE)
            for slot in range(remote_count)
        ]

    def prepare(mask):
        block = own_block ^ mask
        place = rows_of(block)
        q_scale = column(scale_ref[block, 0:1, :], HD)
        k_scale = column(scale_ref[block, 1:2, :], HD)
        q_normed = messages[mask][0].astype(jnp.float32) * q_scale * q_gain[pl.ds(own_head, 1), :]
        k_normed = messages[mask][1].astype(jnp.float32) * k_scale * k_gain[pl.ds(own_head, 1), :]
        q_ref[mask] = q_normed.astype(jnp.bfloat16)
        k_ref[place, :] = k_normed.astype(jnp.bfloat16)
        kt_ref[:, place] = k_normed.T.astype(jnp.bfloat16)
        v_ref[place, :] = messages[mask][2]
        g_ref[mask] = messages[mask][3]

    def scores(mask, slot, place, buffer):
        weight_ref, dprob_ref, stat_ref = buffer
        score = lax.dot_general(
            k_ref[place, :], q_ref[mask], NT, preferred_element_type=jnp.float32
        )
        dprob = lax.dot_general(
            v_ref[place, :], g_ref[mask], NT, preferred_element_type=jnp.float32
        )
        top = jnp.max(score, axis=0, keepdims=True)
        weight = jnp.exp2((score - top) * to_base2)
        weight_ref[slot] = weight
        dprob_ref[slot] = dprob
        stat_ref[0, slot : slot + 1, :] = top * to_base2
        stat_ref[1, slot : slot + 1, :] = jnp.sum(weight, axis=0, keepdims=True)
        stat_ref[2, slot : slot + 1, :] = jnp.sum(weight * dprob, axis=0, keepdims=True)

    def settle(buffer):
        stat_ref = buffer[2]
        tops = stat_ref[0, :n_keys, :]
        shares = jnp.exp2(tops - jnp.max(tops, axis=0, keepdims=True))
        total = jnp.sum(shares * stat_ref[1, :n_keys, :], axis=0, keepdims=True)
        mixed = jnp.sum(shares * stat_ref[2, :n_keys, :], axis=0, keepdims=True)
        inverse = 1.0 / total
        return shares * inverse, mixed * inverse

    def gradients(mask, slot, place, buffer, shares, delta):
        weight_ref, dprob_ref, _ = buffer
        prob = weight_ref[slot] * shares[slot : slot + 1, :]
        dscore = (prob * (dprob_ref[slot] - delta)).astype(jnp.bfloat16)
        ds_ref[slot * TILE : (slot + 1) * TILE, :] = dscore
        kt_picked[:, slot * TILE : (slot + 1) * TILE] = kt_ref[:, place]
        dk_ref[place, :] += jnp.dot(dscore, q_ref[mask], preferred_element_type=jnp.float32)
        dv_ref[place, :] += jnp.dot(
            prob.astype(jnp.bfloat16), g_ref[mask], preferred_element_type=jnp.float32
        )

    def query_gradient(mask):
        dq_t = jnp.dot(kt_picked[...], ds_ref[...], preferred_element_type=jnp.float32)
        dq_ref[mask] = (dq_t * factor).T.astype(jnp.bfloat16)

    def step(mask, buffer, later, later_buffer):
        places = places_of(own_block ^ mask)
        shares, delta = settle(buffer)
        later_places = None if later is None else places_of(own_block ^ later)
        for slot in range(n_keys):
            gradients(mask, slot, places[slot], buffer, shares, delta)
            if later is not None:
                scores(later, slot, later_places[slot], later_buffer)
        query_gradient(mask)

    @pl.when(own_head >= 0)
    def _():
        for mask in range(n_ctx):
            prepare(mask)
        dk_ref[...] = jnp.zeros_like(dk_ref)
        dv_ref[...] = jnp.zeros_like(dv_ref)
        for slot, place in enumerate(places_of(own_block)):
            scores(0, slot, place, buffers[0])

        def two(pair, carry):
            step(2 * pair, buffers[0], 2 * pair + 1, buffers[1])
            step(2 * pair + 1, buffers[1], 2 * pair + 2, buffers[0])
            return carry

        lax.fori_loop(0, n_ctx // 2 - 1, two, 0)
        step(n_ctx - 2, buffers[0], n_ctx - 1, buffers[1])
        step(n_ctx - 1, buffers[1], None, None)
        for mask in range(n_ctx):
            place = rows_of(own_block ^ mask)
            outs[mask][0] = dq_ref[mask]
            outs[mask][1] = (dk_ref[place, :] * factor).astype(jnp.bfloat16)
            outs[mask][2] = dv_ref[place, :].astype(jnp.bfloat16)


def attend(picks, scales, q_gain, k_gain, messages, n_ctx):
    rows = messages[0].shape[1]
    tokens = n_ctx * rows
    n_keys = rows // TILE + picks.shape[1]
    by_block = pltpu.VMEM((n_ctx, rows, HD), jnp.bfloat16)
    buffer = [
        pltpu.VMEM((n_keys, TILE, rows), jnp.float32),
        pltpu.VMEM((n_keys, TILE, rows), jnp.float32),
        pltpu.VMEM((3, -(-n_keys // 8) * 8, rows), jnp.float32),
    ]
    return pl.pallas_call(
        functools.partial(attend_kernel, n_ctx, q_gain.shape[0]),
        out_shape=[jax.ShapeDtypeStruct((3, rows, HD), jnp.bfloat16)] * n_ctx,
        in_specs=[IN_SMEM] + [IN_VMEM] * (3 + n_ctx),
        out_specs=[IN_VMEM] * n_ctx,
        scratch_shapes=[
            by_block,
            by_block,
            pltpu.VMEM((tokens, HD), jnp.bfloat16),
            pltpu.VMEM((HD, tokens), jnp.bfloat16),
            pltpu.VMEM((tokens, HD), jnp.bfloat16),
            by_block,
            pltpu.VMEM((tokens, HD), jnp.float32),
            pltpu.VMEM((tokens, HD), jnp.float32),
            pltpu.VMEM((n_keys * TILE, rows), jnp.bfloat16),
            pltpu.VMEM((HD, n_keys * TILE), jnp.bfloat16),
        ]
        + buffer
        + buffer,
        compiler_params=pltpu.CompilerParams(vmem_limit_bytes=VMEM_BYTES),
    )(picks, scales, q_gain, k_gain, *messages)


def gather_kernel(n_ctx, heads_dev, q_ref, k_ref, q_gain, k_gain, *refs):
    slots = refs[:n_ctx]
    dot_ref, dq_ref, dk_ref, dv_ref = refs[n_ctx:]
    block, group = lax.axis_index("ctx"), lax.axis_index("head")
    for mask, slot in zip(back_masks(n_ctx), slots):
        head = head_at(block ^ mask, group, n_ctx, heads_dev)

        @pl.when(head >= 0)
        def _(head=head, slot=slot):
            place = pl.ds(pl.multiple_of(head * HD, HD), HD)
            for at, out in enumerate((dq_ref, dk_ref, dv_ref)):
                out[:, place] = slot[at]

    for at, (wide_ref, pre_ref, gain) in enumerate(
        ((dq_ref, q_ref, q_gain), (dk_ref, k_ref, k_gain))
    ):
        terms = gain[...] * wide_ref[...].astype(jnp.float32) * pre_ref[...].astype(jnp.float32)
        dot_ref[at : at + 1, :] = row_sums(terms)


def finish_kernel(width_all, q_ref, k_ref, q_gain, k_gain, scale_ref, dot_ref, *refs):
    dq_ref, dk_ref, dq_out, dk_out = refs
    scales = scale_ref[lax.axis_index("ctx")]
    backs = scales**3 * (dot_ref[...] / width_all)
    for at, (pre_ref, gain, grad_ref, out) in enumerate(
        ((q_ref, q_gain, dq_ref, dq_out), (k_ref, k_gain, dk_ref, dk_out))
    ):
        scale = column(scales[at : at + 1, :], HD)
        back = column(backs[at : at + 1, :], HD)
        for first in range(0, pre_ref.shape[1], HD):
            place = slice(first, first + HD)
            wide = pre_ref[:, place].astype(jnp.float32)
            grad = grad_ref[:, place].astype(jnp.float32)
            out[:, place] = (scale * gain[:, place] * grad - wide * back).astype(jnp.bfloat16)


def heads_to_owners(q_pre, k_pre, values, out_grad, q_gain, k_gain, selected):
    n_ctx = lax.axis_size("ctx")
    n_head = lax.axis_size("head")
    rows, width_dev = q_pre.shape
    width_all = width_dev * n_head
    heads_dev = width_dev // HD
    remote_count = selected.shape[2]
    sizes = (n_ctx, n_head, heads_dev)
    params = pltpu.CompilerParams(vmem_limit_bytes=VMEM_BYTES)

    by_row = jax.ShapeDtypeStruct((2, rows), jnp.float32)
    wide = jax.ShapeDtypeStruct((rows, width_dev), jnp.bfloat16)

    squares, sent = pack((q_pre, k_pre, values, out_grad), n_ctx)
    messages = move(there_masks(n_ctx), sent, False, *sizes)

    wishes = selected[0].reshape(1, -1).astype(jnp.float32)
    wishes = jnp.pad(wishes, ((0, 0), (0, rows - wishes.shape[1])))
    small = jnp.concatenate((squares, wishes), axis=0)
    small = jnp.broadcast_to(small[None], (n_ctx,) + small.shape)
    small = lax.all_to_all(small, "ctx", split_axis=0, concat_axis=0, tiled=True)
    squares = lax.psum(small[:, :2], "head")
    scales = lax.rsqrt(squares / width_all + epsilon)
    own_head = head_at(lax.axis_index("ctx"), lax.axis_index("head"), n_ctx, heads_dev)
    first = jnp.maximum(own_head, 0) * remote_count
    picks = lax.dynamic_slice_in_dim(small[:, 2], first, remote_count, 1).astype(jnp.int32)

    q_gains = q_gain.reshape(heads_dev, HD)
    k_gains = k_gain.reshape(heads_dev, HD)
    results = attend(picks, scales, q_gains, k_gains, messages, n_ctx)
    slots = move(back_masks(n_ctx), results, True, *sizes)

    pres = (q_pre, k_pre, q_gain[None], k_gain[None])
    dots, dq_wide, dk_wide, dv = pl.pallas_call(
        functools.partial(gather_kernel, n_ctx, heads_dev),
        out_shape=[by_row, wide, wide, wide],
        in_specs=[IN_VMEM] * (4 + n_ctx),
        out_specs=[IN_VMEM] * 4,
        compiler_params=params,
    )(*pres, *slots)
    dots = lax.psum(dots, "head")
    dq, dk = pl.pallas_call(
        functools.partial(finish_kernel, width_all),
        out_shape=[wide, wide],
        in_specs=[IN_VMEM] * 8,
        out_specs=[IN_VMEM] * 2,
        compiler_params=params,
    )(*pres, scales, dots, dq_wide, dk_wide)
    return dq, dk, dv


def on_device(q_pre, k_pre, values, out_grad, q_gain, k_gain, selected):
    n_ctx = lax.axis_size("ctx")
    tiles_dev, heads_dev, remote_count = selected.shape
    capacity = -(-heads_dev * remote_count // (n_ctx - 1))
    by_head = (n_ctx - 1) * tiles_dev * 7
    by_tile = (n_ctx - 1) * capacity * 6
    paired = n_ctx & (n_ctx - 1) == 0 and n_ctx >= max(heads_dev, 4)
    plan = heads_to_owners if paired and by_head <= by_tile else tiles_to_queries
    return plan(q_pre, k_pre, values, out_grad, q_gain, k_gain, selected)


def solution(mesh):
    placed = (
        P("ctx", "head"),
        P("ctx", "head"),
        P("ctx", "head"),
        P("ctx", "head"),
        P("head"),
        P("head"),
        P("ctx", "head", None),
    )
    return jax.shard_map(
        on_device,
        mesh=mesh,
        in_specs=placed,
        out_specs=(P("ctx", "head"), P("ctx", "head"), P("ctx", "head")),
        check_vma=False,
    )
```

```python
import functools
import math

import jax
import jax.numpy as jnp
from jax import lax
from jax.experimental import pallas as pl
from jax.experimental.pallas import tpu as pltpu
from jax.sharding import PartitionSpec as P

HD = 128
TILE = 128


epsilon = 1e-06


def split_heads(array, heads_dev):
    return array.reshape(array.shape[0], heads_dev, HD).transpose(1, 0, 2)


def merge_heads(array):
    heads_dev, tok_dev, depth = array.shape
    return array.transpose(1, 0, 2).reshape(tok_dev, heads_dev * depth)


def per_tile(array, qt_dev):
    heads_dev, tok_dev, depth = array.shape
    return array.reshape(heads_dev, qt_dev, TILE, depth).transpose(1, 0, 2, 3)


def from_tiles(array):
    qt_dev, heads_dev, rows_tile, depth = array.shape
    return array.transpose(1, 0, 2, 3).reshape(heads_dev, qt_dev * rows_tile, depth)


def table_sum(taken, pieces, heads_dev, qt_dev):
    flat_pieces = pieces.reshape(pieces.shape[0], -1)
    summed = jnp.dot(
        taken, flat_pieces, precision=lax.Precision.HIGHEST, preferred_element_type=jnp.float32
    )
    summed = summed.reshape(heads_dev, qt_dev, 2, TILE, HD).transpose(2, 0, 1, 3, 4)
    return summed.reshape(2, heads_dev, qt_dev * TILE, HD)


def rounded(array):
    return array.astype(jnp.bfloat16)


def finish_norm(wide, scale, gain, grad, dot_sum, width_all):
    return (scale * gain * grad - wide * scale**3 * (dot_sum / width_all)[:, None]).astype(
        jnp.bfloat16
    )


def tiles_to_queries(q_pre, k_pre, values, out_grad, q_gain, k_gain, selected):
    n_ctx = lax.axis_size("ctx")
    tok_dev, width_dev = q_pre.shape
    width_all = width_dev * lax.axis_size("head")
    heads_dev = width_dev // HD
    qt_dev = tok_dev // TILE
    remote_count = selected.shape[2]
    factor = 1.0 / math.sqrt(HD)
    q_wide = q_pre.astype(jnp.float32)
    k_wide = k_pre.astype(jnp.float32)
    q_square, k_square = lax.psum(
        (jnp.sum(q_wide * q_wide, axis=1), jnp.sum(k_wide * k_wide, axis=1)), "head"
    )
    q_scale = lax.rsqrt(q_square / width_all + epsilon)[:, None]
    k_scale = lax.rsqrt(k_square / width_all + epsilon)[:, None]
    q_heads = split_heads(rounded(q_wide * q_scale * q_gain), heads_dev)
    k_heads = split_heads(rounded(k_wide * k_scale * k_gain), heads_dev)
    v_heads = split_heads(values, heads_dev)
    g_heads = split_heads(out_grad, heads_dev)
    q_tiles = per_tile(q_heads, qt_dev)
    g_tiles = per_tile(g_heads, qt_dev)
    k_table = k_heads.reshape(heads_dev * qt_dev, TILE, HD)
    v_table = v_heads.reshape(heads_dev * qt_dev, TILE, HD)
    flat_sel = selected[0].reshape(-1)
    n_slot = flat_sel.shape[0]
    capacity = -(-n_slot // (n_ctx - 1))
    n_buffer = n_ctx * capacity
    owners = flat_sel // qt_dev
    head_of = jnp.arange(n_slot, dtype=jnp.int32) // remote_count
    codes = head_of * qt_dev + flat_sel % qt_dev
    matches = (owners[:, None] == jnp.arange(n_ctx, dtype=jnp.int32)[None, :]).astype(jnp.int32)
    ranks = jnp.sum((jnp.cumsum(matches, axis=0) - matches) * matches, axis=1)
    position = owners * capacity + ranks
    placed = position[None, :] == jnp.arange(n_buffer, dtype=jnp.int32)[:, None]
    request = jnp.sum(jnp.where(placed, codes[None, :] + 1, 0), axis=1) - 1
    asked = lax.all_to_all(
        request.reshape(n_ctx, capacity), "ctx", split_axis=0, concat_axis=0, tiled=True
    ).reshape(n_buffer)
    clipped = jnp.maximum(asked, 0)
    taken = (asked[None, :] == jnp.arange(heads_dev * qt_dev, dtype=jnp.int32)[:, None]).astype(
        jnp.float32
    )
    s_near = (
        jnp.einsum("rhqd,hkd->rhqk", q_tiles, k_heads, preferred_element_type=jnp.float32) * factor
    )
    dp_near = jnp.einsum("rhqd,hkd->rhqk", g_tiles, v_heads, preferred_element_type=jnp.float32)
    near_top = jnp.max(s_near, axis=-1)
    outgoing = jnp.stack((k_table[clipped], v_table[clipped]), axis=1).reshape(
        n_ctx, capacity, 2, TILE, HD
    )
    incoming = lax.all_to_all(outgoing, "ctx", split_axis=0, concat_axis=0, tiled=True).reshape(
        n_buffer, 2, TILE, HD
    )
    slot_kv = incoming[position].reshape(heads_dev, remote_count, 2, TILE, HD)
    far_k = slot_kv[:, :, 0]
    far_v = slot_kv[:, :, 1]
    s_far = (
        jnp.einsum("rhqd,hckd->rhqck", q_tiles, far_k, preferred_element_type=jnp.float32) * factor
    )
    dp_far = jnp.einsum("rhqd,hckd->rhqck", g_tiles, far_v, preferred_element_type=jnp.float32)
    row_top = jnp.maximum(near_top, jnp.max(s_far, axis=(-2, -1)))
    totals = jnp.sum(jnp.exp(s_near - row_top[..., None]), axis=-1) + jnp.sum(
        jnp.exp(s_far - row_top[..., None, None]), axis=(-2, -1)
    )
    lse = row_top + jnp.log(totals)
    p_near = jnp.exp(s_near - lse[..., None])
    p_far = jnp.exp(s_far - lse[..., None, None])
    delta = jnp.sum(p_near * dp_near, axis=-1) + jnp.sum(p_far * dp_far, axis=(-2, -1))
    ds_near = rounded(p_near * (dp_near - delta[..., None]) * factor)
    pb_near = rounded(p_near)
    dq_near = jnp.einsum("rhqk,hkd->rhqd", ds_near, k_heads, preferred_element_type=jnp.float32)
    dk_near = jnp.einsum("rhqk,rhqd->hkd", ds_near, q_tiles, preferred_element_type=jnp.float32)
    dv_near = jnp.einsum("rhqk,rhqd->hkd", pb_near, g_tiles, preferred_element_type=jnp.float32)
    dq_near, dk_near, dv_near = (dq_near, dk_near, dv_near)
    ds_far = rounded(p_far * (dp_far - delta[..., None, None]) * factor)
    pb_far = rounded(p_far)
    dq_far = jnp.einsum("rhqck,hckd->rhqd", ds_far, far_k, preferred_element_type=jnp.float32)
    dq_wide = merge_heads(from_tiles(dq_near + dq_far))
    q_dot = jnp.sum(q_gain * dq_wide * q_wide, axis=1)
    dq_wide, q_dot = (dq_wide, q_dot)
    dk_far = jnp.einsum("rhqck,rhqd->hckd", ds_far, q_tiles, preferred_element_type=jnp.float32)
    dv_far = jnp.einsum("rhqck,rhqd->hckd", pb_far, g_tiles, preferred_element_type=jnp.float32)
    grads = jnp.stack((dk_far, dv_far), axis=2).reshape(n_slot, 2, TILE, HD)
    sending = jnp.zeros((n_buffer, 2, TILE, HD), jnp.float32).at[position].set(grads)
    returned = lax.all_to_all(
        sending.reshape(n_ctx, capacity, 2, TILE, HD),
        "ctx",
        split_axis=0,
        concat_axis=0,
        tiled=True,
    ).reshape(n_buffer, 2, TILE, HD)
    far_sums = table_sum(taken, returned, heads_dev, qt_dev)
    dk_wide = merge_heads(dk_near + far_sums[0])
    dv_heads = dv_near + far_sums[1]
    k_dot = jnp.sum(k_gain * dk_wide * k_wide, axis=1)
    q_dot, k_dot = lax.psum((q_dot, k_dot), "head")
    dq_result = finish_norm(q_wide, q_scale, q_gain, dq_wide, q_dot, width_all)
    dk_result = finish_norm(k_wide, k_scale, k_gain, dk_wide, k_dot, width_all)
    return (dq_result, dk_result, merge_heads(dv_heads).astype(jnp.bfloat16))


VMEM_BYTES = 48 * 2**20
PIECES = 4
NT = (((1,), (1,)), ((), ()))
IN_VMEM = pl.BlockSpec(memory_space=pltpu.VMEM)
IN_SMEM = pl.BlockSpec(memory_space=pltpu.SMEM)


def owners_of(group, n_ctx, heads_dev):
    places = [(4 * head + 1) * n_ctx // (4 * heads_dev) for head in range(heads_dev)]
    return [n_ctx - 1 - place if group % 2 else place for place in places]


def head_at(place, group, n_ctx, heads_dev):
    even = jnp.where(group % 2 == 1, n_ctx - 1 - place, place)
    head = -1
    for index, owner in enumerate(owners_of(0, n_ctx, heads_dev)):
        head = jnp.where(even == owner, index, head)
    return head


def pairs_to_owner(mask, n_ctx, n_head, heads_dev):
    pairs = []
    for group in range(n_head):
        owners = owners_of(group, n_ctx, heads_dev)
        for block in range(n_ctx):
            if block ^ mask in owners:
                pairs.append((block * n_head + group, (block ^ mask) * n_head + group))
    return pairs


def there_masks(n_ctx):
    return list(range(n_ctx - 1, -1, -1))


def back_masks(n_ctx):
    return list(range(n_ctx // 2 - 1, 0, -1)) + list(range(n_ctx - 1, n_ctx // 2 - 1, -1)) + [0]


def move(masks, arrays, back, n_ctx, n_head, heads_dev):
    moved = []
    for mask, array in zip(masks, arrays):
        pairs = pairs_to_owner(mask, n_ctx, n_head, heads_dev)
        if back:
            pairs = [(b, a) for a, b in pairs]
        moved.append(lax.ppermute(array, ("ctx", "head"), pairs) if mask else array)
    return moved


def column(row, width):
    return jnp.broadcast_to(row, (width, row.shape[1])).T


def row_sums(wide):
    total = wide[:, :HD]
    for at in range(HD, wide.shape[1], HD):
        total = total + wide[:, at : at + HD]
    return jnp.sum(total.T, axis=0, keepdims=True)


def pack_kernel(n_ctx, heads_dev, *refs):
    inputs, square_ref, outs = refs[:4], refs[4], refs[5 : 5 + n_ctx]
    held, sems = refs[5 + n_ctx :]
    rows = held.shape[1]
    piece = rows // PIECES
    block, group = lax.axis_index("ctx"), lax.axis_index("head")

    def copy(at, part):
        place = pl.ds(part * piece, piece)
        return pltpu.make_async_copy(
            inputs[at].at[place, :], held.at[at, place, :], sems.at[at, part]
        )

    for at in range(4):
        for part in range(PIECES):
            copy(at, part).start()
    for at in range(4):
        for part in range(PIECES):
            copy(at, part).wait()
    for mask, out in zip(there_masks(n_ctx), outs):
        head = head_at(block ^ mask, group, n_ctx, heads_dev)

        @pl.when(head >= 0)
        def _(head=head, out=out):
            place = pl.ds(pl.multiple_of(head * HD, HD), HD)
            for at in range(4):
                out[at] = held[at, :, place]

    for at in range(2):
        wide = held[at].astype(jnp.float32)
        square_ref[at : at + 1, :] = row_sums(wide * wide)


def pack(arrays, n_ctx):
    rows, width_dev = arrays[0].shape
    result = pl.pallas_call(
        functools.partial(pack_kernel, n_ctx, width_dev // HD),
        out_shape=[jax.ShapeDtypeStruct((2, rows), jnp.float32)]
        + [jax.ShapeDtypeStruct((4, rows, HD), jnp.bfloat16)] * n_ctx,
        in_specs=[pl.BlockSpec(memory_space=pltpu.HBM)] * 4,
        out_specs=[IN_VMEM] * (n_ctx + 1),
        scratch_shapes=[
            pltpu.VMEM((4, rows, width_dev), jnp.bfloat16),
            pltpu.SemaphoreType.DMA((4, PIECES)),
        ],
        compiler_params=pltpu.CompilerParams(vmem_limit_bytes=VMEM_BYTES),
    )(*[pltpu.with_memory_space_constraint(array, pltpu.HBM) for array in arrays])
    return result[0], result[1:]


def attend_kernel(n_ctx, heads_dev, picks, scale_ref, q_gain, k_gain, *refs):
    messages = dict(zip(there_masks(n_ctx), refs[:n_ctx]))
    outs = dict(zip(back_masks(n_ctx), refs[n_ctx : 2 * n_ctx]))
    scratch = refs[2 * n_ctx :]
    q_ref, g_ref, k_ref, kt_ref, v_ref, dq_ref, dk_ref, dv_ref, ds_ref, kt_picked = scratch[:10]
    buffers = (scratch[10:13], scratch[13:16])
    rows = messages[0].shape[1]
    remote_count = picks.shape[1]
    near = rows // TILE
    n_keys = near + remote_count
    factor = 1.0 / math.sqrt(HD)
    to_base2 = factor * math.log2(math.e)
    own_block = lax.axis_index("ctx")
    own_head = head_at(own_block, lax.axis_index("head"), n_ctx, heads_dev)

    def rows_of(block):
        return pl.ds(pl.multiple_of(block * rows, rows), rows)

    def places_of(block):
        return [
            pl.ds(pl.multiple_of(block * rows + tile * TILE, TILE), TILE) for tile in range(near)
        ] + [
            pl.ds(pl.multiple_of(picks[block, slot] * TILE, TILE), TILE)
            for slot in range(remote_count)
        ]

    def prepare(mask):
        block = own_block ^ mask
        place = rows_of(block)
        q_scale = column(scale_ref[block, 0:1, :], HD)
        k_scale = column(scale_ref[block, 1:2, :], HD)
        q_normed = messages[mask][0].astype(jnp.float32) * q_scale * q_gain[pl.ds(own_head, 1), :]
        k_normed = messages[mask][1].astype(jnp.float32) * k_scale * k_gain[pl.ds(own_head, 1), :]
        q_ref[mask] = q_normed.astype(jnp.bfloat16)
        k_ref[place, :] = k_normed.astype(jnp.bfloat16)
        kt_ref[:, place] = k_normed.T.astype(jnp.bfloat16)
        v_ref[place, :] = messages[mask][2]
        g_ref[mask] = messages[mask][3]

    def scores(mask, slot, place, buffer):
        weight_ref, dprob_ref, stat_ref = buffer
        score = lax.dot_general(
            k_ref[place, :], q_ref[mask], NT, preferred_element_type=jnp.float32
        )
        dprob = lax.dot_general(
            v_ref[place, :], g_ref[mask], NT, preferred_element_type=jnp.float32
        )
        top = jnp.max(score, axis=0, keepdims=True)
        weight = jnp.exp2((score - top) * to_base2)
        weight_ref[slot] = weight
        dprob_ref[slot] = dprob
        stat_ref[0, slot : slot + 1, :] = top * to_base2
        stat_ref[1, slot : slot + 1, :] = jnp.sum(weight, axis=0, keepdims=True)
        stat_ref[2, slot : slot + 1, :] = jnp.sum(weight * dprob, axis=0, keepdims=True)

    def settle(buffer):
        stat_ref = buffer[2]
        tops = stat_ref[0, :n_keys, :]
        shares = jnp.exp2(tops - jnp.max(tops, axis=0, keepdims=True))
        total = jnp.sum(shares * stat_ref[1, :n_keys, :], axis=0, keepdims=True)
        mixed = jnp.sum(shares * stat_ref[2, :n_keys, :], axis=0, keepdims=True)
        inverse = 1.0 / total
        return shares * inverse, mixed * inverse

    def gradients(mask, slot, place, buffer, shares, delta):
        weight_ref, dprob_ref, _ = buffer
        prob = weight_ref[slot] * shares[slot : slot + 1, :]
        dscore = (prob * (dprob_ref[slot] - delta)).astype(jnp.bfloat16)
        ds_ref[slot * TILE : (slot + 1) * TILE, :] = dscore
        kt_picked[:, slot * TILE : (slot + 1) * TILE] = kt_ref[:, place]
        dk_ref[place, :] += jnp.dot(dscore, q_ref[mask], preferred_element_type=jnp.float32)
        dv_ref[place, :] += jnp.dot(
            prob.astype(jnp.bfloat16), g_ref[mask], preferred_element_type=jnp.float32
        )

    def query_gradient(mask):
        dq_t = jnp.dot(kt_picked[...], ds_ref[...], preferred_element_type=jnp.float32)
        dq_ref[mask] = (dq_t * factor).T.astype(jnp.bfloat16)

    def step(mask, buffer, later, later_buffer):
        places = places_of(own_block ^ mask)
        shares, delta = settle(buffer)
        later_places = None if later is None else places_of(own_block ^ later)
        for slot in range(n_keys):
            gradients(mask, slot, places[slot], buffer, shares, delta)
            if later is not None:
                scores(later, slot, later_places[slot], later_buffer)
        query_gradient(mask)

    @pl.when(own_head >= 0)
    def _():
        for mask in range(n_ctx):
            prepare(mask)
        dk_ref[...] = jnp.zeros_like(dk_ref)
        dv_ref[...] = jnp.zeros_like(dv_ref)
        for slot, place in enumerate(places_of(own_block)):
            scores(0, slot, place, buffers[0])

        def two(pair, carry):
            step(2 * pair, buffers[0], 2 * pair + 1, buffers[1])
            step(2 * pair + 1, buffers[1], 2 * pair + 2, buffers[0])
            return carry

        lax.fori_loop(0, n_ctx // 2 - 1, two, 0)
        step(n_ctx - 2, buffers[0], n_ctx - 1, buffers[1])
        step(n_ctx - 1, buffers[1], None, None)
        for mask in range(n_ctx):
            place = rows_of(own_block ^ mask)
            outs[mask][0] = dq_ref[mask]
            outs[mask][1] = (dk_ref[place, :] * factor).astype(jnp.bfloat16)
            outs[mask][2] = dv_ref[place, :].astype(jnp.bfloat16)


def attend(picks, scales, q_gain, k_gain, messages, n_ctx):
    rows = messages[0].shape[1]
    tokens = n_ctx * rows
    n_keys = rows // TILE + picks.shape[1]
    by_block = pltpu.VMEM((n_ctx, rows, HD), jnp.bfloat16)
    buffer = [
        pltpu.VMEM((n_keys, TILE, rows), jnp.float32),
        pltpu.VMEM((n_keys, TILE, rows), jnp.float32),
        pltpu.VMEM((3, -(-n_keys // 8) * 8, rows), jnp.float32),
    ]
    return pl.pallas_call(
        functools.partial(attend_kernel, n_ctx, q_gain.shape[0]),
        out_shape=[jax.ShapeDtypeStruct((3, rows, HD), jnp.bfloat16)] * n_ctx,
        in_specs=[IN_SMEM] + [IN_VMEM] * (3 + n_ctx),
        out_specs=[IN_VMEM] * n_ctx,
        scratch_shapes=[
            by_block,
            by_block,
            pltpu.VMEM((tokens, HD), jnp.bfloat16),
            pltpu.VMEM((HD, tokens), jnp.bfloat16),
            pltpu.VMEM((tokens, HD), jnp.bfloat16),
            by_block,
            pltpu.VMEM((tokens, HD), jnp.float32),
            pltpu.VMEM((tokens, HD), jnp.float32),
            pltpu.VMEM((n_keys * TILE, rows), jnp.bfloat16),
            pltpu.VMEM((HD, n_keys * TILE), jnp.bfloat16),
        ]
        + buffer
        + buffer,
        compiler_params=pltpu.CompilerParams(vmem_limit_bytes=VMEM_BYTES),
    )(picks, scales, q_gain, k_gain, *messages)


def gather_kernel(n_ctx, heads_dev, q_ref, k_ref, q_gain, k_gain, *refs):
    slots = refs[:n_ctx]
    dot_ref, dq_ref, dk_ref, dv_ref = refs[n_ctx:]
    block, group = lax.axis_index("ctx"), lax.axis_index("head")
    for mask, slot in zip(back_masks(n_ctx), slots):
        head = head_at(block ^ mask, group, n_ctx, heads_dev)

        @pl.when(head >= 0)
        def _(head=head, slot=slot):
            place = pl.ds(pl.multiple_of(head * HD, HD), HD)
            for at, out in enumerate((dq_ref, dk_ref, dv_ref)):
                out[:, place] = slot[at]

    for at, (wide_ref, pre_ref, gain) in enumerate(
        ((dq_ref, q_ref, q_gain), (dk_ref, k_ref, k_gain))
    ):
        terms = gain[...] * wide_ref[...].astype(jnp.float32) * pre_ref[...].astype(jnp.float32)
        dot = row_sums(terms)
        for target in range(dot_ref.shape[0]):
            dot_ref[target, at : at + 1, :] = dot


def finish_kernel(width_all, q_ref, k_ref, q_gain, k_gain, scale_ref, dot_ref, *refs):
    dq_ref, dk_ref, dq_out, dk_out = refs
    scales = scale_ref[lax.axis_index("ctx")]
    backs = scales**3 * (jnp.sum(dot_ref[...], axis=0) / width_all)
    for at, (pre_ref, gain, grad_ref, out) in enumerate(
        ((q_ref, q_gain, dq_ref, dq_out), (k_ref, k_gain, dk_ref, dk_out))
    ):
        scale = column(scales[at : at + 1, :], HD)
        back = column(backs[at : at + 1, :], HD)
        for first in range(0, pre_ref.shape[1], HD):
            place = slice(first, first + HD)
            wide = pre_ref[:, place].astype(jnp.float32)
            grad = grad_ref[:, place].astype(jnp.float32)
            out[:, place] = (scale * gain[:, place] * grad - wide * back).astype(jnp.bfloat16)


def heads_to_owners(q_pre, k_pre, values, out_grad, q_gain, k_gain, selected):
    n_ctx = lax.axis_size("ctx")
    n_head = lax.axis_size("head")
    rows, width_dev = q_pre.shape
    width_all = width_dev * n_head
    heads_dev = width_dev // HD
    remote_count = selected.shape[2]
    sizes = (n_ctx, n_head, heads_dev)
    params = pltpu.CompilerParams(vmem_limit_bytes=VMEM_BYTES)

    wide = jax.ShapeDtypeStruct((rows, width_dev), jnp.bfloat16)

    squares, sent = pack((q_pre, k_pre, values, out_grad), n_ctx)
    messages = move(there_masks(n_ctx), sent, False, *sizes)

    wishes = selected[0].reshape(1, -1).astype(jnp.float32)
    wishes = jnp.pad(wishes, ((0, 0), (0, rows - wishes.shape[1])))
    small = jnp.concatenate((squares, wishes), axis=0)
    small = jnp.broadcast_to(small[None], (n_ctx * n_head,) + small.shape)
    small = lax.all_to_all(small, ("ctx", "head"), split_axis=0, concat_axis=0, tiled=True)
    small = small.reshape((n_ctx, n_head) + small.shape[1:])
    squares = jnp.sum(small[:, :, :2], axis=1)
    scales = lax.rsqrt(squares / width_all + epsilon)
    group = lax.axis_index("head")
    own_head = head_at(lax.axis_index("ctx"), group, n_ctx, heads_dev)
    first = jnp.maximum(own_head, 0) * remote_count
    picks = lax.dynamic_slice(small, (0, group, 2, first), (n_ctx, 1, 1, remote_count))
    picks = picks.reshape(n_ctx, remote_count).astype(jnp.int32)

    q_gains = q_gain.reshape(heads_dev, HD)
    k_gains = k_gain.reshape(heads_dev, HD)
    results = attend(picks, scales, q_gains, k_gains, messages, n_ctx)
    slots = move(back_masks(n_ctx), results, True, *sizes)

    pres = (q_pre, k_pre, q_gain[None], k_gain[None])
    dots, dq_wide, dk_wide, dv = pl.pallas_call(
        functools.partial(gather_kernel, n_ctx, heads_dev),
        out_shape=[jax.ShapeDtypeStruct((n_head, 2, rows), jnp.float32), wide, wide, wide],
        in_specs=[IN_VMEM] * (4 + n_ctx),
        out_specs=[IN_VMEM] * 4,
        compiler_params=params,
    )(*pres, *slots)
    dots = lax.all_to_all(dots, "head", split_axis=0, concat_axis=0, tiled=True)
    dq, dk = pl.pallas_call(
        functools.partial(finish_kernel, width_all),
        out_shape=[wide, wide],
        in_specs=[IN_VMEM] * 8,
        out_specs=[IN_VMEM] * 2,
        compiler_params=params,
    )(*pres, scales, dots, dq_wide, dk_wide)
    return dq, dk, dv


def on_device(q_pre, k_pre, values, out_grad, q_gain, k_gain, selected):
    n_ctx = lax.axis_size("ctx")
    tiles_dev, heads_dev, remote_count = selected.shape
    capacity = -(-heads_dev * remote_count // (n_ctx - 1))
    by_head = (n_ctx - 1) * tiles_dev * 7
    by_tile = (n_ctx - 1) * capacity * 6
    paired = n_ctx & (n_ctx - 1) == 0 and n_ctx >= max(heads_dev, 4)
    plan = heads_to_owners if paired and by_head <= by_tile else tiles_to_queries
    return plan(q_pre, k_pre, values, out_grad, q_gain, k_gain, selected)


def solution(mesh):
    placed = (
        P("ctx", "head"),
        P("ctx", "head"),
        P("ctx", "head"),
        P("ctx", "head"),
        P("head"),
        P("head"),
        P("ctx", "head", None),
    )
    return jax.shard_map(
        on_device,
        mesh=mesh,
        in_specs=placed,
        out_specs=(P("ctx", "head"), P("ctx", "head"), P("ctx", "head")),
        check_vma=False,
    )
```

```python
import functools
import math

import jax
import jax.numpy as jnp
from jax import lax
from jax.experimental import pallas as pl
from jax.experimental.pallas import tpu as pltpu
from jax.sharding import PartitionSpec as P

HD = 128
TILE = 128


epsilon = 1e-06


def split_heads(array, heads_dev):
    return array.reshape(array.shape[0], heads_dev, HD).transpose(1, 0, 2)


def merge_heads(array):
    heads_dev, tok_dev, depth = array.shape
    return array.transpose(1, 0, 2).reshape(tok_dev, heads_dev * depth)


def per_tile(array, qt_dev):
    heads_dev, tok_dev, depth = array.shape
    return array.reshape(heads_dev, qt_dev, TILE, depth).transpose(1, 0, 2, 3)


def from_tiles(array):
    qt_dev, heads_dev, rows_tile, depth = array.shape
    return array.transpose(1, 0, 2, 3).reshape(heads_dev, qt_dev * rows_tile, depth)


def table_sum(taken, pieces, heads_dev, qt_dev):
    flat_pieces = pieces.reshape(pieces.shape[0], -1)
    summed = jnp.dot(
        taken, flat_pieces, precision=lax.Precision.HIGHEST, preferred_element_type=jnp.float32
    )
    summed = summed.reshape(heads_dev, qt_dev, 2, TILE, HD).transpose(2, 0, 1, 3, 4)
    return summed.reshape(2, heads_dev, qt_dev * TILE, HD)


def rounded(array):
    return array.astype(jnp.bfloat16)


def finish_norm(wide, scale, gain, grad, dot_sum, width_all):
    return (scale * gain * grad - wide * scale**3 * (dot_sum / width_all)[:, None]).astype(
        jnp.bfloat16
    )


def tiles_to_queries(q_pre, k_pre, values, out_grad, q_gain, k_gain, selected):
    n_ctx = lax.axis_size("ctx")
    tok_dev, width_dev = q_pre.shape
    width_all = width_dev * lax.axis_size("head")
    heads_dev = width_dev // HD
    qt_dev = tok_dev // TILE
    remote_count = selected.shape[2]
    factor = 1.0 / math.sqrt(HD)
    q_wide = q_pre.astype(jnp.float32)
    k_wide = k_pre.astype(jnp.float32)
    q_square, k_square = lax.psum(
        (jnp.sum(q_wide * q_wide, axis=1), jnp.sum(k_wide * k_wide, axis=1)), "head"
    )
    q_scale = lax.rsqrt(q_square / width_all + epsilon)[:, None]
    k_scale = lax.rsqrt(k_square / width_all + epsilon)[:, None]
    q_heads = split_heads(rounded(q_wide * q_scale * q_gain), heads_dev)
    k_heads = split_heads(rounded(k_wide * k_scale * k_gain), heads_dev)
    v_heads = split_heads(values, heads_dev)
    g_heads = split_heads(out_grad, heads_dev)
    q_tiles = per_tile(q_heads, qt_dev)
    g_tiles = per_tile(g_heads, qt_dev)
    k_table = k_heads.reshape(heads_dev * qt_dev, TILE, HD)
    v_table = v_heads.reshape(heads_dev * qt_dev, TILE, HD)
    flat_sel = selected[0].reshape(-1)
    n_slot = flat_sel.shape[0]
    capacity = -(-n_slot // (n_ctx - 1))
    n_buffer = n_ctx * capacity
    owners = flat_sel // qt_dev
    head_of = jnp.arange(n_slot, dtype=jnp.int32) // remote_count
    codes = head_of * qt_dev + flat_sel % qt_dev
    matches = (owners[:, None] == jnp.arange(n_ctx, dtype=jnp.int32)[None, :]).astype(jnp.int32)
    ranks = jnp.sum((jnp.cumsum(matches, axis=0) - matches) * matches, axis=1)
    position = owners * capacity + ranks
    placed = position[None, :] == jnp.arange(n_buffer, dtype=jnp.int32)[:, None]
    request = jnp.sum(jnp.where(placed, codes[None, :] + 1, 0), axis=1) - 1
    asked = lax.all_to_all(
        request.reshape(n_ctx, capacity), "ctx", split_axis=0, concat_axis=0, tiled=True
    ).reshape(n_buffer)
    clipped = jnp.maximum(asked, 0)
    taken = (asked[None, :] == jnp.arange(heads_dev * qt_dev, dtype=jnp.int32)[:, None]).astype(
        jnp.float32
    )
    s_near = (
        jnp.einsum("rhqd,hkd->rhqk", q_tiles, k_heads, preferred_element_type=jnp.float32) * factor
    )
    dp_near = jnp.einsum("rhqd,hkd->rhqk", g_tiles, v_heads, preferred_element_type=jnp.float32)
    near_top = jnp.max(s_near, axis=-1)
    outgoing = jnp.stack((k_table[clipped], v_table[clipped]), axis=1).reshape(
        n_ctx, capacity, 2, TILE, HD
    )
    incoming = lax.all_to_all(outgoing, "ctx", split_axis=0, concat_axis=0, tiled=True).reshape(
        n_buffer, 2, TILE, HD
    )
    slot_kv = incoming[position].reshape(heads_dev, remote_count, 2, TILE, HD)
    far_k = slot_kv[:, :, 0]
    far_v = slot_kv[:, :, 1]
    s_far = (
        jnp.einsum("rhqd,hckd->rhqck", q_tiles, far_k, preferred_element_type=jnp.float32) * factor
    )
    dp_far = jnp.einsum("rhqd,hckd->rhqck", g_tiles, far_v, preferred_element_type=jnp.float32)
    row_top = jnp.maximum(near_top, jnp.max(s_far, axis=(-2, -1)))
    totals = jnp.sum(jnp.exp(s_near - row_top[..., None]), axis=-1) + jnp.sum(
        jnp.exp(s_far - row_top[..., None, None]), axis=(-2, -1)
    )
    lse = row_top + jnp.log(totals)
    p_near = jnp.exp(s_near - lse[..., None])
    p_far = jnp.exp(s_far - lse[..., None, None])
    delta = jnp.sum(p_near * dp_near, axis=-1) + jnp.sum(p_far * dp_far, axis=(-2, -1))
    ds_near = rounded(p_near * (dp_near - delta[..., None]) * factor)
    pb_near = rounded(p_near)
    dq_near = jnp.einsum("rhqk,hkd->rhqd", ds_near, k_heads, preferred_element_type=jnp.float32)
    dk_near = jnp.einsum("rhqk,rhqd->hkd", ds_near, q_tiles, preferred_element_type=jnp.float32)
    dv_near = jnp.einsum("rhqk,rhqd->hkd", pb_near, g_tiles, preferred_element_type=jnp.float32)
    dq_near, dk_near, dv_near = (dq_near, dk_near, dv_near)
    ds_far = rounded(p_far * (dp_far - delta[..., None, None]) * factor)
    pb_far = rounded(p_far)
    dq_far = jnp.einsum("rhqck,hckd->rhqd", ds_far, far_k, preferred_element_type=jnp.float32)
    dq_wide = merge_heads(from_tiles(dq_near + dq_far))
    q_dot = jnp.sum(q_gain * dq_wide * q_wide, axis=1)
    dq_wide, q_dot = (dq_wide, q_dot)
    dk_far = jnp.einsum("rhqck,rhqd->hckd", ds_far, q_tiles, preferred_element_type=jnp.float32)
    dv_far = jnp.einsum("rhqck,rhqd->hckd", pb_far, g_tiles, preferred_element_type=jnp.float32)
    grads = jnp.stack((dk_far, dv_far), axis=2).reshape(n_slot, 2, TILE, HD)
    sending = jnp.zeros((n_buffer, 2, TILE, HD), jnp.float32).at[position].set(grads)
    returned = lax.all_to_all(
        sending.reshape(n_ctx, capacity, 2, TILE, HD),
        "ctx",
        split_axis=0,
        concat_axis=0,
        tiled=True,
    ).reshape(n_buffer, 2, TILE, HD)
    far_sums = table_sum(taken, returned, heads_dev, qt_dev)
    dk_wide = merge_heads(dk_near + far_sums[0])
    dv_heads = dv_near + far_sums[1]
    k_dot = jnp.sum(k_gain * dk_wide * k_wide, axis=1)
    q_dot, k_dot = lax.psum((q_dot, k_dot), "head")
    dq_result = finish_norm(q_wide, q_scale, q_gain, dq_wide, q_dot, width_all)
    dk_result = finish_norm(k_wide, k_scale, k_gain, dk_wide, k_dot, width_all)
    return (dq_result, dk_result, merge_heads(dv_heads).astype(jnp.bfloat16))


VMEM_BYTES = 48 * 2**20
PIECES = 4
IN_VMEM = pl.BlockSpec(memory_space=pltpu.VMEM)
IN_SMEM = pl.BlockSpec(memory_space=pltpu.SMEM)


def owners_of(group, n_ctx, heads_dev):
    places = [(4 * head + 1) * n_ctx // (4 * heads_dev) for head in range(heads_dev)]
    return [n_ctx - 1 - place if group % 2 else place for place in places]


def head_at(place, group, n_ctx, heads_dev):
    even = jnp.where(group % 2 == 1, n_ctx - 1 - place, place)
    head = -1
    for index, owner in enumerate(owners_of(0, n_ctx, heads_dev)):
        head = jnp.where(even == owner, index, head)
    return head


def pairs_to_owner(mask, n_ctx, n_head, heads_dev):
    pairs = []
    for group in range(n_head):
        owners = owners_of(group, n_ctx, heads_dev)
        for block in range(n_ctx):
            if block ^ mask in owners:
                pairs.append((block * n_head + group, (block ^ mask) * n_head + group))
    return pairs


def there_masks(n_ctx):
    return list(range(n_ctx - 1, -1, -1))


def back_masks(n_ctx):
    return list(range(n_ctx // 2 - 1, 0, -1)) + list(range(n_ctx - 1, n_ctx // 2 - 1, -1)) + [0]


def move(masks, arrays, back, n_ctx, n_head, heads_dev):
    moved = []
    for mask, array in zip(masks, arrays):
        pairs = pairs_to_owner(mask, n_ctx, n_head, heads_dev)
        if back:
            pairs = [(b, a) for a, b in pairs]
        moved.append(lax.ppermute(array, ("ctx", "head"), pairs) if mask else array)
    return moved


def column(row, width):
    return jnp.broadcast_to(row, (width, row.shape[1])).T


def row_sums(wide):
    total = wide[:, :HD]
    for at in range(HD, wide.shape[1], HD):
        total = total + wide[:, at : at + HD]
    return jnp.sum(total.T, axis=0, keepdims=True)


def pack_kernel(n_ctx, heads_dev, *refs):
    inputs, square_ref, outs = refs[:4], refs[4], refs[5 : 5 + n_ctx]
    held, sems = refs[5 + n_ctx :]
    rows = held.shape[1]
    piece = rows // PIECES
    block, group = lax.axis_index("ctx"), lax.axis_index("head")

    def copy(at, part):
        place = pl.ds(part * piece, piece)
        return pltpu.make_async_copy(
            inputs[at].at[place, :], held.at[at, place, :], sems.at[at, part]
        )

    for at in range(4):
        for part in range(PIECES):
            copy(at, part).start()
    for at in range(4):
        for part in range(PIECES):
            copy(at, part).wait()
    for mask, out in zip(there_masks(n_ctx), outs):
        head = head_at(block ^ mask, group, n_ctx, heads_dev)

        @pl.when(head >= 0)
        def _(head=head, out=out):
            place = pl.ds(pl.multiple_of(head * HD, HD), HD)
            for at in range(4):
                out[at] = held[at, :, place]

    for at in range(2):
        wide = held[at].astype(jnp.float32)
        square_ref[at : at + 1, :] = row_sums(wide * wide)


def pack(arrays, n_ctx):
    rows, width_dev = arrays[0].shape
    result = pl.pallas_call(
        functools.partial(pack_kernel, n_ctx, width_dev // HD),
        out_shape=[jax.ShapeDtypeStruct((2, rows), jnp.float32)]
        + [jax.ShapeDtypeStruct((4, rows, HD), jnp.bfloat16)] * n_ctx,
        in_specs=[pl.BlockSpec(memory_space=pltpu.HBM)] * 4,
        out_specs=[IN_VMEM] * (n_ctx + 1),
        scratch_shapes=[
            pltpu.VMEM((4, rows, width_dev), jnp.bfloat16),
            pltpu.SemaphoreType.DMA((4, PIECES)),
        ],
        compiler_params=pltpu.CompilerParams(vmem_limit_bytes=VMEM_BYTES),
    )(*[pltpu.with_memory_space_constraint(array, pltpu.HBM) for array in arrays])
    return result[0], result[1:]


def attend_kernel(n_ctx, heads_dev, picks, scale_ref, q_gain, k_gain, *refs):
    messages = dict(zip(there_masks(n_ctx), refs[:n_ctx]))
    outs = dict(zip(back_masks(n_ctx), refs[n_ctx : 2 * n_ctx]))
    scratch = refs[2 * n_ctx :]
    q_ref, qt_ref, g_ref, gt_ref, k_ref, kt_ref, v_ref = scratch[:7]
    dq_ref, dk_ref, dv_ref, ds_ref, kt_picked = scratch[7:12]
    buffers = (scratch[12:15], scratch[15:18])
    rows = messages[0].shape[1]
    remote_count = picks.shape[1]
    near = rows // TILE
    n_keys = near + remote_count
    factor = 1.0 / math.sqrt(HD)
    to_base2 = factor * math.log2(math.e)
    own_block = lax.axis_index("ctx")
    own_head = head_at(own_block, lax.axis_index("head"), n_ctx, heads_dev)

    def rows_of(block):
        return pl.ds(pl.multiple_of(block * rows, rows), rows)

    def places_of(block):
        return [
            pl.ds(pl.multiple_of(block * rows + tile * TILE, TILE), TILE) for tile in range(near)
        ] + [
            pl.ds(pl.multiple_of(picks[block, slot] * TILE, TILE), TILE)
            for slot in range(remote_count)
        ]

    def prepare(mask, q_factor, k_factor):
        message = messages[mask]
        block = own_block ^ mask
        place = rows_of(block)
        q_t = message[0].T.astype(jnp.float32) * scale_ref[block, 0:1, :] * q_factor
        k_t = message[1].T.astype(jnp.float32) * scale_ref[block, 1:2, :] * k_factor
        qt_ref[mask] = q_t.astype(jnp.bfloat16)
        kt_ref[:, place] = k_t.astype(jnp.bfloat16)
        q_ref[mask] = q_t.astype(jnp.bfloat16).T
        k_ref[place, :] = k_t.astype(jnp.bfloat16).T
        v_ref[place, :] = message[2]
        g_ref[mask] = message[3]
        gt_ref[mask] = message[3].T

    def scores(mask, slot, place, buffer):
        weight_ref, dprob_ref, stat_ref = buffer
        score = jnp.dot(k_ref[place, :], qt_ref[mask], preferred_element_type=jnp.float32)
        dprob = jnp.dot(v_ref[place, :], gt_ref[mask], preferred_element_type=jnp.float32)
        top = jnp.max(score, axis=0, keepdims=True)
        weight = jnp.exp2((score - top) * to_base2)
        weight_ref[slot] = weight
        dprob_ref[slot] = dprob
        stat_ref[0, slot : slot + 1, :] = top * to_base2
        stat_ref[1, slot : slot + 1, :] = jnp.sum(weight, axis=0, keepdims=True)
        stat_ref[2, slot : slot + 1, :] = jnp.sum(weight * dprob, axis=0, keepdims=True)

    def settle(buffer):
        stat_ref = buffer[2]
        tops = stat_ref[0, :n_keys, :]
        shares = jnp.exp2(tops - jnp.max(tops, axis=0, keepdims=True))
        total = jnp.sum(shares * stat_ref[1, :n_keys, :], axis=0, keepdims=True)
        mixed = jnp.sum(shares * stat_ref[2, :n_keys, :], axis=0, keepdims=True)
        inverse = 1.0 / total
        return shares * inverse, mixed * inverse

    def gradients(mask, slot, place, buffer, shares, delta):
        weight_ref, dprob_ref, _ = buffer
        prob = weight_ref[slot] * shares[slot : slot + 1, :]
        dscore = (prob * (dprob_ref[slot] - delta)).astype(jnp.bfloat16)
        ds_ref[slot * TILE : (slot + 1) * TILE, :] = dscore
        kt_picked[:, slot * TILE : (slot + 1) * TILE] = kt_ref[:, place]
        dk_ref[place, :] += jnp.dot(dscore, q_ref[mask], preferred_element_type=jnp.float32)
        dv_ref[place, :] += jnp.dot(
            prob.astype(jnp.bfloat16), g_ref[mask], preferred_element_type=jnp.float32
        )

    def query_gradient(mask):
        dq_t = jnp.dot(kt_picked[...], ds_ref[...], preferred_element_type=jnp.float32)
        dq_ref[mask] = (dq_t * factor).T.astype(jnp.bfloat16)

    def step(mask, buffer, later, later_buffer):
        places = places_of(own_block ^ mask)
        shares, delta = settle(buffer)
        later_places = None if later is None else places_of(own_block ^ later)
        for slot in range(n_keys):
            gradients(mask, slot, places[slot], buffer, shares, delta)
            if later is not None:
                scores(later, slot, later_places[slot], later_buffer)
        query_gradient(mask)

    @pl.when(own_head >= 0)
    def _():
        q_factor = column(q_gain[pl.ds(own_head, 1), :], rows)
        k_factor = column(k_gain[pl.ds(own_head, 1), :], rows)
        for mask in range(n_ctx):
            prepare(mask, q_factor, k_factor)
        dk_ref[...] = jnp.zeros_like(dk_ref)
        dv_ref[...] = jnp.zeros_like(dv_ref)
        for slot, place in enumerate(places_of(own_block)):
            scores(0, slot, place, buffers[0])

        def two(pair, carry):
            step(2 * pair, buffers[0], 2 * pair + 1, buffers[1])
            step(2 * pair + 1, buffers[1], 2 * pair + 2, buffers[0])
            return carry

        lax.fori_loop(0, n_ctx // 2 - 1, two, 0)
        step(n_ctx - 2, buffers[0], n_ctx - 1, buffers[1])
        step(n_ctx - 1, buffers[1], None, None)
        for mask in range(n_ctx):
            place = rows_of(own_block ^ mask)
            outs[mask][0] = dq_ref[mask]
            outs[mask][1] = (dk_ref[place, :] * factor).astype(jnp.bfloat16)
            outs[mask][2] = dv_ref[place, :].astype(jnp.bfloat16)


def attend(picks, scales, q_gain, k_gain, messages, n_ctx):
    rows = messages[0].shape[1]
    tokens = n_ctx * rows
    n_keys = rows // TILE + picks.shape[1]
    by_block = pltpu.VMEM((n_ctx, rows, HD), jnp.bfloat16)
    by_block_t = pltpu.VMEM((n_ctx, HD, rows), jnp.bfloat16)
    buffer = [
        pltpu.VMEM((n_keys, TILE, rows), jnp.float32),
        pltpu.VMEM((n_keys, TILE, rows), jnp.float32),
        pltpu.VMEM((3, -(-n_keys // 8) * 8, rows), jnp.float32),
    ]
    return pl.pallas_call(
        functools.partial(attend_kernel, n_ctx, q_gain.shape[0]),
        out_shape=[jax.ShapeDtypeStruct((3, rows, HD), jnp.bfloat16)] * n_ctx,
        in_specs=[IN_SMEM] + [IN_VMEM] * (3 + n_ctx),
        out_specs=[IN_VMEM] * n_ctx,
        scratch_shapes=[
            by_block,
            by_block_t,
            by_block,
            by_block_t,
            pltpu.VMEM((tokens, HD), jnp.bfloat16),
            pltpu.VMEM((HD, tokens), jnp.bfloat16),
            pltpu.VMEM((tokens, HD), jnp.bfloat16),
            by_block,
            pltpu.VMEM((tokens, HD), jnp.float32),
            pltpu.VMEM((tokens, HD), jnp.float32),
            pltpu.VMEM((n_keys * TILE, rows), jnp.bfloat16),
            pltpu.VMEM((HD, n_keys * TILE), jnp.bfloat16),
        ]
        + buffer
        + buffer,
        compiler_params=pltpu.CompilerParams(vmem_limit_bytes=VMEM_BYTES),
    )(picks, scales, q_gain, k_gain, *messages)


def gather_kernel(n_ctx, heads_dev, q_ref, k_ref, q_gain, k_gain, *refs):
    slots = refs[:n_ctx]
    dot_ref, dq_ref, dk_ref, dv_ref = refs[n_ctx:]
    block, group = lax.axis_index("ctx"), lax.axis_index("head")
    for mask, slot in zip(back_masks(n_ctx), slots):
        head = head_at(block ^ mask, group, n_ctx, heads_dev)

        @pl.when(head >= 0)
        def _(head=head, slot=slot):
            place = pl.ds(pl.multiple_of(head * HD, HD), HD)
            for at, out in enumerate((dq_ref, dk_ref, dv_ref)):
                out[:, place] = slot[at]

    for at, (wide_ref, pre_ref, gain) in enumerate(
        ((dq_ref, q_ref, q_gain), (dk_ref, k_ref, k_gain))
    ):
        terms = gain[...] * wide_ref[...].astype(jnp.float32) * pre_ref[...].astype(jnp.float32)
        dot_ref[at : at + 1, :] = row_sums(terms)


def finish_kernel(width_all, q_ref, k_ref, q_gain, k_gain, scale_ref, dot_ref, *refs):
    dq_ref, dk_ref, dq_out, dk_out = refs
    scales = scale_ref[lax.axis_index("ctx")]
    backs = scales**3 * (dot_ref[...] / width_all)
    for at, (pre_ref, gain, grad_ref, out) in enumerate(
        ((q_ref, q_gain, dq_ref, dq_out), (k_ref, k_gain, dk_ref, dk_out))
    ):
        scale = column(scales[at : at + 1, :], HD)
        back = column(backs[at : at + 1, :], HD)
        for first in range(0, pre_ref.shape[1], HD):
            place = slice(first, first + HD)
            wide = pre_ref[:, place].astype(jnp.float32)
            grad = grad_ref[:, place].astype(jnp.float32)
            out[:, place] = (scale * gain[:, place] * grad - wide * back).astype(jnp.bfloat16)


def heads_to_owners(q_pre, k_pre, values, out_grad, q_gain, k_gain, selected):
    n_ctx = lax.axis_size("ctx")
    n_head = lax.axis_size("head")
    rows, width_dev = q_pre.shape
    width_all = width_dev * n_head
    heads_dev = width_dev // HD
    remote_count = selected.shape[2]
    sizes = (n_ctx, n_head, heads_dev)
    params = pltpu.CompilerParams(vmem_limit_bytes=VMEM_BYTES)

    by_row = jax.ShapeDtypeStruct((2, rows), jnp.float32)
    wide = jax.ShapeDtypeStruct((rows, width_dev), jnp.bfloat16)

    squares, sent = pack((q_pre, k_pre, values, out_grad), n_ctx)
    messages = move(there_masks(n_ctx), sent, False, *sizes)

    wishes = selected[0].reshape(1, -1).astype(jnp.float32)
    wishes = jnp.pad(wishes, ((0, 0), (0, rows - wishes.shape[1])))
    small = jnp.concatenate((lax.psum(squares, "head"), wishes), axis=0)
    small = jnp.broadcast_to(small[None], (n_ctx,) + small.shape)
    small = lax.all_to_all(small, "ctx", split_axis=0, concat_axis=0, tiled=True)
    scales = lax.rsqrt(small[:, :2] / width_all + epsilon)
    own_head = head_at(lax.axis_index("ctx"), lax.axis_index("head"), n_ctx, heads_dev)
    first = jnp.maximum(own_head, 0) * remote_count
    picks = lax.dynamic_slice_in_dim(small[:, 2], first, remote_count, 1).astype(jnp.int32)

    q_gains = q_gain.reshape(heads_dev, HD)
    k_gains = k_gain.reshape(heads_dev, HD)
    results = attend(picks, scales, q_gains, k_gains, messages, n_ctx)
    slots = move(back_masks(n_ctx), results, True, *sizes)

    pres = (q_pre, k_pre, q_gain[None], k_gain[None])
    dots, dq_wide, dk_wide, dv = pl.pallas_call(
        functools.partial(gather_kernel, n_ctx, heads_dev),
        out_shape=[by_row, wide, wide, wide],
        in_specs=[IN_VMEM] * (4 + n_ctx),
        out_specs=[IN_VMEM] * 4,
        compiler_params=params,
    )(*pres, *slots)
    dots = lax.psum(dots, "head")
    dq, dk = pl.pallas_call(
        functools.partial(finish_kernel, width_all),
        out_shape=[wide, wide],
        in_specs=[IN_VMEM] * 8,
        out_specs=[IN_VMEM] * 2,
        compiler_params=params,
    )(*pres, scales, dots, dq_wide, dk_wide)
    return dq, dk, dv


def on_device(q_pre, k_pre, values, out_grad, q_gain, k_gain, selected):
    n_ctx = lax.axis_size("ctx")
    tiles_dev, heads_dev, remote_count = selected.shape
    capacity = -(-heads_dev * remote_count // (n_ctx - 1))
    by_head = (n_ctx - 1) * tiles_dev * 7
    by_tile = (n_ctx - 1) * capacity * 6
    paired = n_ctx & (n_ctx - 1) == 0 and n_ctx >= max(heads_dev, 4)
    plan = heads_to_owners if paired and by_head <= by_tile else tiles_to_queries
    return plan(q_pre, k_pre, values, out_grad, q_gain, k_gain, selected)


def solution(mesh):
    placed = (
        P("ctx", "head"),
        P("ctx", "head"),
        P("ctx", "head"),
        P("ctx", "head"),
        P("head"),
        P("head"),
        P("ctx", "head", None),
    )
    return jax.shard_map(
        on_device,
        mesh=mesh,
        in_specs=placed,
        out_specs=(P("ctx", "head"), P("ctx", "head"), P("ctx", "head")),
        check_vma=False,
    )
```

```python
import functools
import math

import jax
import jax.numpy as jnp
from jax import lax
from jax.experimental import pallas as pl
from jax.experimental.pallas import tpu as pltpu
from jax.sharding import PartitionSpec as P

HD = 128
TILE = 128


epsilon = 1e-06


def split_heads(array, heads_dev):
    return array.reshape(array.shape[0], heads_dev, HD).transpose(1, 0, 2)


def merge_heads(array):
    heads_dev, tok_dev, depth = array.shape
    return array.transpose(1, 0, 2).reshape(tok_dev, heads_dev * depth)


def per_tile(array, qt_dev):
    heads_dev, tok_dev, depth = array.shape
    return array.reshape(heads_dev, qt_dev, TILE, depth).transpose(1, 0, 2, 3)


def from_tiles(array):
    qt_dev, heads_dev, rows_tile, depth = array.shape
    return array.transpose(1, 0, 2, 3).reshape(heads_dev, qt_dev * rows_tile, depth)


def table_sum(taken, pieces, heads_dev, qt_dev):
    flat_pieces = pieces.reshape(pieces.shape[0], -1)
    summed = jnp.dot(
        taken, flat_pieces, precision=lax.Precision.HIGHEST, preferred_element_type=jnp.float32
    )
    summed = summed.reshape(heads_dev, qt_dev, 2, TILE, HD).transpose(2, 0, 1, 3, 4)
    return summed.reshape(2, heads_dev, qt_dev * TILE, HD)


def rounded(array):
    return array.astype(jnp.bfloat16)


def finish_norm(wide, scale, gain, grad, dot_sum, width_all):
    return (scale * gain * grad - wide * scale**3 * (dot_sum / width_all)[:, None]).astype(
        jnp.bfloat16
    )


def tiles_to_queries(q_pre, k_pre, values, out_grad, q_gain, k_gain, selected):
    n_ctx = lax.axis_size("ctx")
    tok_dev, width_dev = q_pre.shape
    width_all = width_dev * lax.axis_size("head")
    heads_dev = width_dev // HD
    qt_dev = tok_dev // TILE
    remote_count = selected.shape[2]
    factor = 1.0 / math.sqrt(HD)
    q_wide = q_pre.astype(jnp.float32)
    k_wide = k_pre.astype(jnp.float32)
    q_square, k_square = lax.psum(
        (jnp.sum(q_wide * q_wide, axis=1), jnp.sum(k_wide * k_wide, axis=1)), "head"
    )
    q_scale = lax.rsqrt(q_square / width_all + epsilon)[:, None]
    k_scale = lax.rsqrt(k_square / width_all + epsilon)[:, None]
    q_heads = split_heads(rounded(q_wide * q_scale * q_gain), heads_dev)
    k_heads = split_heads(rounded(k_wide * k_scale * k_gain), heads_dev)
    v_heads = split_heads(values, heads_dev)
    g_heads = split_heads(out_grad, heads_dev)
    q_tiles = per_tile(q_heads, qt_dev)
    g_tiles = per_tile(g_heads, qt_dev)
    k_table = k_heads.reshape(heads_dev * qt_dev, TILE, HD)
    v_table = v_heads.reshape(heads_dev * qt_dev, TILE, HD)
    flat_sel = selected[0].reshape(-1)
    n_slot = flat_sel.shape[0]
    capacity = -(-n_slot // (n_ctx - 1))
    n_buffer = n_ctx * capacity
    owners = flat_sel // qt_dev
    head_of = jnp.arange(n_slot, dtype=jnp.int32) // remote_count
    codes = head_of * qt_dev + flat_sel % qt_dev
    matches = (owners[:, None] == jnp.arange(n_ctx, dtype=jnp.int32)[None, :]).astype(jnp.int32)
    ranks = jnp.sum((jnp.cumsum(matches, axis=0) - matches) * matches, axis=1)
    position = owners * capacity + ranks
    placed = position[None, :] == jnp.arange(n_buffer, dtype=jnp.int32)[:, None]
    request = jnp.sum(jnp.where(placed, codes[None, :] + 1, 0), axis=1) - 1
    asked = lax.all_to_all(
        request.reshape(n_ctx, capacity), "ctx", split_axis=0, concat_axis=0, tiled=True
    ).reshape(n_buffer)
    clipped = jnp.maximum(asked, 0)
    taken = (asked[None, :] == jnp.arange(heads_dev * qt_dev, dtype=jnp.int32)[:, None]).astype(
        jnp.float32
    )
    s_near = (
        jnp.einsum("rhqd,hkd->rhqk", q_tiles, k_heads, preferred_element_type=jnp.float32) * factor
    )
    dp_near = jnp.einsum("rhqd,hkd->rhqk", g_tiles, v_heads, preferred_element_type=jnp.float32)
    near_top = jnp.max(s_near, axis=-1)
    outgoing = jnp.stack((k_table[clipped], v_table[clipped]), axis=1).reshape(
        n_ctx, capacity, 2, TILE, HD
    )
    incoming = lax.all_to_all(outgoing, "ctx", split_axis=0, concat_axis=0, tiled=True).reshape(
        n_buffer, 2, TILE, HD
    )
    slot_kv = incoming[position].reshape(heads_dev, remote_count, 2, TILE, HD)
    far_k = slot_kv[:, :, 0]
    far_v = slot_kv[:, :, 1]
    s_far = (
        jnp.einsum("rhqd,hckd->rhqck", q_tiles, far_k, preferred_element_type=jnp.float32) * factor
    )
    dp_far = jnp.einsum("rhqd,hckd->rhqck", g_tiles, far_v, preferred_element_type=jnp.float32)
    row_top = jnp.maximum(near_top, jnp.max(s_far, axis=(-2, -1)))
    totals = jnp.sum(jnp.exp(s_near - row_top[..., None]), axis=-1) + jnp.sum(
        jnp.exp(s_far - row_top[..., None, None]), axis=(-2, -1)
    )
    lse = row_top + jnp.log(totals)
    p_near = jnp.exp(s_near - lse[..., None])
    p_far = jnp.exp(s_far - lse[..., None, None])
    delta = jnp.sum(p_near * dp_near, axis=-1) + jnp.sum(p_far * dp_far, axis=(-2, -1))
    ds_near = rounded(p_near * (dp_near - delta[..., None]) * factor)
    pb_near = rounded(p_near)
    dq_near = jnp.einsum("rhqk,hkd->rhqd", ds_near, k_heads, preferred_element_type=jnp.float32)
    dk_near = jnp.einsum("rhqk,rhqd->hkd", ds_near, q_tiles, preferred_element_type=jnp.float32)
    dv_near = jnp.einsum("rhqk,rhqd->hkd", pb_near, g_tiles, preferred_element_type=jnp.float32)
    dq_near, dk_near, dv_near = (dq_near, dk_near, dv_near)
    ds_far = rounded(p_far * (dp_far - delta[..., None, None]) * factor)
    pb_far = rounded(p_far)
    dq_far = jnp.einsum("rhqck,hckd->rhqd", ds_far, far_k, preferred_element_type=jnp.float32)
    dq_wide = merge_heads(from_tiles(dq_near + dq_far))
    q_dot = jnp.sum(q_gain * dq_wide * q_wide, axis=1)
    dq_wide, q_dot = (dq_wide, q_dot)
    dk_far = jnp.einsum("rhqck,rhqd->hckd", ds_far, q_tiles, preferred_element_type=jnp.float32)
    dv_far = jnp.einsum("rhqck,rhqd->hckd", pb_far, g_tiles, preferred_element_type=jnp.float32)
    grads = jnp.stack((dk_far, dv_far), axis=2).reshape(n_slot, 2, TILE, HD)
    sending = jnp.zeros((n_buffer, 2, TILE, HD), jnp.float32).at[position].set(grads)
    returned = lax.all_to_all(
        sending.reshape(n_ctx, capacity, 2, TILE, HD),
        "ctx",
        split_axis=0,
        concat_axis=0,
        tiled=True,
    ).reshape(n_buffer, 2, TILE, HD)
    far_sums = table_sum(taken, returned, heads_dev, qt_dev)
    dk_wide = merge_heads(dk_near + far_sums[0])
    dv_heads = dv_near + far_sums[1]
    k_dot = jnp.sum(k_gain * dk_wide * k_wide, axis=1)
    q_dot, k_dot = lax.psum((q_dot, k_dot), "head")
    dq_result = finish_norm(q_wide, q_scale, q_gain, dq_wide, q_dot, width_all)
    dk_result = finish_norm(k_wide, k_scale, k_gain, dk_wide, k_dot, width_all)
    return (dq_result, dk_result, merge_heads(dv_heads).astype(jnp.bfloat16))


VMEM_BYTES = 48 * 2**20
PICK_ROWS = 16
PIECES = 4
IN_VMEM = pl.BlockSpec(memory_space=pltpu.VMEM)
IN_SMEM = pl.BlockSpec(memory_space=pltpu.SMEM)


def owners_of(group, n_ctx, heads_dev):
    places = [(4 * head + 1) * n_ctx // (4 * heads_dev) for head in range(heads_dev)]
    return [n_ctx - 1 - place if group % 2 else place for place in places]


def head_at(place, group, n_ctx, heads_dev):
    even = jnp.where(group % 2 == 1, n_ctx - 1 - place, place)
    head = -1
    for index, owner in enumerate(owners_of(0, n_ctx, heads_dev)):
        head = jnp.where(even == owner, index, head)
    return head


def pairs_to_owner(mask, n_ctx, n_head, heads_dev):
    pairs = []
    for group in range(n_head):
        owners = owners_of(group, n_ctx, heads_dev)
        for block in range(n_ctx):
            if block ^ mask in owners:
                pairs.append((block * n_head + group, (block ^ mask) * n_head + group))
    return pairs


def there_masks(n_ctx):
    return list(range(n_ctx - 1, -1, -1))


def back_masks(n_ctx):
    return list(range(n_ctx // 2 - 1, 0, -1)) + list(range(n_ctx - 1, n_ctx // 2 - 1, -1)) + [0]


def move(masks, arrays, back, n_ctx, n_head, heads_dev):
    moved = []
    for mask, array in zip(masks, arrays):
        pairs = pairs_to_owner(mask, n_ctx, n_head, heads_dev)
        if back:
            pairs = [(b, a) for a, b in pairs]
        moved.append(lax.ppermute(array, ("ctx", "head"), pairs) if mask else array)
    return moved


def column(row, width):
    return jnp.broadcast_to(row, (width, row.shape[1])).T


def row_sums(wide):
    total = wide[:, :HD]
    for at in range(HD, wide.shape[1], HD):
        total = total + wide[:, at : at + HD]
    return jnp.sum(total.T, axis=0, keepdims=True)


def load_kernel(*refs):
    inputs, square_ref, outs, sems = refs[:6], refs[6], refs[7:13], refs[13]
    piece = inputs[0].shape[0] // PIECES

    def copies(at):
        if at >= 4:
            return [pltpu.make_async_copy(inputs[at], outs[at], sems.at[at, 0])]
        places = [pl.ds(part * piece, piece) for part in range(PIECES)]
        return [
            pltpu.make_async_copy(
                inputs[at].at[place, :], outs[at].at[place, :], sems.at[at, part]
            )
            for part, place in enumerate(places)
        ]

    for at in range(6):
        for copy in copies(at):
            copy.start()
    for at in range(6):
        for copy in copies(at):
            copy.wait()
        if at < 2:
            wide = outs[at][...].astype(jnp.float32)
            square_ref[at : at + 1, :] = row_sums(wide * wide)


def load(arrays):
    rows = arrays[0].shape[0]
    return pl.pallas_call(
        load_kernel,
        out_shape=[jax.ShapeDtypeStruct((2, rows), jnp.float32)]
        + [jax.ShapeDtypeStruct(array.shape, array.dtype) for array in arrays],
        in_specs=[pl.BlockSpec(memory_space=pltpu.HBM)] * 6,
        out_specs=[IN_VMEM] * 7,
        scratch_shapes=[pltpu.SemaphoreType.DMA((6, PIECES))],
        compiler_params=pltpu.CompilerParams(vmem_limit_bytes=VMEM_BYTES),
    )(*[pltpu.with_memory_space_constraint(array, pltpu.HBM) for array in arrays])


def row_scales(square_ref, width_all):
    return lax.rsqrt(square_ref[...] / width_all + epsilon)


def pack_kernel(n_ctx, width_all, sel, square_ref, q_gain, k_gain, q_ref, k_ref, v_ref, g_ref, *outs):
    heads_dev, remote_count = sel.shape[1:]
    rows = q_ref.shape[0]
    block, group = lax.axis_index("ctx"), lax.axis_index("head")
    scale_rows = row_scales(square_ref, width_all)
    scales = [column(scale_rows[at : at + 1, :], HD) for at in range(2)]
    lane = lax.broadcasted_iota(jnp.int32, (PICK_ROWS, HD), 1)
    for mask, out in zip(there_masks(n_ctx), outs):
        head = head_at(block ^ mask, group, n_ctx, heads_dev)

        @pl.when(head >= 0)
        def _(head=head, out=out):
            place = pl.ds(pl.multiple_of(head * HD, HD), HD)
            for at, (ref, gain) in enumerate(((q_ref, q_gain), (k_ref, k_gain))):
                normed = ref[:, place].astype(jnp.float32) * scales[at] * gain[pl.ds(head, 1), :]
                out[at * rows : (at + 1) * rows, :] = normed.astype(jnp.bfloat16)
            out[2 * rows : 3 * rows, :] = v_ref[:, place]
            out[3 * rows : 4 * rows, :] = g_ref[:, place]
            picks = jnp.zeros((PICK_ROWS, HD), jnp.float32)
            for slot in range(remote_count):
                picks = jnp.where(lane == slot, sel[0, head, slot].astype(jnp.float32), picks)
            out[4 * rows :, :] = picks.astype(jnp.bfloat16)


def attend_kernel(n_ctx, heads_dev, remote_count, *refs):
    messages = dict(zip(there_masks(n_ctx), refs[:n_ctx]))
    outs = dict(zip(back_masks(n_ctx), refs[n_ctx : 2 * n_ctx]))
    scratch = refs[2 * n_ctx :]
    q_ref, qt_ref, g_ref, gt_ref, k_ref, kt_ref, v_ref = scratch[:7]
    dq_ref, dk_ref, dv_ref, ds_ref, kt_picked, picks_ref, picks, sem = scratch[7:15]
    buffers = (scratch[15:18], scratch[18:21])
    rows = q_ref.shape[1]
    near_tiles = rows // TILE
    n_keys = near_tiles + remote_count
    factor = 1.0 / math.sqrt(HD)
    to_base2 = factor * math.log2(math.e)
    own_block = lax.axis_index("ctx")
    own_head = head_at(own_block, lax.axis_index("head"), n_ctx, heads_dev)

    def rows_of(block):
        return pl.ds(pl.multiple_of(block * rows, rows), rows)

    def places_of(mask):
        block = own_block ^ mask
        return [
            pl.ds(pl.multiple_of(block * rows + tile * TILE, TILE), TILE)
            for tile in range(near_tiles)
        ] + [
            pl.ds(pl.multiple_of(picks[mask, slot] * TILE, TILE), TILE)
            for slot in range(remote_count)
        ]

    def prepare(mask):
        place = rows_of(own_block ^ mask)
        query, keys, values, grad = [
            messages[mask][at * rows : (at + 1) * rows, :] for at in range(4)
        ]
        q_ref[mask] = query
        qt_ref[mask] = query.T
        k_ref[place, :] = keys
        kt_ref[:, place] = keys.T
        v_ref[place, :] = values
        g_ref[mask] = grad
        gt_ref[mask] = grad.T

    def scores(mask, slot, place, buffer):
        weight_ref, dprob_ref, stat_ref = buffer
        score = jnp.dot(k_ref[place, :], qt_ref[mask], preferred_element_type=jnp.float32)
        dprob = jnp.dot(v_ref[place, :], gt_ref[mask], preferred_element_type=jnp.float32)
        top = jnp.max(score, axis=0, keepdims=True)
        weight = jnp.exp2((score - top) * to_base2)
        weight_ref[slot] = weight
        dprob_ref[slot] = dprob
        stat_ref[0, slot : slot + 1, :] = top * to_base2
        stat_ref[1, slot : slot + 1, :] = jnp.sum(weight, axis=0, keepdims=True)
        stat_ref[2, slot : slot + 1, :] = jnp.sum(weight * dprob, axis=0, keepdims=True)

    def settle(buffer):
        stat_ref = buffer[2]
        tops = stat_ref[0, :n_keys, :]
        shares = jnp.exp2(tops - jnp.max(tops, axis=0, keepdims=True))
        total = jnp.sum(shares * stat_ref[1, :n_keys, :], axis=0, keepdims=True)
        mixed = jnp.sum(shares * stat_ref[2, :n_keys, :], axis=0, keepdims=True)
        inverse = 1.0 / total
        return shares * inverse, mixed * inverse

    def gradients(mask, slot, place, buffer, shares, delta):
        weight_ref, dprob_ref, _ = buffer
        prob = weight_ref[slot] * shares[slot : slot + 1, :]
        dscore = (prob * (dprob_ref[slot] - delta)).astype(jnp.bfloat16)
        ds_ref[slot * TILE : (slot + 1) * TILE, :] = dscore
        kt_picked[:, slot * TILE : (slot + 1) * TILE] = kt_ref[:, place]
        dk_ref[place, :] += jnp.dot(dscore, q_ref[mask], preferred_element_type=jnp.float32)
        dv_ref[place, :] += jnp.dot(
            prob.astype(jnp.bfloat16), g_ref[mask], preferred_element_type=jnp.float32
        )

    def query_gradient(mask):
        dq_t = jnp.dot(kt_picked[...], ds_ref[...], preferred_element_type=jnp.float32)
        dq_ref[mask] = (dq_t * factor).T.astype(jnp.bfloat16)

    def step(mask, buffer, later, later_buffer):
        places = places_of(mask)
        shares, delta = settle(buffer)
        later_places = None if later is None else places_of(later)
        for slot in range(n_keys):
            gradients(mask, slot, places[slot], buffer, shares, delta)
            if later is not None:
                scores(later, slot, later_places[slot], later_buffer)
        query_gradient(mask)

    @pl.when(own_head >= 0)
    def _():
        for mask in range(n_ctx):
            picked = messages[mask][4 * rows :, :].astype(jnp.float32)
            picks_ref[mask : mask + 1, :] = picked.astype(jnp.int32)[:1, :]
        copy = pltpu.make_async_copy(picks_ref, picks, sem)
        copy.start()
        for mask in range(n_ctx):
            prepare(mask)
        dk_ref[...] = jnp.zeros_like(dk_ref)
        dv_ref[...] = jnp.zeros_like(dv_ref)
        copy.wait()
        for slot, place in enumerate(places_of(0)):
            scores(0, slot, place, buffers[0])

        def two(pair, carry):
            step(2 * pair, buffers[0], 2 * pair + 1, buffers[1])
            step(2 * pair + 1, buffers[1], 2 * pair + 2, buffers[0])
            return carry

        lax.fori_loop(0, n_ctx // 2 - 1, two, 0)
        step(n_ctx - 2, buffers[0], n_ctx - 1, buffers[1])
        step(n_ctx - 1, buffers[1], None, None)
        for mask in range(n_ctx):
            place = rows_of(own_block ^ mask)
            outs[mask][0] = dq_ref[mask]
            outs[mask][1] = (dk_ref[place, :] * factor).astype(jnp.bfloat16)
            outs[mask][2] = dv_ref[place, :].astype(jnp.bfloat16)


def attend(messages, heads_dev, remote_count):
    n_ctx = len(messages)
    rows = (messages[0].shape[0] - PICK_ROWS) // 4
    tokens = n_ctx * rows
    n_keys = rows // TILE + remote_count
    by_block = pltpu.VMEM((n_ctx, rows, HD), jnp.bfloat16)
    by_block_t = pltpu.VMEM((n_ctx, HD, rows), jnp.bfloat16)
    buffer = [
        pltpu.VMEM((n_keys, TILE, rows), jnp.float32),
        pltpu.VMEM((n_keys, TILE, rows), jnp.float32),
        pltpu.VMEM((3, -(-n_keys // 8) * 8, rows), jnp.float32),
    ]
    return pl.pallas_call(
        functools.partial(attend_kernel, n_ctx, heads_dev, remote_count),
        out_shape=[jax.ShapeDtypeStruct((3, rows, HD), jnp.bfloat16)] * n_ctx,
        in_specs=[IN_VMEM] * n_ctx,
        out_specs=[IN_VMEM] * n_ctx,
        scratch_shapes=[
            by_block,
            by_block_t,
            by_block,
            by_block_t,
            pltpu.VMEM((tokens, HD), jnp.bfloat16),
            pltpu.VMEM((HD, tokens), jnp.bfloat16),
            pltpu.VMEM((tokens, HD), jnp.bfloat16),
            by_block,
            pltpu.VMEM((tokens, HD), jnp.float32),
            pltpu.VMEM((tokens, HD), jnp.float32),
            pltpu.VMEM((n_keys * TILE, rows), jnp.bfloat16),
            pltpu.VMEM((HD, n_keys * TILE), jnp.bfloat16),
            pltpu.VMEM((n_ctx, HD), jnp.int32),
            pltpu.SMEM((n_ctx, HD), jnp.int32),
            pltpu.SemaphoreType.DMA,
        ]
        + buffer
        + buffer,
        compiler_params=pltpu.CompilerParams(vmem_limit_bytes=VMEM_BYTES),
    )(*messages)


def gather_kernel(n_ctx, heads_dev, q_ref, k_ref, q_gain, k_gain, *refs):
    slots = refs[:n_ctx]
    dot_ref, dq_ref, dk_ref, dv_ref = refs[n_ctx:]
    block, group = lax.axis_index("ctx"), lax.axis_index("head")
    for mask, slot in zip(back_masks(n_ctx), slots):
        head = head_at(block ^ mask, group, n_ctx, heads_dev)

        @pl.when(head >= 0)
        def _(head=head, slot=slot):
            place = pl.ds(pl.multiple_of(head * HD, HD), HD)
            for at, out in enumerate((dq_ref, dk_ref, dv_ref)):
                out[:, place] = slot[at]

    for at, (wide_ref, pre_ref, gain) in enumerate(
        ((dq_ref, q_ref, q_gain), (dk_ref, k_ref, k_gain))
    ):
        terms = 0.0
        for head in range(heads_dev):
            place = slice(head * HD, (head + 1) * HD)
            grad = wide_ref[:, place].astype(jnp.float32)
            terms += gain[head : head + 1, :] * grad * pre_ref[:, place].astype(jnp.float32)
        dot_ref[at : at + 1, :] = row_sums(terms)


def finish_kernel(width_all, q_ref, k_ref, q_gain, k_gain, square_ref, dot_ref, *refs):
    dq_ref, dk_ref, dq_out, dk_out = refs
    scales = row_scales(square_ref, width_all)
    backs = scales**3 * (dot_ref[...] / width_all)
    for at, (pre_ref, gain, grad_ref, out) in enumerate(
        ((q_ref, q_gain, dq_ref, dq_out), (k_ref, k_gain, dk_ref, dk_out))
    ):
        scale = column(scales[at : at + 1, :], HD)
        back = column(backs[at : at + 1, :], HD)
        for head in range(gain.shape[0]):
            place = slice(head * HD, (head + 1) * HD)
            wide = pre_ref[:, place].astype(jnp.float32)
            grad = grad_ref[:, place].astype(jnp.float32)
            out[:, place] = (scale * gain[head : head + 1, :] * grad - wide * back).astype(jnp.bfloat16)


def heads_to_owners(q_pre, k_pre, values, out_grad, q_gain, k_gain, selected):
    n_ctx = lax.axis_size("ctx")
    n_head = lax.axis_size("head")
    rows, width_dev = q_pre.shape
    width_all = width_dev * n_head
    heads_dev = width_dev // HD
    remote_count = selected.shape[2]
    sizes = (n_ctx, n_head, heads_dev)
    params = pltpu.CompilerParams(vmem_limit_bytes=VMEM_BYTES)
    by_row = jax.ShapeDtypeStruct((2, rows), jnp.float32)
    wide = jax.ShapeDtypeStruct((rows, width_dev), jnp.bfloat16)

    q_gains = q_gain.reshape(heads_dev, HD)
    k_gains = k_gain.reshape(heads_dev, HD)

    squares, q_pre, k_pre, values, out_grad, q_gains, k_gains = load(
        (q_pre, k_pre, values, out_grad, q_gains, k_gains)
    )
    squares = lax.psum(squares, "head")
    sent = pl.pallas_call(
        functools.partial(pack_kernel, n_ctx, width_all),
        out_shape=[jax.ShapeDtypeStruct((4 * rows + PICK_ROWS, HD), jnp.bfloat16)] * n_ctx,
        in_specs=[IN_SMEM] + [IN_VMEM] * 7,
        out_specs=[IN_VMEM] * n_ctx,
        compiler_params=params,
    )(selected, squares, q_gains, k_gains, q_pre, k_pre, values, out_grad)
    messages = move(there_masks(n_ctx), sent, False, *sizes)
    results = attend(messages, heads_dev, remote_count)
    slots = move(back_masks(n_ctx), results, True, *sizes)

    pres = (q_pre, k_pre, q_gains, k_gains)
    dots, dq_wide, dk_wide, dv = pl.pallas_call(
        functools.partial(gather_kernel, n_ctx, heads_dev),
        out_shape=[by_row, wide, wide, wide],
        in_specs=[IN_VMEM] * (4 + n_ctx),
        out_specs=[IN_VMEM] * 4,
        compiler_params=params,
    )(*pres, *slots)
    dots = lax.psum(dots, "head")
    dq, dk = pl.pallas_call(
        functools.partial(finish_kernel, width_all),
        out_shape=[wide, wide],
        in_specs=[IN_VMEM] * 8,
        out_specs=[IN_VMEM] * 2,
        compiler_params=params,
    )(*pres, squares, dots, dq_wide, dk_wide)
    return dq, dk, dv


def on_device(q_pre, k_pre, values, out_grad, q_gain, k_gain, selected):
    n_ctx = lax.axis_size("ctx")
    tiles_dev, heads_dev, remote_count = selected.shape
    capacity = -(-heads_dev * remote_count // (n_ctx - 1))
    by_head = (n_ctx - 1) * tiles_dev * 7
    by_tile = (n_ctx - 1) * capacity * 6
    paired = n_ctx & (n_ctx - 1) == 0 and n_ctx >= max(heads_dev, 4) and n_ctx * tiles_dev <= 256
    plan = heads_to_owners if paired and by_head <= by_tile else tiles_to_queries
    return plan(q_pre, k_pre, values, out_grad, q_gain, k_gain, selected)


def solution(mesh):
    placed = (
        P("ctx", "head"),
        P("ctx", "head"),
        P("ctx", "head"),
        P("ctx", "head"),
        P("head"),
        P("head"),
        P("ctx", "head", None),
    )
    return jax.shard_map(
        on_device,
        mesh=mesh,
        in_specs=placed,
        out_specs=(P("ctx", "head"), P("ctx", "head"), P("ctx", "head")),
        check_vma=False,
    )
```

```python
import functools
import math

import jax
import jax.numpy as jnp
from jax import lax
from jax.experimental import pallas as pl
from jax.experimental.pallas import tpu as pltpu
from jax.sharding import PartitionSpec as P

HD = 128
TILE = 128


epsilon = 1e-06


def split_heads(array, heads_dev):
    return array.reshape(array.shape[0], heads_dev, HD).transpose(1, 0, 2)


def merge_heads(array):
    heads_dev, tok_dev, depth = array.shape
    return array.transpose(1, 0, 2).reshape(tok_dev, heads_dev * depth)


def per_tile(array, qt_dev):
    heads_dev, tok_dev, depth = array.shape
    return array.reshape(heads_dev, qt_dev, TILE, depth).transpose(1, 0, 2, 3)


def from_tiles(array):
    qt_dev, heads_dev, rows_tile, depth = array.shape
    return array.transpose(1, 0, 2, 3).reshape(heads_dev, qt_dev * rows_tile, depth)


def table_sum(taken, pieces, heads_dev, qt_dev):
    flat_pieces = pieces.reshape(pieces.shape[0], -1)
    summed = jnp.dot(
        taken, flat_pieces, precision=lax.Precision.HIGHEST, preferred_element_type=jnp.float32
    )
    summed = summed.reshape(heads_dev, qt_dev, 2, TILE, HD).transpose(2, 0, 1, 3, 4)
    return summed.reshape(2, heads_dev, qt_dev * TILE, HD)


def rounded(array):
    return array.astype(jnp.bfloat16)


def finish_norm(wide, scale, gain, grad, dot_sum, width_all):
    return (scale * gain * grad - wide * scale**3 * (dot_sum / width_all)[:, None]).astype(
        jnp.bfloat16
    )


def tiles_to_queries(q_pre, k_pre, values, out_grad, q_gain, k_gain, selected):
    n_ctx = lax.axis_size("ctx")
    tok_dev, width_dev = q_pre.shape
    width_all = width_dev * lax.axis_size("head")
    heads_dev = width_dev // HD
    qt_dev = tok_dev // TILE
    remote_count = selected.shape[2]
    factor = 1.0 / math.sqrt(HD)
    q_wide = q_pre.astype(jnp.float32)
    k_wide = k_pre.astype(jnp.float32)
    q_square, k_square = lax.psum(
        (jnp.sum(q_wide * q_wide, axis=1), jnp.sum(k_wide * k_wide, axis=1)), "head"
    )
    q_scale = lax.rsqrt(q_square / width_all + epsilon)[:, None]
    k_scale = lax.rsqrt(k_square / width_all + epsilon)[:, None]
    q_heads = split_heads(rounded(q_wide * q_scale * q_gain), heads_dev)
    k_heads = split_heads(rounded(k_wide * k_scale * k_gain), heads_dev)
    v_heads = split_heads(values, heads_dev)
    g_heads = split_heads(out_grad, heads_dev)
    q_tiles = per_tile(q_heads, qt_dev)
    g_tiles = per_tile(g_heads, qt_dev)
    k_table = k_heads.reshape(heads_dev * qt_dev, TILE, HD)
    v_table = v_heads.reshape(heads_dev * qt_dev, TILE, HD)
    flat_sel = selected[0].reshape(-1)
    n_slot = flat_sel.shape[0]
    capacity = -(-n_slot // (n_ctx - 1))
    n_buffer = n_ctx * capacity
    owners = flat_sel // qt_dev
    head_of = jnp.arange(n_slot, dtype=jnp.int32) // remote_count
    codes = head_of * qt_dev + flat_sel % qt_dev
    matches = (owners[:, None] == jnp.arange(n_ctx, dtype=jnp.int32)[None, :]).astype(jnp.int32)
    ranks = jnp.sum((jnp.cumsum(matches, axis=0) - matches) * matches, axis=1)
    position = owners * capacity + ranks
    placed = position[None, :] == jnp.arange(n_buffer, dtype=jnp.int32)[:, None]
    request = jnp.sum(jnp.where(placed, codes[None, :] + 1, 0), axis=1) - 1
    asked = lax.all_to_all(
        request.reshape(n_ctx, capacity), "ctx", split_axis=0, concat_axis=0, tiled=True
    ).reshape(n_buffer)
    clipped = jnp.maximum(asked, 0)
    taken = (asked[None, :] == jnp.arange(heads_dev * qt_dev, dtype=jnp.int32)[:, None]).astype(
        jnp.float32
    )
    s_near = (
        jnp.einsum("rhqd,hkd->rhqk", q_tiles, k_heads, preferred_element_type=jnp.float32) * factor
    )
    dp_near = jnp.einsum("rhqd,hkd->rhqk", g_tiles, v_heads, preferred_element_type=jnp.float32)
    near_top = jnp.max(s_near, axis=-1)
    outgoing = jnp.stack((k_table[clipped], v_table[clipped]), axis=1).reshape(
        n_ctx, capacity, 2, TILE, HD
    )
    incoming = lax.all_to_all(outgoing, "ctx", split_axis=0, concat_axis=0, tiled=True).reshape(
        n_buffer, 2, TILE, HD
    )
    slot_kv = incoming[position].reshape(heads_dev, remote_count, 2, TILE, HD)
    far_k = slot_kv[:, :, 0]
    far_v = slot_kv[:, :, 1]
    s_far = (
        jnp.einsum("rhqd,hckd->rhqck", q_tiles, far_k, preferred_element_type=jnp.float32) * factor
    )
    dp_far = jnp.einsum("rhqd,hckd->rhqck", g_tiles, far_v, preferred_element_type=jnp.float32)
    row_top = jnp.maximum(near_top, jnp.max(s_far, axis=(-2, -1)))
    totals = jnp.sum(jnp.exp(s_near - row_top[..., None]), axis=-1) + jnp.sum(
        jnp.exp(s_far - row_top[..., None, None]), axis=(-2, -1)
    )
    lse = row_top + jnp.log(totals)
    p_near = jnp.exp(s_near - lse[..., None])
    p_far = jnp.exp(s_far - lse[..., None, None])
    delta = jnp.sum(p_near * dp_near, axis=-1) + jnp.sum(p_far * dp_far, axis=(-2, -1))
    ds_near = rounded(p_near * (dp_near - delta[..., None]) * factor)
    pb_near = rounded(p_near)
    dq_near = jnp.einsum("rhqk,hkd->rhqd", ds_near, k_heads, preferred_element_type=jnp.float32)
    dk_near = jnp.einsum("rhqk,rhqd->hkd", ds_near, q_tiles, preferred_element_type=jnp.float32)
    dv_near = jnp.einsum("rhqk,rhqd->hkd", pb_near, g_tiles, preferred_element_type=jnp.float32)
    dq_near, dk_near, dv_near = (dq_near, dk_near, dv_near)
    ds_far = rounded(p_far * (dp_far - delta[..., None, None]) * factor)
    pb_far = rounded(p_far)
    dq_far = jnp.einsum("rhqck,hckd->rhqd", ds_far, far_k, preferred_element_type=jnp.float32)
    dq_wide = merge_heads(from_tiles(dq_near + dq_far))
    q_dot = jnp.sum(q_gain * dq_wide * q_wide, axis=1)
    dq_wide, q_dot = (dq_wide, q_dot)
    dk_far = jnp.einsum("rhqck,rhqd->hckd", ds_far, q_tiles, preferred_element_type=jnp.float32)
    dv_far = jnp.einsum("rhqck,rhqd->hckd", pb_far, g_tiles, preferred_element_type=jnp.float32)
    grads = jnp.stack((dk_far, dv_far), axis=2).reshape(n_slot, 2, TILE, HD)
    sending = jnp.zeros((n_buffer, 2, TILE, HD), jnp.float32).at[position].set(grads)
    returned = lax.all_to_all(
        sending.reshape(n_ctx, capacity, 2, TILE, HD),
        "ctx",
        split_axis=0,
        concat_axis=0,
        tiled=True,
    ).reshape(n_buffer, 2, TILE, HD)
    far_sums = table_sum(taken, returned, heads_dev, qt_dev)
    dk_wide = merge_heads(dk_near + far_sums[0])
    dv_heads = dv_near + far_sums[1]
    k_dot = jnp.sum(k_gain * dk_wide * k_wide, axis=1)
    q_dot, k_dot = lax.psum((q_dot, k_dot), "head")
    dq_result = finish_norm(q_wide, q_scale, q_gain, dq_wide, q_dot, width_all)
    dk_result = finish_norm(k_wide, k_scale, k_gain, dk_wide, k_dot, width_all)
    return (dq_result, dk_result, merge_heads(dv_heads).astype(jnp.bfloat16))


VMEM_BYTES = 48 * 2**20
PIECES = 4
IN_VMEM = pl.BlockSpec(memory_space=pltpu.VMEM)
IN_SMEM = pl.BlockSpec(memory_space=pltpu.SMEM)


def owners_of(group, n_ctx, heads_dev):
    places = [(4 * head + 1) * n_ctx // (4 * heads_dev) for head in range(heads_dev)]
    return [n_ctx - 1 - place if group % 2 else place for place in places]


def head_at(place, group, n_ctx, heads_dev):
    even = jnp.where(group % 2 == 1, n_ctx - 1 - place, place)
    head = -1
    for index, owner in enumerate(owners_of(0, n_ctx, heads_dev)):
        head = jnp.where(even == owner, index, head)
    return head


def pairs_to_owner(mask, n_ctx, n_head, heads_dev):
    pairs = []
    for group in range(n_head):
        owners = owners_of(group, n_ctx, heads_dev)
        for block in range(n_ctx):
            if block ^ mask in owners:
                pairs.append((block * n_head + group, (block ^ mask) * n_head + group))
    return pairs


def there_parts(n_ctx):
    whole = [(mask, 0, 4) for mask in range(n_ctx - 1, 1, -1)]
    return whole + [(1, 0, 2), (1, 2, 2), (0, 0, 4)]


def back_masks(n_ctx):
    half = n_ctx // 2
    return [2, 1] + list(range(n_ctx - 1, half - 1, -1)) + list(range(half - 1, 2, -1)) + [0]


def move(masks, arrays, back, n_ctx, n_head, heads_dev):
    moved = []
    for mask, array in zip(masks, arrays):
        pairs = pairs_to_owner(mask, n_ctx, n_head, heads_dev)
        if back:
            pairs = [(b, a) for a, b in pairs]
        moved.append(lax.ppermute(array, ("ctx", "head"), pairs) if mask else array)
    return moved


def column(row, width):
    return jnp.broadcast_to(row, (width, row.shape[1])).T


def row_sums(wide):
    total = wide[:, :HD]
    for at in range(HD, wide.shape[1], HD):
        total = total + wide[:, at : at + HD]
    return jnp.sum(total.T, axis=0, keepdims=True)


def pack_kernel(n_ctx, heads_dev, *refs):
    inputs, square_ref, outs = refs[:4], refs[4], refs[5:-2]
    held, sems = refs[-2:]
    rows = held.shape[1]
    piece = rows // PIECES
    block, group = lax.axis_index("ctx"), lax.axis_index("head")

    def copy(at, part):
        place = pl.ds(part * piece, piece)
        return pltpu.make_async_copy(
            inputs[at].at[place, :], held.at[at, place, :], sems.at[at, part]
        )

    for at in range(4):
        for part in range(PIECES):
            copy(at, part).start()
    for at in range(4):
        for part in range(PIECES):
            copy(at, part).wait()
    for (mask, first, count), out in zip(there_parts(n_ctx), outs):
        head = head_at(block ^ mask, group, n_ctx, heads_dev)

        @pl.when(head >= 0)
        def _(first=first, count=count, head=head, out=out):
            place = pl.ds(pl.multiple_of(head * HD, HD), HD)
            for at in range(count):
                out[at] = held[first + at, :, place]

    for at in range(2):
        wide = held[at].astype(jnp.float32)
        square_ref[at : at + 1, :] = row_sums(wide * wide)


def pack(arrays, n_ctx):
    rows, width_dev = arrays[0].shape
    result = pl.pallas_call(
        functools.partial(pack_kernel, n_ctx, width_dev // HD),
        out_shape=[jax.ShapeDtypeStruct((2, rows), jnp.float32)]
        + [
            jax.ShapeDtypeStruct((count, rows, HD), jnp.bfloat16)
            for _, _, count in there_parts(n_ctx)
        ],
        in_specs=[pl.BlockSpec(memory_space=pltpu.HBM)] * 4,
        out_specs=[IN_VMEM] * (n_ctx + 2),
        scratch_shapes=[
            pltpu.VMEM((4, rows, width_dev), jnp.bfloat16),
            pltpu.SemaphoreType.DMA((4, PIECES)),
        ],
        compiler_params=pltpu.CompilerParams(vmem_limit_bytes=VMEM_BYTES),
    )(*[pltpu.with_memory_space_constraint(array, pltpu.HBM) for array in arrays])
    return result[0], result[1:]


def attend_kernel(n_ctx, heads_dev, picks, scale_ref, q_gain, k_gain, *refs):
    messages = {}
    for (mask, first, count), ref in zip(there_parts(n_ctx), refs):
        for at in range(count):
            messages[mask, first + at] = ref.at[at]
    outs = dict(zip(back_masks(n_ctx), refs[n_ctx + 1 :]))
    scratch = refs[2 * n_ctx + 1 :]
    q_ref, qt_ref, g_ref, gt_ref, k_ref, kt_ref, v_ref = scratch[:7]
    dq_ref, dk_ref, dv_ref, ds_ref, kt_picked = scratch[7:12]
    buffers = (scratch[12:15], scratch[15:18])
    rows = messages[0, 0].shape[0]
    remote_count = picks.shape[1]
    near = rows // TILE
    n_keys = near + remote_count
    factor = 1.0 / math.sqrt(HD)
    to_base2 = factor * math.log2(math.e)
    own_block = lax.axis_index("ctx")
    own_head = head_at(own_block, lax.axis_index("head"), n_ctx, heads_dev)

    def rows_of(block):
        return pl.ds(pl.multiple_of(block * rows, rows), rows)

    def places_of(block):
        return [
            pl.ds(pl.multiple_of(block * rows + tile * TILE, TILE), TILE) for tile in range(near)
        ] + [
            pl.ds(pl.multiple_of(picks[block, slot] * TILE, TILE), TILE)
            for slot in range(remote_count)
        ]

    def prepare(mask, q_factor, k_factor):
        block = own_block ^ mask
        query, keys, values, grad = [messages[mask, at][...] for at in range(4)]
        place = rows_of(block)
        q_t = query.T.astype(jnp.float32) * scale_ref[block, 0:1, :] * q_factor
        k_t = keys.T.astype(jnp.float32) * scale_ref[block, 1:2, :] * k_factor
        qt_ref[mask] = q_t.astype(jnp.bfloat16)
        kt_ref[:, place] = k_t.astype(jnp.bfloat16)
        q_ref[mask] = q_t.astype(jnp.bfloat16).T
        k_ref[place, :] = k_t.astype(jnp.bfloat16).T
        v_ref[place, :] = values
        g_ref[mask] = grad
        gt_ref[mask] = grad.T

    def scores(mask, slot, place, buffer):
        weight_ref, dprob_ref, stat_ref = buffer
        score = jnp.dot(k_ref[place, :], qt_ref[mask], preferred_element_type=jnp.float32)
        dprob = jnp.dot(v_ref[place, :], gt_ref[mask], preferred_element_type=jnp.float32)
        top = jnp.max(score, axis=0, keepdims=True)
        weight = jnp.exp2((score - top) * to_base2)
        weight_ref[slot] = weight
        dprob_ref[slot] = dprob
        stat_ref[0, slot : slot + 1, :] = top * to_base2
        stat_ref[1, slot : slot + 1, :] = jnp.sum(weight, axis=0, keepdims=True)
        stat_ref[2, slot : slot + 1, :] = jnp.sum(weight * dprob, axis=0, keepdims=True)

    def settle(buffer):
        stat_ref = buffer[2]
        tops = stat_ref[0, :n_keys, :]
        shares = jnp.exp2(tops - jnp.max(tops, axis=0, keepdims=True))
        total = jnp.sum(shares * stat_ref[1, :n_keys, :], axis=0, keepdims=True)
        mixed = jnp.sum(shares * stat_ref[2, :n_keys, :], axis=0, keepdims=True)
        inverse = 1.0 / total
        return shares * inverse, mixed * inverse

    def gradients(mask, slot, place, buffer, shares, delta):
        weight_ref, dprob_ref, _ = buffer
        prob = weight_ref[slot] * shares[slot : slot + 1, :]
        dscore = (prob * (dprob_ref[slot] - delta)).astype(jnp.bfloat16)
        ds_ref[slot * TILE : (slot + 1) * TILE, :] = dscore
        kt_picked[:, slot * TILE : (slot + 1) * TILE] = kt_ref[:, place]
        dk_ref[place, :] += jnp.dot(dscore, q_ref[mask], preferred_element_type=jnp.float32)
        dv_ref[place, :] += jnp.dot(
            prob.astype(jnp.bfloat16), g_ref[mask], preferred_element_type=jnp.float32
        )

    def query_gradient(mask):
        dq_t = jnp.dot(kt_picked[...], ds_ref[...], preferred_element_type=jnp.float32)
        dq_ref[mask] = (dq_t * factor).T.astype(jnp.bfloat16)

    def step(mask, buffer, later, later_buffer):
        places = places_of(own_block ^ mask)
        shares, delta = settle(buffer)
        later_places = None if later is None else places_of(own_block ^ later)
        for slot in range(n_keys):
            gradients(mask, slot, places[slot], buffer, shares, delta)
            if later is not None:
                scores(later, slot, later_places[slot], later_buffer)
        query_gradient(mask)

    @pl.when(own_head >= 0)
    def _():
        q_factor = column(q_gain[pl.ds(own_head, 1), :], rows)
        k_factor = column(k_gain[pl.ds(own_head, 1), :], rows)
        for mask in range(n_ctx):
            prepare(mask, q_factor, k_factor)
        dk_ref[...] = jnp.zeros_like(dk_ref)
        dv_ref[...] = jnp.zeros_like(dv_ref)
        for slot, place in enumerate(places_of(own_block)):
            scores(0, slot, place, buffers[0])

        def two(pair, carry):
            step(2 * pair, buffers[0], 2 * pair + 1, buffers[1])
            step(2 * pair + 1, buffers[1], 2 * pair + 2, buffers[0])
            return carry

        lax.fori_loop(0, n_ctx // 2 - 1, two, 0)
        step(n_ctx - 2, buffers[0], n_ctx - 1, buffers[1])
        step(n_ctx - 1, buffers[1], None, None)
        for mask in range(n_ctx):
            place = rows_of(own_block ^ mask)
            outs[mask][0] = dq_ref[mask]
            outs[mask][1] = (dk_ref[place, :] * factor).astype(jnp.bfloat16)
            outs[mask][2] = dv_ref[place, :].astype(jnp.bfloat16)


def attend(picks, scales, q_gain, k_gain, messages, n_ctx):
    rows = messages[0].shape[1]
    tokens = n_ctx * rows
    n_keys = rows // TILE + picks.shape[1]
    by_block = pltpu.VMEM((n_ctx, rows, HD), jnp.bfloat16)
    by_block_t = pltpu.VMEM((n_ctx, HD, rows), jnp.bfloat16)
    buffer = [
        pltpu.VMEM((n_keys, TILE, rows), jnp.float32),
        pltpu.VMEM((n_keys, TILE, rows), jnp.float32),
        pltpu.VMEM((3, -(-n_keys // 8) * 8, rows), jnp.float32),
    ]
    return pl.pallas_call(
        functools.partial(attend_kernel, n_ctx, q_gain.shape[0]),
        out_shape=[jax.ShapeDtypeStruct((3, rows, HD), jnp.bfloat16)] * n_ctx,
        in_specs=[IN_SMEM] + [IN_VMEM] * (3 + len(messages)),
        out_specs=[IN_VMEM] * n_ctx,
        scratch_shapes=[
            by_block,
            by_block_t,
            by_block,
            by_block_t,
            pltpu.VMEM((tokens, HD), jnp.bfloat16),
            pltpu.VMEM((HD, tokens), jnp.bfloat16),
            pltpu.VMEM((tokens, HD), jnp.bfloat16),
            by_block,
            pltpu.VMEM((tokens, HD), jnp.float32),
            pltpu.VMEM((tokens, HD), jnp.float32),
            pltpu.VMEM((n_keys * TILE, rows), jnp.bfloat16),
            pltpu.VMEM((HD, n_keys * TILE), jnp.bfloat16),
        ]
        + buffer
        + buffer,
        compiler_params=pltpu.CompilerParams(vmem_limit_bytes=VMEM_BYTES),
    )(picks, scales, q_gain, k_gain, *messages)


def gather_kernel(n_ctx, heads_dev, q_ref, k_ref, q_gain, k_gain, *refs):
    slots = refs[:n_ctx]
    dot_ref, dq_ref, dk_ref, dv_ref = refs[n_ctx:]
    block, group = lax.axis_index("ctx"), lax.axis_index("head")
    for mask, slot in zip(back_masks(n_ctx), slots):
        head = head_at(block ^ mask, group, n_ctx, heads_dev)

        @pl.when(head >= 0)
        def _(head=head, slot=slot):
            place = pl.ds(pl.multiple_of(head * HD, HD), HD)
            for at, out in enumerate((dq_ref, dk_ref, dv_ref)):
                out[:, place] = slot[at]

    for at, (wide_ref, pre_ref, gain) in enumerate(
        ((dq_ref, q_ref, q_gain), (dk_ref, k_ref, k_gain))
    ):
        terms = gain[...] * wide_ref[...].astype(jnp.float32) * pre_ref[...].astype(jnp.float32)
        dot_ref[at : at + 1, :] = row_sums(terms)


def finish_kernel(width_all, q_ref, k_ref, q_gain, k_gain, scale_ref, dot_ref, *refs):
    dq_ref, dk_ref, dq_out, dk_out = refs
    scales = scale_ref[lax.axis_index("ctx")]
    backs = scales**3 * (dot_ref[...] / width_all)
    for at, (pre_ref, gain, grad_ref, out) in enumerate(
        ((q_ref, q_gain, dq_ref, dq_out), (k_ref, k_gain, dk_ref, dk_out))
    ):
        scale = column(scales[at : at + 1, :], HD)
        back = column(backs[at : at + 1, :], HD)
        for first in range(0, pre_ref.shape[1], HD):
            place = slice(first, first + HD)
            wide = pre_ref[:, place].astype(jnp.float32)
            grad = grad_ref[:, place].astype(jnp.float32)
            out[:, place] = (scale * gain[:, place] * grad - wide * back).astype(jnp.bfloat16)


def heads_to_owners(q_pre, k_pre, values, out_grad, q_gain, k_gain, selected):
    n_ctx = lax.axis_size("ctx")
    n_head = lax.axis_size("head")
    rows, width_dev = q_pre.shape
    width_all = width_dev * n_head
    heads_dev = width_dev // HD
    remote_count = selected.shape[2]
    sizes = (n_ctx, n_head, heads_dev)
    params = pltpu.CompilerParams(vmem_limit_bytes=VMEM_BYTES)

    by_row = jax.ShapeDtypeStruct((2, rows), jnp.float32)
    wide = jax.ShapeDtypeStruct((rows, width_dev), jnp.bfloat16)

    squares, sent = pack((q_pre, k_pre, values, out_grad), n_ctx)
    masks = [mask for mask, _, _ in there_parts(n_ctx)]
    messages = move(masks, sent, False, *sizes)

    wishes = selected[0].reshape(1, -1).astype(jnp.float32)
    wishes = jnp.pad(wishes, ((0, 0), (0, rows - wishes.shape[1])))
    small = jnp.concatenate((lax.psum(squares, "head"), wishes), axis=0)
    small = jnp.broadcast_to(small[None], (n_ctx,) + small.shape)
    small = lax.all_to_all(small, "ctx", split_axis=0, concat_axis=0, tiled=True)
    scales = lax.rsqrt(small[:, :2] / width_all + epsilon)
    own_head = head_at(lax.axis_index("ctx"), lax.axis_index("head"), n_ctx, heads_dev)
    first = jnp.maximum(own_head, 0) * remote_count
    picks = lax.dynamic_slice_in_dim(small[:, 2], first, remote_count, 1).astype(jnp.int32)

    q_gains = q_gain.reshape(heads_dev, HD)
    k_gains = k_gain.reshape(heads_dev, HD)
    results = attend(picks, scales, q_gains, k_gains, messages, n_ctx)
    slots = move(back_masks(n_ctx), results, True, *sizes)

    pres = (q_pre, k_pre, q_gain[None], k_gain[None])
    dots, dq_wide, dk_wide, dv = pl.pallas_call(
        functools.partial(gather_kernel, n_ctx, heads_dev),
        out_shape=[by_row, wide, wide, wide],
        in_specs=[IN_VMEM] * (4 + n_ctx),
        out_specs=[IN_VMEM] * 4,
        compiler_params=params,
    )(*pres, *slots)
    dots = lax.psum(dots, "head")
    dq, dk = pl.pallas_call(
        functools.partial(finish_kernel, width_all),
        out_shape=[wide, wide],
        in_specs=[IN_VMEM] * 8,
        out_specs=[IN_VMEM] * 2,
        compiler_params=params,
    )(*pres, scales, dots, dq_wide, dk_wide)
    return dq, dk, dv


def on_device(q_pre, k_pre, values, out_grad, q_gain, k_gain, selected):
    n_ctx = lax.axis_size("ctx")
    tiles_dev, heads_dev, remote_count = selected.shape
    capacity = -(-heads_dev * remote_count // (n_ctx - 1))
    by_head = (n_ctx - 1) * tiles_dev * 7
    by_tile = (n_ctx - 1) * capacity * 6
    paired = n_ctx & (n_ctx - 1) == 0 and n_ctx >= max(heads_dev, 4)
    plan = heads_to_owners if paired and by_head <= by_tile else tiles_to_queries
    return plan(q_pre, k_pre, values, out_grad, q_gain, k_gain, selected)


def solution(mesh):
    placed = (
        P("ctx", "head"),
        P("ctx", "head"),
        P("ctx", "head"),
        P("ctx", "head"),
        P("head"),
        P("head"),
        P("ctx", "head", None),
    )
    return jax.shard_map(
        on_device,
        mesh=mesh,
        in_specs=placed,
        out_specs=(P("ctx", "head"), P("ctx", "head"), P("ctx", "head")),
        check_vma=False,
    )
```

```python
import functools
import math

import jax
import jax.numpy as jnp
from jax import lax
from jax.experimental import pallas as pl
from jax.experimental.pallas import tpu as pltpu
from jax.sharding import PartitionSpec as P

HD = 128
TILE = 128


epsilon = 1e-06


def split_heads(array, heads_dev):
    return array.reshape(array.shape[0], heads_dev, HD).transpose(1, 0, 2)


def merge_heads(array):
    heads_dev, tok_dev, depth = array.shape
    return array.transpose(1, 0, 2).reshape(tok_dev, heads_dev * depth)


def per_tile(array, qt_dev):
    heads_dev, tok_dev, depth = array.shape
    return array.reshape(heads_dev, qt_dev, TILE, depth).transpose(1, 0, 2, 3)


def from_tiles(array):
    qt_dev, heads_dev, rows_tile, depth = array.shape
    return array.transpose(1, 0, 2, 3).reshape(heads_dev, qt_dev * rows_tile, depth)


def table_sum(taken, pieces, heads_dev, qt_dev):
    flat_pieces = pieces.reshape(pieces.shape[0], -1)
    summed = jnp.dot(
        taken, flat_pieces, precision=lax.Precision.HIGHEST, preferred_element_type=jnp.float32
    )
    summed = summed.reshape(heads_dev, qt_dev, 2, TILE, HD).transpose(2, 0, 1, 3, 4)
    return summed.reshape(2, heads_dev, qt_dev * TILE, HD)


def rounded(array):
    return array.astype(jnp.bfloat16)


def finish_norm(wide, scale, gain, grad, dot_sum, width_all):
    return (scale * gain * grad - wide * scale**3 * (dot_sum / width_all)[:, None]).astype(
        jnp.bfloat16
    )


def tiles_to_queries(q_pre, k_pre, values, out_grad, q_gain, k_gain, selected):
    n_ctx = lax.axis_size("ctx")
    tok_dev, width_dev = q_pre.shape
    width_all = width_dev * lax.axis_size("head")
    heads_dev = width_dev // HD
    qt_dev = tok_dev // TILE
    remote_count = selected.shape[2]
    factor = 1.0 / math.sqrt(HD)
    q_wide = q_pre.astype(jnp.float32)
    k_wide = k_pre.astype(jnp.float32)
    q_square, k_square = lax.psum(
        (jnp.sum(q_wide * q_wide, axis=1), jnp.sum(k_wide * k_wide, axis=1)), "head"
    )
    q_scale = lax.rsqrt(q_square / width_all + epsilon)[:, None]
    k_scale = lax.rsqrt(k_square / width_all + epsilon)[:, None]
    q_heads = split_heads(rounded(q_wide * q_scale * q_gain), heads_dev)
    k_heads = split_heads(rounded(k_wide * k_scale * k_gain), heads_dev)
    v_heads = split_heads(values, heads_dev)
    g_heads = split_heads(out_grad, heads_dev)
    q_tiles = per_tile(q_heads, qt_dev)
    g_tiles = per_tile(g_heads, qt_dev)
    k_table = k_heads.reshape(heads_dev * qt_dev, TILE, HD)
    v_table = v_heads.reshape(heads_dev * qt_dev, TILE, HD)
    flat_sel = selected[0].reshape(-1)
    n_slot = flat_sel.shape[0]
    capacity = -(-n_slot // (n_ctx - 1))
    n_buffer = n_ctx * capacity
    owners = flat_sel // qt_dev
    head_of = jnp.arange(n_slot, dtype=jnp.int32) // remote_count
    codes = head_of * qt_dev + flat_sel % qt_dev
    matches = (owners[:, None] == jnp.arange(n_ctx, dtype=jnp.int32)[None, :]).astype(jnp.int32)
    ranks = jnp.sum((jnp.cumsum(matches, axis=0) - matches) * matches, axis=1)
    position = owners * capacity + ranks
    placed = position[None, :] == jnp.arange(n_buffer, dtype=jnp.int32)[:, None]
    request = jnp.sum(jnp.where(placed, codes[None, :] + 1, 0), axis=1) - 1
    asked = lax.all_to_all(
        request.reshape(n_ctx, capacity), "ctx", split_axis=0, concat_axis=0, tiled=True
    ).reshape(n_buffer)
    clipped = jnp.maximum(asked, 0)
    taken = (asked[None, :] == jnp.arange(heads_dev * qt_dev, dtype=jnp.int32)[:, None]).astype(
        jnp.float32
    )
    s_near = (
        jnp.einsum("rhqd,hkd->rhqk", q_tiles, k_heads, preferred_element_type=jnp.float32) * factor
    )
    dp_near = jnp.einsum("rhqd,hkd->rhqk", g_tiles, v_heads, preferred_element_type=jnp.float32)
    near_top = jnp.max(s_near, axis=-1)
    outgoing = jnp.stack((k_table[clipped], v_table[clipped]), axis=1).reshape(
        n_ctx, capacity, 2, TILE, HD
    )
    incoming = lax.all_to_all(outgoing, "ctx", split_axis=0, concat_axis=0, tiled=True).reshape(
        n_buffer, 2, TILE, HD
    )
    slot_kv = incoming[position].reshape(heads_dev, remote_count, 2, TILE, HD)
    far_k = slot_kv[:, :, 0]
    far_v = slot_kv[:, :, 1]
    s_far = (
        jnp.einsum("rhqd,hckd->rhqck", q_tiles, far_k, preferred_element_type=jnp.float32) * factor
    )
    dp_far = jnp.einsum("rhqd,hckd->rhqck", g_tiles, far_v, preferred_element_type=jnp.float32)
    row_top = jnp.maximum(near_top, jnp.max(s_far, axis=(-2, -1)))
    totals = jnp.sum(jnp.exp(s_near - row_top[..., None]), axis=-1) + jnp.sum(
        jnp.exp(s_far - row_top[..., None, None]), axis=(-2, -1)
    )
    lse = row_top + jnp.log(totals)
    p_near = jnp.exp(s_near - lse[..., None])
    p_far = jnp.exp(s_far - lse[..., None, None])
    delta = jnp.sum(p_near * dp_near, axis=-1) + jnp.sum(p_far * dp_far, axis=(-2, -1))
    ds_near = rounded(p_near * (dp_near - delta[..., None]) * factor)
    pb_near = rounded(p_near)
    dq_near = jnp.einsum("rhqk,hkd->rhqd", ds_near, k_heads, preferred_element_type=jnp.float32)
    dk_near = jnp.einsum("rhqk,rhqd->hkd", ds_near, q_tiles, preferred_element_type=jnp.float32)
    dv_near = jnp.einsum("rhqk,rhqd->hkd", pb_near, g_tiles, preferred_element_type=jnp.float32)
    dq_near, dk_near, dv_near = (dq_near, dk_near, dv_near)
    ds_far = rounded(p_far * (dp_far - delta[..., None, None]) * factor)
    pb_far = rounded(p_far)
    dq_far = jnp.einsum("rhqck,hckd->rhqd", ds_far, far_k, preferred_element_type=jnp.float32)
    dq_wide = merge_heads(from_tiles(dq_near + dq_far))
    q_dot = jnp.sum(q_gain * dq_wide * q_wide, axis=1)
    dq_wide, q_dot = (dq_wide, q_dot)
    dk_far = jnp.einsum("rhqck,rhqd->hckd", ds_far, q_tiles, preferred_element_type=jnp.float32)
    dv_far = jnp.einsum("rhqck,rhqd->hckd", pb_far, g_tiles, preferred_element_type=jnp.float32)
    grads = jnp.stack((dk_far, dv_far), axis=2).reshape(n_slot, 2, TILE, HD)
    sending = jnp.zeros((n_buffer, 2, TILE, HD), jnp.float32).at[position].set(grads)
    returned = lax.all_to_all(
        sending.reshape(n_ctx, capacity, 2, TILE, HD),
        "ctx",
        split_axis=0,
        concat_axis=0,
        tiled=True,
    ).reshape(n_buffer, 2, TILE, HD)
    far_sums = table_sum(taken, returned, heads_dev, qt_dev)
    dk_wide = merge_heads(dk_near + far_sums[0])
    dv_heads = dv_near + far_sums[1]
    k_dot = jnp.sum(k_gain * dk_wide * k_wide, axis=1)
    q_dot, k_dot = lax.psum((q_dot, k_dot), "head")
    dq_result = finish_norm(q_wide, q_scale, q_gain, dq_wide, q_dot, width_all)
    dk_result = finish_norm(k_wide, k_scale, k_gain, dk_wide, k_dot, width_all)
    return (dq_result, dk_result, merge_heads(dv_heads).astype(jnp.bfloat16))


VMEM_BYTES = 48 * 2**20
PIECES = 4
IN_VMEM = pl.BlockSpec(memory_space=pltpu.VMEM)
IN_SMEM = pl.BlockSpec(memory_space=pltpu.SMEM)


def owners_of(group, n_ctx, heads_dev):
    places = [(4 * head + 1) * n_ctx // (4 * heads_dev) for head in range(heads_dev)]
    return [n_ctx - 1 - place if group % 2 else place for place in places]


def head_at(place, group, n_ctx, heads_dev):
    even = jnp.where(group % 2 == 1, n_ctx - 1 - place, place)
    head = -1
    for index, owner in enumerate(owners_of(0, n_ctx, heads_dev)):
        head = jnp.where(even == owner, index, head)
    return head


def pairs_to_owner(mask, n_ctx, n_head, heads_dev):
    pairs = []
    for group in range(n_head):
        owners = owners_of(group, n_ctx, heads_dev)
        for block in range(n_ctx):
            if block ^ mask in owners:
                pairs.append((block * n_head + group, (block ^ mask) * n_head + group))
    return pairs


def there_masks(n_ctx):
    return list(range(n_ctx - 1, -1, -1))


def back_masks(n_ctx):
    return list(range(n_ctx // 2 - 1, 0, -1)) + list(range(n_ctx - 1, n_ctx // 2 - 1, -1)) + [0]


def move(masks, arrays, back, n_ctx, n_head, heads_dev):
    moved = []
    for mask, array in zip(masks, arrays):
        pairs = pairs_to_owner(mask, n_ctx, n_head, heads_dev)
        if back:
            pairs = [(b, a) for a, b in pairs]
        moved.append(lax.ppermute(array, ("ctx", "head"), pairs) if mask else array)
    return moved


def column(row, width):
    return jnp.broadcast_to(row, (width, row.shape[1])).T


def row_sums(wide):
    total = wide[:, :HD]
    for at in range(HD, wide.shape[1], HD):
        total = total + wide[:, at : at + HD]
    return jnp.sum(total.T, axis=0, keepdims=True)


def pack_kernel(n_ctx, heads_dev, *refs):
    inputs, square_ref, outs = refs[:4], refs[4], refs[5 : 5 + n_ctx]
    held, sems = refs[5 + n_ctx :]
    rows = held.shape[1]
    piece = rows // PIECES
    block, group = lax.axis_index("ctx"), lax.axis_index("head")

    def copy(at, part):
        place = pl.ds(part * piece, piece)
        return pltpu.make_async_copy(
            inputs[at].at[place, :], held.at[at, place, :], sems.at[at, part]
        )

    for at in range(4):
        for part in range(PIECES):
            copy(at, part).start()
    for at in range(4):
        for part in range(PIECES):
            copy(at, part).wait()
    for mask, out in zip(there_masks(n_ctx), outs):
        head = head_at(block ^ mask, group, n_ctx, heads_dev)

        @pl.when(head >= 0)
        def _(head=head, out=out):
            place = pl.ds(pl.multiple_of(head * HD, HD), HD)
            for at in range(4):
                out[at] = held[at, :, place]

    for at in range(2):
        wide = held[at].astype(jnp.float32)
        square_ref[at : at + 1, :] = row_sums(wide * wide)


def pack(arrays, n_ctx):
    rows, width_dev = arrays[0].shape
    result = pl.pallas_call(
        functools.partial(pack_kernel, n_ctx, width_dev // HD),
        out_shape=[jax.ShapeDtypeStruct((2, rows), jnp.float32)]
        + [jax.ShapeDtypeStruct((4, rows, HD), jnp.bfloat16)] * n_ctx,
        in_specs=[pl.BlockSpec(memory_space=pltpu.HBM)] * 4,
        out_specs=[IN_VMEM] * (n_ctx + 1),
        scratch_shapes=[
            pltpu.VMEM((4, rows, width_dev), jnp.bfloat16),
            pltpu.SemaphoreType.DMA((4, PIECES)),
        ],
        compiler_params=pltpu.CompilerParams(vmem_limit_bytes=VMEM_BYTES),
    )(*[pltpu.with_memory_space_constraint(array, pltpu.HBM) for array in arrays])
    return result[0], result[1:]


def attend_kernel(n_ctx, heads_dev, picks, scale_ref, q_gain, k_gain, *refs):
    messages = dict(zip(there_masks(n_ctx), refs[:n_ctx]))
    outs = dict(zip(back_masks(n_ctx), refs[n_ctx : 2 * n_ctx]))
    scratch = refs[2 * n_ctx :]
    q_ref, qt_ref, g_ref, gt_ref, k_ref, kt_ref, v_ref = scratch[:7]
    dq_ref, dk_ref, dv_ref, kt_picked, k_picked, v_picked = scratch[7:13]
    buffers = (scratch[13:18], scratch[18:23])
    rows = messages[0].shape[1]
    remote_count = picks.shape[1]
    near = rows // TILE
    n_keys = near + remote_count
    factor = 1.0 / math.sqrt(HD)
    to_base2 = factor * math.log2(math.e)
    own_block = lax.axis_index("ctx")
    own_head = head_at(own_block, lax.axis_index("head"), n_ctx, heads_dev)

    def rows_of(block):
        return pl.ds(pl.multiple_of(block * rows, rows), rows)

    def places_of(block):
        return [
            pl.ds(pl.multiple_of(block * rows + tile * TILE, TILE), TILE) for tile in range(near)
        ] + [
            pl.ds(pl.multiple_of(picks[block, slot] * TILE, TILE), TILE)
            for slot in range(remote_count)
        ]

    def prepare(mask, q_factor, k_factor):
        message = messages[mask]
        block = own_block ^ mask
        place = rows_of(block)
        q_t = message[0].T.astype(jnp.float32) * scale_ref[block, 0:1, :] * q_factor
        k_t = message[1].T.astype(jnp.float32) * scale_ref[block, 1:2, :] * k_factor
        qt_ref[mask] = q_t.astype(jnp.bfloat16)
        kt_ref[:, place] = k_t.astype(jnp.bfloat16)
        q_ref[mask] = q_t.astype(jnp.bfloat16).T
        k_ref[place, :] = k_t.astype(jnp.bfloat16).T
        v_ref[place, :] = message[2]
        g_ref[mask] = message[3]
        gt_ref[mask] = message[3].T

    def tiles(first, count=1):
        return slice(first * TILE, (first + count) * TILE)

    def scores(mask, group, places, buffer):
        weight_ref, dprob_ref, stat_ref = buffer[:3]
        for slot in group:
            k_picked[tiles(slot), :] = k_ref[places[slot], :]
            v_picked[tiles(slot), :] = v_ref[places[slot], :]
        picked = tiles(group[0], len(group))
        score_all = jnp.dot(
            k_picked[picked, :], qt_ref[mask], preferred_element_type=jnp.float32
        )
        dprob_all = jnp.dot(
            v_picked[picked, :], gt_ref[mask], preferred_element_type=jnp.float32
        )
        for at, slot in enumerate(group):
            score = score_all[tiles(at), :]
            dprob = dprob_all[tiles(at), :]
            top = jnp.max(score, axis=0, keepdims=True)
            weight = jnp.exp2((score - top) * to_base2)
            weight_ref[slot] = weight
            dprob_ref[slot] = dprob
            stat_ref[0, slot : slot + 1, :] = top * to_base2
            stat_ref[1, slot : slot + 1, :] = jnp.sum(weight, axis=0, keepdims=True)
            stat_ref[2, slot : slot + 1, :] = jnp.sum(weight * dprob, axis=0, keepdims=True)

    def settle(buffer):
        stat_ref = buffer[2]
        tops = stat_ref[0, :n_keys, :]
        shares = jnp.exp2(tops - jnp.max(tops, axis=0, keepdims=True))
        total = jnp.sum(shares * stat_ref[1, :n_keys, :], axis=0, keepdims=True)
        mixed = jnp.sum(shares * stat_ref[2, :n_keys, :], axis=0, keepdims=True)
        inverse = 1.0 / total
        return shares * inverse, mixed * inverse

    def gradients(group, buffer, shares, delta):
        weight_ref, dprob_ref, _, ds_ref, pb_ref = buffer
        for slot in group:
            prob = weight_ref[slot] * shares[slot : slot + 1, :]
            pb_ref[tiles(slot), :] = prob.astype(jnp.bfloat16)
            ds_ref[tiles(slot), :] = (prob * (dprob_ref[slot] - delta)).astype(jnp.bfloat16)

    def products(mask, group, places, buffer):
        ds_ref, pb_ref = buffer[3:]
        picked = tiles(group[0], len(group))
        dk = jnp.dot(ds_ref[picked, :], q_ref[mask], preferred_element_type=jnp.float32)
        dv = jnp.dot(pb_ref[picked, :], g_ref[mask], preferred_element_type=jnp.float32)
        for at, slot in enumerate(group):
            dk_ref[places[slot], :] += dk[tiles(at), :]
            dv_ref[places[slot], :] += dv[tiles(at), :]
            kt_picked[:, tiles(slot)] = kt_ref[:, places[slot]]

    def query_gradient(mask, buffer):
        dq_t = jnp.dot(kt_picked[...], buffer[3][...], preferred_element_type=jnp.float32)
        dq_ref[mask] = (dq_t * factor).T.astype(jnp.bfloat16)

    groups = [range(first, min(first + 3, n_keys)) for first in range(0, n_keys, 3)]

    def step(now, before, after):
        if now is not None:
            shares, delta = settle(now[1])
        if before is not None:
            before_places = places_of(own_block ^ before[0])
        if after is not None:
            after_places = places_of(own_block ^ after[0])
        for group in groups:
            if before is not None:
                products(before[0], group, before_places, before[1])
            if now is not None:
                gradients(group, now[1], shares, delta)
            if after is not None:
                scores(after[0], group, after_places, after[1])
        if before is not None:
            query_gradient(*before)

    @pl.when(own_head >= 0)
    def _():
        q_factor = column(q_gain[pl.ds(own_head, 1), :], rows)
        k_factor = column(k_gain[pl.ds(own_head, 1), :], rows)
        for mask in range(n_ctx):
            prepare(mask, q_factor, k_factor)
        dk_ref[...] = jnp.zeros_like(dk_ref)
        dv_ref[...] = jnp.zeros_like(dv_ref)
        even, odd = buffers
        step(None, None, (0, even))
        step((0, even), None, (1, odd))

        def two(pair, carry):
            mask = 2 * pair
            step((mask + 1, odd), (mask, even), (mask + 2, even))
            step((mask + 2, even), (mask + 1, odd), (mask + 3, odd))
            return carry

        lax.fori_loop(0, n_ctx // 2 - 1, two, 0)
        step((n_ctx - 1, odd), (n_ctx - 2, even), None)
        step(None, (n_ctx - 1, odd), None)
        for mask in range(n_ctx):
            place = rows_of(own_block ^ mask)
            outs[mask][0] = dq_ref[mask]
            outs[mask][1] = (dk_ref[place, :] * factor).astype(jnp.bfloat16)
            outs[mask][2] = dv_ref[place, :].astype(jnp.bfloat16)


def attend(picks, scales, q_gain, k_gain, messages, n_ctx):
    rows = messages[0].shape[1]
    tokens = n_ctx * rows
    n_keys = rows // TILE + picks.shape[1]
    by_block = pltpu.VMEM((n_ctx, rows, HD), jnp.bfloat16)
    by_block_t = pltpu.VMEM((n_ctx, HD, rows), jnp.bfloat16)
    buffer = [
        pltpu.VMEM((n_keys, TILE, rows), jnp.float32),
        pltpu.VMEM((n_keys, TILE, rows), jnp.float32),
        pltpu.VMEM((3, -(-n_keys // 8) * 8, rows), jnp.float32),
        pltpu.VMEM((n_keys * TILE, rows), jnp.bfloat16),
        pltpu.VMEM((n_keys * TILE, rows), jnp.bfloat16),
    ]
    return pl.pallas_call(
        functools.partial(attend_kernel, n_ctx, q_gain.shape[0]),
        out_shape=[jax.ShapeDtypeStruct((3, rows, HD), jnp.bfloat16)] * n_ctx,
        in_specs=[IN_SMEM] + [IN_VMEM] * (3 + n_ctx),
        out_specs=[IN_VMEM] * n_ctx,
        scratch_shapes=[
            by_block,
            by_block_t,
            by_block,
            by_block_t,
            pltpu.VMEM((tokens, HD), jnp.bfloat16),
            pltpu.VMEM((HD, tokens), jnp.bfloat16),
            pltpu.VMEM((tokens, HD), jnp.bfloat16),
            by_block,
            pltpu.VMEM((tokens, HD), jnp.float32),
            pltpu.VMEM((tokens, HD), jnp.float32),
            pltpu.VMEM((HD, n_keys * TILE), jnp.bfloat16),
            pltpu.VMEM((n_keys * TILE, HD), jnp.bfloat16),
            pltpu.VMEM((n_keys * TILE, HD), jnp.bfloat16),
        ]
        + buffer
        + buffer,
        compiler_params=pltpu.CompilerParams(vmem_limit_bytes=VMEM_BYTES),
    )(picks, scales, q_gain, k_gain, *messages)


def gather_kernel(n_ctx, heads_dev, q_ref, k_ref, q_gain, k_gain, *refs):
    slots = refs[:n_ctx]
    dot_ref, dq_ref, dk_ref, dv_ref = refs[n_ctx:]
    block, group = lax.axis_index("ctx"), lax.axis_index("head")
    for mask, slot in zip(back_masks(n_ctx), slots):
        head = head_at(block ^ mask, group, n_ctx, heads_dev)

        @pl.when(head >= 0)
        def _(head=head, slot=slot):
            place = pl.ds(pl.multiple_of(head * HD, HD), HD)
            for at, out in enumerate((dq_ref, dk_ref, dv_ref)):
                out[:, place] = slot[at]

    for at, (wide_ref, pre_ref, gain) in enumerate(
        ((dq_ref, q_ref, q_gain), (dk_ref, k_ref, k_gain))
    ):
        terms = gain[...] * wide_ref[...].astype(jnp.float32) * pre_ref[...].astype(jnp.float32)
        dot_ref[at : at + 1, :] = row_sums(terms)


def finish_kernel(width_all, q_ref, k_ref, q_gain, k_gain, scale_ref, dot_ref, *refs):
    dq_ref, dk_ref, dq_out, dk_out = refs
    scales = scale_ref[lax.axis_index("ctx")]
    backs = scales**3 * (dot_ref[...] / width_all)
    for at, (pre_ref, gain, grad_ref, out) in enumerate(
        ((q_ref, q_gain, dq_ref, dq_out), (k_ref, k_gain, dk_ref, dk_out))
    ):
        scale = column(scales[at : at + 1, :], HD)
        back = column(backs[at : at + 1, :], HD)
        for first in range(0, pre_ref.shape[1], HD):
            place = slice(first, first + HD)
            wide = pre_ref[:, place].astype(jnp.float32)
            grad = grad_ref[:, place].astype(jnp.float32)
            out[:, place] = (scale * gain[:, place] * grad - wide * back).astype(jnp.bfloat16)


def heads_to_owners(q_pre, k_pre, values, out_grad, q_gain, k_gain, selected):
    n_ctx = lax.axis_size("ctx")
    n_head = lax.axis_size("head")
    rows, width_dev = q_pre.shape
    width_all = width_dev * n_head
    heads_dev = width_dev // HD
    remote_count = selected.shape[2]
    sizes = (n_ctx, n_head, heads_dev)
    params = pltpu.CompilerParams(vmem_limit_bytes=VMEM_BYTES)

    by_row = jax.ShapeDtypeStruct((2, rows), jnp.float32)
    wide = jax.ShapeDtypeStruct((rows, width_dev), jnp.bfloat16)

    squares, sent = pack((q_pre, k_pre, values, out_grad), n_ctx)
    messages = move(there_masks(n_ctx), sent, False, *sizes)

    wishes = selected[0].reshape(1, -1).astype(jnp.float32)
    wishes = jnp.pad(wishes, ((0, 0), (0, rows - wishes.shape[1])))
    small = jnp.concatenate((lax.psum(squares, "head"), wishes), axis=0)
    small = jnp.broadcast_to(small[None], (n_ctx,) + small.shape)
    small = lax.all_to_all(small, "ctx", split_axis=0, concat_axis=0, tiled=True)
    scales = lax.rsqrt(small[:, :2] / width_all + epsilon)
    own_head = head_at(lax.axis_index("ctx"), lax.axis_index("head"), n_ctx, heads_dev)
    first = jnp.maximum(own_head, 0) * remote_count
    picks = lax.dynamic_slice_in_dim(small[:, 2], first, remote_count, 1).astype(jnp.int32)

    q_gains = q_gain.reshape(heads_dev, HD)
    k_gains = k_gain.reshape(heads_dev, HD)
    results = attend(picks, scales, q_gains, k_gains, messages, n_ctx)
    slots = move(back_masks(n_ctx), results, True, *sizes)

    pres = (q_pre, k_pre, q_gain[None], k_gain[None])
    dots, dq_wide, dk_wide, dv = pl.pallas_call(
        functools.partial(gather_kernel, n_ctx, heads_dev),
        out_shape=[by_row, wide, wide, wide],
        in_specs=[IN_VMEM] * (4 + n_ctx),
        out_specs=[IN_VMEM] * 4,
        compiler_params=params,
    )(*pres, *slots)
    dots = lax.psum(dots, "head")
    dq, dk = pl.pallas_call(
        functools.partial(finish_kernel, width_all),
        out_shape=[wide, wide],
        in_specs=[IN_VMEM] * 8,
        out_specs=[IN_VMEM] * 2,
        compiler_params=params,
    )(*pres, scales, dots, dq_wide, dk_wide)
    return dq, dk, dv


def on_device(q_pre, k_pre, values, out_grad, q_gain, k_gain, selected):
    n_ctx = lax.axis_size("ctx")
    tiles_dev, heads_dev, remote_count = selected.shape
    capacity = -(-heads_dev * remote_count // (n_ctx - 1))
    by_head = (n_ctx - 1) * tiles_dev * 7
    by_tile = (n_ctx - 1) * capacity * 6
    paired = n_ctx & (n_ctx - 1) == 0 and n_ctx >= max(heads_dev, 4)
    plan = heads_to_owners if paired and by_head <= by_tile else tiles_to_queries
    return plan(q_pre, k_pre, values, out_grad, q_gain, k_gain, selected)


def solution(mesh):
    placed = (
        P("ctx", "head"),
        P("ctx", "head"),
        P("ctx", "head"),
        P("ctx", "head"),
        P("head"),
        P("head"),
        P("ctx", "head", None),
    )
    return jax.shard_map(
        on_device,
        mesh=mesh,
        in_specs=placed,
        out_specs=(P("ctx", "head"), P("ctx", "head"), P("ctx", "head")),
        check_vma=False,
    )
```

```python
import functools
import math

import jax
import jax.numpy as jnp
from jax import lax
from jax.experimental import pallas as pl
from jax.experimental.pallas import tpu as pltpu
from jax.sharding import PartitionSpec as P

HD = 128
TILE = 128


epsilon = 1e-06


def split_heads(array, heads_dev):
    return array.reshape(array.shape[0], heads_dev, HD).transpose(1, 0, 2)


def merge_heads(array):
    heads_dev, tok_dev, depth = array.shape
    return array.transpose(1, 0, 2).reshape(tok_dev, heads_dev * depth)


def per_tile(array, qt_dev):
    heads_dev, tok_dev, depth = array.shape
    return array.reshape(heads_dev, qt_dev, TILE, depth).transpose(1, 0, 2, 3)


def from_tiles(array):
    qt_dev, heads_dev, rows_tile, depth = array.shape
    return array.transpose(1, 0, 2, 3).reshape(heads_dev, qt_dev * rows_tile, depth)


def table_sum(taken, pieces, heads_dev, qt_dev):
    flat_pieces = pieces.reshape(pieces.shape[0], -1)
    summed = jnp.dot(
        taken, flat_pieces, precision=lax.Precision.HIGHEST, preferred_element_type=jnp.float32
    )
    summed = summed.reshape(heads_dev, qt_dev, 2, TILE, HD).transpose(2, 0, 1, 3, 4)
    return summed.reshape(2, heads_dev, qt_dev * TILE, HD)


def rounded(array):
    return array.astype(jnp.bfloat16)


def finish_norm(wide, scale, gain, grad, dot_sum, width_all):
    return (scale * gain * grad - wide * scale**3 * (dot_sum / width_all)[:, None]).astype(
        jnp.bfloat16
    )


def tiles_to_queries(q_pre, k_pre, values, out_grad, q_gain, k_gain, selected):
    n_ctx = lax.axis_size("ctx")
    tok_dev, width_dev = q_pre.shape
    width_all = width_dev * lax.axis_size("head")
    heads_dev = width_dev // HD
    qt_dev = tok_dev // TILE
    remote_count = selected.shape[2]
    factor = 1.0 / math.sqrt(HD)
    q_wide = q_pre.astype(jnp.float32)
    k_wide = k_pre.astype(jnp.float32)
    q_square, k_square = lax.psum(
        (jnp.sum(q_wide * q_wide, axis=1), jnp.sum(k_wide * k_wide, axis=1)), "head"
    )
    q_scale = lax.rsqrt(q_square / width_all + epsilon)[:, None]
    k_scale = lax.rsqrt(k_square / width_all + epsilon)[:, None]
    q_heads = split_heads(rounded(q_wide * q_scale * q_gain), heads_dev)
    k_heads = split_heads(rounded(k_wide * k_scale * k_gain), heads_dev)
    v_heads = split_heads(values, heads_dev)
    g_heads = split_heads(out_grad, heads_dev)
    q_tiles = per_tile(q_heads, qt_dev)
    g_tiles = per_tile(g_heads, qt_dev)
    k_table = k_heads.reshape(heads_dev * qt_dev, TILE, HD)
    v_table = v_heads.reshape(heads_dev * qt_dev, TILE, HD)
    flat_sel = selected[0].reshape(-1)
    n_slot = flat_sel.shape[0]
    capacity = -(-n_slot // (n_ctx - 1))
    n_buffer = n_ctx * capacity
    owners = flat_sel // qt_dev
    head_of = jnp.arange(n_slot, dtype=jnp.int32) // remote_count
    codes = head_of * qt_dev + flat_sel % qt_dev
    matches = (owners[:, None] == jnp.arange(n_ctx, dtype=jnp.int32)[None, :]).astype(jnp.int32)
    ranks = jnp.sum((jnp.cumsum(matches, axis=0) - matches) * matches, axis=1)
    position = owners * capacity + ranks
    placed = position[None, :] == jnp.arange(n_buffer, dtype=jnp.int32)[:, None]
    request = jnp.sum(jnp.where(placed, codes[None, :] + 1, 0), axis=1) - 1
    asked = lax.all_to_all(
        request.reshape(n_ctx, capacity), "ctx", split_axis=0, concat_axis=0, tiled=True
    ).reshape(n_buffer)
    clipped = jnp.maximum(asked, 0)
    taken = (asked[None, :] == jnp.arange(heads_dev * qt_dev, dtype=jnp.int32)[:, None]).astype(
        jnp.float32
    )
    s_near = (
        jnp.einsum("rhqd,hkd->rhqk", q_tiles, k_heads, preferred_element_type=jnp.float32) * factor
    )
    dp_near = jnp.einsum("rhqd,hkd->rhqk", g_tiles, v_heads, preferred_element_type=jnp.float32)
    near_top = jnp.max(s_near, axis=-1)
    outgoing = jnp.stack((k_table[clipped], v_table[clipped]), axis=1).reshape(
        n_ctx, capacity, 2, TILE, HD
    )
    incoming = lax.all_to_all(outgoing, "ctx", split_axis=0, concat_axis=0, tiled=True).reshape(
        n_buffer, 2, TILE, HD
    )
    slot_kv = incoming[position].reshape(heads_dev, remote_count, 2, TILE, HD)
    far_k = slot_kv[:, :, 0]
    far_v = slot_kv[:, :, 1]
    s_far = (
        jnp.einsum("rhqd,hckd->rhqck", q_tiles, far_k, preferred_element_type=jnp.float32) * factor
    )
    dp_far = jnp.einsum("rhqd,hckd->rhqck", g_tiles, far_v, preferred_element_type=jnp.float32)
    row_top = jnp.maximum(near_top, jnp.max(s_far, axis=(-2, -1)))
    totals = jnp.sum(jnp.exp(s_near - row_top[..., None]), axis=-1) + jnp.sum(
        jnp.exp(s_far - row_top[..., None, None]), axis=(-2, -1)
    )
    lse = row_top + jnp.log(totals)
    p_near = jnp.exp(s_near - lse[..., None])
    p_far = jnp.exp(s_far - lse[..., None, None])
    delta = jnp.sum(p_near * dp_near, axis=-1) + jnp.sum(p_far * dp_far, axis=(-2, -1))
    ds_near = rounded(p_near * (dp_near - delta[..., None]) * factor)
    pb_near = rounded(p_near)
    dq_near = jnp.einsum("rhqk,hkd->rhqd", ds_near, k_heads, preferred_element_type=jnp.float32)
    dk_near = jnp.einsum("rhqk,rhqd->hkd", ds_near, q_tiles, preferred_element_type=jnp.float32)
    dv_near = jnp.einsum("rhqk,rhqd->hkd", pb_near, g_tiles, preferred_element_type=jnp.float32)
    dq_near, dk_near, dv_near = (dq_near, dk_near, dv_near)
    ds_far = rounded(p_far * (dp_far - delta[..., None, None]) * factor)
    pb_far = rounded(p_far)
    dq_far = jnp.einsum("rhqck,hckd->rhqd", ds_far, far_k, preferred_element_type=jnp.float32)
    dq_wide = merge_heads(from_tiles(dq_near + dq_far))
    q_dot = jnp.sum(q_gain * dq_wide * q_wide, axis=1)
    dq_wide, q_dot = (dq_wide, q_dot)
    dk_far = jnp.einsum("rhqck,rhqd->hckd", ds_far, q_tiles, preferred_element_type=jnp.float32)
    dv_far = jnp.einsum("rhqck,rhqd->hckd", pb_far, g_tiles, preferred_element_type=jnp.float32)
    grads = jnp.stack((dk_far, dv_far), axis=2).reshape(n_slot, 2, TILE, HD)
    sending = jnp.zeros((n_buffer, 2, TILE, HD), jnp.float32).at[position].set(grads)
    returned = lax.all_to_all(
        sending.reshape(n_ctx, capacity, 2, TILE, HD),
        "ctx",
        split_axis=0,
        concat_axis=0,
        tiled=True,
    ).reshape(n_buffer, 2, TILE, HD)
    far_sums = table_sum(taken, returned, heads_dev, qt_dev)
    dk_wide = merge_heads(dk_near + far_sums[0])
    dv_heads = dv_near + far_sums[1]
    k_dot = jnp.sum(k_gain * dk_wide * k_wide, axis=1)
    q_dot, k_dot = lax.psum((q_dot, k_dot), "head")
    dq_result = finish_norm(q_wide, q_scale, q_gain, dq_wide, q_dot, width_all)
    dk_result = finish_norm(k_wide, k_scale, k_gain, dk_wide, k_dot, width_all)
    return (dq_result, dk_result, merge_heads(dv_heads).astype(jnp.bfloat16))


VMEM_BYTES = 48 * 2**20
PIECES = 4
STRIP = 64
IN_VMEM = pl.BlockSpec(memory_space=pltpu.VMEM)
IN_SMEM = pl.BlockSpec(memory_space=pltpu.SMEM)


def owners_of(group, n_ctx, heads_dev):
    places = [(4 * head + 1) * n_ctx // (4 * heads_dev) for head in range(heads_dev)]
    return [n_ctx - 1 - place if group % 2 else place for place in places]


def head_at(place, group, n_ctx, heads_dev):
    even = jnp.where(group % 2 == 1, n_ctx - 1 - place, place)
    head = -1
    for index, owner in enumerate(owners_of(0, n_ctx, heads_dev)):
        head = jnp.where(even == owner, index, head)
    return head


def pairs_to_owner(mask, n_ctx, n_head, heads_dev):
    pairs = []
    for group in range(n_head):
        owners = owners_of(group, n_ctx, heads_dev)
        for block in range(n_ctx):
            if block ^ mask in owners:
                pairs.append((block * n_head + group, (block ^ mask) * n_head + group))
    return pairs


def there_masks(n_ctx):
    return list(range(n_ctx - 1, -1, -1))


def back_masks(n_ctx):
    return list(range(n_ctx // 2 - 1, 0, -1)) + list(range(n_ctx - 1, n_ctx // 2 - 1, -1)) + [0]


def move(masks, arrays, back, n_ctx, n_head, heads_dev):
    moved = []
    for mask, array in zip(masks, arrays):
        pairs = pairs_to_owner(mask, n_ctx, n_head, heads_dev)
        if back:
            pairs = [(b, a) for a, b in pairs]
        moved.append(lax.ppermute(array, ("ctx", "head"), pairs) if mask else array)
    return moved


def column(row, width):
    return jnp.broadcast_to(row, (width, row.shape[1])).T


def row_sums(wide):
    total = wide[:, :HD]
    for at in range(HD, wide.shape[1], HD):
        total = total + wide[:, at : at + HD]
    return jnp.sum(total.T, axis=0, keepdims=True)


def pack_kernel(n_ctx, heads_dev, *refs):
    inputs, square_ref, outs = refs[:4], refs[4], refs[5 : 5 + n_ctx]
    held, sems = refs[5 + n_ctx :]
    rows = held.shape[1]
    piece = rows // PIECES
    block, group = lax.axis_index("ctx"), lax.axis_index("head")

    def copy(at, part):
        place = pl.ds(part * piece, piece)
        return pltpu.make_async_copy(
            inputs[at].at[place, :], held.at[at, place, :], sems.at[at, part]
        )

    for at in range(4):
        for part in range(PIECES):
            copy(at, part).start()
    for at in range(4):
        for part in range(PIECES):
            copy(at, part).wait()
    for mask, out in zip(there_masks(n_ctx), outs):
        head = head_at(block ^ mask, group, n_ctx, heads_dev)

        @pl.when(head >= 0)
        def _(head=head, out=out):
            place = pl.ds(pl.multiple_of(head * HD, HD), HD)
            for at in range(4):
                out[at] = held[at, :, place]

    for at in range(2):
        wide = held[at].astype(jnp.float32)
        square_ref[at : at + 1, :] = row_sums(wide * wide)


def pack(arrays, n_ctx):
    rows, width_dev = arrays[0].shape
    result = pl.pallas_call(
        functools.partial(pack_kernel, n_ctx, width_dev // HD),
        out_shape=[jax.ShapeDtypeStruct((2, rows), jnp.float32)]
        + [jax.ShapeDtypeStruct((4, rows, HD), jnp.bfloat16)] * n_ctx,
        in_specs=[pl.BlockSpec(memory_space=pltpu.HBM)] * 4,
        out_specs=[IN_VMEM] * (n_ctx + 1),
        scratch_shapes=[
            pltpu.VMEM((4, rows, width_dev), jnp.bfloat16),
            pltpu.SemaphoreType.DMA((4, PIECES)),
        ],
        compiler_params=pltpu.CompilerParams(vmem_limit_bytes=VMEM_BYTES),
    )(*[pltpu.with_memory_space_constraint(array, pltpu.HBM) for array in arrays])
    return result[0], result[1:]


def attend_kernel(n_ctx, heads_dev, picks, scale_ref, q_gain, k_gain, *refs):
    messages = dict(zip(there_masks(n_ctx), refs[:n_ctx]))
    outs = dict(zip(back_masks(n_ctx), refs[n_ctx : 2 * n_ctx]))
    scratch = refs[2 * n_ctx :]
    q_ref, qt_ref, g_ref, gt_ref, k_ref, kt_ref, v_ref = scratch[:7]
    dq_ref, dk_ref, dv_ref, kt_picked, k_picked, v_picked = scratch[7:13]
    buffers = (scratch[13:18], scratch[18:23])
    rows = messages[0].shape[1]
    remote_count = picks.shape[1]
    near = rows // TILE
    n_keys = near + remote_count
    n_strips = n_keys * TILE // STRIP
    factor = 1.0 / math.sqrt(HD)
    to_base2 = factor * math.log2(math.e)
    own_block = lax.axis_index("ctx")
    own_head = head_at(own_block, lax.axis_index("head"), n_ctx, heads_dev)

    def rows_of(block):
        return pl.ds(pl.multiple_of(block * rows, rows), rows)

    def places_of(block):
        return [
            pl.ds(pl.multiple_of(block * rows + tile * TILE, TILE), TILE) for tile in range(near)
        ] + [
            pl.ds(pl.multiple_of(picks[block, slot] * TILE, TILE), TILE)
            for slot in range(remote_count)
        ]

    def prepare(mask, q_factor, k_factor):
        message = messages[mask]
        block = own_block ^ mask
        place = rows_of(block)
        q_t = message[0].T.astype(jnp.float32) * scale_ref[block, 0:1, :] * q_factor
        k_t = message[1].T.astype(jnp.float32) * scale_ref[block, 1:2, :] * k_factor
        qt_ref[mask] = q_t.astype(jnp.bfloat16)
        kt_ref[:, place] = k_t.astype(jnp.bfloat16)
        q_ref[mask] = q_t.astype(jnp.bfloat16).T
        k_ref[place, :] = k_t.astype(jnp.bfloat16).T
        v_ref[place, :] = message[2]
        g_ref[mask] = message[3]
        gt_ref[mask] = message[3].T

    def tiles(first, count=1):
        return slice(first * TILE, (first + count) * TILE)

    def scores(mask, group, places, buffer):
        weight_ref, dprob_ref, stat_ref = buffer[:3]
        for slot in group:
            k_picked[tiles(slot), :] = k_ref[places[slot], :]
            v_picked[tiles(slot), :] = v_ref[places[slot], :]
        picked = tiles(group[0], len(group))
        score_all = jnp.dot(
            k_picked[picked, :], qt_ref[mask], preferred_element_type=jnp.float32
        )
        dprob_all = jnp.dot(
            v_picked[picked, :], gt_ref[mask], preferred_element_type=jnp.float32
        )
        for at in range(len(group) * TILE // STRIP):
            strip = group[0] * TILE // STRIP + at
            part = slice(at * STRIP, (at + 1) * STRIP)
            score = score_all[part, :]
            dprob = dprob_all[part, :]
            top = jnp.max(score, axis=0, keepdims=True)
            weight = jnp.exp2((score - top) * to_base2)
            weight_ref[strip] = weight
            dprob_ref[strip] = dprob
            stat_ref[0, strip : strip + 1, :] = top * to_base2
            stat_ref[1, strip : strip + 1, :] = jnp.sum(weight, axis=0, keepdims=True)
            stat_ref[2, strip : strip + 1, :] = jnp.sum(weight * dprob, axis=0, keepdims=True)

    def settle(buffer):
        stat_ref = buffer[2]
        tops = stat_ref[0, :n_strips, :]
        shares = jnp.exp2(tops - jnp.max(tops, axis=0, keepdims=True))
        total = jnp.sum(shares * stat_ref[1, :n_strips, :], axis=0, keepdims=True)
        mixed = jnp.sum(shares * stat_ref[2, :n_strips, :], axis=0, keepdims=True)
        inverse = 1.0 / total
        return shares * inverse, mixed * inverse

    def gradients(group, buffer, shares, delta):
        weight_ref, dprob_ref, _, ds_ref, pb_ref = buffer
        for strip in range(group[0] * TILE // STRIP, (group[-1] + 1) * TILE // STRIP):
            part = slice(strip * STRIP, (strip + 1) * STRIP)
            prob = weight_ref[strip] * shares[strip : strip + 1, :]
            pb_ref[part, :] = prob.astype(jnp.bfloat16)
            ds_ref[part, :] = (prob * (dprob_ref[strip] - delta)).astype(jnp.bfloat16)

    def products(mask, group, places, buffer):
        ds_ref, pb_ref = buffer[3:]
        picked = tiles(group[0], len(group))
        dk = jnp.dot(ds_ref[picked, :], q_ref[mask], preferred_element_type=jnp.float32)
        dv = jnp.dot(pb_ref[picked, :], g_ref[mask], preferred_element_type=jnp.float32)
        for at, slot in enumerate(group):
            dk_ref[places[slot], :] += dk[tiles(at), :]
            dv_ref[places[slot], :] += dv[tiles(at), :]
            kt_picked[:, tiles(slot)] = kt_ref[:, places[slot]]

    def query_gradient(mask, buffer):
        dq_t = jnp.dot(kt_picked[...], buffer[3][...], preferred_element_type=jnp.float32)
        dq_ref[mask] = (dq_t * factor).T.astype(jnp.bfloat16)

    groups = [range(first, min(first + 3, n_keys)) for first in range(0, n_keys, 3)]

    def step(now, before, after):
        if now is not None:
            shares, delta = settle(now[1])
        if before is not None:
            before_places = places_of(own_block ^ before[0])
        if after is not None:
            after_places = places_of(own_block ^ after[0])
        for group in groups:
            if before is not None:
                products(before[0], group, before_places, before[1])
            if now is not None:
                gradients(group, now[1], shares, delta)
            if after is not None:
                scores(after[0], group, after_places, after[1])
        if before is not None:
            query_gradient(*before)

    @pl.when(own_head >= 0)
    def _():
        q_factor = column(q_gain[pl.ds(own_head, 1), :], rows)
        k_factor = column(k_gain[pl.ds(own_head, 1), :], rows)
        for mask in range(n_ctx):
            prepare(mask, q_factor, k_factor)
        dk_ref[...] = jnp.zeros_like(dk_ref)
        dv_ref[...] = jnp.zeros_like(dv_ref)
        even, odd = buffers
        step(None, None, (0, even))
        step((0, even), None, (1, odd))

        def two(pair, carry):
            mask = 2 * pair
            step((mask + 1, odd), (mask, even), (mask + 2, even))
            step((mask + 2, even), (mask + 1, odd), (mask + 3, odd))
            return carry

        lax.fori_loop(0, n_ctx // 2 - 1, two, 0)
        step((n_ctx - 1, odd), (n_ctx - 2, even), None)
        step(None, (n_ctx - 1, odd), None)
        for mask in range(n_ctx):
            place = rows_of(own_block ^ mask)
            outs[mask][0] = dq_ref[mask]
            outs[mask][1] = (dk_ref[place, :] * factor).astype(jnp.bfloat16)
            outs[mask][2] = dv_ref[place, :].astype(jnp.bfloat16)


def attend(picks, scales, q_gain, k_gain, messages, n_ctx):
    rows = messages[0].shape[1]
    tokens = n_ctx * rows
    n_keys = rows // TILE + picks.shape[1]
    n_strips = n_keys * TILE // STRIP
    by_block = pltpu.VMEM((n_ctx, rows, HD), jnp.bfloat16)
    by_block_t = pltpu.VMEM((n_ctx, HD, rows), jnp.bfloat16)
    buffer = [
        pltpu.VMEM((n_strips, STRIP, rows), jnp.float32),
        pltpu.VMEM((n_strips, STRIP, rows), jnp.float32),
        pltpu.VMEM((3, -(-n_strips // 8) * 8, rows), jnp.float32),
        pltpu.VMEM((n_keys * TILE, rows), jnp.bfloat16),
        pltpu.VMEM((n_keys * TILE, rows), jnp.bfloat16),
    ]
    return pl.pallas_call(
        functools.partial(attend_kernel, n_ctx, q_gain.shape[0]),
        out_shape=[jax.ShapeDtypeStruct((3, rows, HD), jnp.bfloat16)] * n_ctx,
        in_specs=[IN_SMEM] + [IN_VMEM] * (3 + n_ctx),
        out_specs=[IN_VMEM] * n_ctx,
        scratch_shapes=[
            by_block,
            by_block_t,
            by_block,
            by_block_t,
            pltpu.VMEM((tokens, HD), jnp.bfloat16),
            pltpu.VMEM((HD, tokens), jnp.bfloat16),
            pltpu.VMEM((tokens, HD), jnp.bfloat16),
            by_block,
            pltpu.VMEM((tokens, HD), jnp.float32),
            pltpu.VMEM((tokens, HD), jnp.float32),
            pltpu.VMEM((HD, n_keys * TILE), jnp.bfloat16),
            pltpu.VMEM((n_keys * TILE, HD), jnp.bfloat16),
            pltpu.VMEM((n_keys * TILE, HD), jnp.bfloat16),
        ]
        + buffer
        + buffer,
        compiler_params=pltpu.CompilerParams(vmem_limit_bytes=VMEM_BYTES),
    )(picks, scales, q_gain, k_gain, *messages)


def gather_kernel(n_ctx, heads_dev, q_ref, k_ref, q_gain, k_gain, *refs):
    slots = refs[:n_ctx]
    dot_ref, dq_ref, dk_ref, dv_out, dv_ref, sems = refs[n_ctx:]
    piece = dv_ref.shape[0] // PIECES
    block, group = lax.axis_index("ctx"), lax.axis_index("head")

    def spread(at, out):
        for mask, slot in zip(back_masks(n_ctx), slots):
            head = head_at(block ^ mask, group, n_ctx, heads_dev)

            @pl.when(head >= 0)
            def _(head=head, slot=slot):
                place = pl.ds(pl.multiple_of(head * HD, HD), HD)
                out[:, place] = slot[at]

    spread(2, dv_ref)
    places = [pl.ds(part * piece, piece) for part in range(PIECES)]
    copies = [
        pltpu.make_async_copy(dv_ref.at[place, :], dv_out.at[place, :], sems.at[part])
        for part, place in enumerate(places)
    ]
    for copy in copies:
        copy.start()
    for at, (wide_ref, pre_ref, gain) in enumerate(
        ((dq_ref, q_ref, q_gain), (dk_ref, k_ref, k_gain))
    ):
        spread(at, wide_ref)
        terms = gain[...] * wide_ref[...].astype(jnp.float32) * pre_ref[...].astype(jnp.float32)
        dot_ref[at : at + 1, :] = row_sums(terms)
    for copy in copies:
        copy.wait()


def finish_kernel(width_all, q_ref, k_ref, q_gain, k_gain, scale_ref, dot_ref, *refs):
    dq_ref, dk_ref, dq_out, dk_out, held, sems = refs
    piece = q_ref.shape[0] // PIECES
    scales = scale_ref[lax.axis_index("ctx")]
    backs = scales**3 * (dot_ref[...] / width_all)
    copies = []
    for at, (pre_ref, gain, grad_ref, out) in enumerate(
        ((q_ref, q_gain, dq_ref, dq_out), (k_ref, k_gain, dk_ref, dk_out))
    ):
        scale_all = column(scales[at : at + 1, :], HD)
        back_all = column(backs[at : at + 1, :], HD)
        for part in range(PIECES):
            rows = slice(part * piece, (part + 1) * piece)
            scale, back = scale_all[rows, :], back_all[rows, :]
            for first in range(0, pre_ref.shape[1], HD):
                place = slice(first, first + HD)
                wide = pre_ref[rows, place].astype(jnp.float32)
                grad = grad_ref[rows, place].astype(jnp.float32)
                result = scale * gain[:, place] * grad - wide * back
                held[at, rows, place] = result.astype(jnp.bfloat16)
            copies.append(
                pltpu.make_async_copy(held.at[at, rows, :], out.at[rows, :], sems.at[at, part])
            )
            copies[-1].start()
    for copy in copies:
        copy.wait()


def heads_to_owners(q_pre, k_pre, values, out_grad, q_gain, k_gain, selected):
    n_ctx = lax.axis_size("ctx")
    n_head = lax.axis_size("head")
    rows, width_dev = q_pre.shape
    width_all = width_dev * n_head
    heads_dev = width_dev // HD
    remote_count = selected.shape[2]
    sizes = (n_ctx, n_head, heads_dev)
    params = pltpu.CompilerParams(vmem_limit_bytes=VMEM_BYTES)

    by_row = jax.ShapeDtypeStruct((2, rows), jnp.float32)
    wide = jax.ShapeDtypeStruct((rows, width_dev), jnp.bfloat16)

    squares, sent = pack((q_pre, k_pre, values, out_grad), n_ctx)
    messages = move(there_masks(n_ctx), sent, False, *sizes)

    wishes = selected[0].reshape(1, -1).astype(jnp.float32)
    wishes = jnp.pad(wishes, ((0, 0), (0, rows - wishes.shape[1])))
    small = jnp.concatenate((lax.psum(squares, "head"), wishes), axis=0)
    small = jnp.broadcast_to(small[None], (n_ctx,) + small.shape)
    small = lax.all_to_all(small, "ctx", split_axis=0, concat_axis=0, tiled=True)
    scales = lax.rsqrt(small[:, :2] / width_all + epsilon)
    own_head = head_at(lax.axis_index("ctx"), lax.axis_index("head"), n_ctx, heads_dev)
    first = jnp.maximum(own_head, 0) * remote_count
    picks = lax.dynamic_slice_in_dim(small[:, 2], first, remote_count, 1).astype(jnp.int32)

    q_gains = q_gain.reshape(heads_dev, HD)
    k_gains = k_gain.reshape(heads_dev, HD)
    results = attend(picks, scales, q_gains, k_gains, messages, n_ctx)
    slots = move(back_masks(n_ctx), results, True, *sizes)

    pres = (q_pre, k_pre, q_gain[None], k_gain[None])
    dots, dq_wide, dk_wide, dv = pl.pallas_call(
        functools.partial(gather_kernel, n_ctx, heads_dev),
        out_shape=[by_row, wide, wide, wide],
        in_specs=[IN_VMEM] * (4 + n_ctx),
        out_specs=[IN_VMEM] * 3 + [pl.BlockSpec(memory_space=pltpu.HBM)],
        scratch_shapes=[
            pltpu.VMEM((rows, width_dev), jnp.bfloat16),
            pltpu.SemaphoreType.DMA((PIECES,)),
        ],
        compiler_params=params,
    )(*pres, *slots)
    dots = lax.psum(dots, "head")
    dq, dk = pl.pallas_call(
        functools.partial(finish_kernel, width_all),
        out_shape=[wide, wide],
        in_specs=[IN_VMEM] * 8,
        out_specs=[pl.BlockSpec(memory_space=pltpu.HBM)] * 2,
        scratch_shapes=[
            pltpu.VMEM((2, rows, width_dev), jnp.bfloat16),
            pltpu.SemaphoreType.DMA((2, PIECES)),
        ],
        compiler_params=params,
    )(*pres, scales, dots, dq_wide, dk_wide)
    return dq, dk, dv


def on_device(q_pre, k_pre, values, out_grad, q_gain, k_gain, selected):
    n_ctx = lax.axis_size("ctx")
    tiles_dev, heads_dev, remote_count = selected.shape
    capacity = -(-heads_dev * remote_count // (n_ctx - 1))
    by_head = (n_ctx - 1) * tiles_dev * 7
    by_tile = (n_ctx - 1) * capacity * 6
    paired = n_ctx & (n_ctx - 1) == 0 and n_ctx >= max(heads_dev, 4)
    plan = heads_to_owners if paired and by_head <= by_tile else tiles_to_queries
    return plan(q_pre, k_pre, values, out_grad, q_gain, k_gain, selected)


def solution(mesh):
    placed = (
        P("ctx", "head"),
        P("ctx", "head"),
        P("ctx", "head"),
        P("ctx", "head"),
        P("head"),
        P("head"),
        P("ctx", "head", None),
    )
    return jax.shard_map(
        on_device,
        mesh=mesh,
        in_specs=placed,
        out_specs=(P("ctx", "head"), P("ctx", "head"), P("ctx", "head")),
        check_vma=False,
    )
```

```python
import functools
import math

import jax
import jax.numpy as jnp
from jax import lax
from jax.experimental import pallas as pl
from jax.experimental.pallas import tpu as pltpu
from jax.sharding import PartitionSpec as P

HD = 128
TILE = 128


epsilon = 1e-06


def split_heads(array, heads_dev):
    return array.reshape(array.shape[0], heads_dev, HD).transpose(1, 0, 2)


def merge_heads(array):
    heads_dev, tok_dev, depth = array.shape
    return array.transpose(1, 0, 2).reshape(tok_dev, heads_dev * depth)


def per_tile(array, qt_dev):
    heads_dev, tok_dev, depth = array.shape
    return array.reshape(heads_dev, qt_dev, TILE, depth).transpose(1, 0, 2, 3)


def from_tiles(array):
    qt_dev, heads_dev, rows_tile, depth = array.shape
    return array.transpose(1, 0, 2, 3).reshape(heads_dev, qt_dev * rows_tile, depth)


def table_sum(taken, pieces, heads_dev, qt_dev):
    flat_pieces = pieces.reshape(pieces.shape[0], -1)
    summed = jnp.dot(
        taken, flat_pieces, precision=lax.Precision.HIGHEST, preferred_element_type=jnp.float32
    )
    summed = summed.reshape(heads_dev, qt_dev, 2, TILE, HD).transpose(2, 0, 1, 3, 4)
    return summed.reshape(2, heads_dev, qt_dev * TILE, HD)


def rounded(array):
    return array.astype(jnp.bfloat16)


def finish_norm(wide, scale, gain, grad, dot_sum, width_all):
    return (scale * gain * grad - wide * scale**3 * (dot_sum / width_all)[:, None]).astype(
        jnp.bfloat16
    )


def tiles_to_queries(q_pre, k_pre, values, out_grad, q_gain, k_gain, selected):
    n_ctx = lax.axis_size("ctx")
    tok_dev, width_dev = q_pre.shape
    width_all = width_dev * lax.axis_size("head")
    heads_dev = width_dev // HD
    qt_dev = tok_dev // TILE
    remote_count = selected.shape[2]
    factor = 1.0 / math.sqrt(HD)
    q_wide = q_pre.astype(jnp.float32)
    k_wide = k_pre.astype(jnp.float32)
    q_square, k_square = lax.psum(
        (jnp.sum(q_wide * q_wide, axis=1), jnp.sum(k_wide * k_wide, axis=1)), "head"
    )
    q_scale = lax.rsqrt(q_square / width_all + epsilon)[:, None]
    k_scale = lax.rsqrt(k_square / width_all + epsilon)[:, None]
    q_heads = split_heads(rounded(q_wide * q_scale * q_gain), heads_dev)
    k_heads = split_heads(rounded(k_wide * k_scale * k_gain), heads_dev)
    v_heads = split_heads(values, heads_dev)
    g_heads = split_heads(out_grad, heads_dev)
    q_tiles = per_tile(q_heads, qt_dev)
    g_tiles = per_tile(g_heads, qt_dev)
    k_table = k_heads.reshape(heads_dev * qt_dev, TILE, HD)
    v_table = v_heads.reshape(heads_dev * qt_dev, TILE, HD)
    flat_sel = selected[0].reshape(-1)
    n_slot = flat_sel.shape[0]
    capacity = -(-n_slot // (n_ctx - 1))
    n_buffer = n_ctx * capacity
    owners = flat_sel // qt_dev
    head_of = jnp.arange(n_slot, dtype=jnp.int32) // remote_count
    codes = head_of * qt_dev + flat_sel % qt_dev
    matches = (owners[:, None] == jnp.arange(n_ctx, dtype=jnp.int32)[None, :]).astype(jnp.int32)
    ranks = jnp.sum((jnp.cumsum(matches, axis=0) - matches) * matches, axis=1)
    position = owners * capacity + ranks
    placed = position[None, :] == jnp.arange(n_buffer, dtype=jnp.int32)[:, None]
    request = jnp.sum(jnp.where(placed, codes[None, :] + 1, 0), axis=1) - 1
    asked = lax.all_to_all(
        request.reshape(n_ctx, capacity), "ctx", split_axis=0, concat_axis=0, tiled=True
    ).reshape(n_buffer)
    clipped = jnp.maximum(asked, 0)
    taken = (asked[None, :] == jnp.arange(heads_dev * qt_dev, dtype=jnp.int32)[:, None]).astype(
        jnp.float32
    )
    s_near = (
        jnp.einsum("rhqd,hkd->rhqk", q_tiles, k_heads, preferred_element_type=jnp.float32) * factor
    )
    dp_near = jnp.einsum("rhqd,hkd->rhqk", g_tiles, v_heads, preferred_element_type=jnp.float32)
    near_top = jnp.max(s_near, axis=-1)
    outgoing = jnp.stack((k_table[clipped], v_table[clipped]), axis=1).reshape(
        n_ctx, capacity, 2, TILE, HD
    )
    incoming = lax.all_to_all(outgoing, "ctx", split_axis=0, concat_axis=0, tiled=True).reshape(
        n_buffer, 2, TILE, HD
    )
    slot_kv = incoming[position].reshape(heads_dev, remote_count, 2, TILE, HD)
    far_k = slot_kv[:, :, 0]
    far_v = slot_kv[:, :, 1]
    s_far = (
        jnp.einsum("rhqd,hckd->rhqck", q_tiles, far_k, preferred_element_type=jnp.float32) * factor
    )
    dp_far = jnp.einsum("rhqd,hckd->rhqck", g_tiles, far_v, preferred_element_type=jnp.float32)
    row_top = jnp.maximum(near_top, jnp.max(s_far, axis=(-2, -1)))
    totals = jnp.sum(jnp.exp(s_near - row_top[..., None]), axis=-1) + jnp.sum(
        jnp.exp(s_far - row_top[..., None, None]), axis=(-2, -1)
    )
    lse = row_top + jnp.log(totals)
    p_near = jnp.exp(s_near - lse[..., None])
    p_far = jnp.exp(s_far - lse[..., None, None])
    delta = jnp.sum(p_near * dp_near, axis=-1) + jnp.sum(p_far * dp_far, axis=(-2, -1))
    ds_near = rounded(p_near * (dp_near - delta[..., None]) * factor)
    pb_near = rounded(p_near)
    dq_near = jnp.einsum("rhqk,hkd->rhqd", ds_near, k_heads, preferred_element_type=jnp.float32)
    dk_near = jnp.einsum("rhqk,rhqd->hkd", ds_near, q_tiles, preferred_element_type=jnp.float32)
    dv_near = jnp.einsum("rhqk,rhqd->hkd", pb_near, g_tiles, preferred_element_type=jnp.float32)
    dq_near, dk_near, dv_near = (dq_near, dk_near, dv_near)
    ds_far = rounded(p_far * (dp_far - delta[..., None, None]) * factor)
    pb_far = rounded(p_far)
    dq_far = jnp.einsum("rhqck,hckd->rhqd", ds_far, far_k, preferred_element_type=jnp.float32)
    dq_wide = merge_heads(from_tiles(dq_near + dq_far))
    q_dot = jnp.sum(q_gain * dq_wide * q_wide, axis=1)
    dq_wide, q_dot = (dq_wide, q_dot)
    dk_far = jnp.einsum("rhqck,rhqd->hckd", ds_far, q_tiles, preferred_element_type=jnp.float32)
    dv_far = jnp.einsum("rhqck,rhqd->hckd", pb_far, g_tiles, preferred_element_type=jnp.float32)
    grads = jnp.stack((dk_far, dv_far), axis=2).reshape(n_slot, 2, TILE, HD)
    sending = jnp.zeros((n_buffer, 2, TILE, HD), jnp.float32).at[position].set(grads)
    returned = lax.all_to_all(
        sending.reshape(n_ctx, capacity, 2, TILE, HD),
        "ctx",
        split_axis=0,
        concat_axis=0,
        tiled=True,
    ).reshape(n_buffer, 2, TILE, HD)
    far_sums = table_sum(taken, returned, heads_dev, qt_dev)
    dk_wide = merge_heads(dk_near + far_sums[0])
    dv_heads = dv_near + far_sums[1]
    k_dot = jnp.sum(k_gain * dk_wide * k_wide, axis=1)
    q_dot, k_dot = lax.psum((q_dot, k_dot), "head")
    dq_result = finish_norm(q_wide, q_scale, q_gain, dq_wide, q_dot, width_all)
    dk_result = finish_norm(k_wide, k_scale, k_gain, dk_wide, k_dot, width_all)
    return (dq_result, dk_result, merge_heads(dv_heads).astype(jnp.bfloat16))


VMEM_BYTES = 48 * 2**20
PIECES = 4
STRIP = 64
NT = (((1,), (1,)), ((), ()))
TN = (((0,), (0,)), ((), ()))
IN_VMEM = pl.BlockSpec(memory_space=pltpu.VMEM)
IN_SMEM = pl.BlockSpec(memory_space=pltpu.SMEM)


def owners_of(group, n_ctx, heads_dev):
    places = [(4 * head + 1) * n_ctx // (4 * heads_dev) for head in range(heads_dev)]
    return [n_ctx - 1 - place if group % 2 else place for place in places]


def head_at(place, group, n_ctx, heads_dev):
    even = jnp.where(group % 2 == 1, n_ctx - 1 - place, place)
    head = -1
    for index, owner in enumerate(owners_of(0, n_ctx, heads_dev)):
        head = jnp.where(even == owner, index, head)
    return head


def pairs_to_owner(mask, n_ctx, n_head, heads_dev):
    pairs = []
    for group in range(n_head):
        owners = owners_of(group, n_ctx, heads_dev)
        for block in range(n_ctx):
            if block ^ mask in owners:
                pairs.append((block * n_head + group, (block ^ mask) * n_head + group))
    return pairs


def there_masks(n_ctx):
    return list(range(n_ctx - 1, -1, -1))


def back_masks(n_ctx):
    return list(range(n_ctx // 2 - 1, 0, -1)) + list(range(n_ctx - 1, n_ctx // 2 - 1, -1)) + [0]


def move(masks, arrays, back, n_ctx, n_head, heads_dev):
    moved = []
    for mask, array in zip(masks, arrays):
        pairs = pairs_to_owner(mask, n_ctx, n_head, heads_dev)
        if back:
            pairs = [(b, a) for a, b in pairs]
        moved.append(lax.ppermute(array, ("ctx", "head"), pairs) if mask else array)
    return moved


def column(row, width):
    high = row.astype(jnp.bfloat16).astype(jnp.float32)
    middle = (row - high).astype(jnp.bfloat16).astype(jnp.float32)
    part = lax.broadcasted_iota(jnp.int32, (8, row.shape[1]), 0)
    parts = jnp.where(part == 2, row - high - middle, 0.0)
    parts = jnp.where(part == 1, middle, parts)
    parts = jnp.where(part == 0, high, parts).astype(jnp.bfloat16)
    ones = jnp.ones((8, width), jnp.bfloat16)
    return lax.dot_general(parts, ones, TN, preferred_element_type=jnp.float32)


def transposed(array):
    size = array.shape[1]
    same = lax.broadcasted_iota(jnp.int32, (size, size), 0) == lax.broadcasted_iota(
        jnp.int32, (size, size), 1
    )
    unit = jnp.where(same, 1.0, 0.0).astype(jnp.bfloat16)
    return lax.dot_general(unit, array, NT, preferred_element_type=jnp.float32)


def row_sums(wide):
    total = wide[:, :HD]
    for at in range(HD, wide.shape[1], HD):
        total = total + wide[:, at : at + HD]
    return jnp.sum(total.T, axis=0, keepdims=True)


def pack_kernel(n_ctx, heads_dev, *refs):
    inputs, square_ref, outs = refs[:4], refs[4], refs[5 : 5 + n_ctx]
    held, sems = refs[5 + n_ctx :]
    rows = held.shape[1]
    piece = rows // PIECES
    block, group = lax.axis_index("ctx"), lax.axis_index("head")

    def copy(at, part):
        place = pl.ds(part * piece, piece)
        return pltpu.make_async_copy(
            inputs[at].at[place, :], held.at[at, place, :], sems.at[at, part]
        )

    for at in range(4):
        for part in range(PIECES):
            copy(at, part).start()
    for at in range(4):
        for part in range(PIECES):
            copy(at, part).wait()
    for mask, out in zip(there_masks(n_ctx), outs):
        head = head_at(block ^ mask, group, n_ctx, heads_dev)

        @pl.when(head >= 0)
        def _(head=head, out=out):
            place = pl.ds(pl.multiple_of(head * HD, HD), HD)
            for at in range(4):
                out[at] = held[at, :, place]

    for at in range(2):
        wide = held[at].astype(jnp.float32)
        square_ref[at : at + 1, :] = row_sums(wide * wide)


def pack(arrays, n_ctx):
    rows, width_dev = arrays[0].shape
    result = pl.pallas_call(
        functools.partial(pack_kernel, n_ctx, width_dev // HD),
        out_shape=[jax.ShapeDtypeStruct((2, rows), jnp.float32)]
        + [jax.ShapeDtypeStruct((4, rows, HD), jnp.bfloat16)] * n_ctx,
        in_specs=[pl.BlockSpec(memory_space=pltpu.HBM)] * 4,
        out_specs=[IN_VMEM] * (n_ctx + 1),
        scratch_shapes=[
            pltpu.VMEM((4, rows, width_dev), jnp.bfloat16),
            pltpu.SemaphoreType.DMA((4, PIECES)),
        ],
        compiler_params=pltpu.CompilerParams(vmem_limit_bytes=VMEM_BYTES),
    )(*[pltpu.with_memory_space_constraint(array, pltpu.HBM) for array in arrays])
    return result[0], result[1:]


def attend_kernel(n_ctx, heads_dev, picks, scale_ref, q_gain, k_gain, *refs):
    messages = dict(zip(there_masks(n_ctx), refs[:n_ctx]))
    outs = dict(zip(back_masks(n_ctx), refs[n_ctx : 2 * n_ctx]))
    scratch = refs[2 * n_ctx :]
    q_ref, g_ref, k_ref, kt_ref, v_ref = scratch[:5]
    dq_ref, dk_ref, dv_ref, kt_picked, k_picked, v_picked = scratch[5:11]
    buffers = (scratch[11:16], scratch[16:21])
    rows = messages[0].shape[1]
    remote_count = picks.shape[1]
    near = rows // TILE
    n_keys = near + remote_count
    n_strips = n_keys * TILE // STRIP
    factor = 1.0 / math.sqrt(HD)
    to_base2 = factor * math.log2(math.e)
    own_block = lax.axis_index("ctx")
    own_head = head_at(own_block, lax.axis_index("head"), n_ctx, heads_dev)

    def rows_of(block):
        return pl.ds(pl.multiple_of(block * rows, rows), rows)

    def places_of(block):
        return [
            pl.ds(pl.multiple_of(block * rows + tile * TILE, TILE), TILE) for tile in range(near)
        ] + [
            pl.ds(pl.multiple_of(picks[block, slot] * TILE, TILE), TILE)
            for slot in range(remote_count)
        ]

    def prepare(mask):
        message = messages[mask]
        block = own_block ^ mask
        place = rows_of(block)
        q_scale = column(scale_ref[block, 0:1, :], HD)
        k_scale = column(scale_ref[block, 1:2, :], HD)
        q_normed = message[0].astype(jnp.float32) * q_scale * q_gain[pl.ds(own_head, 1), :]
        k_normed = message[1].astype(jnp.float32) * k_scale * k_gain[pl.ds(own_head, 1), :]
        keys = k_normed.astype(jnp.bfloat16)
        q_ref[mask] = q_normed.astype(jnp.bfloat16)
        k_ref[place, :] = keys
        kt_ref[:, place] = transposed(keys).astype(jnp.bfloat16)
        v_ref[place, :] = message[2]
        g_ref[mask] = message[3]

    def tiles(first, count=1):
        return slice(first * TILE, (first + count) * TILE)

    def scores(mask, group, places, buffer):
        weight_ref, dprob_ref, stat_ref = buffer[:3]
        for slot in group:
            k_picked[tiles(slot), :] = k_ref[places[slot], :]
            v_picked[tiles(slot), :] = v_ref[places[slot], :]
        picked = tiles(group[0], len(group))
        score_all = lax.dot_general(
            k_picked[picked, :], q_ref[mask], NT, preferred_element_type=jnp.float32
        )
        dprob_all = lax.dot_general(
            v_picked[picked, :], g_ref[mask], NT, preferred_element_type=jnp.float32
        )
        for at in range(len(group) * TILE // STRIP):
            strip = group[0] * TILE // STRIP + at
            part = slice(at * STRIP, (at + 1) * STRIP)
            score = score_all[part, :]
            dprob = dprob_all[part, :]
            top = jnp.max(score, axis=0, keepdims=True)
            weight = jnp.exp2((score - top) * to_base2)
            weight_ref[strip] = weight
            dprob_ref[strip] = dprob
            stat_ref[0, strip : strip + 1, :] = top * to_base2
            stat_ref[1, strip : strip + 1, :] = jnp.sum(weight, axis=0, keepdims=True)
            stat_ref[2, strip : strip + 1, :] = jnp.sum(weight * dprob, axis=0, keepdims=True)

    def settle(buffer):
        stat_ref = buffer[2]
        tops = stat_ref[0, :n_strips, :]
        shares = jnp.exp2(tops - jnp.max(tops, axis=0, keepdims=True))
        total = jnp.sum(shares * stat_ref[1, :n_strips, :], axis=0, keepdims=True)
        mixed = jnp.sum(shares * stat_ref[2, :n_strips, :], axis=0, keepdims=True)
        inverse = 1.0 / total
        return shares * inverse, mixed * inverse

    def gradients(group, buffer, shares, delta):
        weight_ref, dprob_ref, _, ds_ref, pb_ref = buffer
        for strip in range(group[0] * TILE // STRIP, (group[-1] + 1) * TILE // STRIP):
            part = slice(strip * STRIP, (strip + 1) * STRIP)
            prob = weight_ref[strip] * shares[strip : strip + 1, :]
            pb_ref[part, :] = prob.astype(jnp.bfloat16)
            ds_ref[part, :] = (prob * (dprob_ref[strip] - delta)).astype(jnp.bfloat16)

    def products(mask, group, places, buffer):
        ds_ref, pb_ref = buffer[3:]
        picked = tiles(group[0], len(group))
        dk = jnp.dot(ds_ref[picked, :], q_ref[mask], preferred_element_type=jnp.float32)
        dv = jnp.dot(pb_ref[picked, :], g_ref[mask], preferred_element_type=jnp.float32)
        for at, slot in enumerate(group):
            dk_ref[places[slot], :] += dk[tiles(at), :]
            dv_ref[places[slot], :] += dv[tiles(at), :]
            kt_picked[:, tiles(slot)] = kt_ref[:, places[slot]]

    def query_gradient(mask, buffer):
        dq_t = jnp.dot(kt_picked[...], buffer[3][...], preferred_element_type=jnp.float32)
        dq_ref[mask] = transposed((dq_t * factor).astype(jnp.bfloat16)).astype(jnp.bfloat16)

    groups = [range(first, min(first + 3, n_keys)) for first in range(0, n_keys, 3)]

    def step(now, before, after):
        if now is not None:
            shares, delta = settle(now[1])
        if before is not None:
            before_places = places_of(own_block ^ before[0])
        if after is not None:
            after_places = places_of(own_block ^ after[0])
        for group in groups:
            if before is not None:
                products(before[0], group, before_places, before[1])
            if now is not None:
                gradients(group, now[1], shares, delta)
            if after is not None:
                scores(after[0], group, after_places, after[1])
        if before is not None:
            query_gradient(*before)

    @pl.when(own_head >= 0)
    def _():
        for mask in range(n_ctx):
            prepare(mask)
        dk_ref[...] = jnp.zeros_like(dk_ref)
        dv_ref[...] = jnp.zeros_like(dv_ref)
        even, odd = buffers
        step(None, None, (0, even))
        step((0, even), None, (1, odd))

        def two(pair, carry):
            mask = 2 * pair
            step((mask + 1, odd), (mask, even), (mask + 2, even))
            step((mask + 2, even), (mask + 1, odd), (mask + 3, odd))
            return carry

        lax.fori_loop(0, n_ctx // 2 - 1, two, 0)
        step((n_ctx - 1, odd), (n_ctx - 2, even), None)
        step(None, (n_ctx - 1, odd), None)
        for mask in range(n_ctx):
            place = rows_of(own_block ^ mask)
            outs[mask][0] = dq_ref[mask]
            outs[mask][1] = (dk_ref[place, :] * factor).astype(jnp.bfloat16)
            outs[mask][2] = dv_ref[place, :].astype(jnp.bfloat16)


def attend(picks, scales, q_gain, k_gain, messages, n_ctx):
    rows = messages[0].shape[1]
    tokens = n_ctx * rows
    n_keys = rows // TILE + picks.shape[1]
    n_strips = n_keys * TILE // STRIP
    by_block = pltpu.VMEM((n_ctx, rows, HD), jnp.bfloat16)
    buffer = [
        pltpu.VMEM((n_strips, STRIP, rows), jnp.float32),
        pltpu.VMEM((n_strips, STRIP, rows), jnp.float32),
        pltpu.VMEM((3, -(-n_strips // 8) * 8, rows), jnp.float32),
        pltpu.VMEM((n_keys * TILE, rows), jnp.bfloat16),
        pltpu.VMEM((n_keys * TILE, rows), jnp.bfloat16),
    ]
    return pl.pallas_call(
        functools.partial(attend_kernel, n_ctx, q_gain.shape[0]),
        out_shape=[jax.ShapeDtypeStruct((3, rows, HD), jnp.bfloat16)] * n_ctx,
        in_specs=[IN_SMEM] + [IN_VMEM] * (3 + n_ctx),
        out_specs=[IN_VMEM] * n_ctx,
        scratch_shapes=[
            by_block,
            by_block,
            pltpu.VMEM((tokens, HD), jnp.bfloat16),
            pltpu.VMEM((HD, tokens), jnp.bfloat16),
            pltpu.VMEM((tokens, HD), jnp.bfloat16),
            by_block,
            pltpu.VMEM((tokens, HD), jnp.float32),
            pltpu.VMEM((tokens, HD), jnp.float32),
            pltpu.VMEM((HD, n_keys * TILE), jnp.bfloat16),
            pltpu.VMEM((n_keys * TILE, HD), jnp.bfloat16),
            pltpu.VMEM((n_keys * TILE, HD), jnp.bfloat16),
        ]
        + buffer
        + buffer,
        compiler_params=pltpu.CompilerParams(vmem_limit_bytes=VMEM_BYTES),
    )(picks, scales, q_gain, k_gain, *messages)


def gather_kernel(n_ctx, heads_dev, q_ref, k_ref, q_gain, k_gain, *refs):
    slots = refs[:n_ctx]
    dot_ref, dq_ref, dk_ref, dv_out, dv_ref, sems = refs[n_ctx:]
    piece = dv_ref.shape[0] // PIECES
    block, group = lax.axis_index("ctx"), lax.axis_index("head")

    def spread(at, out):
        for mask, slot in zip(back_masks(n_ctx), slots):
            head = head_at(block ^ mask, group, n_ctx, heads_dev)

            @pl.when(head >= 0)
            def _(head=head, slot=slot):
                place = pl.ds(pl.multiple_of(head * HD, HD), HD)
                out[:, place] = slot[at]

    spread(2, dv_ref)
    places = [pl.ds(part * piece, piece) for part in range(PIECES)]
    copies = [
        pltpu.make_async_copy(dv_ref.at[place, :], dv_out.at[place, :], sems.at[part])
        for part, place in enumerate(places)
    ]
    for copy in copies:
        copy.start()
    for at, (wide_ref, pre_ref, gain) in enumerate(
        ((dq_ref, q_ref, q_gain), (dk_ref, k_ref, k_gain))
    ):
        spread(at, wide_ref)
        terms = gain[...] * wide_ref[...].astype(jnp.float32) * pre_ref[...].astype(jnp.float32)
        dot_ref[at : at + 1, :] = row_sums(terms)
    for copy in copies:
        copy.wait()


def finish_kernel(width_all, q_ref, k_ref, q_gain, k_gain, scale_ref, dot_ref, *refs):
    dq_ref, dk_ref, dq_out, dk_out, held, sems = refs
    piece = q_ref.shape[0] // PIECES
    scales = scale_ref[lax.axis_index("ctx")]
    backs = scales**3 * (dot_ref[...] / width_all)
    copies = []
    for at, (pre_ref, gain, grad_ref, out) in enumerate(
        ((q_ref, q_gain, dq_ref, dq_out), (k_ref, k_gain, dk_ref, dk_out))
    ):
        scale_all = column(scales[at : at + 1, :], HD)
        back_all = column(backs[at : at + 1, :], HD)
        for part in range(PIECES):
            rows = slice(part * piece, (part + 1) * piece)
            scale, back = scale_all[rows, :], back_all[rows, :]
            for first in range(0, pre_ref.shape[1], HD):
                place = slice(first, first + HD)
                wide = pre_ref[rows, place].astype(jnp.float32)
                grad = grad_ref[rows, place].astype(jnp.float32)
                result = scale * gain[:, place] * grad - wide * back
                held[at, rows, place] = result.astype(jnp.bfloat16)
            copies.append(
                pltpu.make_async_copy(held.at[at, rows, :], out.at[rows, :], sems.at[at, part])
            )
            copies[-1].start()
    for copy in copies:
        copy.wait()


def heads_to_owners(q_pre, k_pre, values, out_grad, q_gain, k_gain, selected):
    n_ctx = lax.axis_size("ctx")
    n_head = lax.axis_size("head")
    rows, width_dev = q_pre.shape
    width_all = width_dev * n_head
    heads_dev = width_dev // HD
    remote_count = selected.shape[2]
    sizes = (n_ctx, n_head, heads_dev)
    params = pltpu.CompilerParams(vmem_limit_bytes=VMEM_BYTES)

    by_row = jax.ShapeDtypeStruct((2, rows), jnp.float32)
    wide = jax.ShapeDtypeStruct((rows, width_dev), jnp.bfloat16)

    squares, sent = pack((q_pre, k_pre, values, out_grad), n_ctx)
    messages = move(there_masks(n_ctx), sent, False, *sizes)

    wishes = selected[0].reshape(1, -1).astype(jnp.float32)
    wishes = jnp.pad(wishes, ((0, 0), (0, rows - wishes.shape[1])))
    small = jnp.concatenate((lax.psum(squares, "head"), wishes), axis=0)
    small = jnp.broadcast_to(small[None], (n_ctx,) + small.shape)
    small = lax.all_to_all(small, "ctx", split_axis=0, concat_axis=0, tiled=True)
    scales = lax.rsqrt(small[:, :2] / width_all + epsilon)
    own_head = head_at(lax.axis_index("ctx"), lax.axis_index("head"), n_ctx, heads_dev)
    first = jnp.maximum(own_head, 0) * remote_count
    picks = lax.dynamic_slice_in_dim(small[:, 2], first, remote_count, 1).astype(jnp.int32)

    q_gains = q_gain.reshape(heads_dev, HD)
    k_gains = k_gain.reshape(heads_dev, HD)
    results = attend(picks, scales, q_gains, k_gains, messages, n_ctx)
    slots = move(back_masks(n_ctx), results, True, *sizes)

    pres = (q_pre, k_pre, q_gain[None], k_gain[None])
    dots, dq_wide, dk_wide, dv = pl.pallas_call(
        functools.partial(gather_kernel, n_ctx, heads_dev),
        out_shape=[by_row, wide, wide, wide],
        in_specs=[IN_VMEM] * (4 + n_ctx),
        out_specs=[IN_VMEM] * 3 + [pl.BlockSpec(memory_space=pltpu.HBM)],
        scratch_shapes=[
            pltpu.VMEM((rows, width_dev), jnp.bfloat16),
            pltpu.SemaphoreType.DMA((PIECES,)),
        ],
        compiler_params=params,
    )(*pres, *slots)
    dots = lax.psum(dots, "head")
    dq, dk = pl.pallas_call(
        functools.partial(finish_kernel, width_all),
        out_shape=[wide, wide],
        in_specs=[IN_VMEM] * 8,
        out_specs=[pl.BlockSpec(memory_space=pltpu.HBM)] * 2,
        scratch_shapes=[
            pltpu.VMEM((2, rows, width_dev), jnp.bfloat16),
            pltpu.SemaphoreType.DMA((2, PIECES)),
        ],
        compiler_params=params,
    )(*pres, scales, dots, dq_wide, dk_wide)
    return dq, dk, dv


def on_device(q_pre, k_pre, values, out_grad, q_gain, k_gain, selected):
    n_ctx = lax.axis_size("ctx")
    tiles_dev, heads_dev, remote_count = selected.shape
    capacity = -(-heads_dev * remote_count // (n_ctx - 1))
    by_head = (n_ctx - 1) * tiles_dev * 7
    by_tile = (n_ctx - 1) * capacity * 6
    paired = n_ctx & (n_ctx - 1) == 0 and n_ctx >= max(heads_dev, 4)
    plan = heads_to_owners if paired and by_head <= by_tile else tiles_to_queries
    return plan(q_pre, k_pre, values, out_grad, q_gain, k_gain, selected)


def solution(mesh):
    placed = (
        P("ctx", "head"),
        P("ctx", "head"),
        P("ctx", "head"),
        P("ctx", "head"),
        P("head"),
        P("head"),
        P("ctx", "head", None),
    )
    return jax.shard_map(
        on_device,
        mesh=mesh,
        in_specs=placed,
        out_specs=(P("ctx", "head"), P("ctx", "head"), P("ctx", "head")),
        check_vma=False,
    )
```

```python
import functools
import math

import jax
import jax.numpy as jnp
from jax import lax
from jax.experimental import pallas as pl
from jax.experimental.pallas import tpu as pltpu
from jax.sharding import PartitionSpec as P

HD = 128
TILE = 128


epsilon = 1e-06


def split_heads(array, heads_dev):
    return array.reshape(array.shape[0], heads_dev, HD).transpose(1, 0, 2)


def merge_heads(array):
    heads_dev, tok_dev, depth = array.shape
    return array.transpose(1, 0, 2).reshape(tok_dev, heads_dev * depth)


def per_tile(array, qt_dev):
    heads_dev, tok_dev, depth = array.shape
    return array.reshape(heads_dev, qt_dev, TILE, depth).transpose(1, 0, 2, 3)


def from_tiles(array):
    qt_dev, heads_dev, rows_tile, depth = array.shape
    return array.transpose(1, 0, 2, 3).reshape(heads_dev, qt_dev * rows_tile, depth)


def table_sum(taken, pieces, heads_dev, qt_dev):
    flat_pieces = pieces.reshape(pieces.shape[0], -1)
    summed = jnp.dot(
        taken, flat_pieces, precision=lax.Precision.HIGHEST, preferred_element_type=jnp.float32
    )
    summed = summed.reshape(heads_dev, qt_dev, 2, TILE, HD).transpose(2, 0, 1, 3, 4)
    return summed.reshape(2, heads_dev, qt_dev * TILE, HD)


def rounded(array):
    return array.astype(jnp.bfloat16)


def finish_norm(wide, scale, gain, grad, dot_sum, width_all):
    return (scale * gain * grad - wide * scale**3 * (dot_sum / width_all)[:, None]).astype(
        jnp.bfloat16
    )


def tiles_to_queries(q_pre, k_pre, values, out_grad, q_gain, k_gain, selected):
    n_ctx = lax.axis_size("ctx")
    tok_dev, width_dev = q_pre.shape
    width_all = width_dev * lax.axis_size("head")
    heads_dev = width_dev // HD
    qt_dev = tok_dev // TILE
    remote_count = selected.shape[2]
    factor = 1.0 / math.sqrt(HD)
    q_wide = q_pre.astype(jnp.float32)
    k_wide = k_pre.astype(jnp.float32)
    q_square, k_square = lax.psum(
        (jnp.sum(q_wide * q_wide, axis=1), jnp.sum(k_wide * k_wide, axis=1)), "head"
    )
    q_scale = lax.rsqrt(q_square / width_all + epsilon)[:, None]
    k_scale = lax.rsqrt(k_square / width_all + epsilon)[:, None]
    q_heads = split_heads(rounded(q_wide * q_scale * q_gain), heads_dev)
    k_heads = split_heads(rounded(k_wide * k_scale * k_gain), heads_dev)
    v_heads = split_heads(values, heads_dev)
    g_heads = split_heads(out_grad, heads_dev)
    q_tiles = per_tile(q_heads, qt_dev)
    g_tiles = per_tile(g_heads, qt_dev)
    k_table = k_heads.reshape(heads_dev * qt_dev, TILE, HD)
    v_table = v_heads.reshape(heads_dev * qt_dev, TILE, HD)
    flat_sel = selected[0].reshape(-1)
    n_slot = flat_sel.shape[0]
    capacity = -(-n_slot // (n_ctx - 1))
    n_buffer = n_ctx * capacity
    owners = flat_sel // qt_dev
    head_of = jnp.arange(n_slot, dtype=jnp.int32) // remote_count
    codes = head_of * qt_dev + flat_sel % qt_dev
    matches = (owners[:, None] == jnp.arange(n_ctx, dtype=jnp.int32)[None, :]).astype(jnp.int32)
    ranks = jnp.sum((jnp.cumsum(matches, axis=0) - matches) * matches, axis=1)
    position = owners * capacity + ranks
    placed = position[None, :] == jnp.arange(n_buffer, dtype=jnp.int32)[:, None]
    request = jnp.sum(jnp.where(placed, codes[None, :] + 1, 0), axis=1) - 1
    asked = lax.all_to_all(
        request.reshape(n_ctx, capacity), "ctx", split_axis=0, concat_axis=0, tiled=True
    ).reshape(n_buffer)
    clipped = jnp.maximum(asked, 0)
    taken = (asked[None, :] == jnp.arange(heads_dev * qt_dev, dtype=jnp.int32)[:, None]).astype(
        jnp.float32
    )
    s_near = (
        jnp.einsum("rhqd,hkd->rhqk", q_tiles, k_heads, preferred_element_type=jnp.float32) * factor
    )
    dp_near = jnp.einsum("rhqd,hkd->rhqk", g_tiles, v_heads, preferred_element_type=jnp.float32)
    near_top = jnp.max(s_near, axis=-1)
    outgoing = jnp.stack((k_table[clipped], v_table[clipped]), axis=1).reshape(
        n_ctx, capacity, 2, TILE, HD
    )
    incoming = lax.all_to_all(outgoing, "ctx", split_axis=0, concat_axis=0, tiled=True).reshape(
        n_buffer, 2, TILE, HD
    )
    slot_kv = incoming[position].reshape(heads_dev, remote_count, 2, TILE, HD)
    far_k = slot_kv[:, :, 0]
    far_v = slot_kv[:, :, 1]
    s_far = (
        jnp.einsum("rhqd,hckd->rhqck", q_tiles, far_k, preferred_element_type=jnp.float32) * factor
    )
    dp_far = jnp.einsum("rhqd,hckd->rhqck", g_tiles, far_v, preferred_element_type=jnp.float32)
    row_top = jnp.maximum(near_top, jnp.max(s_far, axis=(-2, -1)))
    totals = jnp.sum(jnp.exp(s_near - row_top[..., None]), axis=-1) + jnp.sum(
        jnp.exp(s_far - row_top[..., None, None]), axis=(-2, -1)
    )
    lse = row_top + jnp.log(totals)
    p_near = jnp.exp(s_near - lse[..., None])
    p_far = jnp.exp(s_far - lse[..., None, None])
    delta = jnp.sum(p_near * dp_near, axis=-1) + jnp.sum(p_far * dp_far, axis=(-2, -1))
    ds_near = rounded(p_near * (dp_near - delta[..., None]) * factor)
    pb_near = rounded(p_near)
    dq_near = jnp.einsum("rhqk,hkd->rhqd", ds_near, k_heads, preferred_element_type=jnp.float32)
    dk_near = jnp.einsum("rhqk,rhqd->hkd", ds_near, q_tiles, preferred_element_type=jnp.float32)
    dv_near = jnp.einsum("rhqk,rhqd->hkd", pb_near, g_tiles, preferred_element_type=jnp.float32)
    dq_near, dk_near, dv_near = (dq_near, dk_near, dv_near)
    ds_far = rounded(p_far * (dp_far - delta[..., None, None]) * factor)
    pb_far = rounded(p_far)
    dq_far = jnp.einsum("rhqck,hckd->rhqd", ds_far, far_k, preferred_element_type=jnp.float32)
    dq_wide = merge_heads(from_tiles(dq_near + dq_far))
    q_dot = jnp.sum(q_gain * dq_wide * q_wide, axis=1)
    dq_wide, q_dot = (dq_wide, q_dot)
    dk_far = jnp.einsum("rhqck,rhqd->hckd", ds_far, q_tiles, preferred_element_type=jnp.float32)
    dv_far = jnp.einsum("rhqck,rhqd->hckd", pb_far, g_tiles, preferred_element_type=jnp.float32)
    grads = jnp.stack((dk_far, dv_far), axis=2).reshape(n_slot, 2, TILE, HD)
    sending = jnp.zeros((n_buffer, 2, TILE, HD), jnp.float32).at[position].set(grads)
    returned = lax.all_to_all(
        sending.reshape(n_ctx, capacity, 2, TILE, HD),
        "ctx",
        split_axis=0,
        concat_axis=0,
        tiled=True,
    ).reshape(n_buffer, 2, TILE, HD)
    far_sums = table_sum(taken, returned, heads_dev, qt_dev)
    dk_wide = merge_heads(dk_near + far_sums[0])
    dv_heads = dv_near + far_sums[1]
    k_dot = jnp.sum(k_gain * dk_wide * k_wide, axis=1)
    q_dot, k_dot = lax.psum((q_dot, k_dot), "head")
    dq_result = finish_norm(q_wide, q_scale, q_gain, dq_wide, q_dot, width_all)
    dk_result = finish_norm(k_wide, k_scale, k_gain, dk_wide, k_dot, width_all)
    return (dq_result, dk_result, merge_heads(dv_heads).astype(jnp.bfloat16))


VMEM_BYTES = 48 * 2**20
PIECES = 4
IN_VMEM = pl.BlockSpec(memory_space=pltpu.VMEM)
IN_SMEM = pl.BlockSpec(memory_space=pltpu.SMEM)


def owners_of(group, n_ctx, heads_dev):
    places = [(4 * head + 1) * n_ctx // (4 * heads_dev) for head in range(heads_dev)]
    return [n_ctx - 1 - place if group % 2 else place for place in places]


def head_at(place, group, n_ctx, heads_dev):
    even = jnp.where(group % 2 == 1, n_ctx - 1 - place, place)
    head = -1
    for index, owner in enumerate(owners_of(0, n_ctx, heads_dev)):
        head = jnp.where(even == owner, index, head)
    return head


def pairs_to_owner(mask, n_ctx, n_head, heads_dev):
    pairs = []
    for group in range(n_head):
        owners = owners_of(group, n_ctx, heads_dev)
        for block in range(n_ctx):
            if block ^ mask in owners:
                pairs.append((block * n_head + group, (block ^ mask) * n_head + group))
    return pairs


def there_masks(n_ctx):
    return list(range(n_ctx - 1, -1, -1))


def back_masks(n_ctx):
    return list(range(n_ctx // 2 - 1, 0, -1)) + list(range(n_ctx - 1, n_ctx // 2 - 1, -1)) + [0]


def move(masks, arrays, back, n_ctx, n_head, heads_dev):
    moved = []
    for mask, array in zip(masks, arrays):
        pairs = pairs_to_owner(mask, n_ctx, n_head, heads_dev)
        if back:
            pairs = [(b, a) for a, b in pairs]
        moved.append(lax.ppermute(array, ("ctx", "head"), pairs) if mask else array)
    return moved


def column(row, width):
    return jnp.broadcast_to(row, (width, row.shape[1])).T


def row_sums(wide):
    total = wide[:, :HD]
    for at in range(HD, wide.shape[1], HD):
        total = total + wide[:, at : at + HD]
    return jnp.sum(total.T, axis=0, keepdims=True)


def pack_kernel(n_ctx, heads_dev, *refs):
    inputs, square_ref, outs = refs[:4], refs[4], refs[5 : 5 + n_ctx]
    held, sems = refs[5 + n_ctx :]
    rows = held.shape[1]
    piece = rows // PIECES
    block, group = lax.axis_index("ctx"), lax.axis_index("head")

    def copy(at, part):
        place = pl.ds(part * piece, piece)
        return pltpu.make_async_copy(
            inputs[at].at[place, :], held.at[at, place, :], sems.at[at, part]
        )

    for at in range(4):
        for part in range(PIECES):
            copy(at, part).start()
    for at in range(4):
        for part in range(PIECES):
            copy(at, part).wait()
    for mask, out in zip(there_masks(n_ctx), outs):
        head = head_at(block ^ mask, group, n_ctx, heads_dev)

        @pl.when(head >= 0)
        def _(head=head, out=out):
            place = pl.ds(pl.multiple_of(head * HD, HD), HD)
            for at in range(4):
                out[at] = held[at, :, place]

    for at in range(2):
        wide = held[at].astype(jnp.float32)
        square_ref[at : at + 1, :] = row_sums(wide * wide)


def pack(arrays, n_ctx):
    rows, width_dev = arrays[0].shape
    result = pl.pallas_call(
        functools.partial(pack_kernel, n_ctx, width_dev // HD),
        out_shape=[jax.ShapeDtypeStruct((2, rows), jnp.float32)]
        + [jax.ShapeDtypeStruct((4, rows, HD), jnp.bfloat16)] * n_ctx,
        in_specs=[pl.BlockSpec(memory_space=pltpu.HBM)] * 4,
        out_specs=[IN_VMEM] * (n_ctx + 1),
        scratch_shapes=[
            pltpu.VMEM((4, rows, width_dev), jnp.bfloat16),
            pltpu.SemaphoreType.DMA((4, PIECES)),
        ],
        compiler_params=pltpu.CompilerParams(vmem_limit_bytes=VMEM_BYTES),
    )(*[pltpu.with_memory_space_constraint(array, pltpu.HBM) for array in arrays])
    return result[0], result[1:]


def attend_kernel(n_ctx, heads_dev, picks, scale_ref, q_gain, k_gain, *refs):
    messages = dict(zip(there_masks(n_ctx), refs[:n_ctx]))
    outs = dict(zip(back_masks(n_ctx), refs[n_ctx : 2 * n_ctx]))
    scratch = refs[2 * n_ctx :]
    q_ref, qt_ref, g_ref, gt_ref, k_ref, kt_ref, v_ref = scratch[:7]
    dq_ref, dk_ref, dv_ref, kt_picked, k_picked, v_picked = scratch[7:13]
    buffers = (scratch[13:18], scratch[18:23])
    rows = messages[0].shape[1]
    remote_count = picks.shape[1]
    near = rows // TILE
    n_keys = near + remote_count
    in_sublanes = (TILE // 8, 8, rows)
    factor = 1.0 / math.sqrt(HD)
    to_base2 = factor * math.log2(math.e)
    own_block = lax.axis_index("ctx")
    own_head = head_at(own_block, lax.axis_index("head"), n_ctx, heads_dev)

    def rows_of(block):
        return pl.ds(pl.multiple_of(block * rows, rows), rows)

    def places_of(block):
        return [
            pl.ds(pl.multiple_of(block * rows + tile * TILE, TILE), TILE) for tile in range(near)
        ] + [
            pl.ds(pl.multiple_of(picks[block, slot] * TILE, TILE), TILE)
            for slot in range(remote_count)
        ]

    def prepare(mask, q_factor, k_factor):
        message = messages[mask]
        block = own_block ^ mask
        place = rows_of(block)
        q_t = message[0].T.astype(jnp.float32) * scale_ref[block, 0:1, :] * q_factor
        k_t = message[1].T.astype(jnp.float32) * scale_ref[block, 1:2, :] * k_factor
        qt_ref[mask] = q_t.astype(jnp.bfloat16)
        kt_ref[:, place] = k_t.astype(jnp.bfloat16)
        q_ref[mask] = q_t.astype(jnp.bfloat16).T
        k_ref[place, :] = k_t.astype(jnp.bfloat16).T
        v_ref[place, :] = message[2]
        g_ref[mask] = message[3]
        gt_ref[mask] = message[3].T

    def tiles(first, count=1):
        return slice(first * TILE, (first + count) * TILE)

    def scores(mask, group, places, buffer):
        weight_ref, dprob_ref, stat_ref = buffer[:3]
        for slot in group:
            k_picked[tiles(slot), :] = k_ref[places[slot], :]
            v_picked[tiles(slot), :] = v_ref[places[slot], :]
        picked = tiles(group[0], len(group))
        score_all = jnp.dot(
            k_picked[picked, :], qt_ref[mask], preferred_element_type=jnp.float32
        )
        dprob_all = jnp.dot(
            v_picked[picked, :], gt_ref[mask], preferred_element_type=jnp.float32
        )
        for at, slot in enumerate(group):
            score = score_all[tiles(at), :].reshape(in_sublanes)
            dprob = dprob_all[tiles(at), :].reshape(in_sublanes)
            top = jnp.max(score, axis=0)
            weight = jnp.exp2((score - top) * to_base2)
            weight_ref[slot] = weight
            dprob_ref[slot] = dprob
            stat_ref[0, slot] = top * to_base2
            stat_ref[1, slot] = jnp.sum(weight, axis=0)
            stat_ref[2, slot] = jnp.sum(weight * dprob, axis=0)

    def settle(buffer):
        tops, totals, mixed = [buffer[2][at] for at in range(3)]
        highest = jnp.max(jnp.max(tops, axis=0), axis=0, keepdims=True)
        shares = jnp.exp2(tops - highest)
        total = jnp.sum(jnp.sum(shares * totals, axis=0), axis=0, keepdims=True)
        delta = jnp.sum(jnp.sum(shares * mixed, axis=0), axis=0, keepdims=True)
        inverse = 1.0 / total
        return shares * inverse, delta * inverse

    def gradients(group, buffer, shares, delta):
        weight_ref, dprob_ref, _, ds_ref, pb_ref = buffer
        for slot in group:
            prob = weight_ref[slot] * shares[slot]
            dscore = prob * (dprob_ref[slot] - delta)
            pb_ref[tiles(slot), :] = prob.reshape(TILE, rows).astype(jnp.bfloat16)
            ds_ref[tiles(slot), :] = dscore.reshape(TILE, rows).astype(jnp.bfloat16)

    def products(mask, group, places, buffer):
        ds_ref, pb_ref = buffer[3:]
        picked = tiles(group[0], len(group))
        dk = jnp.dot(ds_ref[picked, :], q_ref[mask], preferred_element_type=jnp.float32)
        dv = jnp.dot(pb_ref[picked, :], g_ref[mask], preferred_element_type=jnp.float32)
        for at, slot in enumerate(group):
            dk_ref[places[slot], :] += dk[tiles(at), :]
            dv_ref[places[slot], :] += dv[tiles(at), :]
            kt_picked[:, tiles(slot)] = kt_ref[:, places[slot]]

    def query_gradient(mask, buffer):
        dq_t = jnp.dot(kt_picked[...], buffer[3][...], preferred_element_type=jnp.float32)
        dq_ref[mask] = (dq_t * factor).astype(jnp.bfloat16).T

    groups = [range(first, min(first + 3, n_keys)) for first in range(0, n_keys, 3)]

    def step(now, before, after):
        if now is not None:
            shares, delta = settle(now[1])
        if before is not None:
            before_places = places_of(own_block ^ before[0])
        if after is not None:
            after_places = places_of(own_block ^ after[0])
        for group in groups:
            if before is not None:
                products(before[0], group, before_places, before[1])
            if now is not None:
                gradients(group, now[1], shares, delta)
            if after is not None:
                scores(after[0], group, after_places, after[1])
        if before is not None:
            query_gradient(*before)

    @pl.when(own_head >= 0)
    def _():
        q_factor = column(q_gain[pl.ds(own_head, 1), :], rows)
        k_factor = column(k_gain[pl.ds(own_head, 1), :], rows)
        for mask in range(n_ctx):
            prepare(mask, q_factor, k_factor)
        dk_ref[...] = jnp.zeros_like(dk_ref)
        dv_ref[...] = jnp.zeros_like(dv_ref)
        even, odd = buffers
        step(None, None, (0, even))
        step((0, even), None, (1, odd))

        def two(pair, carry):
            mask = 2 * pair
            step((mask + 1, odd), (mask, even), (mask + 2, even))
            step((mask + 2, even), (mask + 1, odd), (mask + 3, odd))
            return carry

        lax.fori_loop(0, n_ctx // 2 - 1, two, 0)
        step((n_ctx - 1, odd), (n_ctx - 2, even), None)
        step(None, (n_ctx - 1, odd), None)
        for mask in range(n_ctx):
            place = rows_of(own_block ^ mask)
            outs[mask][0] = dq_ref[mask]
            outs[mask][1] = (dk_ref[place, :] * factor).astype(jnp.bfloat16)
            outs[mask][2] = dv_ref[place, :].astype(jnp.bfloat16)


def attend(picks, scales, q_gain, k_gain, messages, n_ctx):
    rows = messages[0].shape[1]
    tokens = n_ctx * rows
    n_keys = rows // TILE + picks.shape[1]
    by_block = pltpu.VMEM((n_ctx, rows, HD), jnp.bfloat16)
    by_block_t = pltpu.VMEM((n_ctx, HD, rows), jnp.bfloat16)
    buffer = [
        pltpu.VMEM((n_keys, TILE // 8, 8, rows), jnp.float32),
        pltpu.VMEM((n_keys, TILE // 8, 8, rows), jnp.float32),
        pltpu.VMEM((3, n_keys, 8, rows), jnp.float32),
        pltpu.VMEM((n_keys * TILE, rows), jnp.bfloat16),
        pltpu.VMEM((n_keys * TILE, rows), jnp.bfloat16),
    ]
    return pl.pallas_call(
        functools.partial(attend_kernel, n_ctx, q_gain.shape[0]),
        out_shape=[jax.ShapeDtypeStruct((3, rows, HD), jnp.bfloat16)] * n_ctx,
        in_specs=[IN_SMEM] + [IN_VMEM] * (3 + n_ctx),
        out_specs=[IN_VMEM] * n_ctx,
        scratch_shapes=[
            by_block,
            by_block_t,
            by_block,
            by_block_t,
            pltpu.VMEM((tokens, HD), jnp.bfloat16),
            pltpu.VMEM((HD, tokens), jnp.bfloat16),
            pltpu.VMEM((tokens, HD), jnp.bfloat16),
            by_block,
            pltpu.VMEM((tokens, HD), jnp.float32),
            pltpu.VMEM((tokens, HD), jnp.float32),
            pltpu.VMEM((HD, n_keys * TILE), jnp.bfloat16),
            pltpu.VMEM((n_keys * TILE, HD), jnp.bfloat16),
            pltpu.VMEM((n_keys * TILE, HD), jnp.bfloat16),
        ]
        + buffer
        + buffer,
        compiler_params=pltpu.CompilerParams(vmem_limit_bytes=VMEM_BYTES),
    )(picks, scales, q_gain, k_gain, *messages)


def gather_kernel(n_ctx, heads_dev, q_ref, k_ref, q_gain, k_gain, *refs):
    slots = refs[:n_ctx]
    dot_ref, dq_ref, dk_ref, dv_out, dv_ref, sems = refs[n_ctx:]
    piece = dv_ref.shape[0] // PIECES
    block, group = lax.axis_index("ctx"), lax.axis_index("head")

    def spread(at, out):
        for mask, slot in zip(back_masks(n_ctx), slots):
            head = head_at(block ^ mask, group, n_ctx, heads_dev)

            @pl.when(head >= 0)
            def _(head=head, slot=slot):
                place = pl.ds(pl.multiple_of(head * HD, HD), HD)
                out[:, place] = slot[at]

    spread(2, dv_ref)
    places = [pl.ds(part * piece, piece) for part in range(PIECES)]
    copies = [
        pltpu.make_async_copy(dv_ref.at[place, :], dv_out.at[place, :], sems.at[part])
        for part, place in enumerate(places)
    ]
    for copy in copies:
        copy.start()
    for at, (wide_ref, pre_ref, gain) in enumerate(
        ((dq_ref, q_ref, q_gain), (dk_ref, k_ref, k_gain))
    ):
        spread(at, wide_ref)
        terms = gain[...] * wide_ref[...].astype(jnp.float32) * pre_ref[...].astype(jnp.float32)
        dot_ref[at : at + 1, :] = row_sums(terms)
    for copy in copies:
        copy.wait()


def finish_kernel(width_all, q_ref, k_ref, q_gain, k_gain, scale_ref, dot_ref, *refs):
    dq_ref, dk_ref, dq_out, dk_out, held, sems = refs
    piece = q_ref.shape[0] // PIECES
    scales = scale_ref[lax.axis_index("ctx")]
    backs = scales**3 * (dot_ref[...] / width_all)
    copies = []
    for at, (pre_ref, gain, grad_ref, out) in enumerate(
        ((q_ref, q_gain, dq_ref, dq_out), (k_ref, k_gain, dk_ref, dk_out))
    ):
        scale_all = column(scales[at : at + 1, :], HD)
        back_all = column(backs[at : at + 1, :], HD)
        for part in range(PIECES):
            rows = slice(part * piece, (part + 1) * piece)
            scale, back = scale_all[rows, :], back_all[rows, :]
            for first in range(0, pre_ref.shape[1], HD):
                place = slice(first, first + HD)
                wide = pre_ref[rows, place].astype(jnp.float32)
                grad = grad_ref[rows, place].astype(jnp.float32)
                result = scale * gain[:, place] * grad - wide * back
                held[at, rows, place] = result.astype(jnp.bfloat16)
            copies.append(
                pltpu.make_async_copy(held.at[at, rows, :], out.at[rows, :], sems.at[at, part])
            )
            copies[-1].start()
    for copy in copies:
        copy.wait()


def heads_to_owners(q_pre, k_pre, values, out_grad, q_gain, k_gain, selected):
    n_ctx = lax.axis_size("ctx")
    n_head = lax.axis_size("head")
    rows, width_dev = q_pre.shape
    width_all = width_dev * n_head
    heads_dev = width_dev // HD
    remote_count = selected.shape[2]
    sizes = (n_ctx, n_head, heads_dev)
    params = pltpu.CompilerParams(vmem_limit_bytes=VMEM_BYTES)

    by_row = jax.ShapeDtypeStruct((2, rows), jnp.float32)
    wide = jax.ShapeDtypeStruct((rows, width_dev), jnp.bfloat16)

    squares, sent = pack((q_pre, k_pre, values, out_grad), n_ctx)
    messages = move(there_masks(n_ctx), sent, False, *sizes)

    wishes = selected[0].reshape(1, -1).astype(jnp.float32)
    wishes = jnp.pad(wishes, ((0, 0), (0, rows - wishes.shape[1])))
    small = jnp.concatenate((lax.psum(squares, "head"), wishes), axis=0)
    small = jnp.broadcast_to(small[None], (n_ctx,) + small.shape)
    small = lax.all_to_all(small, "ctx", split_axis=0, concat_axis=0, tiled=True)
    scales = lax.rsqrt(small[:, :2] / width_all + epsilon)
    own_head = head_at(lax.axis_index("ctx"), lax.axis_index("head"), n_ctx, heads_dev)
    first = jnp.maximum(own_head, 0) * remote_count
    picks = lax.dynamic_slice_in_dim(small[:, 2], first, remote_count, 1).astype(jnp.int32)

    q_gains = q_gain.reshape(heads_dev, HD)
    k_gains = k_gain.reshape(heads_dev, HD)
    results = attend(picks, scales, q_gains, k_gains, messages, n_ctx)
    slots = move(back_masks(n_ctx), results, True, *sizes)

    pres = (q_pre, k_pre, q_gain[None], k_gain[None])
    dots, dq_wide, dk_wide, dv = pl.pallas_call(
        functools.partial(gather_kernel, n_ctx, heads_dev),
        out_shape=[by_row, wide, wide, wide],
        in_specs=[IN_VMEM] * (4 + n_ctx),
        out_specs=[IN_VMEM] * 3 + [pl.BlockSpec(memory_space=pltpu.HBM)],
        scratch_shapes=[
            pltpu.VMEM((rows, width_dev), jnp.bfloat16),
            pltpu.SemaphoreType.DMA((PIECES,)),
        ],
        compiler_params=params,
    )(*pres, *slots)
    dots = lax.psum(dots, "head")
    dq, dk = pl.pallas_call(
        functools.partial(finish_kernel, width_all),
        out_shape=[wide, wide],
        in_specs=[IN_VMEM] * 8,
        out_specs=[pl.BlockSpec(memory_space=pltpu.HBM)] * 2,
        scratch_shapes=[
            pltpu.VMEM((2, rows, width_dev), jnp.bfloat16),
            pltpu.SemaphoreType.DMA((2, PIECES)),
        ],
        compiler_params=params,
    )(*pres, scales, dots, dq_wide, dk_wide)
    return dq, dk, dv


def on_device(q_pre, k_pre, values, out_grad, q_gain, k_gain, selected):
    n_ctx = lax.axis_size("ctx")
    tiles_dev, heads_dev, remote_count = selected.shape
    capacity = -(-heads_dev * remote_count // (n_ctx - 1))
    by_head = (n_ctx - 1) * tiles_dev * 7
    by_tile = (n_ctx - 1) * capacity * 6
    paired = n_ctx & (n_ctx - 1) == 0 and n_ctx >= max(heads_dev, 4)
    plan = heads_to_owners if paired and by_head <= by_tile else tiles_to_queries
    return plan(q_pre, k_pre, values, out_grad, q_gain, k_gain, selected)


def solution(mesh):
    placed = (
        P("ctx", "head"),
        P("ctx", "head"),
        P("ctx", "head"),
        P("ctx", "head"),
        P("head"),
        P("head"),
        P("ctx", "head", None),
    )
    return jax.shard_map(
        on_device,
        mesh=mesh,
        in_specs=placed,
        out_specs=(P("ctx", "head"), P("ctx", "head"), P("ctx", "head")),
        check_vma=False,
    )
```

```python
import functools
import math

import jax
import jax.numpy as jnp
from jax import lax
from jax.experimental import pallas as pl
from jax.experimental.pallas import tpu as pltpu
from jax.sharding import PartitionSpec as P

HD = 128
TILE = 128


epsilon = 1e-06


def split_heads(array, heads_dev):
    return array.reshape(array.shape[0], heads_dev, HD).transpose(1, 0, 2)


def merge_heads(array):
    heads_dev, tok_dev, depth = array.shape
    return array.transpose(1, 0, 2).reshape(tok_dev, heads_dev * depth)


def per_tile(array, qt_dev):
    heads_dev, tok_dev, depth = array.shape
    return array.reshape(heads_dev, qt_dev, TILE, depth).transpose(1, 0, 2, 3)


def from_tiles(array):
    qt_dev, heads_dev, rows_tile, depth = array.shape
    return array.transpose(1, 0, 2, 3).reshape(heads_dev, qt_dev * rows_tile, depth)


def table_sum(taken, pieces, heads_dev, qt_dev):
    flat_pieces = pieces.reshape(pieces.shape[0], -1)
    summed = jnp.dot(
        taken, flat_pieces, precision=lax.Precision.HIGHEST, preferred_element_type=jnp.float32
    )
    summed = summed.reshape(heads_dev, qt_dev, 2, TILE, HD).transpose(2, 0, 1, 3, 4)
    return summed.reshape(2, heads_dev, qt_dev * TILE, HD)


def rounded(array):
    return array.astype(jnp.bfloat16)


def finish_norm(wide, scale, gain, grad, dot_sum, width_all):
    return (scale * gain * grad - wide * scale**3 * (dot_sum / width_all)[:, None]).astype(
        jnp.bfloat16
    )


def tiles_to_queries(q_pre, k_pre, values, out_grad, q_gain, k_gain, selected):
    n_ctx = lax.axis_size("ctx")
    tok_dev, width_dev = q_pre.shape
    width_all = width_dev * lax.axis_size("head")
    heads_dev = width_dev // HD
    qt_dev = tok_dev // TILE
    remote_count = selected.shape[2]
    factor = 1.0 / math.sqrt(HD)
    q_wide = q_pre.astype(jnp.float32)
    k_wide = k_pre.astype(jnp.float32)
    q_square, k_square = lax.psum(
        (jnp.sum(q_wide * q_wide, axis=1), jnp.sum(k_wide * k_wide, axis=1)), "head"
    )
    q_scale = lax.rsqrt(q_square / width_all + epsilon)[:, None]
    k_scale = lax.rsqrt(k_square / width_all + epsilon)[:, None]
    q_heads = split_heads(rounded(q_wide * q_scale * q_gain), heads_dev)
    k_heads = split_heads(rounded(k_wide * k_scale * k_gain), heads_dev)
    v_heads = split_heads(values, heads_dev)
    g_heads = split_heads(out_grad, heads_dev)
    q_tiles = per_tile(q_heads, qt_dev)
    g_tiles = per_tile(g_heads, qt_dev)
    k_table = k_heads.reshape(heads_dev * qt_dev, TILE, HD)
    v_table = v_heads.reshape(heads_dev * qt_dev, TILE, HD)
    flat_sel = selected[0].reshape(-1)
    n_slot = flat_sel.shape[0]
    capacity = -(-n_slot // (n_ctx - 1))
    n_buffer = n_ctx * capacity
    owners = flat_sel // qt_dev
    head_of = jnp.arange(n_slot, dtype=jnp.int32) // remote_count
    codes = head_of * qt_dev + flat_sel % qt_dev
    matches = (owners[:, None] == jnp.arange(n_ctx, dtype=jnp.int32)[None, :]).astype(jnp.int32)
    ranks = jnp.sum((jnp.cumsum(matches, axis=0) - matches) * matches, axis=1)
    position = owners * capacity + ranks
    placed = position[None, :] == jnp.arange(n_buffer, dtype=jnp.int32)[:, None]
    request = jnp.sum(jnp.where(placed, codes[None, :] + 1, 0), axis=1) - 1
    asked = lax.all_to_all(
        request.reshape(n_ctx, capacity), "ctx", split_axis=0, concat_axis=0, tiled=True
    ).reshape(n_buffer)
    clipped = jnp.maximum(asked, 0)
    taken = (asked[None, :] == jnp.arange(heads_dev * qt_dev, dtype=jnp.int32)[:, None]).astype(
        jnp.float32
    )
    s_near = (
        jnp.einsum("rhqd,hkd->rhqk", q_tiles, k_heads, preferred_element_type=jnp.float32) * factor
    )
    dp_near = jnp.einsum("rhqd,hkd->rhqk", g_tiles, v_heads, preferred_element_type=jnp.float32)
    near_top = jnp.max(s_near, axis=-1)
    outgoing = jnp.stack((k_table[clipped], v_table[clipped]), axis=1).reshape(
        n_ctx, capacity, 2, TILE, HD
    )
    incoming = lax.all_to_all(outgoing, "ctx", split_axis=0, concat_axis=0, tiled=True).reshape(
        n_buffer, 2, TILE, HD
    )
    slot_kv = incoming[position].reshape(heads_dev, remote_count, 2, TILE, HD)
    far_k = slot_kv[:, :, 0]
    far_v = slot_kv[:, :, 1]
    s_far = (
        jnp.einsum("rhqd,hckd->rhqck", q_tiles, far_k, preferred_element_type=jnp.float32) * factor
    )
    dp_far = jnp.einsum("rhqd,hckd->rhqck", g_tiles, far_v, preferred_element_type=jnp.float32)
    row_top = jnp.maximum(near_top, jnp.max(s_far, axis=(-2, -1)))
    totals = jnp.sum(jnp.exp(s_near - row_top[..., None]), axis=-1) + jnp.sum(
        jnp.exp(s_far - row_top[..., None, None]), axis=(-2, -1)
    )
    lse = row_top + jnp.log(totals)
    p_near = jnp.exp(s_near - lse[..., None])
    p_far = jnp.exp(s_far - lse[..., None, None])
    delta = jnp.sum(p_near * dp_near, axis=-1) + jnp.sum(p_far * dp_far, axis=(-2, -1))
    ds_near = rounded(p_near * (dp_near - delta[..., None]) * factor)
    pb_near = rounded(p_near)
    dq_near = jnp.einsum("rhqk,hkd->rhqd", ds_near, k_heads, preferred_element_type=jnp.float32)
    dk_near = jnp.einsum("rhqk,rhqd->hkd", ds_near, q_tiles, preferred_element_type=jnp.float32)
    dv_near = jnp.einsum("rhqk,rhqd->hkd", pb_near, g_tiles, preferred_element_type=jnp.float32)
    dq_near, dk_near, dv_near = (dq_near, dk_near, dv_near)
    ds_far = rounded(p_far * (dp_far - delta[..., None, None]) * factor)
    pb_far = rounded(p_far)
    dq_far = jnp.einsum("rhqck,hckd->rhqd", ds_far, far_k, preferred_element_type=jnp.float32)
    dq_wide = merge_heads(from_tiles(dq_near + dq_far))
    q_dot = jnp.sum(q_gain * dq_wide * q_wide, axis=1)
    dq_wide, q_dot = (dq_wide, q_dot)
    dk_far = jnp.einsum("rhqck,rhqd->hckd", ds_far, q_tiles, preferred_element_type=jnp.float32)
    dv_far = jnp.einsum("rhqck,rhqd->hckd", pb_far, g_tiles, preferred_element_type=jnp.float32)
    grads = jnp.stack((dk_far, dv_far), axis=2).reshape(n_slot, 2, TILE, HD)
    sending = jnp.zeros((n_buffer, 2, TILE, HD), jnp.float32).at[position].set(grads)
    returned = lax.all_to_all(
        sending.reshape(n_ctx, capacity, 2, TILE, HD),
        "ctx",
        split_axis=0,
        concat_axis=0,
        tiled=True,
    ).reshape(n_buffer, 2, TILE, HD)
    far_sums = table_sum(taken, returned, heads_dev, qt_dev)
    dk_wide = merge_heads(dk_near + far_sums[0])
    dv_heads = dv_near + far_sums[1]
    k_dot = jnp.sum(k_gain * dk_wide * k_wide, axis=1)
    q_dot, k_dot = lax.psum((q_dot, k_dot), "head")
    dq_result = finish_norm(q_wide, q_scale, q_gain, dq_wide, q_dot, width_all)
    dk_result = finish_norm(k_wide, k_scale, k_gain, dk_wide, k_dot, width_all)
    return (dq_result, dk_result, merge_heads(dv_heads).astype(jnp.bfloat16))


VMEM_BYTES = 48 * 2**20
PIECES = 8
IN_VMEM = pl.BlockSpec(memory_space=pltpu.VMEM)
IN_SMEM = pl.BlockSpec(memory_space=pltpu.SMEM)


def owners_of(group, n_ctx, heads_dev):
    places = [(4 * head + 1) * n_ctx // (4 * heads_dev) for head in range(heads_dev)]
    return [n_ctx - 1 - place if group % 2 else place for place in places]


def head_at(place, group, n_ctx, heads_dev):
    even = jnp.where(group % 2 == 1, n_ctx - 1 - place, place)
    head = -1
    for index, owner in enumerate(owners_of(0, n_ctx, heads_dev)):
        head = jnp.where(even == owner, index, head)
    return head


def pairs_to_owner(mask, n_ctx, n_head, heads_dev):
    pairs = []
    for group in range(n_head):
        owners = owners_of(group, n_ctx, heads_dev)
        for block in range(n_ctx):
            if block ^ mask in owners:
                pairs.append((block * n_head + group, (block ^ mask) * n_head + group))
    return pairs


def there_masks(n_ctx):
    far = range(n_ctx - 1, n_ctx // 2 - 1, -1)
    near = list(range(n_ctx // 2 - 1, 2, -1)) + [1, 2]
    return [mask for mask in far if mask % 2] + [mask for mask in far if not mask % 2] + near + [0]


def back_masks(n_ctx):
    return list(range(n_ctx // 2 - 1, 0, -1)) + list(range(n_ctx - 1, n_ctx // 2 - 1, -1)) + [0]


def move(masks, arrays, back, n_ctx, n_head, heads_dev):
    moved = []
    for mask, array in zip(masks, arrays):
        pairs = pairs_to_owner(mask, n_ctx, n_head, heads_dev)
        if back:
            pairs = [(b, a) for a, b in pairs]
        moved.append(lax.ppermute(array, ("ctx", "head"), pairs) if mask else array)
    return moved


def column(row, width):
    return jnp.broadcast_to(row, (width, row.shape[1])).T


def row_sums(wide):
    total = wide[:, :HD]
    for at in range(HD, wide.shape[1], HD):
        total = total + wide[:, at : at + HD]
    return jnp.sum(total.T, axis=0, keepdims=True)


def pack_kernel(n_ctx, heads_dev, *refs):
    inputs, square_ref, outs = refs[:4], refs[4], refs[5 : 5 + n_ctx]
    held, sems = refs[5 + n_ctx :]
    rows = held.shape[1]
    piece = rows // PIECES
    block, group = lax.axis_index("ctx"), lax.axis_index("head")

    def copy(at, part):
        place = pl.ds(part * piece, piece)
        return pltpu.make_async_copy(
            inputs[at].at[place, :], held.at[at, place, :], sems.at[at, part]
        )

    for at in range(4):
        for part in range(PIECES):
            copy(at, part).start()
    for at in range(4):
        for part in range(PIECES):
            copy(at, part).wait()
    for mask, out in zip(there_masks(n_ctx), outs):
        head = head_at(block ^ mask, group, n_ctx, heads_dev)

        @pl.when(head >= 0)
        def _(head=head, out=out):
            place = pl.ds(pl.multiple_of(head * HD, HD), HD)
            for at in range(4):
                out[at] = held[at, :, place]

    for at in range(2):
        wide = held[at].astype(jnp.float32)
        square_ref[at : at + 1, :] = row_sums(wide * wide)


def pack(arrays, n_ctx):
    rows, width_dev = arrays[0].shape
    result = pl.pallas_call(
        functools.partial(pack_kernel, n_ctx, width_dev // HD),
        out_shape=[jax.ShapeDtypeStruct((2, rows), jnp.float32)]
        + [jax.ShapeDtypeStruct((4, rows, HD), jnp.bfloat16)] * n_ctx,
        in_specs=[pl.BlockSpec(memory_space=pltpu.HBM)] * 4,
        out_specs=[IN_VMEM] * (n_ctx + 1),
        scratch_shapes=[
            pltpu.VMEM((4, rows, width_dev), jnp.bfloat16),
            pltpu.SemaphoreType.DMA((4, PIECES)),
        ],
        compiler_params=pltpu.CompilerParams(vmem_limit_bytes=VMEM_BYTES),
    )(*[pltpu.with_memory_space_constraint(array, pltpu.HBM) for array in arrays])
    return result[0], result[1:]


def attend_kernel(n_ctx, heads_dev, picks, scale_ref, q_gain, k_gain, *refs):
    messages = dict(zip(there_masks(n_ctx), refs[:n_ctx]))
    outs = dict(zip(back_masks(n_ctx), refs[n_ctx : 2 * n_ctx]))
    scratch = refs[2 * n_ctx :]
    q_ref, qt_ref, g_ref, gt_ref, k_ref, kt_ref, v_ref = scratch[:7]
    dq_ref, dk_ref, dv_ref, kt_picked, k_picked, v_picked = scratch[7:13]
    buffers = (scratch[13:18], scratch[18:23])
    rows = messages[0].shape[1]
    remote_count = picks.shape[1]
    near = rows // TILE
    n_keys = near + remote_count
    in_sublanes = (TILE // 8, 8, rows)
    factor = 1.0 / math.sqrt(HD)
    to_base2 = factor * math.log2(math.e)
    own_block = lax.axis_index("ctx")
    own_head = head_at(own_block, lax.axis_index("head"), n_ctx, heads_dev)

    def rows_of(block):
        return pl.ds(pl.multiple_of(block * rows, rows), rows)

    def places_of(block):
        return [
            pl.ds(pl.multiple_of(block * rows + tile * TILE, TILE), TILE) for tile in range(near)
        ] + [
            pl.ds(pl.multiple_of(picks[block, slot] * TILE, TILE), TILE)
            for slot in range(remote_count)
        ]

    def prepare(mask, q_factor, k_factor):
        message = messages[mask]
        block = own_block ^ mask
        place = rows_of(block)
        q_t = message[0].T.astype(jnp.float32) * scale_ref[block, 0:1, :] * q_factor
        k_t = message[1].T.astype(jnp.float32) * scale_ref[block, 1:2, :] * k_factor
        qt_ref[mask] = q_t.astype(jnp.bfloat16)
        kt_ref[:, place] = k_t.astype(jnp.bfloat16)
        q_ref[mask] = q_t.astype(jnp.bfloat16).T
        k_ref[place, :] = k_t.astype(jnp.bfloat16).T
        v_ref[place, :] = message[2]
        g_ref[mask] = message[3]
        gt_ref[mask] = message[3].T

    def tiles(first, count=1):
        return slice(first * TILE, (first + count) * TILE)

    def scores(mask, group, places, buffer):
        weight_ref, dprob_ref, stat_ref = buffer[:3]
        for slot in group:
            k_picked[tiles(slot), :] = k_ref[places[slot], :]
            v_picked[tiles(slot), :] = v_ref[places[slot], :]
        picked = tiles(group[0], len(group))
        score_all = jnp.dot(
            k_picked[picked, :], qt_ref[mask], preferred_element_type=jnp.float32
        )
        dprob_all = jnp.dot(
            v_picked[picked, :], gt_ref[mask], preferred_element_type=jnp.float32
        )
        for at, slot in enumerate(group):
            score = score_all[tiles(at), :].reshape(in_sublanes)
            dprob = dprob_all[tiles(at), :].reshape(in_sublanes)
            top = jnp.max(score, axis=0)
            weight = jnp.exp2((score - top) * to_base2)
            weight_ref[slot] = weight
            dprob_ref[slot] = dprob
            stat_ref[0, slot] = top * to_base2
            stat_ref[1, slot] = jnp.sum(weight, axis=0)
            stat_ref[2, slot] = jnp.sum(weight * dprob, axis=0)

    def settle(buffer):
        tops, totals, mixed = [buffer[2][at] for at in range(3)]
        highest = jnp.max(jnp.max(tops, axis=0), axis=0, keepdims=True)
        shares = jnp.exp2(tops - highest)
        total = jnp.sum(jnp.sum(shares * totals, axis=0), axis=0, keepdims=True)
        delta = jnp.sum(jnp.sum(shares * mixed, axis=0), axis=0, keepdims=True)
        inverse = 1.0 / total
        return shares * inverse, delta * inverse

    def gradients(group, buffer, shares, delta):
        weight_ref, dprob_ref, _, ds_ref, pb_ref = buffer
        for slot in group:
            prob = weight_ref[slot] * shares[slot]
            dscore = prob * (dprob_ref[slot] - delta)
            pb_ref[tiles(slot), :] = prob.reshape(TILE, rows).astype(jnp.bfloat16)
            ds_ref[tiles(slot), :] = dscore.reshape(TILE, rows).astype(jnp.bfloat16)

    def products(mask, group, places, buffer):
        ds_ref, pb_ref = buffer[3:]
        picked = tiles(group[0], len(group))
        dk = jnp.dot(ds_ref[picked, :], q_ref[mask], preferred_element_type=jnp.float32)
        dv = jnp.dot(pb_ref[picked, :], g_ref[mask], preferred_element_type=jnp.float32)
        for at, slot in enumerate(group):
            dk_ref[places[slot], :] += dk[tiles(at), :]
            dv_ref[places[slot], :] += dv[tiles(at), :]
            kt_picked[:, tiles(slot)] = kt_ref[:, places[slot]]

    def query_gradient(mask, buffer):
        dq_t = jnp.dot(kt_picked[...], buffer[3][...], preferred_element_type=jnp.float32)
        dq_ref[mask] = (dq_t * factor).astype(jnp.bfloat16).T

    groups = [range(first, min(first + 3, n_keys)) for first in range(0, n_keys, 3)]

    def step(now, before, after):
        if now is not None:
            shares, delta = settle(now[1])
        if before is not None:
            before_places = places_of(own_block ^ before[0])
        if after is not None:
            after_places = places_of(own_block ^ after[0])
        for group in groups:
            if before is not None:
                products(before[0], group, before_places, before[1])
            if now is not None:
                gradients(group, now[1], shares, delta)
            if after is not None:
                scores(after[0], group, after_places, after[1])
        if before is not None:
            query_gradient(*before)

    @pl.when(own_head >= 0)
    def _():
        q_factor = column(q_gain[pl.ds(own_head, 1), :], rows)
        k_factor = column(k_gain[pl.ds(own_head, 1), :], rows)
        for mask in range(n_ctx):
            prepare(mask, q_factor, k_factor)
        dk_ref[...] = jnp.zeros_like(dk_ref)
        dv_ref[...] = jnp.zeros_like(dv_ref)
        even, odd = buffers
        step(None, None, (0, even))
        step((0, even), None, (1, odd))

        def two(pair, carry):
            mask = 2 * pair
            step((mask + 1, odd), (mask, even), (mask + 2, even))
            step((mask + 2, even), (mask + 1, odd), (mask + 3, odd))
            return carry

        lax.fori_loop(0, n_ctx // 2 - 1, two, 0)
        step((n_ctx - 1, odd), (n_ctx - 2, even), None)
        step(None, (n_ctx - 1, odd), None)
        for mask in range(n_ctx):
            place = rows_of(own_block ^ mask)
            outs[mask][0] = dq_ref[mask]
            outs[mask][1] = (dk_ref[place, :] * factor).astype(jnp.bfloat16)
            outs[mask][2] = dv_ref[place, :].astype(jnp.bfloat16)


def attend(picks, scales, q_gain, k_gain, messages, n_ctx):
    rows = messages[0].shape[1]
    tokens = n_ctx * rows
    n_keys = rows // TILE + picks.shape[1]
    by_block = pltpu.VMEM((n_ctx, rows, HD), jnp.bfloat16)
    by_block_t = pltpu.VMEM((n_ctx, HD, rows), jnp.bfloat16)
    buffer = [
        pltpu.VMEM((n_keys, TILE // 8, 8, rows), jnp.float32),
        pltpu.VMEM((n_keys, TILE // 8, 8, rows), jnp.float32),
        pltpu.VMEM((3, n_keys, 8, rows), jnp.float32),
        pltpu.VMEM((n_keys * TILE, rows), jnp.bfloat16),
        pltpu.VMEM((n_keys * TILE, rows), jnp.bfloat16),
    ]
    return pl.pallas_call(
        functools.partial(attend_kernel, n_ctx, q_gain.shape[0]),
        out_shape=[jax.ShapeDtypeStruct((3, rows, HD), jnp.bfloat16)] * n_ctx,
        in_specs=[IN_SMEM] + [IN_VMEM] * (3 + n_ctx),
        out_specs=[IN_VMEM] * n_ctx,
        scratch_shapes=[
            by_block,
            by_block_t,
            by_block,
            by_block_t,
            pltpu.VMEM((tokens, HD), jnp.bfloat16),
            pltpu.VMEM((HD, tokens), jnp.bfloat16),
            pltpu.VMEM((tokens, HD), jnp.bfloat16),
            by_block,
            pltpu.VMEM((tokens, HD), jnp.float32),
            pltpu.VMEM((tokens, HD), jnp.float32),
            pltpu.VMEM((HD, n_keys * TILE), jnp.bfloat16),
            pltpu.VMEM((n_keys * TILE, HD), jnp.bfloat16),
            pltpu.VMEM((n_keys * TILE, HD), jnp.bfloat16),
        ]
        + buffer
        + buffer,
        compiler_params=pltpu.CompilerParams(vmem_limit_bytes=VMEM_BYTES),
    )(picks, scales, q_gain, k_gain, *messages)


def gather_kernel(n_ctx, heads_dev, q_ref, k_ref, q_gain, k_gain, *refs):
    slots = refs[:n_ctx]
    dot_ref, dq_ref, dk_ref, dv_out, dv_ref, sems = refs[n_ctx:]
    piece = dv_ref.shape[0] // PIECES
    block, group = lax.axis_index("ctx"), lax.axis_index("head")

    def spread(at, out):
        for mask, slot in zip(back_masks(n_ctx), slots):
            head = head_at(block ^ mask, group, n_ctx, heads_dev)

            @pl.when(head >= 0)
            def _(head=head, slot=slot):
                place = pl.ds(pl.multiple_of(head * HD, HD), HD)
                out[:, place] = slot[at]

    spread(2, dv_ref)
    places = [pl.ds(part * piece, piece) for part in range(PIECES)]
    copies = [
        pltpu.make_async_copy(dv_ref.at[place, :], dv_out.at[place, :], sems.at[part])
        for part, place in enumerate(places)
    ]
    for copy in copies:
        copy.start()
    for at, (wide_ref, pre_ref, gain) in enumerate(
        ((dq_ref, q_ref, q_gain), (dk_ref, k_ref, k_gain))
    ):
        spread(at, wide_ref)
        terms = gain[...] * wide_ref[...].astype(jnp.float32) * pre_ref[...].astype(jnp.float32)
        dot_ref[at : at + 1, :] = row_sums(terms)
    for copy in copies:
        copy.wait()


def finish_kernel(width_all, q_ref, k_ref, q_gain, k_gain, scale_ref, dot_ref, *refs):
    dq_ref, dk_ref, dq_out, dk_out, held, sems = refs
    piece = q_ref.shape[0] // PIECES
    scales = scale_ref[lax.axis_index("ctx")]
    backs = scales**3 * (dot_ref[...] / width_all)
    copies = []
    for at, (pre_ref, gain, grad_ref, out) in enumerate(
        ((q_ref, q_gain, dq_ref, dq_out), (k_ref, k_gain, dk_ref, dk_out))
    ):
        scale_all = column(scales[at : at + 1, :], HD)
        back_all = column(backs[at : at + 1, :], HD)
        for part in range(PIECES):
            rows = slice(part * piece, (part + 1) * piece)
            scale, back = scale_all[rows, :], back_all[rows, :]
            for first in range(0, pre_ref.shape[1], HD):
                place = slice(first, first + HD)
                wide = pre_ref[rows, place].astype(jnp.float32)
                grad = grad_ref[rows, place].astype(jnp.float32)
                result = scale * gain[:, place] * grad - wide * back
                held[at, rows, place] = result.astype(jnp.bfloat16)
            copies.append(
                pltpu.make_async_copy(held.at[at, rows, :], out.at[rows, :], sems.at[at, part])
            )
            copies[-1].start()
    for copy in copies:
        copy.wait()


def heads_to_owners(q_pre, k_pre, values, out_grad, q_gain, k_gain, selected):
    n_ctx = lax.axis_size("ctx")
    n_head = lax.axis_size("head")
    rows, width_dev = q_pre.shape
    width_all = width_dev * n_head
    heads_dev = width_dev // HD
    remote_count = selected.shape[2]
    sizes = (n_ctx, n_head, heads_dev)
    params = pltpu.CompilerParams(vmem_limit_bytes=VMEM_BYTES)

    by_row = jax.ShapeDtypeStruct((2, rows), jnp.float32)
    wide = jax.ShapeDtypeStruct((rows, width_dev), jnp.bfloat16)

    squares, sent = pack((q_pre, k_pre, values, out_grad), n_ctx)
    messages = move(there_masks(n_ctx), sent, False, *sizes)

    wishes = selected[0].reshape(1, -1).astype(jnp.float32)
    wishes = jnp.pad(wishes, ((0, 0), (0, rows - wishes.shape[1])))
    small = jnp.concatenate((lax.psum(squares, "head"), wishes), axis=0)
    small = jnp.broadcast_to(small[None], (n_ctx,) + small.shape)
    small = lax.all_to_all(small, "ctx", split_axis=0, concat_axis=0, tiled=True)
    scales = lax.rsqrt(small[:, :2] / width_all + epsilon)
    own_head = head_at(lax.axis_index("ctx"), lax.axis_index("head"), n_ctx, heads_dev)
    first = jnp.maximum(own_head, 0) * remote_count
    picks = lax.dynamic_slice_in_dim(small[:, 2], first, remote_count, 1).astype(jnp.int32)

    q_gains = q_gain.reshape(heads_dev, HD)
    k_gains = k_gain.reshape(heads_dev, HD)
    results = attend(picks, scales, q_gains, k_gains, messages, n_ctx)
    slots = move(back_masks(n_ctx), results, True, *sizes)

    pres = (q_pre, k_pre, q_gain[None], k_gain[None])
    dots, dq_wide, dk_wide, dv = pl.pallas_call(
        functools.partial(gather_kernel, n_ctx, heads_dev),
        out_shape=[by_row, wide, wide, wide],
        in_specs=[IN_VMEM] * (4 + n_ctx),
        out_specs=[IN_VMEM] * 3 + [pl.BlockSpec(memory_space=pltpu.HBM)],
        scratch_shapes=[
            pltpu.VMEM((rows, width_dev), jnp.bfloat16),
            pltpu.SemaphoreType.DMA((PIECES,)),
        ],
        compiler_params=params,
    )(*pres, *slots)
    dots = lax.psum(dots, "head")
    dq, dk = pl.pallas_call(
        functools.partial(finish_kernel, width_all),
        out_shape=[wide, wide],
        in_specs=[IN_VMEM] * 8,
        out_specs=[pl.BlockSpec(memory_space=pltpu.HBM)] * 2,
        scratch_shapes=[
            pltpu.VMEM((2, rows, width_dev), jnp.bfloat16),
            pltpu.SemaphoreType.DMA((2, PIECES)),
        ],
        compiler_params=params,
    )(*pres, scales, dots, dq_wide, dk_wide)
    return dq, dk, dv


def on_device(q_pre, k_pre, values, out_grad, q_gain, k_gain, selected):
    n_ctx = lax.axis_size("ctx")
    tiles_dev, heads_dev, remote_count = selected.shape
    capacity = -(-heads_dev * remote_count // (n_ctx - 1))
    by_head = (n_ctx - 1) * tiles_dev * 7
    by_tile = (n_ctx - 1) * capacity * 6
    paired = n_ctx & (n_ctx - 1) == 0 and n_ctx >= max(heads_dev, 4)
    plan = heads_to_owners if paired and by_head <= by_tile else tiles_to_queries
    return plan(q_pre, k_pre, values, out_grad, q_gain, k_gain, selected)


def solution(mesh):
    placed = (
        P("ctx", "head"),
        P("ctx", "head"),
        P("ctx", "head"),
        P("ctx", "head"),
        P("head"),
        P("head"),
        P("ctx", "head", None),
    )
    return jax.shard_map(
        on_device,
        mesh=mesh,
        in_specs=placed,
        out_specs=(P("ctx", "head"), P("ctx", "head"), P("ctx", "head")),
        check_vma=False,
    )
```

```python
import functools
import math

import jax
import jax.numpy as jnp
from jax import lax
from jax.experimental import pallas as pl
from jax.experimental.pallas import tpu as pltpu
from jax.sharding import PartitionSpec as P

HD = 128
TILE = 128


epsilon = 1e-06


def split_heads(array, heads_dev):
    return array.reshape(array.shape[0], heads_dev, HD).transpose(1, 0, 2)


def merge_heads(array):
    heads_dev, tok_dev, depth = array.shape
    return array.transpose(1, 0, 2).reshape(tok_dev, heads_dev * depth)


def per_tile(array, qt_dev):
    heads_dev, tok_dev, depth = array.shape
    return array.reshape(heads_dev, qt_dev, TILE, depth).transpose(1, 0, 2, 3)


def from_tiles(array):
    qt_dev, heads_dev, rows_tile, depth = array.shape
    return array.transpose(1, 0, 2, 3).reshape(heads_dev, qt_dev * rows_tile, depth)


def table_sum(taken, pieces, heads_dev, qt_dev):
    flat_pieces = pieces.reshape(pieces.shape[0], -1)
    summed = jnp.dot(
        taken, flat_pieces, precision=lax.Precision.HIGHEST, preferred_element_type=jnp.float32
    )
    summed = summed.reshape(heads_dev, qt_dev, 2, TILE, HD).transpose(2, 0, 1, 3, 4)
    return summed.reshape(2, heads_dev, qt_dev * TILE, HD)


def rounded(array):
    return array.astype(jnp.bfloat16)


def finish_norm(wide, scale, gain, grad, dot_sum, width_all):
    return (scale * gain * grad - wide * scale**3 * (dot_sum / width_all)[:, None]).astype(
        jnp.bfloat16
    )


def tiles_to_queries(q_pre, k_pre, values, out_grad, q_gain, k_gain, selected):
    n_ctx = lax.axis_size("ctx")
    tok_dev, width_dev = q_pre.shape
    width_all = width_dev * lax.axis_size("head")
    heads_dev = width_dev // HD
    qt_dev = tok_dev // TILE
    remote_count = selected.shape[2]
    factor = 1.0 / math.sqrt(HD)
    q_wide = q_pre.astype(jnp.float32)
    k_wide = k_pre.astype(jnp.float32)
    q_square, k_square = lax.psum(
        (jnp.sum(q_wide * q_wide, axis=1), jnp.sum(k_wide * k_wide, axis=1)), "head"
    )
    q_scale = lax.rsqrt(q_square / width_all + epsilon)[:, None]
    k_scale = lax.rsqrt(k_square / width_all + epsilon)[:, None]
    q_heads = split_heads(rounded(q_wide * q_scale * q_gain), heads_dev)
    k_heads = split_heads(rounded(k_wide * k_scale * k_gain), heads_dev)
    v_heads = split_heads(values, heads_dev)
    g_heads = split_heads(out_grad, heads_dev)
    q_tiles = per_tile(q_heads, qt_dev)
    g_tiles = per_tile(g_heads, qt_dev)
    k_table = k_heads.reshape(heads_dev * qt_dev, TILE, HD)
    v_table = v_heads.reshape(heads_dev * qt_dev, TILE, HD)
    flat_sel = selected[0].reshape(-1)
    n_slot = flat_sel.shape[0]
    capacity = -(-n_slot // (n_ctx - 1))
    n_buffer = n_ctx * capacity
    owners = flat_sel // qt_dev
    head_of = jnp.arange(n_slot, dtype=jnp.int32) // remote_count
    codes = head_of * qt_dev + flat_sel % qt_dev
    matches = (owners[:, None] == jnp.arange(n_ctx, dtype=jnp.int32)[None, :]).astype(jnp.int32)
    ranks = jnp.sum((jnp.cumsum(matches, axis=0) - matches) * matches, axis=1)
    position = owners * capacity + ranks
    placed = position[None, :] == jnp.arange(n_buffer, dtype=jnp.int32)[:, None]
    request = jnp.sum(jnp.where(placed, codes[None, :] + 1, 0), axis=1) - 1
    asked = lax.all_to_all(
        request.reshape(n_ctx, capacity), "ctx", split_axis=0, concat_axis=0, tiled=True
    ).reshape(n_buffer)
    clipped = jnp.maximum(asked, 0)
    taken = (asked[None, :] == jnp.arange(heads_dev * qt_dev, dtype=jnp.int32)[:, None]).astype(
        jnp.float32
    )
    s_near = (
        jnp.einsum("rhqd,hkd->rhqk", q_tiles, k_heads, preferred_element_type=jnp.float32) * factor
    )
    dp_near = jnp.einsum("rhqd,hkd->rhqk", g_tiles, v_heads, preferred_element_type=jnp.float32)
    near_top = jnp.max(s_near, axis=-1)
    outgoing = jnp.stack((k_table[clipped], v_table[clipped]), axis=1).reshape(
        n_ctx, capacity, 2, TILE, HD
    )
    incoming = lax.all_to_all(outgoing, "ctx", split_axis=0, concat_axis=0, tiled=True).reshape(
        n_buffer, 2, TILE, HD
    )
    slot_kv = incoming[position].reshape(heads_dev, remote_count, 2, TILE, HD)
    far_k = slot_kv[:, :, 0]
    far_v = slot_kv[:, :, 1]
    s_far = (
        jnp.einsum("rhqd,hckd->rhqck", q_tiles, far_k, preferred_element_type=jnp.float32) * factor
    )
    dp_far = jnp.einsum("rhqd,hckd->rhqck", g_tiles, far_v, preferred_element_type=jnp.float32)
    row_top = jnp.maximum(near_top, jnp.max(s_far, axis=(-2, -1)))
    totals = jnp.sum(jnp.exp(s_near - row_top[..., None]), axis=-1) + jnp.sum(
        jnp.exp(s_far - row_top[..., None, None]), axis=(-2, -1)
    )
    lse = row_top + jnp.log(totals)
    p_near = jnp.exp(s_near - lse[..., None])
    p_far = jnp.exp(s_far - lse[..., None, None])
    delta = jnp.sum(p_near * dp_near, axis=-1) + jnp.sum(p_far * dp_far, axis=(-2, -1))
    ds_near = rounded(p_near * (dp_near - delta[..., None]) * factor)
    pb_near = rounded(p_near)
    dq_near = jnp.einsum("rhqk,hkd->rhqd", ds_near, k_heads, preferred_element_type=jnp.float32)
    dk_near = jnp.einsum("rhqk,rhqd->hkd", ds_near, q_tiles, preferred_element_type=jnp.float32)
    dv_near = jnp.einsum("rhqk,rhqd->hkd", pb_near, g_tiles, preferred_element_type=jnp.float32)
    dq_near, dk_near, dv_near = (dq_near, dk_near, dv_near)
    ds_far = rounded(p_far * (dp_far - delta[..., None, None]) * factor)
    pb_far = rounded(p_far)
    dq_far = jnp.einsum("rhqck,hckd->rhqd", ds_far, far_k, preferred_element_type=jnp.float32)
    dq_wide = merge_heads(from_tiles(dq_near + dq_far))
    q_dot = jnp.sum(q_gain * dq_wide * q_wide, axis=1)
    dq_wide, q_dot = (dq_wide, q_dot)
    dk_far = jnp.einsum("rhqck,rhqd->hckd", ds_far, q_tiles, preferred_element_type=jnp.float32)
    dv_far = jnp.einsum("rhqck,rhqd->hckd", pb_far, g_tiles, preferred_element_type=jnp.float32)
    grads = jnp.stack((dk_far, dv_far), axis=2).reshape(n_slot, 2, TILE, HD)
    sending = jnp.zeros((n_buffer, 2, TILE, HD), jnp.float32).at[position].set(grads)
    returned = lax.all_to_all(
        sending.reshape(n_ctx, capacity, 2, TILE, HD),
        "ctx",
        split_axis=0,
        concat_axis=0,
        tiled=True,
    ).reshape(n_buffer, 2, TILE, HD)
    far_sums = table_sum(taken, returned, heads_dev, qt_dev)
    dk_wide = merge_heads(dk_near + far_sums[0])
    dv_heads = dv_near + far_sums[1]
    k_dot = jnp.sum(k_gain * dk_wide * k_wide, axis=1)
    q_dot, k_dot = lax.psum((q_dot, k_dot), "head")
    dq_result = finish_norm(q_wide, q_scale, q_gain, dq_wide, q_dot, width_all)
    dk_result = finish_norm(k_wide, k_scale, k_gain, dk_wide, k_dot, width_all)
    return (dq_result, dk_result, merge_heads(dv_heads).astype(jnp.bfloat16))


VMEM_BYTES = 48 * 2**20
PIECES = 4
IN_VMEM = pl.BlockSpec(memory_space=pltpu.VMEM)
IN_SMEM = pl.BlockSpec(memory_space=pltpu.SMEM)


def owners_of(group, n_ctx, heads_dev):
    places = [(4 * head + 1) * n_ctx // (4 * heads_dev) for head in range(heads_dev)]
    return [n_ctx - 1 - place if group % 2 else place for place in places]


def head_at(place, group, n_ctx, heads_dev):
    even = jnp.where(group % 2 == 1, n_ctx - 1 - place, place)
    head = -1
    for index, owner in enumerate(owners_of(0, n_ctx, heads_dev)):
        head = jnp.where(even == owner, index, head)
    return head


def pairs_to_owner(mask, n_ctx, n_head, heads_dev):
    pairs = []
    for group in range(n_head):
        owners = owners_of(group, n_ctx, heads_dev)
        for block in range(n_ctx):
            if block ^ mask in owners:
                pairs.append((block * n_head + group, (block ^ mask) * n_head + group))
    return pairs


def there_masks(n_ctx):
    far = range(n_ctx - 1, n_ctx // 2 - 1, -1)
    odd = [mask for mask in far if mask % 2]
    even = [mask for mask in far if not mask % 2]
    return odd + [1] + even + list(range(n_ctx // 2 - 1, 1, -1)) + [0]


def back_masks(n_ctx):
    return list(range(n_ctx // 2 - 1, 0, -1)) + list(range(n_ctx - 1, n_ctx // 2 - 1, -1)) + [0]


def move(masks, arrays, back, n_ctx, n_head, heads_dev):
    moved = []
    for mask, array in zip(masks, arrays):
        pairs = pairs_to_owner(mask, n_ctx, n_head, heads_dev)
        if back:
            pairs = [(b, a) for a, b in pairs]
        moved.append(lax.ppermute(array, ("ctx", "head"), pairs) if mask else array)
    return moved


def column(row, width):
    return jnp.broadcast_to(row, (width, row.shape[1])).T


def row_sums(wide):
    total = wide[:, :HD]
    for at in range(HD, wide.shape[1], HD):
        total = total + wide[:, at : at + HD]
    return jnp.sum(total.T, axis=0, keepdims=True)


def pack_kernel(n_ctx, heads_dev, *refs):
    inputs, square_ref, outs = refs[:4], refs[4], refs[5 : 5 + n_ctx]
    held, sems = refs[5 + n_ctx :]
    rows = held.shape[1]
    piece = rows // PIECES
    block, group = lax.axis_index("ctx"), lax.axis_index("head")

    def copy(at, part):
        place = pl.ds(part * piece, piece)
        return pltpu.make_async_copy(
            inputs[at].at[place, :], held.at[at, place, :], sems.at[at, part]
        )

    for at in range(4):
        for part in range(PIECES):
            copy(at, part).start()
    for at in range(4):
        for part in range(PIECES):
            copy(at, part).wait()
    for mask, out in zip(there_masks(n_ctx), outs):
        head = head_at(block ^ mask, group, n_ctx, heads_dev)

        @pl.when(head >= 0)
        def _(head=head, out=out):
            place = pl.ds(pl.multiple_of(head * HD, HD), HD)
            for at in range(4):
                out[at] = held[at, :, place]

    for at in range(2):
        wide = held[at].astype(jnp.float32)
        square_ref[at : at + 1, :] = row_sums(wide * wide)


def pack(arrays, n_ctx):
    rows, width_dev = arrays[0].shape
    result = pl.pallas_call(
        functools.partial(pack_kernel, n_ctx, width_dev // HD),
        out_shape=[jax.ShapeDtypeStruct((2, rows), jnp.float32)]
        + [jax.ShapeDtypeStruct((4, rows, HD), jnp.bfloat16)] * n_ctx,
        in_specs=[pl.BlockSpec(memory_space=pltpu.HBM)] * 4,
        out_specs=[IN_VMEM] * (n_ctx + 1),
        scratch_shapes=[
            pltpu.VMEM((4, rows, width_dev), jnp.bfloat16),
            pltpu.SemaphoreType.DMA((4, PIECES)),
        ],
        compiler_params=pltpu.CompilerParams(vmem_limit_bytes=VMEM_BYTES),
    )(*[pltpu.with_memory_space_constraint(array, pltpu.HBM) for array in arrays])
    return result[0], result[1:]


def attend_kernel(n_ctx, heads_dev, picks, scale_ref, q_gain, k_gain, *refs):
    messages = dict(zip(there_masks(n_ctx), refs[:n_ctx]))
    outs = dict(zip(back_masks(n_ctx), refs[n_ctx : 2 * n_ctx]))
    scratch = refs[2 * n_ctx :]
    q_ref, qt_ref, g_ref, gt_ref, k_ref, kt_ref, v_ref = scratch[:7]
    dq_ref, dk_ref, dv_ref, kt_picked, k_picked, v_picked = scratch[7:13]
    buffers = (scratch[13:18], scratch[18:23])
    rows = messages[0].shape[1]
    remote_count = picks.shape[1]
    near = rows // TILE
    n_keys = near + remote_count
    in_sublanes = (TILE // 8, 8, rows)
    factor = 1.0 / math.sqrt(HD)
    to_base2 = factor * math.log2(math.e)
    own_block = lax.axis_index("ctx")
    own_head = head_at(own_block, lax.axis_index("head"), n_ctx, heads_dev)

    def rows_of(block):
        return pl.ds(pl.multiple_of(block * rows, rows), rows)

    def places_of(block):
        return [
            pl.ds(pl.multiple_of(block * rows + tile * TILE, TILE), TILE) for tile in range(near)
        ] + [
            pl.ds(pl.multiple_of(picks[block, slot] * TILE, TILE), TILE)
            for slot in range(remote_count)
        ]

    def prepare(mask, q_factor, k_factor):
        message = messages[mask]
        block = own_block ^ mask
        place = rows_of(block)
        q_t = message[0].T.astype(jnp.float32) * scale_ref[block, 0:1, :] * q_factor
        k_t = message[1].T.astype(jnp.float32) * scale_ref[block, 1:2, :] * k_factor
        qt_ref[mask] = q_t.astype(jnp.bfloat16)
        kt_ref[:, place] = k_t.astype(jnp.bfloat16)
        q_ref[mask] = q_t.astype(jnp.bfloat16).T
        k_ref[place, :] = k_t.astype(jnp.bfloat16).T
        v_ref[place, :] = message[2]
        g_ref[mask] = message[3]
        gt_ref[mask] = message[3].T

    def tiles(first, count=1):
        return slice(first * TILE, (first + count) * TILE)

    def scores(mask, group, places, buffer):
        weight_ref, dprob_ref, stat_ref = buffer[:3]
        for slot in group:
            k_picked[tiles(slot), :] = k_ref[places[slot], :]
            v_picked[tiles(slot), :] = v_ref[places[slot], :]
        picked = tiles(group[0], len(group))
        score_all = jnp.dot(
            k_picked[picked, :], qt_ref[mask], preferred_element_type=jnp.float32
        )
        dprob_all = jnp.dot(
            v_picked[picked, :], gt_ref[mask], preferred_element_type=jnp.float32
        )
        for at, slot in enumerate(group):
            score = score_all[tiles(at), :].reshape(in_sublanes)
            dprob = dprob_all[tiles(at), :].reshape(in_sublanes)
            top = jnp.max(score, axis=0)
            weight = jnp.exp2((score - top) * to_base2)
            weight_ref[slot] = weight
            dprob_ref[slot] = dprob
            stat_ref[0, slot] = top * to_base2
            stat_ref[1, slot] = jnp.sum(weight, axis=0)
            stat_ref[2, slot] = jnp.sum(weight * dprob, axis=0)

    def settle(buffer):
        tops, totals, mixed = [buffer[2][at] for at in range(3)]
        highest = jnp.max(jnp.max(tops, axis=0), axis=0, keepdims=True)
        shares = jnp.exp2(tops - highest)
        total = jnp.sum(jnp.sum(shares * totals, axis=0), axis=0, keepdims=True)
        delta = jnp.sum(jnp.sum(shares * mixed, axis=0), axis=0, keepdims=True)
        inverse = 1.0 / total
        return shares * inverse, delta * inverse

    def gradients(group, buffer, shares, delta):
        weight_ref, dprob_ref, _, ds_ref, pb_ref = buffer
        for slot in group:
            prob = weight_ref[slot] * shares[slot]
            dscore = prob * (dprob_ref[slot] - delta)
            pb_ref[tiles(slot), :] = prob.reshape(TILE, rows).astype(jnp.bfloat16)
            ds_ref[tiles(slot), :] = dscore.reshape(TILE, rows).astype(jnp.bfloat16)

    def products(mask, group, places, buffer):
        ds_ref, pb_ref = buffer[3:]
        picked = tiles(group[0], len(group))
        dk = jnp.dot(ds_ref[picked, :], q_ref[mask], preferred_element_type=jnp.float32)
        dv = jnp.dot(pb_ref[picked, :], g_ref[mask], preferred_element_type=jnp.float32)
        for at, slot in enumerate(group):
            dk_ref[places[slot], :] += dk[tiles(at), :]
            dv_ref[places[slot], :] += dv[tiles(at), :]
            kt_picked[:, tiles(slot)] = kt_ref[:, places[slot]]

    def query_gradient(mask, buffer):
        dq_t = jnp.dot(kt_picked[...], buffer[3][...], preferred_element_type=jnp.float32)
        dq_ref[mask] = (dq_t * factor).astype(jnp.bfloat16).T

    groups = [range(first, min(first + 3, n_keys)) for first in range(0, n_keys, 3)]

    def step(now, before, after):
        if now is not None:
            shares, delta = settle(now[1])
        if before is not None:
            before_places = places_of(own_block ^ before[0])
        if after is not None:
            after_places = places_of(own_block ^ after[0])
        for group in groups:
            if before is not None:
                products(before[0], group, before_places, before[1])
            if now is not None:
                gradients(group, now[1], shares, delta)
            if after is not None:
                scores(after[0], group, after_places, after[1])
        if before is not None:
            query_gradient(*before)

    @pl.when(own_head >= 0)
    def _():
        q_factor = column(q_gain[pl.ds(own_head, 1), :], rows)
        k_factor = column(k_gain[pl.ds(own_head, 1), :], rows)
        for mask in range(n_ctx):
            prepare(mask, q_factor, k_factor)
        dk_ref[...] = jnp.zeros_like(dk_ref)
        dv_ref[...] = jnp.zeros_like(dv_ref)
        even, odd = buffers
        step(None, None, (0, even))
        step((0, even), None, (1, odd))

        def two(pair, carry):
            mask = 2 * pair
            step((mask + 1, odd), (mask, even), (mask + 2, even))
            step((mask + 2, even), (mask + 1, odd), (mask + 3, odd))
            return carry

        lax.fori_loop(0, n_ctx // 2 - 1, two, 0)
        step((n_ctx - 1, odd), (n_ctx - 2, even), None)
        step(None, (n_ctx - 1, odd), None)
        for mask in range(n_ctx):
            place = rows_of(own_block ^ mask)
            outs[mask][0] = dq_ref[mask]
            outs[mask][1] = (dk_ref[place, :] * factor).astype(jnp.bfloat16)
            outs[mask][2] = dv_ref[place, :].astype(jnp.bfloat16)


def attend(picks, scales, q_gain, k_gain, messages, n_ctx):
    rows = messages[0].shape[1]
    tokens = n_ctx * rows
    n_keys = rows // TILE + picks.shape[1]
    by_block = pltpu.VMEM((n_ctx, rows, HD), jnp.bfloat16)
    by_block_t = pltpu.VMEM((n_ctx, HD, rows), jnp.bfloat16)
    buffer = [
        pltpu.VMEM((n_keys, TILE // 8, 8, rows), jnp.float32),
        pltpu.VMEM((n_keys, TILE // 8, 8, rows), jnp.float32),
        pltpu.VMEM((3, n_keys, 8, rows), jnp.float32),
        pltpu.VMEM((n_keys * TILE, rows), jnp.bfloat16),
        pltpu.VMEM((n_keys * TILE, rows), jnp.bfloat16),
    ]
    return pl.pallas_call(
        functools.partial(attend_kernel, n_ctx, q_gain.shape[0]),
        out_shape=[jax.ShapeDtypeStruct((3, rows, HD), jnp.bfloat16)] * n_ctx,
        in_specs=[IN_SMEM] + [IN_VMEM] * (3 + n_ctx),
        out_specs=[IN_VMEM] * n_ctx,
        scratch_shapes=[
            by_block,
            by_block_t,
            by_block,
            by_block_t,
            pltpu.VMEM((tokens, HD), jnp.bfloat16),
            pltpu.VMEM((HD, tokens), jnp.bfloat16),
            pltpu.VMEM((tokens, HD), jnp.bfloat16),
            by_block,
            pltpu.VMEM((tokens, HD), jnp.float32),
            pltpu.VMEM((tokens, HD), jnp.float32),
            pltpu.VMEM((HD, n_keys * TILE), jnp.bfloat16),
            pltpu.VMEM((n_keys * TILE, HD), jnp.bfloat16),
            pltpu.VMEM((n_keys * TILE, HD), jnp.bfloat16),
        ]
        + buffer
        + buffer,
        compiler_params=pltpu.CompilerParams(vmem_limit_bytes=VMEM_BYTES),
    )(picks, scales, q_gain, k_gain, *messages)


def gather_kernel(n_ctx, heads_dev, q_ref, k_ref, q_gain, k_gain, *refs):
    slots = refs[:n_ctx]
    dot_ref, dq_ref, dk_ref, dv_out, dv_ref, sems = refs[n_ctx:]
    piece = dv_ref.shape[0] // PIECES
    block, group = lax.axis_index("ctx"), lax.axis_index("head")

    def spread(at, out):
        for mask, slot in zip(back_masks(n_ctx), slots):
            head = head_at(block ^ mask, group, n_ctx, heads_dev)

            @pl.when(head >= 0)
            def _(head=head, slot=slot):
                place = pl.ds(pl.multiple_of(head * HD, HD), HD)
                out[:, place] = slot[at]

    spread(2, dv_ref)
    places = [pl.ds(part * piece, piece) for part in range(PIECES)]
    copies = [
        pltpu.make_async_copy(dv_ref.at[place, :], dv_out.at[place, :], sems.at[part])
        for part, place in enumerate(places)
    ]
    for copy in copies:
        copy.start()
    for at, (wide_ref, pre_ref, gain) in enumerate(
        ((dq_ref, q_ref, q_gain), (dk_ref, k_ref, k_gain))
    ):
        spread(at, wide_ref)
        terms = gain[...] * wide_ref[...].astype(jnp.float32) * pre_ref[...].astype(jnp.float32)
        dot_ref[at : at + 1, :] = row_sums(terms)
    for copy in copies:
        copy.wait()


def finish_kernel(width_all, q_ref, k_ref, q_gain, k_gain, scale_ref, dot_ref, *refs):
    dq_ref, dk_ref, dq_out, dk_out, held, sems = refs
    piece = q_ref.shape[0] // PIECES
    scales = scale_ref[lax.axis_index("ctx")]
    backs = scales**3 * (dot_ref[...] / width_all)
    copies = []
    for at, (pre_ref, gain, grad_ref, out) in enumerate(
        ((q_ref, q_gain, dq_ref, dq_out), (k_ref, k_gain, dk_ref, dk_out))
    ):
        scale_all = column(scales[at : at + 1, :], HD)
        back_all = column(backs[at : at + 1, :], HD)
        for part in range(PIECES):
            rows = slice(part * piece, (part + 1) * piece)
            scale, back = scale_all[rows, :], back_all[rows, :]
            for first in range(0, pre_ref.shape[1], HD):
                place = slice(first, first + HD)
                wide = pre_ref[rows, place].astype(jnp.float32)
                grad = grad_ref[rows, place].astype(jnp.float32)
                result = scale * gain[:, place] * grad - wide * back
                held[at, rows, place] = result.astype(jnp.bfloat16)
            copies.append(
                pltpu.make_async_copy(held.at[at, rows, :], out.at[rows, :], sems.at[at, part])
            )
            copies[-1].start()
    for copy in copies:
        copy.wait()


def heads_to_owners(q_pre, k_pre, values, out_grad, q_gain, k_gain, selected):
    n_ctx = lax.axis_size("ctx")
    n_head = lax.axis_size("head")
    rows, width_dev = q_pre.shape
    width_all = width_dev * n_head
    heads_dev = width_dev // HD
    remote_count = selected.shape[2]
    sizes = (n_ctx, n_head, heads_dev)
    params = pltpu.CompilerParams(vmem_limit_bytes=VMEM_BYTES)

    by_row = jax.ShapeDtypeStruct((2, rows), jnp.float32)
    wide = jax.ShapeDtypeStruct((rows, width_dev), jnp.bfloat16)

    squares, sent = pack((q_pre, k_pre, values, out_grad), n_ctx)
    messages = move(there_masks(n_ctx), sent, False, *sizes)

    wishes = selected[0].reshape(1, -1).astype(jnp.float32)
    wishes = jnp.pad(wishes, ((0, 0), (0, rows - wishes.shape[1])))
    small = jnp.concatenate((lax.psum(squares, "head"), wishes), axis=0)
    small = jnp.broadcast_to(small[None], (n_ctx,) + small.shape)
    small = lax.all_to_all(small, "ctx", split_axis=0, concat_axis=0, tiled=True)
    scales = lax.rsqrt(small[:, :2] / width_all + epsilon)
    own_head = head_at(lax.axis_index("ctx"), lax.axis_index("head"), n_ctx, heads_dev)
    first = jnp.maximum(own_head, 0) * remote_count
    picks = lax.dynamic_slice_in_dim(small[:, 2], first, remote_count, 1).astype(jnp.int32)

    q_gains = q_gain.reshape(heads_dev, HD)
    k_gains = k_gain.reshape(heads_dev, HD)
    results = attend(picks, scales, q_gains, k_gains, messages, n_ctx)
    slots = move(back_masks(n_ctx), results, True, *sizes)

    pres = (q_pre, k_pre, q_gain[None], k_gain[None])
    dots, dq_wide, dk_wide, dv = pl.pallas_call(
        functools.partial(gather_kernel, n_ctx, heads_dev),
        out_shape=[by_row, wide, wide, wide],
        in_specs=[IN_VMEM] * (4 + n_ctx),
        out_specs=[IN_VMEM] * 3 + [pl.BlockSpec(memory_space=pltpu.HBM)],
        scratch_shapes=[
            pltpu.VMEM((rows, width_dev), jnp.bfloat16),
            pltpu.SemaphoreType.DMA((PIECES,)),
        ],
        compiler_params=params,
    )(*pres, *slots)
    dots = lax.psum(dots, "head")
    dq, dk = pl.pallas_call(
        functools.partial(finish_kernel, width_all),
        out_shape=[wide, wide],
        in_specs=[IN_VMEM] * 8,
        out_specs=[pl.BlockSpec(memory_space=pltpu.HBM)] * 2,
        scratch_shapes=[
            pltpu.VMEM((2, rows, width_dev), jnp.bfloat16),
            pltpu.SemaphoreType.DMA((2, PIECES)),
        ],
        compiler_params=params,
    )(*pres, scales, dots, dq_wide, dk_wide)
    return dq, dk, dv


def on_device(q_pre, k_pre, values, out_grad, q_gain, k_gain, selected):
    n_ctx = lax.axis_size("ctx")
    tiles_dev, heads_dev, remote_count = selected.shape
    capacity = -(-heads_dev * remote_count // (n_ctx - 1))
    by_head = (n_ctx - 1) * tiles_dev * 7
    by_tile = (n_ctx - 1) * capacity * 6
    paired = n_ctx & (n_ctx - 1) == 0 and n_ctx >= max(heads_dev, 4)
    plan = heads_to_owners if paired and by_head <= by_tile else tiles_to_queries
    return plan(q_pre, k_pre, values, out_grad, q_gain, k_gain, selected)


def solution(mesh):
    placed = (
        P("ctx", "head"),
        P("ctx", "head"),
        P("ctx", "head"),
        P("ctx", "head"),
        P("head"),
        P("head"),
        P("ctx", "head", None),
    )
    return jax.shard_map(
        on_device,
        mesh=mesh,
        in_specs=placed,
        out_specs=(P("ctx", "head"), P("ctx", "head"), P("ctx", "head")),
        check_vma=False,
    )
```

```python
import functools
import math

import jax
import jax.numpy as jnp
from jax import lax
from jax.experimental import pallas as pl
from jax.experimental.pallas import tpu as pltpu
from jax.sharding import PartitionSpec as P

HD = 128
TILE = 128


epsilon = 1e-06


def split_heads(array, heads_dev):
    return array.reshape(array.shape[0], heads_dev, HD).transpose(1, 0, 2)


def merge_heads(array):
    heads_dev, tok_dev, depth = array.shape
    return array.transpose(1, 0, 2).reshape(tok_dev, heads_dev * depth)


def per_tile(array, qt_dev):
    heads_dev, tok_dev, depth = array.shape
    return array.reshape(heads_dev, qt_dev, TILE, depth).transpose(1, 0, 2, 3)


def from_tiles(array):
    qt_dev, heads_dev, rows_tile, depth = array.shape
    return array.transpose(1, 0, 2, 3).reshape(heads_dev, qt_dev * rows_tile, depth)


def table_sum(taken, pieces, heads_dev, qt_dev):
    flat_pieces = pieces.reshape(pieces.shape[0], -1)
    summed = jnp.dot(
        taken, flat_pieces, precision=lax.Precision.HIGHEST, preferred_element_type=jnp.float32
    )
    summed = summed.reshape(heads_dev, qt_dev, 2, TILE, HD).transpose(2, 0, 1, 3, 4)
    return summed.reshape(2, heads_dev, qt_dev * TILE, HD)


def rounded(array):
    return array.astype(jnp.bfloat16)


def finish_norm(wide, scale, gain, grad, dot_sum, width_all):
    return (scale * gain * grad - wide * scale**3 * (dot_sum / width_all)[:, None]).astype(
        jnp.bfloat16
    )


def tiles_to_queries(q_pre, k_pre, values, out_grad, q_gain, k_gain, selected):
    n_ctx = lax.axis_size("ctx")
    tok_dev, width_dev = q_pre.shape
    width_all = width_dev * lax.axis_size("head")
    heads_dev = width_dev // HD
    qt_dev = tok_dev // TILE
    remote_count = selected.shape[2]
    factor = 1.0 / math.sqrt(HD)
    q_wide = q_pre.astype(jnp.float32)
    k_wide = k_pre.astype(jnp.float32)
    q_square, k_square = lax.psum(
        (jnp.sum(q_wide * q_wide, axis=1), jnp.sum(k_wide * k_wide, axis=1)), "head"
    )
    q_scale = lax.rsqrt(q_square / width_all + epsilon)[:, None]
    k_scale = lax.rsqrt(k_square / width_all + epsilon)[:, None]
    q_heads = split_heads(rounded(q_wide * q_scale * q_gain), heads_dev)
    k_heads = split_heads(rounded(k_wide * k_scale * k_gain), heads_dev)
    v_heads = split_heads(values, heads_dev)
    g_heads = split_heads(out_grad, heads_dev)
    q_tiles = per_tile(q_heads, qt_dev)
    g_tiles = per_tile(g_heads, qt_dev)
    k_table = k_heads.reshape(heads_dev * qt_dev, TILE, HD)
    v_table = v_heads.reshape(heads_dev * qt_dev, TILE, HD)
    flat_sel = selected[0].reshape(-1)
    n_slot = flat_sel.shape[0]
    capacity = -(-n_slot // (n_ctx - 1))
    n_buffer = n_ctx * capacity
    owners = flat_sel // qt_dev
    head_of = jnp.arange(n_slot, dtype=jnp.int32) // remote_count
    codes = head_of * qt_dev + flat_sel % qt_dev
    matches = (owners[:, None] == jnp.arange(n_ctx, dtype=jnp.int32)[None, :]).astype(jnp.int32)
    ranks = jnp.sum((jnp.cumsum(matches, axis=0) - matches) * matches, axis=1)
    position = owners * capacity + ranks
    placed = position[None, :] == jnp.arange(n_buffer, dtype=jnp.int32)[:, None]
    request = jnp.sum(jnp.where(placed, codes[None, :] + 1, 0), axis=1) - 1
    asked = lax.all_to_all(
        request.reshape(n_ctx, capacity), "ctx", split_axis=0, concat_axis=0, tiled=True
    ).reshape(n_buffer)
    clipped = jnp.maximum(asked, 0)
    taken = (asked[None, :] == jnp.arange(heads_dev * qt_dev, dtype=jnp.int32)[:, None]).astype(
        jnp.float32
    )
    s_near = (
        jnp.einsum("rhqd,hkd->rhqk", q_tiles, k_heads, preferred_element_type=jnp.float32) * factor
    )
    dp_near = jnp.einsum("rhqd,hkd->rhqk", g_tiles, v_heads, preferred_element_type=jnp.float32)
    near_top = jnp.max(s_near, axis=-1)
    outgoing = jnp.stack((k_table[clipped], v_table[clipped]), axis=1).reshape(
        n_ctx, capacity, 2, TILE, HD
    )
    incoming = lax.all_to_all(outgoing, "ctx", split_axis=0, concat_axis=0, tiled=True).reshape(
        n_buffer, 2, TILE, HD
    )
    slot_kv = incoming[position].reshape(heads_dev, remote_count, 2, TILE, HD)
    far_k = slot_kv[:, :, 0]
    far_v = slot_kv[:, :, 1]
    s_far = (
        jnp.einsum("rhqd,hckd->rhqck", q_tiles, far_k, preferred_element_type=jnp.float32) * factor
    )
    dp_far = jnp.einsum("rhqd,hckd->rhqck", g_tiles, far_v, preferred_element_type=jnp.float32)
    row_top = jnp.maximum(near_top, jnp.max(s_far, axis=(-2, -1)))
    totals = jnp.sum(jnp.exp(s_near - row_top[..., None]), axis=-1) + jnp.sum(
        jnp.exp(s_far - row_top[..., None, None]), axis=(-2, -1)
    )
    lse = row_top + jnp.log(totals)
    p_near = jnp.exp(s_near - lse[..., None])
    p_far = jnp.exp(s_far - lse[..., None, None])
    delta = jnp.sum(p_near * dp_near, axis=-1) + jnp.sum(p_far * dp_far, axis=(-2, -1))
    ds_near = rounded(p_near * (dp_near - delta[..., None]) * factor)
    pb_near = rounded(p_near)
    dq_near = jnp.einsum("rhqk,hkd->rhqd", ds_near, k_heads, preferred_element_type=jnp.float32)
    dk_near = jnp.einsum("rhqk,rhqd->hkd", ds_near, q_tiles, preferred_element_type=jnp.float32)
    dv_near = jnp.einsum("rhqk,rhqd->hkd", pb_near, g_tiles, preferred_element_type=jnp.float32)
    dq_near, dk_near, dv_near = (dq_near, dk_near, dv_near)
    ds_far = rounded(p_far * (dp_far - delta[..., None, None]) * factor)
    pb_far = rounded(p_far)
    dq_far = jnp.einsum("rhqck,hckd->rhqd", ds_far, far_k, preferred_element_type=jnp.float32)
    dq_wide = merge_heads(from_tiles(dq_near + dq_far))
    q_dot = jnp.sum(q_gain * dq_wide * q_wide, axis=1)
    dq_wide, q_dot = (dq_wide, q_dot)
    dk_far = jnp.einsum("rhqck,rhqd->hckd", ds_far, q_tiles, preferred_element_type=jnp.float32)
    dv_far = jnp.einsum("rhqck,rhqd->hckd", pb_far, g_tiles, preferred_element_type=jnp.float32)
    grads = jnp.stack((dk_far, dv_far), axis=2).reshape(n_slot, 2, TILE, HD)
    sending = jnp.zeros((n_buffer, 2, TILE, HD), jnp.float32).at[position].set(grads)
    returned = lax.all_to_all(
        sending.reshape(n_ctx, capacity, 2, TILE, HD),
        "ctx",
        split_axis=0,
        concat_axis=0,
        tiled=True,
    ).reshape(n_buffer, 2, TILE, HD)
    far_sums = table_sum(taken, returned, heads_dev, qt_dev)
    dk_wide = merge_heads(dk_near + far_sums[0])
    dv_heads = dv_near + far_sums[1]
    k_dot = jnp.sum(k_gain * dk_wide * k_wide, axis=1)
    q_dot, k_dot = lax.psum((q_dot, k_dot), "head")
    dq_result = finish_norm(q_wide, q_scale, q_gain, dq_wide, q_dot, width_all)
    dk_result = finish_norm(k_wide, k_scale, k_gain, dk_wide, k_dot, width_all)
    return (dq_result, dk_result, merge_heads(dv_heads).astype(jnp.bfloat16))


VMEM_BYTES = 48 * 2**20
PIECES = 4
NOTE_ROWS = 32
IN_VMEM = pl.BlockSpec(memory_space=pltpu.VMEM)
IN_SMEM = pl.BlockSpec(memory_space=pltpu.SMEM)


def owners_of(group, n_ctx, heads_dev):
    places = [(4 * head + 1) * n_ctx // (4 * heads_dev) for head in range(heads_dev)]
    return [n_ctx - 1 - place if group % 2 else place for place in places]


def head_at(place, group, n_ctx, heads_dev):
    even = jnp.where(group % 2 == 1, n_ctx - 1 - place, place)
    head = -1
    for index, owner in enumerate(owners_of(0, n_ctx, heads_dev)):
        head = jnp.where(even == owner, index, head)
    return head


def pairs_to_owner(mask, n_ctx, n_head, heads_dev):
    pairs = []
    for group in range(n_head):
        owners = owners_of(group, n_ctx, heads_dev)
        for block in range(n_ctx):
            if block ^ mask in owners:
                pairs.append((block * n_head + group, (block ^ mask) * n_head + group))
    return pairs


def there_masks(n_ctx):
    return list(range(n_ctx - 1, -1, -1))


def back_masks(n_ctx):
    return [2, 1] + list(range(n_ctx - 1, 2, -1)) + [0]


def move(masks, arrays, back, n_ctx, n_head, heads_dev):
    moved = []
    for mask, array in zip(masks, arrays):
        pairs = pairs_to_owner(mask, n_ctx, n_head, heads_dev)
        if back:
            pairs = [(b, a) for a, b in pairs]
        moved.append(lax.ppermute(array, ("ctx", "head"), pairs) if mask else array)
    return moved


def column(row, width):
    return jnp.broadcast_to(row, (width, row.shape[1])).T


def row_sums(wide):
    total = wide[:, :HD]
    for at in range(HD, wide.shape[1], HD):
        total = total + wide[:, at : at + HD]
    return jnp.sum(total.T, axis=0, keepdims=True)


def pack_kernel(n_ctx, heads_dev, *refs):
    inputs, square_ref, outs = refs[:4], refs[4], refs[5 : 5 + n_ctx]
    held, sems = refs[5 + n_ctx :]
    rows = held.shape[1]
    piece = rows // PIECES
    block, group = lax.axis_index("ctx"), lax.axis_index("head")

    def copy(at, part):
        place = pl.ds(part * piece, piece)
        return pltpu.make_async_copy(
            inputs[at].at[place, :], held.at[at, place, :], sems.at[at, part]
        )

    for at in range(4):
        for part in range(PIECES):
            copy(at, part).start()
    for at in range(4):
        for part in range(PIECES):
            copy(at, part).wait()
    for mask, out in zip(there_masks(n_ctx), outs):
        head = head_at(block ^ mask, group, n_ctx, heads_dev)

        @pl.when(head >= 0)
        def _(head=head, out=out):
            place = pl.ds(pl.multiple_of(head * HD, HD), HD)
            for at in range(4):
                out[at * rows : (at + 1) * rows, :] = held[at, :, place]

    for at in range(2):
        wide = held[at].astype(jnp.float32)
        square_ref[at : at + 1, :] = row_sums(wide * wide)


def pack(arrays, n_ctx):
    rows, width_dev = arrays[0].shape
    result = pl.pallas_call(
        functools.partial(pack_kernel, n_ctx, width_dev // HD),
        out_shape=[jax.ShapeDtypeStruct((2, rows), jnp.float32)]
        + [jax.ShapeDtypeStruct((4 * rows + NOTE_ROWS, HD), jnp.bfloat16)] * n_ctx,
        in_specs=[pl.BlockSpec(memory_space=pltpu.HBM)] * 4,
        out_specs=[IN_VMEM] * (n_ctx + 1),
        scratch_shapes=[
            pltpu.VMEM((4, rows, width_dev), jnp.bfloat16),
            pltpu.SemaphoreType.DMA((4, PIECES)),
        ],
        compiler_params=pltpu.CompilerParams(vmem_limit_bytes=VMEM_BYTES),
    )(*[pltpu.with_memory_space_constraint(array, pltpu.HBM) for array in arrays])
    return result[0], result[1:]


def row_scales(squares, width_all):
    return lax.rsqrt(squares / width_all + epsilon)


def note_kernel(width_all, own_ref, other_ref, *refs):
    count = (len(refs) - 1) // 2
    outs, note = refs[count:-1], refs[-1]
    for at, ref in enumerate((own_ref, other_ref)):
        scales = row_scales(ref[0:2, :], width_all)
        for half in range(2):
            first = 4 * at + 2 * half
            note[first : first + 2, :] = scales[:, half * HD : (half + 1) * HD]
    scales = note[0:8, :]
    high = scales.astype(jnp.bfloat16).astype(jnp.float32)
    middle = (scales - high).astype(jnp.bfloat16).astype(jnp.float32)
    note[0:8, :] = high
    note[8:16, :] = middle
    note[16:24, :] = scales - high - middle
    note[24:32, :] = jnp.zeros((8, HD), jnp.float32)
    note[24:25, :] = own_ref[2:3, :HD]
    note[25:26, :] = other_ref[2:3, :HD]
    for out in outs:
        out[-NOTE_ROWS:, :] = note[...].astype(jnp.bfloat16)


def add_note(own, other, messages, width_all):
    count = len(messages)
    return pl.pallas_call(
        functools.partial(note_kernel, width_all),
        out_shape=[jax.ShapeDtypeStruct(array.shape, array.dtype) for array in messages],
        in_specs=[IN_VMEM] * (2 + count),
        out_specs=[IN_VMEM] * count,
        scratch_shapes=[pltpu.VMEM((NOTE_ROWS, HD), jnp.float32)],
        input_output_aliases={2 + at: at for at in range(count)},
        compiler_params=pltpu.CompilerParams(vmem_limit_bytes=VMEM_BYTES),
    )(own, other, *messages)


def attend_kernel(n_ctx, heads_dev, remote_count, q_gain, k_gain, *refs):
    messages = dict(zip(there_masks(n_ctx), refs[:n_ctx]))
    outs = dict(zip(back_masks(n_ctx), refs[n_ctx : 2 * n_ctx]))
    scratch = refs[2 * n_ctx :]
    q_ref, qt_ref, g_ref, gt_ref, k_ref, kt_ref, v_ref = scratch[:7]
    dq_ref, dk_ref, dv_ref, kt_picked, k_picked, v_picked = scratch[7:13]
    scale_ref, picks_ref, picks, sem = scratch[13:17]
    buffers = (scratch[17:22], scratch[22:27])
    rows = q_ref.shape[1]
    half = n_ctx // 2
    near = rows // TILE
    n_keys = near + remote_count
    in_sublanes = (TILE // 8, 8, rows)
    factor = 1.0 / math.sqrt(HD)
    to_base2 = factor * math.log2(math.e)
    own_block = lax.axis_index("ctx")
    own_head = head_at(own_block, lax.axis_index("head"), n_ctx, heads_dev)

    def rows_of(block):
        return pl.ds(pl.multiple_of(block * rows, rows), rows)

    def places_of(mask):
        block = own_block ^ mask
        return [
            pl.ds(pl.multiple_of(block * rows + tile * TILE, TILE), TILE) for tile in range(near)
        ] + [
            pl.ds(pl.multiple_of(picks[mask, own_head * remote_count + slot] * TILE, TILE), TILE)
            for slot in range(remote_count)
        ]

    def read_note(mask):
        note = messages[mask][-NOTE_ROWS:, :].astype(jnp.float32)
        scales = note[0:8, :] + note[8:16, :] + note[16:24, :]
        for at, block_mask in enumerate((mask, mask ^ half)):
            for part in range(2):
                first = 4 * at + 2 * part
                scale_ref[block_mask, 0:2, part * HD : (part + 1) * HD] = scales[
                    first : first + 2, :
                ]
            picks_ref[block_mask : block_mask + 1, :] = note[24 + at : 25 + at, :].astype(jnp.int32)

    def prepare(mask, q_factor, k_factor):
        query, keys, values, grad = [
            messages[mask][at * rows : (at + 1) * rows, :] for at in range(4)
        ]
        place = rows_of(own_block ^ mask)
        q_t = query.T.astype(jnp.float32) * scale_ref[mask, 0:1, :] * q_factor
        k_t = keys.T.astype(jnp.float32) * scale_ref[mask, 1:2, :] * k_factor
        qt_ref[mask] = q_t.astype(jnp.bfloat16)
        kt_ref[:, place] = k_t.astype(jnp.bfloat16)
        q_ref[mask] = q_t.astype(jnp.bfloat16).T
        k_ref[place, :] = k_t.astype(jnp.bfloat16).T
        v_ref[place, :] = values
        g_ref[mask] = grad
        gt_ref[mask] = grad.T

    def tiles(first, count=1):
        return slice(first * TILE, (first + count) * TILE)

    def scores(mask, group, places, buffer):
        weight_ref, dprob_ref, stat_ref = buffer[:3]
        for slot in group:
            k_picked[tiles(slot), :] = k_ref[places[slot], :]
            v_picked[tiles(slot), :] = v_ref[places[slot], :]
        picked = tiles(group[0], len(group))
        score_all = jnp.dot(
            k_picked[picked, :], qt_ref[mask], preferred_element_type=jnp.float32
        )
        dprob_all = jnp.dot(
            v_picked[picked, :], gt_ref[mask], preferred_element_type=jnp.float32
        )
        for at, slot in enumerate(group):
            score = score_all[tiles(at), :].reshape(in_sublanes)
            dprob = dprob_all[tiles(at), :].reshape(in_sublanes)
            top = jnp.max(score, axis=0)
            weight = jnp.exp2((score - top) * to_base2)
            weight_ref[slot] = weight
            dprob_ref[slot] = dprob
            stat_ref[0, slot] = top * to_base2
            stat_ref[1, slot] = jnp.sum(weight, axis=0)
            stat_ref[2, slot] = jnp.sum(weight * dprob, axis=0)

    def settle(buffer):
        tops, totals, mixed = [buffer[2][at] for at in range(3)]
        highest = jnp.max(jnp.max(tops, axis=0), axis=0, keepdims=True)
        shares = jnp.exp2(tops - highest)
        total = jnp.sum(jnp.sum(shares * totals, axis=0), axis=0, keepdims=True)
        delta = jnp.sum(jnp.sum(shares * mixed, axis=0), axis=0, keepdims=True)
        inverse = 1.0 / total
        return shares * inverse, delta * inverse

    def gradients(group, buffer, shares, delta):
        weight_ref, dprob_ref, _, ds_ref, pb_ref = buffer
        for slot in group:
            prob = weight_ref[slot] * shares[slot]
            dscore = prob * (dprob_ref[slot] - delta)
            pb_ref[tiles(slot), :] = prob.reshape(TILE, rows).astype(jnp.bfloat16)
            ds_ref[tiles(slot), :] = dscore.reshape(TILE, rows).astype(jnp.bfloat16)

    def products(mask, group, places, buffer):
        ds_ref, pb_ref = buffer[3:]
        picked = tiles(group[0], len(group))
        dk = jnp.dot(ds_ref[picked, :], q_ref[mask], preferred_element_type=jnp.float32)
        dv = jnp.dot(pb_ref[picked, :], g_ref[mask], preferred_element_type=jnp.float32)
        for at, slot in enumerate(group):
            dk_ref[places[slot], :] += dk[tiles(at), :]
            dv_ref[places[slot], :] += dv[tiles(at), :]
            kt_picked[:, tiles(slot)] = kt_ref[:, places[slot]]

    def query_gradient(mask, buffer):
        dq_t = jnp.dot(kt_picked[...], buffer[3][...], preferred_element_type=jnp.float32)
        dq_ref[mask] = (dq_t * factor).astype(jnp.bfloat16).T

    groups = [range(first, min(first + 3, n_keys)) for first in range(0, n_keys, 3)]

    def step(now, before, after):
        if now is not None:
            shares, delta = settle(now[1])
        if before is not None:
            before_places = places_of(before[0])
        if after is not None:
            after_places = places_of(after[0])
        for group in groups:
            if before is not None:
                products(before[0], group, before_places, before[1])
            if now is not None:
                gradients(group, now[1], shares, delta)
            if after is not None:
                scores(after[0], group, after_places, after[1])
        if before is not None:
            query_gradient(*before)

    @pl.when(own_head >= 0)
    def _():
        q_factor = column(q_gain[pl.ds(own_head, 1), :], rows)
        k_factor = column(k_gain[pl.ds(own_head, 1), :], rows)
        for mask in range(half):
            read_note(mask)
        copy = pltpu.make_async_copy(picks_ref, picks, sem)
        copy.start()
        for mask in range(n_ctx):
            prepare(mask, q_factor, k_factor)
        copy.wait()
        dk_ref[...] = jnp.zeros_like(dk_ref)
        dv_ref[...] = jnp.zeros_like(dv_ref)
        even, odd = buffers
        step(None, None, (0, even))
        step((0, even), None, (1, odd))

        def two(pair, carry):
            mask = 2 * pair
            step((mask + 1, odd), (mask, even), (mask + 2, even))
            step((mask + 2, even), (mask + 1, odd), (mask + 3, odd))
            return carry

        lax.fori_loop(0, n_ctx // 2 - 1, two, 0)
        step((n_ctx - 1, odd), (n_ctx - 2, even), None)
        step(None, (n_ctx - 1, odd), None)
        for mask in range(n_ctx):
            place = rows_of(own_block ^ mask)
            outs[mask][0] = dq_ref[mask]
            outs[mask][1] = (dk_ref[place, :] * factor).astype(jnp.bfloat16)
            outs[mask][2] = dv_ref[place, :].astype(jnp.bfloat16)


def attend(remote_count, q_gain, k_gain, messages, n_ctx):
    rows = (messages[0].shape[0] - NOTE_ROWS) // 4
    tokens = n_ctx * rows
    n_keys = rows // TILE + remote_count
    by_block = pltpu.VMEM((n_ctx, rows, HD), jnp.bfloat16)
    by_block_t = pltpu.VMEM((n_ctx, HD, rows), jnp.bfloat16)
    buffer = [
        pltpu.VMEM((n_keys, TILE // 8, 8, rows), jnp.float32),
        pltpu.VMEM((n_keys, TILE // 8, 8, rows), jnp.float32),
        pltpu.VMEM((3, n_keys, 8, rows), jnp.float32),
        pltpu.VMEM((n_keys * TILE, rows), jnp.bfloat16),
        pltpu.VMEM((n_keys * TILE, rows), jnp.bfloat16),
    ]
    return pl.pallas_call(
        functools.partial(attend_kernel, n_ctx, q_gain.shape[0], remote_count),
        out_shape=[jax.ShapeDtypeStruct((3, rows, HD), jnp.bfloat16)] * n_ctx,
        in_specs=[IN_VMEM] * (2 + n_ctx),
        out_specs=[IN_VMEM] * n_ctx,
        scratch_shapes=[
            by_block,
            by_block_t,
            by_block,
            by_block_t,
            pltpu.VMEM((tokens, HD), jnp.bfloat16),
            pltpu.VMEM((HD, tokens), jnp.bfloat16),
            pltpu.VMEM((tokens, HD), jnp.bfloat16),
            by_block,
            pltpu.VMEM((tokens, HD), jnp.float32),
            pltpu.VMEM((tokens, HD), jnp.float32),
            pltpu.VMEM((HD, n_keys * TILE), jnp.bfloat16),
            pltpu.VMEM((n_keys * TILE, HD), jnp.bfloat16),
            pltpu.VMEM((n_keys * TILE, HD), jnp.bfloat16),
            pltpu.VMEM((n_ctx, 2, rows), jnp.float32),
            pltpu.VMEM((n_ctx, HD), jnp.int32),
            pltpu.SMEM((n_ctx, HD), jnp.int32),
            pltpu.SemaphoreType.DMA,
        ]
        + buffer
        + buffer,
        compiler_params=pltpu.CompilerParams(vmem_limit_bytes=VMEM_BYTES),
    )(q_gain, k_gain, *messages)


def gather_kernel(n_ctx, heads_dev, q_ref, k_ref, q_gain, k_gain, *refs):
    slots = refs[:n_ctx]
    dot_ref, dq_ref, dk_ref, dv_out, dv_ref, sems = refs[n_ctx:]
    piece = dv_ref.shape[0] // PIECES
    block, group = lax.axis_index("ctx"), lax.axis_index("head")

    def spread(at, out):
        for mask, slot in zip(back_masks(n_ctx), slots):
            head = head_at(block ^ mask, group, n_ctx, heads_dev)

            @pl.when(head >= 0)
            def _(head=head, slot=slot):
                place = pl.ds(pl.multiple_of(head * HD, HD), HD)
                out[:, place] = slot[at]

    spread(2, dv_ref)
    places = [pl.ds(part * piece, piece) for part in range(PIECES)]
    copies = [
        pltpu.make_async_copy(dv_ref.at[place, :], dv_out.at[place, :], sems.at[part])
        for part, place in enumerate(places)
    ]
    for copy in copies:
        copy.start()
    for at, (wide_ref, pre_ref, gain) in enumerate(
        ((dq_ref, q_ref, q_gain), (dk_ref, k_ref, k_gain))
    ):
        spread(at, wide_ref)
        terms = gain[...] * wide_ref[...].astype(jnp.float32) * pre_ref[...].astype(jnp.float32)
        dot_ref[at : at + 1, :] = row_sums(terms)
    for copy in copies:
        copy.wait()


def finish_kernel(width_all, q_ref, k_ref, q_gain, k_gain, scale_ref, dot_ref, *refs):
    dq_ref, dk_ref, dq_out, dk_out, held, sems = refs
    piece = q_ref.shape[0] // PIECES
    scales = row_scales(scale_ref[0:2, :], width_all)
    backs = scales**3 * (dot_ref[...] / width_all)
    copies = []
    for at, (pre_ref, gain, grad_ref, out) in enumerate(
        ((q_ref, q_gain, dq_ref, dq_out), (k_ref, k_gain, dk_ref, dk_out))
    ):
        scale_all = column(scales[at : at + 1, :], HD)
        back_all = column(backs[at : at + 1, :], HD)
        for part in range(PIECES):
            rows = slice(part * piece, (part + 1) * piece)
            scale, back = scale_all[rows, :], back_all[rows, :]
            for first in range(0, pre_ref.shape[1], HD):
                place = slice(first, first + HD)
                wide = pre_ref[rows, place].astype(jnp.float32)
                grad = grad_ref[rows, place].astype(jnp.float32)
                result = scale * gain[:, place] * grad - wide * back
                held[at, rows, place] = result.astype(jnp.bfloat16)
            copies.append(
                pltpu.make_async_copy(held.at[at, rows, :], out.at[rows, :], sems.at[at, part])
            )
            copies[-1].start()
    for copy in copies:
        copy.wait()


def heads_to_owners(q_pre, k_pre, values, out_grad, q_gain, k_gain, selected):
    n_ctx = lax.axis_size("ctx")
    n_head = lax.axis_size("head")
    rows, width_dev = q_pre.shape
    width_all = width_dev * n_head
    heads_dev = width_dev // HD
    remote_count = selected.shape[2]
    sizes = (n_ctx, n_head, heads_dev)
    params = pltpu.CompilerParams(vmem_limit_bytes=VMEM_BYTES)

    by_row = jax.ShapeDtypeStruct((2, rows), jnp.float32)
    wide = jax.ShapeDtypeStruct((rows, width_dev), jnp.bfloat16)

    squares, sent = pack((q_pre, k_pre, values, out_grad), n_ctx)
    there = there_masks(n_ctx)
    half = n_ctx // 2
    far = move(there[:half], sent[:half], False, *sizes)

    wishes = selected[0].reshape(1, -1).astype(jnp.float32)
    wishes = jnp.pad(wishes, ((0, 0), (0, rows - wishes.shape[1])))
    own = jnp.concatenate((lax.psum(squares, "head"), wishes), axis=0)
    across = [
        (block * n_head + group, (block ^ half) * n_head + group)
        for block in range(n_ctx)
        for group in range(n_head)
    ]
    other = lax.ppermute(own, ("ctx", "head"), across)
    near = add_note(own, other, sent[half:], width_all)
    messages = far + move(there[half:], near, False, *sizes)

    q_gains = q_gain.reshape(heads_dev, HD)
    k_gains = k_gain.reshape(heads_dev, HD)
    results = attend(remote_count, q_gains, k_gains, messages, n_ctx)
    slots = move(back_masks(n_ctx), results, True, *sizes)

    pres = (q_pre, k_pre, q_gain[None], k_gain[None])
    dots, dq_wide, dk_wide, dv = pl.pallas_call(
        functools.partial(gather_kernel, n_ctx, heads_dev),
        out_shape=[by_row, wide, wide, wide],
        in_specs=[IN_VMEM] * (4 + n_ctx),
        out_specs=[IN_VMEM] * 3 + [pl.BlockSpec(memory_space=pltpu.HBM)],
        scratch_shapes=[
            pltpu.VMEM((rows, width_dev), jnp.bfloat16),
            pltpu.SemaphoreType.DMA((PIECES,)),
        ],
        compiler_params=params,
    )(*pres, *slots)
    dots = lax.psum(dots, "head")
    dq, dk = pl.pallas_call(
        functools.partial(finish_kernel, width_all),
        out_shape=[wide, wide],
        in_specs=[IN_VMEM] * 8,
        out_specs=[pl.BlockSpec(memory_space=pltpu.HBM)] * 2,
        scratch_shapes=[
            pltpu.VMEM((2, rows, width_dev), jnp.bfloat16),
            pltpu.SemaphoreType.DMA((2, PIECES)),
        ],
        compiler_params=params,
    )(*pres, own, dots, dq_wide, dk_wide)
    return dq, dk, dv


def on_device(q_pre, k_pre, values, out_grad, q_gain, k_gain, selected):
    n_ctx = lax.axis_size("ctx")
    tiles_dev, heads_dev, remote_count = selected.shape
    capacity = -(-heads_dev * remote_count // (n_ctx - 1))
    by_head = (n_ctx - 1) * tiles_dev * 7
    by_tile = (n_ctx - 1) * capacity * 6
    paired = n_ctx & (n_ctx - 1) == 0 and n_ctx >= max(heads_dev, 4)
    paired = paired and n_ctx * tiles_dev <= 256 and heads_dev * remote_count <= HD
    plan = heads_to_owners if paired and by_head <= by_tile else tiles_to_queries
    return plan(q_pre, k_pre, values, out_grad, q_gain, k_gain, selected)


def solution(mesh):
    placed = (
        P("ctx", "head"),
        P("ctx", "head"),
        P("ctx", "head"),
        P("ctx", "head"),
        P("head"),
        P("head"),
        P("ctx", "head", None),
    )
    return jax.shard_map(
        on_device,
        mesh=mesh,
        in_specs=placed,
        out_specs=(P("ctx", "head"), P("ctx", "head"), P("ctx", "head")),
        check_vma=False,
    )
```

```python
import functools
import math

import jax
import jax.numpy as jnp
from jax import lax
from jax.experimental import pallas as pl
from jax.experimental.pallas import tpu as pltpu
from jax.sharding import PartitionSpec as P

HD = 128
TILE = 128


epsilon = 1e-06


def split_heads(array, heads_dev):
    return array.reshape(array.shape[0], heads_dev, HD).transpose(1, 0, 2)


def merge_heads(array):
    heads_dev, tok_dev, depth = array.shape
    return array.transpose(1, 0, 2).reshape(tok_dev, heads_dev * depth)


def per_tile(array, qt_dev):
    heads_dev, tok_dev, depth = array.shape
    return array.reshape(heads_dev, qt_dev, TILE, depth).transpose(1, 0, 2, 3)


def from_tiles(array):
    qt_dev, heads_dev, rows_tile, depth = array.shape
    return array.transpose(1, 0, 2, 3).reshape(heads_dev, qt_dev * rows_tile, depth)


def table_sum(taken, pieces, heads_dev, qt_dev):
    flat_pieces = pieces.reshape(pieces.shape[0], -1)
    summed = jnp.dot(
        taken, flat_pieces, precision=lax.Precision.HIGHEST, preferred_element_type=jnp.float32
    )
    summed = summed.reshape(heads_dev, qt_dev, 2, TILE, HD).transpose(2, 0, 1, 3, 4)
    return summed.reshape(2, heads_dev, qt_dev * TILE, HD)


def rounded(array):
    return array.astype(jnp.bfloat16)


def finish_norm(wide, scale, gain, grad, dot_sum, width_all):
    return (scale * gain * grad - wide * scale**3 * (dot_sum / width_all)[:, None]).astype(
        jnp.bfloat16
    )


def tiles_to_queries(q_pre, k_pre, values, out_grad, q_gain, k_gain, selected):
    n_ctx = lax.axis_size("ctx")
    tok_dev, width_dev = q_pre.shape
    width_all = width_dev * lax.axis_size("head")
    heads_dev = width_dev // HD
    qt_dev = tok_dev // TILE
    remote_count = selected.shape[2]
    factor = 1.0 / math.sqrt(HD)
    q_wide = q_pre.astype(jnp.float32)
    k_wide = k_pre.astype(jnp.float32)
    q_square, k_square = lax.psum(
        (jnp.sum(q_wide * q_wide, axis=1), jnp.sum(k_wide * k_wide, axis=1)), "head"
    )
    q_scale = lax.rsqrt(q_square / width_all + epsilon)[:, None]
    k_scale = lax.rsqrt(k_square / width_all + epsilon)[:, None]
    q_heads = split_heads(rounded(q_wide * q_scale * q_gain), heads_dev)
    k_heads = split_heads(rounded(k_wide * k_scale * k_gain), heads_dev)
    v_heads = split_heads(values, heads_dev)
    g_heads = split_heads(out_grad, heads_dev)
    q_tiles = per_tile(q_heads, qt_dev)
    g_tiles = per_tile(g_heads, qt_dev)
    k_table = k_heads.reshape(heads_dev * qt_dev, TILE, HD)
    v_table = v_heads.reshape(heads_dev * qt_dev, TILE, HD)
    flat_sel = selected[0].reshape(-1)
    n_slot = flat_sel.shape[0]
    capacity = -(-n_slot // (n_ctx - 1))
    n_buffer = n_ctx * capacity
    owners = flat_sel // qt_dev
    head_of = jnp.arange(n_slot, dtype=jnp.int32) // remote_count
    codes = head_of * qt_dev + flat_sel % qt_dev
    matches = (owners[:, None] == jnp.arange(n_ctx, dtype=jnp.int32)[None, :]).astype(jnp.int32)
    ranks = jnp.sum((jnp.cumsum(matches, axis=0) - matches) * matches, axis=1)
    position = owners * capacity + ranks
    placed = position[None, :] == jnp.arange(n_buffer, dtype=jnp.int32)[:, None]
    request = jnp.sum(jnp.where(placed, codes[None, :] + 1, 0), axis=1) - 1
    asked = lax.all_to_all(
        request.reshape(n_ctx, capacity), "ctx", split_axis=0, concat_axis=0, tiled=True
    ).reshape(n_buffer)
    clipped = jnp.maximum(asked, 0)
    taken = (asked[None, :] == jnp.arange(heads_dev * qt_dev, dtype=jnp.int32)[:, None]).astype(
        jnp.float32
    )
    s_near = (
        jnp.einsum("rhqd,hkd->rhqk", q_tiles, k_heads, preferred_element_type=jnp.float32) * factor
    )
    dp_near = jnp.einsum("rhqd,hkd->rhqk", g_tiles, v_heads, preferred_element_type=jnp.float32)
    near_top = jnp.max(s_near, axis=-1)
    outgoing = jnp.stack((k_table[clipped], v_table[clipped]), axis=1).reshape(
        n_ctx, capacity, 2, TILE, HD
    )
    incoming = lax.all_to_all(outgoing, "ctx", split_axis=0, concat_axis=0, tiled=True).reshape(
        n_buffer, 2, TILE, HD
    )
    slot_kv = incoming[position].reshape(heads_dev, remote_count, 2, TILE, HD)
    far_k = slot_kv[:, :, 0]
    far_v = slot_kv[:, :, 1]
    s_far = (
        jnp.einsum("rhqd,hckd->rhqck", q_tiles, far_k, preferred_element_type=jnp.float32) * factor
    )
    dp_far = jnp.einsum("rhqd,hckd->rhqck", g_tiles, far_v, preferred_element_type=jnp.float32)
    row_top = jnp.maximum(near_top, jnp.max(s_far, axis=(-2, -1)))
    totals = jnp.sum(jnp.exp(s_near - row_top[..., None]), axis=-1) + jnp.sum(
        jnp.exp(s_far - row_top[..., None, None]), axis=(-2, -1)
    )
    lse = row_top + jnp.log(totals)
    p_near = jnp.exp(s_near - lse[..., None])
    p_far = jnp.exp(s_far - lse[..., None, None])
    delta = jnp.sum(p_near * dp_near, axis=-1) + jnp.sum(p_far * dp_far, axis=(-2, -1))
    ds_near = rounded(p_near * (dp_near - delta[..., None]) * factor)
    pb_near = rounded(p_near)
    dq_near = jnp.einsum("rhqk,hkd->rhqd", ds_near, k_heads, preferred_element_type=jnp.float32)
    dk_near = jnp.einsum("rhqk,rhqd->hkd", ds_near, q_tiles, preferred_element_type=jnp.float32)
    dv_near = jnp.einsum("rhqk,rhqd->hkd", pb_near, g_tiles, preferred_element_type=jnp.float32)
    dq_near, dk_near, dv_near = (dq_near, dk_near, dv_near)
    ds_far = rounded(p_far * (dp_far - delta[..., None, None]) * factor)
    pb_far = rounded(p_far)
    dq_far = jnp.einsum("rhqck,hckd->rhqd", ds_far, far_k, preferred_element_type=jnp.float32)
    dq_wide = merge_heads(from_tiles(dq_near + dq_far))
    q_dot = jnp.sum(q_gain * dq_wide * q_wide, axis=1)
    dq_wide, q_dot = (dq_wide, q_dot)
    dk_far = jnp.einsum("rhqck,rhqd->hckd", ds_far, q_tiles, preferred_element_type=jnp.float32)
    dv_far = jnp.einsum("rhqck,rhqd->hckd", pb_far, g_tiles, preferred_element_type=jnp.float32)
    grads = jnp.stack((dk_far, dv_far), axis=2).reshape(n_slot, 2, TILE, HD)
    sending = jnp.zeros((n_buffer, 2, TILE, HD), jnp.float32).at[position].set(grads)
    returned = lax.all_to_all(
        sending.reshape(n_ctx, capacity, 2, TILE, HD),
        "ctx",
        split_axis=0,
        concat_axis=0,
        tiled=True,
    ).reshape(n_buffer, 2, TILE, HD)
    far_sums = table_sum(taken, returned, heads_dev, qt_dev)
    dk_wide = merge_heads(dk_near + far_sums[0])
    dv_heads = dv_near + far_sums[1]
    k_dot = jnp.sum(k_gain * dk_wide * k_wide, axis=1)
    q_dot, k_dot = lax.psum((q_dot, k_dot), "head")
    dq_result = finish_norm(q_wide, q_scale, q_gain, dq_wide, q_dot, width_all)
    dk_result = finish_norm(k_wide, k_scale, k_gain, dk_wide, k_dot, width_all)
    return (dq_result, dk_result, merge_heads(dv_heads).astype(jnp.bfloat16))


VMEM_BYTES = 48 * 2**20
PIECES = 4
IN_VMEM = pl.BlockSpec(memory_space=pltpu.VMEM)
IN_SMEM = pl.BlockSpec(memory_space=pltpu.SMEM)


def owners_of(group, n_ctx, heads_dev):
    places = [(4 * head + 1) * n_ctx // (4 * heads_dev) for head in range(heads_dev)]
    return [n_ctx - 1 - place if group % 2 else place for place in places]


def head_at(place, group, n_ctx, heads_dev):
    even = jnp.where(group % 2 == 1, n_ctx - 1 - place, place)
    head = -1
    for index, owner in enumerate(owners_of(0, n_ctx, heads_dev)):
        head = jnp.where(even == owner, index, head)
    return head


def pairs_to_owner(mask, n_ctx, n_head, heads_dev):
    pairs = []
    for group in range(n_head):
        owners = owners_of(group, n_ctx, heads_dev)
        for block in range(n_ctx):
            if block ^ mask in owners:
                pairs.append((block * n_head + group, (block ^ mask) * n_head + group))
    return pairs


def there_masks(n_ctx):
    return list(range(n_ctx - 1, -1, -1))


def back_masks(n_ctx):
    half = n_ctx // 2
    far = list(range(n_ctx - 2, half, -1)) + [n_ctx - 1, half]
    return list(range(half - 1, 0, -1)) + far + [0]


def move(masks, arrays, back, n_ctx, n_head, heads_dev):
    moved = []
    for mask, array in zip(masks, arrays):
        pairs = pairs_to_owner(mask, n_ctx, n_head, heads_dev)
        if back:
            pairs = [(b, a) for a, b in pairs]
        moved.append(lax.ppermute(array, ("ctx", "head"), pairs) if mask else array)
    return moved


def column(row, width):
    return jnp.broadcast_to(row, (width, row.shape[1])).T


def row_sums(wide):
    total = wide[:, :HD]
    for at in range(HD, wide.shape[1], HD):
        total = total + wide[:, at : at + HD]
    return jnp.sum(total.T, axis=0, keepdims=True)


def pack_kernel(n_ctx, heads_dev, *refs):
    inputs, square_ref, outs = refs[:4], refs[4], refs[5 : 5 + n_ctx]
    held, sems = refs[5 + n_ctx :]
    rows = held.shape[1]
    piece = rows // PIECES
    block, group = lax.axis_index("ctx"), lax.axis_index("head")

    def copy(at, part):
        place = pl.ds(part * piece, piece)
        return pltpu.make_async_copy(
            inputs[at].at[place, :], held.at[at, place, :], sems.at[at, part]
        )

    for at in range(4):
        for part in range(PIECES):
            copy(at, part).start()
    for at in range(4):
        for part in range(PIECES):
            copy(at, part).wait()
    for mask, out in zip(there_masks(n_ctx), outs):
        head = head_at(block ^ mask, group, n_ctx, heads_dev)

        @pl.when(head >= 0)
        def _(head=head, out=out):
            place = pl.ds(pl.multiple_of(head * HD, HD), HD)
            for at in range(4):
                out[at] = held[at, :, place]

    for at in range(2):
        wide = held[at].astype(jnp.float32)
        square_ref[at : at + 1, :] = row_sums(wide * wide)


def pack(arrays, n_ctx):
    rows, width_dev = arrays[0].shape
    result = pl.pallas_call(
        functools.partial(pack_kernel, n_ctx, width_dev // HD),
        out_shape=[jax.ShapeDtypeStruct((2, rows), jnp.float32)]
        + [jax.ShapeDtypeStruct((4, rows, HD), jnp.bfloat16)] * n_ctx,
        in_specs=[pl.BlockSpec(memory_space=pltpu.HBM)] * 4,
        out_specs=[IN_VMEM] * (n_ctx + 1),
        scratch_shapes=[
            pltpu.VMEM((4, rows, width_dev), jnp.bfloat16),
            pltpu.SemaphoreType.DMA((4, PIECES)),
        ],
        compiler_params=pltpu.CompilerParams(vmem_limit_bytes=VMEM_BYTES),
    )(*[pltpu.with_memory_space_constraint(array, pltpu.HBM) for array in arrays])
    return result[0], result[1:]


def attend_kernel(n_ctx, heads_dev, picks, scale_ref, q_gain, k_gain, *refs):
    messages = dict(zip(there_masks(n_ctx), refs[:n_ctx]))
    outs = dict(zip(back_masks(n_ctx), refs[n_ctx : 2 * n_ctx]))
    scratch = refs[2 * n_ctx :]
    q_ref, qt_ref, g_ref, gt_ref, k_ref, kt_ref, v_ref = scratch[:7]
    dq_ref, dk_ref, dv_ref, kt_picked, k_picked, v_picked = scratch[7:13]
    buffers = (scratch[13:18], scratch[18:23])
    rows = messages[0].shape[1]
    remote_count = picks.shape[1]
    near = rows // TILE
    n_keys = near + remote_count
    in_sublanes = (TILE // 8, 8, rows)
    factor = 1.0 / math.sqrt(HD)
    to_base2 = factor * math.log2(math.e)
    own_block = lax.axis_index("ctx")
    own_head = head_at(own_block, lax.axis_index("head"), n_ctx, heads_dev)

    def rows_of(block):
        return pl.ds(pl.multiple_of(block * rows, rows), rows)

    def places_of(block):
        return [
            pl.ds(pl.multiple_of(block * rows + tile * TILE, TILE), TILE) for tile in range(near)
        ] + [
            pl.ds(pl.multiple_of(picks[block, slot] * TILE, TILE), TILE)
            for slot in range(remote_count)
        ]

    def prepare(mask, q_factor, k_factor):
        message = messages[mask]
        block = own_block ^ mask
        place = rows_of(block)
        q_t = message[0].T.astype(jnp.float32) * scale_ref[block, 0:1, :] * q_factor
        k_t = message[1].T.astype(jnp.float32) * scale_ref[block, 1:2, :] * k_factor
        qt_ref[mask] = q_t.astype(jnp.bfloat16)
        kt_ref[:, place] = k_t.astype(jnp.bfloat16)
        q_ref[mask] = q_t.astype(jnp.bfloat16).T
        k_ref[place, :] = k_t.astype(jnp.bfloat16).T
        v_ref[place, :] = message[2]
        g_ref[mask] = message[3]
        gt_ref[mask] = message[3].T

    def tiles(first, count=1):
        return slice(first * TILE, (first + count) * TILE)

    def scores(mask, group, places, buffer):
        weight_ref, dprob_ref, stat_ref = buffer[:3]
        for slot in group:
            k_picked[tiles(slot), :] = k_ref[places[slot], :]
            v_picked[tiles(slot), :] = v_ref[places[slot], :]
        picked = tiles(group[0], len(group))
        score_all = jnp.dot(
            k_picked[picked, :], qt_ref[mask], preferred_element_type=jnp.float32
        )
        dprob_all = jnp.dot(
            v_picked[picked, :], gt_ref[mask], preferred_element_type=jnp.float32
        )
        for at, slot in enumerate(group):
            score = score_all[tiles(at), :].reshape(in_sublanes)
            dprob = dprob_all[tiles(at), :].reshape(in_sublanes)
            top = jnp.max(score, axis=0)
            weight = jnp.exp2((score - top) * to_base2)
            weight_ref[slot] = weight
            dprob_ref[slot] = dprob
            stat_ref[0, slot] = top * to_base2
            stat_ref[1, slot] = jnp.sum(weight, axis=0)
            stat_ref[2, slot] = jnp.sum(weight * dprob, axis=0)

    def settle(buffer):
        tops, totals, mixed = [buffer[2][at] for at in range(3)]
        highest = jnp.max(jnp.max(tops, axis=0), axis=0, keepdims=True)
        shares = jnp.exp2(tops - highest)
        total = jnp.sum(jnp.sum(shares * totals, axis=0), axis=0, keepdims=True)
        delta = jnp.sum(jnp.sum(shares * mixed, axis=0), axis=0, keepdims=True)
        inverse = 1.0 / total
        return shares * inverse, delta * inverse

    def gradients(group, buffer, shares, delta):
        weight_ref, dprob_ref, _, ds_ref, pb_ref = buffer
        for slot in group:
            prob = weight_ref[slot] * shares[slot]
            dscore = prob * (dprob_ref[slot] - delta)
            pb_ref[tiles(slot), :] = prob.reshape(TILE, rows).astype(jnp.bfloat16)
            ds_ref[tiles(slot), :] = dscore.reshape(TILE, rows).astype(jnp.bfloat16)

    def products(mask, group, places, buffer):
        ds_ref, pb_ref = buffer[3:]
        picked = tiles(group[0], len(group))
        dk = jnp.dot(ds_ref[picked, :], q_ref[mask], preferred_element_type=jnp.float32)
        dv = jnp.dot(pb_ref[picked, :], g_ref[mask], preferred_element_type=jnp.float32)
        for at, slot in enumerate(group):
            dk_ref[places[slot], :] += dk[tiles(at), :]
            dv_ref[places[slot], :] += dv[tiles(at), :]
            kt_picked[:, tiles(slot)] = kt_ref[:, places[slot]]

    def query_gradient(mask, buffer):
        dq_t = jnp.dot(kt_picked[...], buffer[3][...], preferred_element_type=jnp.float32)
        dq_ref[mask] = (dq_t * factor).astype(jnp.bfloat16).T

    groups = [range(first, min(first + 3, n_keys)) for first in range(0, n_keys, 3)]

    def step(now, before, after):
        if now is not None:
            shares, delta = settle(now[1])
        if before is not None:
            before_places = places_of(own_block ^ before[0])
        if after is not None:
            after_places = places_of(own_block ^ after[0])
        for group in groups:
            if before is not None:
                products(before[0], group, before_places, before[1])
            if now is not None:
                gradients(group, now[1], shares, delta)
            if after is not None:
                scores(after[0], group, after_places, after[1])
        if before is not None:
            query_gradient(*before)

    @pl.when(own_head >= 0)
    def _():
        q_factor = column(q_gain[pl.ds(own_head, 1), :], rows)
        k_factor = column(k_gain[pl.ds(own_head, 1), :], rows)
        for mask in range(n_ctx):
            prepare(mask, q_factor, k_factor)
        dk_ref[...] = jnp.zeros_like(dk_ref)
        dv_ref[...] = jnp.zeros_like(dv_ref)
        even, odd = buffers
        step(None, None, (0, even))
        step((0, even), None, (1, odd))

        def two(pair, carry):
            mask = 2 * pair
            step((mask + 1, odd), (mask, even), (mask + 2, even))
            step((mask + 2, even), (mask + 1, odd), (mask + 3, odd))
            return carry

        lax.fori_loop(0, n_ctx // 2 - 1, two, 0)
        step((n_ctx - 1, odd), (n_ctx - 2, even), None)
        step(None, (n_ctx - 1, odd), None)
        for mask in range(n_ctx):
            place = rows_of(own_block ^ mask)
            outs[mask][0] = dq_ref[mask]
            outs[mask][1] = (dk_ref[place, :] * factor).astype(jnp.bfloat16)
            outs[mask][2] = dv_ref[place, :].astype(jnp.bfloat16)


def attend(picks, scales, q_gain, k_gain, messages, n_ctx):
    rows = messages[0].shape[1]
    tokens = n_ctx * rows
    n_keys = rows // TILE + picks.shape[1]
    by_block = pltpu.VMEM((n_ctx, rows, HD), jnp.bfloat16)
    by_block_t = pltpu.VMEM((n_ctx, HD, rows), jnp.bfloat16)
    buffer = [
        pltpu.VMEM((n_keys, TILE // 8, 8, rows), jnp.float32),
        pltpu.VMEM((n_keys, TILE // 8, 8, rows), jnp.float32),
        pltpu.VMEM((3, n_keys, 8, rows), jnp.float32),
        pltpu.VMEM((n_keys * TILE, rows), jnp.bfloat16),
        pltpu.VMEM((n_keys * TILE, rows), jnp.bfloat16),
    ]
    return pl.pallas_call(
        functools.partial(attend_kernel, n_ctx, q_gain.shape[0]),
        out_shape=[jax.ShapeDtypeStruct((3, rows, HD), jnp.bfloat16)] * n_ctx,
        in_specs=[IN_SMEM] + [IN_VMEM] * (3 + n_ctx),
        out_specs=[IN_VMEM] * n_ctx,
        scratch_shapes=[
            by_block,
            by_block_t,
            by_block,
            by_block_t,
            pltpu.VMEM((tokens, HD), jnp.bfloat16),
            pltpu.VMEM((HD, tokens), jnp.bfloat16),
            pltpu.VMEM((tokens, HD), jnp.bfloat16),
            by_block,
            pltpu.VMEM((tokens, HD), jnp.float32),
            pltpu.VMEM((tokens, HD), jnp.float32),
            pltpu.VMEM((HD, n_keys * TILE), jnp.bfloat16),
            pltpu.VMEM((n_keys * TILE, HD), jnp.bfloat16),
            pltpu.VMEM((n_keys * TILE, HD), jnp.bfloat16),
        ]
        + buffer
        + buffer,
        compiler_params=pltpu.CompilerParams(vmem_limit_bytes=VMEM_BYTES),
    )(picks, scales, q_gain, k_gain, *messages)


def gather_kernel(n_ctx, heads_dev, q_ref, k_ref, q_gain, k_gain, *refs):
    slots = refs[:n_ctx]
    dot_ref, dq_ref, dk_ref, dv_out, dv_ref, sems = refs[n_ctx:]
    piece = dv_ref.shape[0] // PIECES
    block, group = lax.axis_index("ctx"), lax.axis_index("head")

    def spread(at, out):
        for mask, slot in zip(back_masks(n_ctx), slots):
            head = head_at(block ^ mask, group, n_ctx, heads_dev)

            @pl.when(head >= 0)
            def _(head=head, slot=slot):
                place = pl.ds(pl.multiple_of(head * HD, HD), HD)
                out[:, place] = slot[at]

    spread(2, dv_ref)
    places = [pl.ds(part * piece, piece) for part in range(PIECES)]
    copies = [
        pltpu.make_async_copy(dv_ref.at[place, :], dv_out.at[place, :], sems.at[part])
        for part, place in enumerate(places)
    ]
    for copy in copies:
        copy.start()
    for at, (wide_ref, pre_ref, gain) in enumerate(
        ((dq_ref, q_ref, q_gain), (dk_ref, k_ref, k_gain))
    ):
        spread(at, wide_ref)
        terms = gain[...] * wide_ref[...].astype(jnp.float32) * pre_ref[...].astype(jnp.float32)
        dot_ref[at : at + 1, :] = row_sums(terms)
    for copy in copies:
        copy.wait()


def finish_kernel(width_all, q_ref, k_ref, q_gain, k_gain, scale_ref, dot_ref, *refs):
    dq_ref, dk_ref, dq_out, dk_out, held, sems = refs
    piece = q_ref.shape[0] // PIECES
    scales = scale_ref[lax.axis_index("ctx")]
    backs = scales**3 * (dot_ref[...] / width_all)
    copies = []
    for at, (pre_ref, gain, grad_ref, out) in enumerate(
        ((q_ref, q_gain, dq_ref, dq_out), (k_ref, k_gain, dk_ref, dk_out))
    ):
        scale_all = column(scales[at : at + 1, :], HD)
        back_all = column(backs[at : at + 1, :], HD)
        for part in range(PIECES):
            rows = slice(part * piece, (part + 1) * piece)
            scale, back = scale_all[rows, :], back_all[rows, :]
            for first in range(0, pre_ref.shape[1], HD):
                place = slice(first, first + HD)
                wide = pre_ref[rows, place].astype(jnp.float32)
                grad = grad_ref[rows, place].astype(jnp.float32)
                result = scale * gain[:, place] * grad - wide * back
                held[at, rows, place] = result.astype(jnp.bfloat16)
            copies.append(
                pltpu.make_async_copy(held.at[at, rows, :], out.at[rows, :], sems.at[at, part])
            )
            copies[-1].start()
    for copy in copies:
        copy.wait()


def heads_to_owners(q_pre, k_pre, values, out_grad, q_gain, k_gain, selected):
    n_ctx = lax.axis_size("ctx")
    n_head = lax.axis_size("head")
    rows, width_dev = q_pre.shape
    width_all = width_dev * n_head
    heads_dev = width_dev // HD
    remote_count = selected.shape[2]
    sizes = (n_ctx, n_head, heads_dev)
    params = pltpu.CompilerParams(vmem_limit_bytes=VMEM_BYTES)

    by_row = jax.ShapeDtypeStruct((2, rows), jnp.float32)
    wide = jax.ShapeDtypeStruct((rows, width_dev), jnp.bfloat16)

    squares, sent = pack((q_pre, k_pre, values, out_grad), n_ctx)
    messages = move(there_masks(n_ctx), sent, False, *sizes)

    wishes = selected[0].reshape(1, -1).astype(jnp.float32)
    wishes = jnp.pad(wishes, ((0, 0), (0, rows - wishes.shape[1])))
    small = jnp.concatenate((lax.psum(squares, "head"), wishes), axis=0)
    small = jnp.broadcast_to(small[None], (n_ctx,) + small.shape)
    small = lax.all_to_all(small, "ctx", split_axis=0, concat_axis=0, tiled=True)
    scales = lax.rsqrt(small[:, :2] / width_all + epsilon)
    own_head = head_at(lax.axis_index("ctx"), lax.axis_index("head"), n_ctx, heads_dev)
    first = jnp.maximum(own_head, 0) * remote_count
    picks = lax.dynamic_slice_in_dim(small[:, 2], first, remote_count, 1).astype(jnp.int32)

    q_gains = q_gain.reshape(heads_dev, HD)
    k_gains = k_gain.reshape(heads_dev, HD)
    results = attend(picks, scales, q_gains, k_gains, messages, n_ctx)
    slots = move(back_masks(n_ctx), results, True, *sizes)

    pres = (q_pre, k_pre, q_gain[None], k_gain[None])
    dots, dq_wide, dk_wide, dv = pl.pallas_call(
        functools.partial(gather_kernel, n_ctx, heads_dev),
        out_shape=[by_row, wide, wide, wide],
        in_specs=[IN_VMEM] * (4 + n_ctx),
        out_specs=[IN_VMEM] * 3 + [pl.BlockSpec(memory_space=pltpu.HBM)],
        scratch_shapes=[
            pltpu.VMEM((rows, width_dev), jnp.bfloat16),
            pltpu.SemaphoreType.DMA((PIECES,)),
        ],
        compiler_params=params,
    )(*pres, *slots)
    dots = lax.psum(dots, "head")
    dq, dk = pl.pallas_call(
        functools.partial(finish_kernel, width_all),
        out_shape=[wide, wide],
        in_specs=[IN_VMEM] * 8,
        out_specs=[pl.BlockSpec(memory_space=pltpu.HBM)] * 2,
        scratch_shapes=[
            pltpu.VMEM((2, rows, width_dev), jnp.bfloat16),
            pltpu.SemaphoreType.DMA((2, PIECES)),
        ],
        compiler_params=params,
    )(*pres, scales, dots, dq_wide, dk_wide)
    return dq, dk, dv


def on_device(q_pre, k_pre, values, out_grad, q_gain, k_gain, selected):
    n_ctx = lax.axis_size("ctx")
    tiles_dev, heads_dev, remote_count = selected.shape
    capacity = -(-heads_dev * remote_count // (n_ctx - 1))
    by_head = (n_ctx - 1) * tiles_dev * 7
    by_tile = (n_ctx - 1) * capacity * 6
    paired = n_ctx & (n_ctx - 1) == 0 and n_ctx >= max(heads_dev, 4)
    plan = heads_to_owners if paired and by_head <= by_tile else tiles_to_queries
    return plan(q_pre, k_pre, values, out_grad, q_gain, k_gain, selected)


def solution(mesh):
    placed = (
        P("ctx", "head"),
        P("ctx", "head"),
        P("ctx", "head"),
        P("ctx", "head"),
        P("head"),
        P("head"),
        P("ctx", "head", None),
    )
    return jax.shard_map(
        on_device,
        mesh=mesh,
        in_specs=placed,
        out_specs=(P("ctx", "head"), P("ctx", "head"), P("ctx", "head")),
        check_vma=False,
    )
```

```python
import functools
import math

import jax
import jax.numpy as jnp
from jax import lax
from jax.experimental import pallas as pl
from jax.experimental.pallas import tpu as pltpu
from jax.sharding import PartitionSpec as P

HD = 128
TILE = 128


epsilon = 1e-06


def split_heads(array, heads_dev):
    return array.reshape(array.shape[0], heads_dev, HD).transpose(1, 0, 2)


def merge_heads(array):
    heads_dev, tok_dev, depth = array.shape
    return array.transpose(1, 0, 2).reshape(tok_dev, heads_dev * depth)


def per_tile(array, qt_dev):
    heads_dev, tok_dev, depth = array.shape
    return array.reshape(heads_dev, qt_dev, TILE, depth).transpose(1, 0, 2, 3)


def from_tiles(array):
    qt_dev, heads_dev, rows_tile, depth = array.shape
    return array.transpose(1, 0, 2, 3).reshape(heads_dev, qt_dev * rows_tile, depth)


def table_sum(taken, pieces, heads_dev, qt_dev):
    flat_pieces = pieces.reshape(pieces.shape[0], -1)
    summed = jnp.dot(
        taken, flat_pieces, precision=lax.Precision.HIGHEST, preferred_element_type=jnp.float32
    )
    summed = summed.reshape(heads_dev, qt_dev, 2, TILE, HD).transpose(2, 0, 1, 3, 4)
    return summed.reshape(2, heads_dev, qt_dev * TILE, HD)


def rounded(array):
    return array.astype(jnp.bfloat16)


def finish_norm(wide, scale, gain, grad, dot_sum, width_all):
    return (scale * gain * grad - wide * scale**3 * (dot_sum / width_all)[:, None]).astype(
        jnp.bfloat16
    )


def tiles_to_queries(q_pre, k_pre, values, out_grad, q_gain, k_gain, selected):
    n_ctx = lax.axis_size("ctx")
    tok_dev, width_dev = q_pre.shape
    width_all = width_dev * lax.axis_size("head")
    heads_dev = width_dev // HD
    qt_dev = tok_dev // TILE
    remote_count = selected.shape[2]
    factor = 1.0 / math.sqrt(HD)
    q_wide = q_pre.astype(jnp.float32)
    k_wide = k_pre.astype(jnp.float32)
    q_square, k_square = lax.psum(
        (jnp.sum(q_wide * q_wide, axis=1), jnp.sum(k_wide * k_wide, axis=1)), "head"
    )
    q_scale = lax.rsqrt(q_square / width_all + epsilon)[:, None]
    k_scale = lax.rsqrt(k_square / width_all + epsilon)[:, None]
    q_heads = split_heads(rounded(q_wide * q_scale * q_gain), heads_dev)
    k_heads = split_heads(rounded(k_wide * k_scale * k_gain), heads_dev)
    v_heads = split_heads(values, heads_dev)
    g_heads = split_heads(out_grad, heads_dev)
    q_tiles = per_tile(q_heads, qt_dev)
    g_tiles = per_tile(g_heads, qt_dev)
    k_table = k_heads.reshape(heads_dev * qt_dev, TILE, HD)
    v_table = v_heads.reshape(heads_dev * qt_dev, TILE, HD)
    flat_sel = selected[0].reshape(-1)
    n_slot = flat_sel.shape[0]
    capacity = -(-n_slot // (n_ctx - 1))
    n_buffer = n_ctx * capacity
    owners = flat_sel // qt_dev
    head_of = jnp.arange(n_slot, dtype=jnp.int32) // remote_count
    codes = head_of * qt_dev + flat_sel % qt_dev
    matches = (owners[:, None] == jnp.arange(n_ctx, dtype=jnp.int32)[None, :]).astype(jnp.int32)
    ranks = jnp.sum((jnp.cumsum(matches, axis=0) - matches) * matches, axis=1)
    position = owners * capacity + ranks
    placed = position[None, :] == jnp.arange(n_buffer, dtype=jnp.int32)[:, None]
    request = jnp.sum(jnp.where(placed, codes[None, :] + 1, 0), axis=1) - 1
    asked = lax.all_to_all(
        request.reshape(n_ctx, capacity), "ctx", split_axis=0, concat_axis=0, tiled=True
    ).reshape(n_buffer)
    clipped = jnp.maximum(asked, 0)
    taken = (asked[None, :] == jnp.arange(heads_dev * qt_dev, dtype=jnp.int32)[:, None]).astype(
        jnp.float32
    )
    s_near = (
        jnp.einsum("rhqd,hkd->rhqk", q_tiles, k_heads, preferred_element_type=jnp.float32) * factor
    )
    dp_near = jnp.einsum("rhqd,hkd->rhqk", g_tiles, v_heads, preferred_element_type=jnp.float32)
    near_top = jnp.max(s_near, axis=-1)
    outgoing = jnp.stack((k_table[clipped], v_table[clipped]), axis=1).reshape(
        n_ctx, capacity, 2, TILE, HD
    )
    incoming = lax.all_to_all(outgoing, "ctx", split_axis=0, concat_axis=0, tiled=True).reshape(
        n_buffer, 2, TILE, HD
    )
    slot_kv = incoming[position].reshape(heads_dev, remote_count, 2, TILE, HD)
    far_k = slot_kv[:, :, 0]
    far_v = slot_kv[:, :, 1]
    s_far = (
        jnp.einsum("rhqd,hckd->rhqck", q_tiles, far_k, preferred_element_type=jnp.float32) * factor
    )
    dp_far = jnp.einsum("rhqd,hckd->rhqck", g_tiles, far_v, preferred_element_type=jnp.float32)
    row_top = jnp.maximum(near_top, jnp.max(s_far, axis=(-2, -1)))
    totals = jnp.sum(jnp.exp(s_near - row_top[..., None]), axis=-1) + jnp.sum(
        jnp.exp(s_far - row_top[..., None, None]), axis=(-2, -1)
    )
    lse = row_top + jnp.log(totals)
    p_near = jnp.exp(s_near - lse[..., None])
    p_far = jnp.exp(s_far - lse[..., None, None])
    delta = jnp.sum(p_near * dp_near, axis=-1) + jnp.sum(p_far * dp_far, axis=(-2, -1))
    ds_near = rounded(p_near * (dp_near - delta[..., None]) * factor)
    pb_near = rounded(p_near)
    dq_near = jnp.einsum("rhqk,hkd->rhqd", ds_near, k_heads, preferred_element_type=jnp.float32)
    dk_near = jnp.einsum("rhqk,rhqd->hkd", ds_near, q_tiles, preferred_element_type=jnp.float32)
    dv_near = jnp.einsum("rhqk,rhqd->hkd", pb_near, g_tiles, preferred_element_type=jnp.float32)
    dq_near, dk_near, dv_near = (dq_near, dk_near, dv_near)
    ds_far = rounded(p_far * (dp_far - delta[..., None, None]) * factor)
    pb_far = rounded(p_far)
    dq_far = jnp.einsum("rhqck,hckd->rhqd", ds_far, far_k, preferred_element_type=jnp.float32)
    dq_wide = merge_heads(from_tiles(dq_near + dq_far))
    q_dot = jnp.sum(q_gain * dq_wide * q_wide, axis=1)
    dq_wide, q_dot = (dq_wide, q_dot)
    dk_far = jnp.einsum("rhqck,rhqd->hckd", ds_far, q_tiles, preferred_element_type=jnp.float32)
    dv_far = jnp.einsum("rhqck,rhqd->hckd", pb_far, g_tiles, preferred_element_type=jnp.float32)
    grads = jnp.stack((dk_far, dv_far), axis=2).reshape(n_slot, 2, TILE, HD)
    sending = jnp.zeros((n_buffer, 2, TILE, HD), jnp.float32).at[position].set(grads)
    returned = lax.all_to_all(
        sending.reshape(n_ctx, capacity, 2, TILE, HD),
        "ctx",
        split_axis=0,
        concat_axis=0,
        tiled=True,
    ).reshape(n_buffer, 2, TILE, HD)
    far_sums = table_sum(taken, returned, heads_dev, qt_dev)
    dk_wide = merge_heads(dk_near + far_sums[0])
    dv_heads = dv_near + far_sums[1]
    k_dot = jnp.sum(k_gain * dk_wide * k_wide, axis=1)
    q_dot, k_dot = lax.psum((q_dot, k_dot), "head")
    dq_result = finish_norm(q_wide, q_scale, q_gain, dq_wide, q_dot, width_all)
    dk_result = finish_norm(k_wide, k_scale, k_gain, dk_wide, k_dot, width_all)
    return (dq_result, dk_result, merge_heads(dv_heads).astype(jnp.bfloat16))


VMEM_BYTES = 48 * 2**20
PIECES = 4
STRIP = 64
IN_VMEM = pl.BlockSpec(memory_space=pltpu.VMEM)
IN_SMEM = pl.BlockSpec(memory_space=pltpu.SMEM)


def owners_of(group, n_ctx, heads_dev):
    places = [(4 * head + 1) * n_ctx // (4 * heads_dev) for head in range(heads_dev)]
    return [n_ctx - 1 - place if group % 2 else place for place in places]


def head_at(place, group, n_ctx, heads_dev):
    even = jnp.where(group % 2 == 1, n_ctx - 1 - place, place)
    head = -1
    for index, owner in enumerate(owners_of(0, n_ctx, heads_dev)):
        head = jnp.where(even == owner, index, head)
    return head


def pairs_to_owner(mask, n_ctx, n_head, heads_dev):
    pairs = []
    for group in range(n_head):
        owners = owners_of(group, n_ctx, heads_dev)
        for block in range(n_ctx):
            if block ^ mask in owners:
                pairs.append((block * n_head + group, (block ^ mask) * n_head + group))
    return pairs


def there_masks(n_ctx):
    half = n_ctx // 2
    far = list(range(n_ctx - 2, half, -1)) + [n_ctx - 1, half]
    return far + list(range(half - 1, -1, -1))


def back_masks(n_ctx):
    return list(range(n_ctx // 2 - 1, 0, -1)) + list(range(n_ctx - 1, n_ctx // 2 - 1, -1)) + [0]


def move(masks, arrays, back, n_ctx, n_head, heads_dev):
    moved = []
    for mask, array in zip(masks, arrays):
        pairs = pairs_to_owner(mask, n_ctx, n_head, heads_dev)
        if back:
            pairs = [(b, a) for a, b in pairs]
        moved.append(lax.ppermute(array, ("ctx", "head"), pairs) if mask else array)
    return moved


def column(row, width):
    return jnp.broadcast_to(row, (width, row.shape[1])).T


def row_sums(wide):
    total = wide[:, :HD]
    for at in range(HD, wide.shape[1], HD):
        total = total + wide[:, at : at + HD]
    return jnp.sum(total.T, axis=0, keepdims=True)


def pack_kernel(n_ctx, heads_dev, *refs):
    inputs, square_ref, outs = refs[:4], refs[4], refs[5 : 5 + n_ctx]
    held, sems = refs[5 + n_ctx :]
    rows = held.shape[1]
    piece = rows // PIECES
    block, group = lax.axis_index("ctx"), lax.axis_index("head")

    def copy(at, part):
        place = pl.ds(part * piece, piece)
        return pltpu.make_async_copy(
            inputs[at].at[place, :], held.at[at, place, :], sems.at[at, part]
        )

    for at in range(4):
        for part in range(PIECES):
            copy(at, part).start()
    for at in range(4):
        for part in range(PIECES):
            copy(at, part).wait()
    for mask, out in zip(there_masks(n_ctx), outs):
        head = head_at(block ^ mask, group, n_ctx, heads_dev)

        @pl.when(head >= 0)
        def _(head=head, out=out):
            place = pl.ds(pl.multiple_of(head * HD, HD), HD)
            for at in range(4):
                out[at] = held[at, :, place]

    for at in range(2):
        wide = held[at].astype(jnp.float32)
        square_ref[at : at + 1, :] = row_sums(wide * wide)


def pack(arrays, n_ctx):
    rows, width_dev = arrays[0].shape
    result = pl.pallas_call(
        functools.partial(pack_kernel, n_ctx, width_dev // HD),
        out_shape=[jax.ShapeDtypeStruct((2, rows), jnp.float32)]
        + [jax.ShapeDtypeStruct((4, rows, HD), jnp.bfloat16)] * n_ctx,
        in_specs=[pl.BlockSpec(memory_space=pltpu.HBM)] * 4,
        out_specs=[IN_VMEM] * (n_ctx + 1),
        scratch_shapes=[
            pltpu.VMEM((4, rows, width_dev), jnp.bfloat16),
            pltpu.SemaphoreType.DMA((4, PIECES)),
        ],
        compiler_params=pltpu.CompilerParams(vmem_limit_bytes=VMEM_BYTES),
    )(*[pltpu.with_memory_space_constraint(array, pltpu.HBM) for array in arrays])
    return result[0], result[1:]


def attend_kernel(n_ctx, heads_dev, picks, scale_ref, q_gain, k_gain, *refs):
    messages = dict(zip(there_masks(n_ctx), refs[:n_ctx]))
    outs = dict(zip(back_masks(n_ctx), refs[n_ctx : 2 * n_ctx]))
    scratch = refs[2 * n_ctx :]
    q_ref, qt_ref, g_ref, gt_ref, k_ref, kt_ref, v_ref = scratch[:7]
    dq_ref, dk_ref, dv_ref, kt_picked, k_picked, v_picked = scratch[7:13]
    buffers = (scratch[13:18], scratch[18:23])
    rows = messages[0].shape[1]
    remote_count = picks.shape[1]
    near = rows // TILE
    n_keys = near + remote_count
    n_strips = n_keys * TILE // STRIP
    factor = 1.0 / math.sqrt(HD)
    to_base2 = factor * math.log2(math.e)
    own_block = lax.axis_index("ctx")
    own_head = head_at(own_block, lax.axis_index("head"), n_ctx, heads_dev)

    def rows_of(block):
        return pl.ds(pl.multiple_of(block * rows, rows), rows)

    def places_of(block):
        return [
            pl.ds(pl.multiple_of(block * rows + tile * TILE, TILE), TILE) for tile in range(near)
        ] + [
            pl.ds(pl.multiple_of(picks[block, slot] * TILE, TILE), TILE)
            for slot in range(remote_count)
        ]

    def prepare(mask, q_factor, k_factor):
        message = messages[mask]
        block = own_block ^ mask
        place = rows_of(block)
        q_t = message[0].T.astype(jnp.float32) * scale_ref[block, 0:1, :] * q_factor
        k_t = message[1].T.astype(jnp.float32) * scale_ref[block, 1:2, :] * k_factor
        qt_ref[mask] = q_t.astype(jnp.bfloat16)
        kt_ref[:, place] = k_t.astype(jnp.bfloat16)
        q_ref[mask] = q_t.astype(jnp.bfloat16).T
        k_ref[place, :] = k_t.astype(jnp.bfloat16).T
        v_ref[place, :] = message[2]
        g_ref[mask] = message[3]
        gt_ref[mask] = message[3].T

    def tiles(first, count=1):
        return slice(first * TILE, (first + count) * TILE)

    def scores(mask, group, places, buffer):
        weight_ref, dprob_ref, stat_ref = buffer[:3]
        for slot in group:
            k_picked[tiles(slot), :] = k_ref[places[slot], :]
            v_picked[tiles(slot), :] = v_ref[places[slot], :]
        picked = tiles(group[0], len(group))
        score_all = jnp.dot(
            k_picked[picked, :], qt_ref[mask], preferred_element_type=jnp.float32
        )
        dprob_all = jnp.dot(
            v_picked[picked, :], gt_ref[mask], preferred_element_type=jnp.float32
        )
        for at in range(len(group) * TILE // STRIP):
            strip = group[0] * TILE // STRIP + at
            part = slice(at * STRIP, (at + 1) * STRIP)
            score = score_all[part, :]
            dprob = dprob_all[part, :]
            top = jnp.max(score, axis=0, keepdims=True)
            weight = jnp.exp2((score - top) * to_base2)
            weight_ref[strip] = weight
            dprob_ref[strip] = dprob
            stat_ref[0, strip : strip + 1, :] = top * to_base2
            stat_ref[1, strip : strip + 1, :] = jnp.sum(weight, axis=0, keepdims=True)
            stat_ref[2, strip : strip + 1, :] = jnp.sum(weight * dprob, axis=0, keepdims=True)

    def settle(buffer):
        stat_ref = buffer[2]
        tops = stat_ref[0, :n_strips, :]
        shares = jnp.exp2(tops - jnp.max(tops, axis=0, keepdims=True))
        total = jnp.sum(shares * stat_ref[1, :n_strips, :], axis=0, keepdims=True)
        mixed = jnp.sum(shares * stat_ref[2, :n_strips, :], axis=0, keepdims=True)
        inverse = 1.0 / total
        return shares * inverse, mixed * inverse

    def gradients(group, buffer, shares, delta):
        weight_ref, dprob_ref, _, ds_ref, pb_ref = buffer
        for strip in range(group[0] * TILE // STRIP, (group[-1] + 1) * TILE // STRIP):
            part = slice(strip * STRIP, (strip + 1) * STRIP)
            prob = weight_ref[strip] * shares[strip : strip + 1, :]
            pb_ref[part, :] = prob.astype(jnp.bfloat16)
            ds_ref[part, :] = (prob * (dprob_ref[strip] - delta)).astype(jnp.bfloat16)

    def products(mask, group, places, buffer):
        ds_ref, pb_ref = buffer[3:]
        picked = tiles(group[0], len(group))
        dk = jnp.dot(ds_ref[picked, :], q_ref[mask], preferred_element_type=jnp.float32)
        dv = jnp.dot(pb_ref[picked, :], g_ref[mask], preferred_element_type=jnp.float32)
        for at, slot in enumerate(group):
            dk_ref[places[slot], :] += dk[tiles(at), :]
            dv_ref[places[slot], :] += dv[tiles(at), :]
            kt_picked[:, tiles(slot)] = kt_ref[:, places[slot]]

    def query_gradient(mask, buffer):
        dq_t = jnp.dot(kt_picked[...], buffer[3][...], preferred_element_type=jnp.float32)
        dq_ref[mask] = (dq_t * factor).astype(jnp.bfloat16).T

    groups = [range(first, min(first + 3, n_keys)) for first in range(0, n_keys, 3)]

    def step(now, before, after):
        if now is not None:
            shares, delta = settle(now[1])
        if before is not None:
            before_places = places_of(own_block ^ before[0])
        if after is not None:
            after_places = places_of(own_block ^ after[0])
        for group in groups:
            if before is not None:
                products(before[0], group, before_places, before[1])
            if now is not None:
                gradients(group, now[1], shares, delta)
            if after is not None:
                scores(after[0], group, after_places, after[1])
        if before is not None:
            query_gradient(*before)

    @pl.when(own_head >= 0)
    def _():
        q_factor = column(q_gain[pl.ds(own_head, 1), :], rows)
        k_factor = column(k_gain[pl.ds(own_head, 1), :], rows)
        for mask in range(n_ctx):
            prepare(mask, q_factor, k_factor)
        dk_ref[...] = jnp.zeros_like(dk_ref)
        dv_ref[...] = jnp.zeros_like(dv_ref)
        even, odd = buffers
        step(None, None, (0, even))
        step((0, even), None, (1, odd))

        def two(pair, carry):
            mask = 2 * pair
            step((mask + 1, odd), (mask, even), (mask + 2, even))
            step((mask + 2, even), (mask + 1, odd), (mask + 3, odd))
            return carry

        lax.fori_loop(0, n_ctx // 2 - 1, two, 0)
        step((n_ctx - 1, odd), (n_ctx - 2, even), None)
        step(None, (n_ctx - 1, odd), None)
        for mask in range(n_ctx):
            place = rows_of(own_block ^ mask)
            outs[mask][0] = dq_ref[mask]
            outs[mask][1] = (dk_ref[place, :] * factor).astype(jnp.bfloat16)
            outs[mask][2] = dv_ref[place, :].astype(jnp.bfloat16)


def attend(picks, scales, q_gain, k_gain, messages, n_ctx):
    rows = messages[0].shape[1]
    tokens = n_ctx * rows
    n_keys = rows // TILE + picks.shape[1]
    n_strips = n_keys * TILE // STRIP
    by_block = pltpu.VMEM((n_ctx, rows, HD), jnp.bfloat16)
    by_block_t = pltpu.VMEM((n_ctx, HD, rows), jnp.bfloat16)
    buffer = [
        pltpu.VMEM((n_strips, STRIP, rows), jnp.float32),
        pltpu.VMEM((n_strips, STRIP, rows), jnp.float32),
        pltpu.VMEM((3, -(-n_strips // 8) * 8, rows), jnp.float32),
        pltpu.VMEM((n_keys * TILE, rows), jnp.bfloat16),
        pltpu.VMEM((n_keys * TILE, rows), jnp.bfloat16),
    ]
    return pl.pallas_call(
        functools.partial(attend_kernel, n_ctx, q_gain.shape[0]),
        out_shape=[jax.ShapeDtypeStruct((3, rows, HD), jnp.bfloat16)] * n_ctx,
        in_specs=[IN_SMEM] + [IN_VMEM] * (3 + n_ctx),
        out_specs=[IN_VMEM] * n_ctx,
        scratch_shapes=[
            by_block,
            by_block_t,
            by_block,
            by_block_t,
            pltpu.VMEM((tokens, HD), jnp.bfloat16),
            pltpu.VMEM((HD, tokens), jnp.bfloat16),
            pltpu.VMEM((tokens, HD), jnp.bfloat16),
            by_block,
            pltpu.VMEM((tokens, HD), jnp.float32),
            pltpu.VMEM((tokens, HD), jnp.float32),
            pltpu.VMEM((HD, n_keys * TILE), jnp.bfloat16),
            pltpu.VMEM((n_keys * TILE, HD), jnp.bfloat16),
            pltpu.VMEM((n_keys * TILE, HD), jnp.bfloat16),
        ]
        + buffer
        + buffer,
        compiler_params=pltpu.CompilerParams(vmem_limit_bytes=VMEM_BYTES),
    )(picks, scales, q_gain, k_gain, *messages)


def gather_kernel(n_ctx, heads_dev, q_ref, k_ref, q_gain, k_gain, *refs):
    slots = refs[:n_ctx]
    dot_ref, dq_ref, dk_ref, dv_out, dv_ref, sems = refs[n_ctx:]
    piece = dv_ref.shape[0] // PIECES
    block, group = lax.axis_index("ctx"), lax.axis_index("head")

    def spread(at, out):
        for mask, slot in zip(back_masks(n_ctx), slots):
            head = head_at(block ^ mask, group, n_ctx, heads_dev)

            @pl.when(head >= 0)
            def _(head=head, slot=slot):
                place = pl.ds(pl.multiple_of(head * HD, HD), HD)
                out[:, place] = slot[at]

    spread(2, dv_ref)
    places = [pl.ds(part * piece, piece) for part in range(PIECES)]
    copies = [
        pltpu.make_async_copy(dv_ref.at[place, :], dv_out.at[place, :], sems.at[part])
        for part, place in enumerate(places)
    ]
    for copy in copies:
        copy.start()
    for at, (wide_ref, pre_ref, gain) in enumerate(
        ((dq_ref, q_ref, q_gain), (dk_ref, k_ref, k_gain))
    ):
        spread(at, wide_ref)
        terms = gain[...] * wide_ref[...].astype(jnp.float32) * pre_ref[...].astype(jnp.float32)
        dot_ref[at : at + 1, :] = row_sums(terms)
    for copy in copies:
        copy.wait()


def finish_kernel(width_all, q_ref, k_ref, q_gain, k_gain, scale_ref, dot_ref, *refs):
    dq_ref, dk_ref, dq_out, dk_out, held, sems = refs
    piece = q_ref.shape[0] // PIECES
    scales = scale_ref[lax.axis_index("ctx")]
    backs = scales**3 * (dot_ref[...] / width_all)
    copies = []
    for at, (pre_ref, gain, grad_ref, out) in enumerate(
        ((q_ref, q_gain, dq_ref, dq_out), (k_ref, k_gain, dk_ref, dk_out))
    ):
        scale_all = column(scales[at : at + 1, :], HD)
        back_all = column(backs[at : at + 1, :], HD)
        for part in range(PIECES):
            rows = slice(part * piece, (part + 1) * piece)
            scale, back = scale_all[rows, :], back_all[rows, :]
            for first in range(0, pre_ref.shape[1], HD):
                place = slice(first, first + HD)
                wide = pre_ref[rows, place].astype(jnp.float32)
                grad = grad_ref[rows, place].astype(jnp.float32)
                result = scale * gain[:, place] * grad - wide * back
                held[at, rows, place] = result.astype(jnp.bfloat16)
            copies.append(
                pltpu.make_async_copy(held.at[at, rows, :], out.at[rows, :], sems.at[at, part])
            )
            copies[-1].start()
    for copy in copies:
        copy.wait()


def heads_to_owners(q_pre, k_pre, values, out_grad, q_gain, k_gain, selected):
    n_ctx = lax.axis_size("ctx")
    n_head = lax.axis_size("head")
    rows, width_dev = q_pre.shape
    width_all = width_dev * n_head
    heads_dev = width_dev // HD
    remote_count = selected.shape[2]
    sizes = (n_ctx, n_head, heads_dev)
    params = pltpu.CompilerParams(vmem_limit_bytes=VMEM_BYTES)

    by_row = jax.ShapeDtypeStruct((2, rows), jnp.float32)
    wide = jax.ShapeDtypeStruct((rows, width_dev), jnp.bfloat16)

    squares, sent = pack((q_pre, k_pre, values, out_grad), n_ctx)
    messages = move(there_masks(n_ctx), sent, False, *sizes)

    wishes = selected[0].reshape(1, -1).astype(jnp.float32)
    wishes = jnp.pad(wishes, ((0, 0), (0, rows - wishes.shape[1])))
    small = jnp.concatenate((lax.psum(squares, "head"), wishes), axis=0)
    small = jnp.broadcast_to(small[None], (n_ctx,) + small.shape)
    small = lax.all_to_all(small, "ctx", split_axis=0, concat_axis=0, tiled=True)
    scales = lax.rsqrt(small[:, :2] / width_all + epsilon)
    own_head = head_at(lax.axis_index("ctx"), lax.axis_index("head"), n_ctx, heads_dev)
    first = jnp.maximum(own_head, 0) * remote_count
    picks = lax.dynamic_slice_in_dim(small[:, 2], first, remote_count, 1).astype(jnp.int32)

    q_gains = q_gain.reshape(heads_dev, HD)
    k_gains = k_gain.reshape(heads_dev, HD)
    results = attend(picks, scales, q_gains, k_gains, messages, n_ctx)
    slots = move(back_masks(n_ctx), results, True, *sizes)

    pres = (q_pre, k_pre, q_gain[None], k_gain[None])
    dots, dq_wide, dk_wide, dv = pl.pallas_call(
        functools.partial(gather_kernel, n_ctx, heads_dev),
        out_shape=[by_row, wide, wide, wide],
        in_specs=[IN_VMEM] * (4 + n_ctx),
        out_specs=[IN_VMEM] * 3 + [pl.BlockSpec(memory_space=pltpu.HBM)],
        scratch_shapes=[
            pltpu.VMEM((rows, width_dev), jnp.bfloat16),
            pltpu.SemaphoreType.DMA((PIECES,)),
        ],
        compiler_params=params,
    )(*pres, *slots)
    dots = lax.psum(dots, "head")
    dq, dk = pl.pallas_call(
        functools.partial(finish_kernel, width_all),
        out_shape=[wide, wide],
        in_specs=[IN_VMEM] * 8,
        out_specs=[pl.BlockSpec(memory_space=pltpu.HBM)] * 2,
        scratch_shapes=[
            pltpu.VMEM((2, rows, width_dev), jnp.bfloat16),
            pltpu.SemaphoreType.DMA((2, PIECES)),
        ],
        compiler_params=params,
    )(*pres, scales, dots, dq_wide, dk_wide)
    return dq, dk, dv


def on_device(q_pre, k_pre, values, out_grad, q_gain, k_gain, selected):
    n_ctx = lax.axis_size("ctx")
    tiles_dev, heads_dev, remote_count = selected.shape
    capacity = -(-heads_dev * remote_count // (n_ctx - 1))
    by_head = (n_ctx - 1) * tiles_dev * 7
    by_tile = (n_ctx - 1) * capacity * 6
    paired = n_ctx & (n_ctx - 1) == 0 and n_ctx >= max(heads_dev, 4)
    plan = heads_to_owners if paired and by_head <= by_tile else tiles_to_queries
    return plan(q_pre, k_pre, values, out_grad, q_gain, k_gain, selected)


def solution(mesh):
    placed = (
        P("ctx", "head"),
        P("ctx", "head"),
        P("ctx", "head"),
        P("ctx", "head"),
        P("head"),
        P("head"),
        P("ctx", "head", None),
    )
    return jax.shard_map(
        on_device,
        mesh=mesh,
        in_specs=placed,
        out_specs=(P("ctx", "head"), P("ctx", "head"), P("ctx", "head")),
        check_vma=False,
    )
```

```python
import functools
import math

import jax
import jax.numpy as jnp
from jax import lax
from jax.experimental import pallas as pl
from jax.experimental.pallas import tpu as pltpu
from jax.sharding import PartitionSpec as P

HD = 128
TILE = 128


epsilon = 1e-06


def split_heads(array, heads_dev):
    return array.reshape(array.shape[0], heads_dev, HD).transpose(1, 0, 2)


def merge_heads(array):
    heads_dev, tok_dev, depth = array.shape
    return array.transpose(1, 0, 2).reshape(tok_dev, heads_dev * depth)


def per_tile(array, qt_dev):
    heads_dev, tok_dev, depth = array.shape
    return array.reshape(heads_dev, qt_dev, TILE, depth).transpose(1, 0, 2, 3)


def from_tiles(array):
    qt_dev, heads_dev, rows_tile, depth = array.shape
    return array.transpose(1, 0, 2, 3).reshape(heads_dev, qt_dev * rows_tile, depth)


def table_sum(taken, pieces, heads_dev, qt_dev):
    flat_pieces = pieces.reshape(pieces.shape[0], -1)
    summed = jnp.dot(
        taken, flat_pieces, precision=lax.Precision.HIGHEST, preferred_element_type=jnp.float32
    )
    summed = summed.reshape(heads_dev, qt_dev, 2, TILE, HD).transpose(2, 0, 1, 3, 4)
    return summed.reshape(2, heads_dev, qt_dev * TILE, HD)


def rounded(array):
    return array.astype(jnp.bfloat16)


def finish_norm(wide, scale, gain, grad, dot_sum, width_all):
    return (scale * gain * grad - wide * scale**3 * (dot_sum / width_all)[:, None]).astype(
        jnp.bfloat16
    )


def tiles_to_queries(q_pre, k_pre, values, out_grad, q_gain, k_gain, selected):
    n_ctx = lax.axis_size("ctx")
    tok_dev, width_dev = q_pre.shape
    width_all = width_dev * lax.axis_size("head")
    heads_dev = width_dev // HD
    qt_dev = tok_dev // TILE
    remote_count = selected.shape[2]
    factor = 1.0 / math.sqrt(HD)
    q_wide = q_pre.astype(jnp.float32)
    k_wide = k_pre.astype(jnp.float32)
    q_square, k_square = lax.psum(
        (jnp.sum(q_wide * q_wide, axis=1), jnp.sum(k_wide * k_wide, axis=1)), "head"
    )
    q_scale = lax.rsqrt(q_square / width_all + epsilon)[:, None]
    k_scale = lax.rsqrt(k_square / width_all + epsilon)[:, None]
    q_heads = split_heads(rounded(q_wide * q_scale * q_gain), heads_dev)
    k_heads = split_heads(rounded(k_wide * k_scale * k_gain), heads_dev)
    v_heads = split_heads(values, heads_dev)
    g_heads = split_heads(out_grad, heads_dev)
    q_tiles = per_tile(q_heads, qt_dev)
    g_tiles = per_tile(g_heads, qt_dev)
    k_table = k_heads.reshape(heads_dev * qt_dev, TILE, HD)
    v_table = v_heads.reshape(heads_dev * qt_dev, TILE, HD)
    flat_sel = selected[0].reshape(-1)
    n_slot = flat_sel.shape[0]
    capacity = -(-n_slot // (n_ctx - 1))
    n_buffer = n_ctx * capacity
    owners = flat_sel // qt_dev
    head_of = jnp.arange(n_slot, dtype=jnp.int32) // remote_count
    codes = head_of * qt_dev + flat_sel % qt_dev
    matches = (owners[:, None] == jnp.arange(n_ctx, dtype=jnp.int32)[None, :]).astype(jnp.int32)
    ranks = jnp.sum((jnp.cumsum(matches, axis=0) - matches) * matches, axis=1)
    position = owners * capacity + ranks
    placed = position[None, :] == jnp.arange(n_buffer, dtype=jnp.int32)[:, None]
    request = jnp.sum(jnp.where(placed, codes[None, :] + 1, 0), axis=1) - 1
    asked = lax.all_to_all(
        request.reshape(n_ctx, capacity), "ctx", split_axis=0, concat_axis=0, tiled=True
    ).reshape(n_buffer)
    clipped = jnp.maximum(asked, 0)
    taken = (asked[None, :] == jnp.arange(heads_dev * qt_dev, dtype=jnp.int32)[:, None]).astype(
        jnp.float32
    )
    s_near = (
        jnp.einsum("rhqd,hkd->rhqk", q_tiles, k_heads, preferred_element_type=jnp.float32) * factor
    )
    dp_near = jnp.einsum("rhqd,hkd->rhqk", g_tiles, v_heads, preferred_element_type=jnp.float32)
    near_top = jnp.max(s_near, axis=-1)
    outgoing = jnp.stack((k_table[clipped], v_table[clipped]), axis=1).reshape(
        n_ctx, capacity, 2, TILE, HD
    )
    incoming = lax.all_to_all(outgoing, "ctx", split_axis=0, concat_axis=0, tiled=True).reshape(
        n_buffer, 2, TILE, HD
    )
    slot_kv = incoming[position].reshape(heads_dev, remote_count, 2, TILE, HD)
    far_k = slot_kv[:, :, 0]
    far_v = slot_kv[:, :, 1]
    s_far = (
        jnp.einsum("rhqd,hckd->rhqck", q_tiles, far_k, preferred_element_type=jnp.float32) * factor
    )
    dp_far = jnp.einsum("rhqd,hckd->rhqck", g_tiles, far_v, preferred_element_type=jnp.float32)
    row_top = jnp.maximum(near_top, jnp.max(s_far, axis=(-2, -1)))
    totals = jnp.sum(jnp.exp(s_near - row_top[..., None]), axis=-1) + jnp.sum(
        jnp.exp(s_far - row_top[..., None, None]), axis=(-2, -1)
    )
    lse = row_top + jnp.log(totals)
    p_near = jnp.exp(s_near - lse[..., None])
    p_far = jnp.exp(s_far - lse[..., None, None])
    delta = jnp.sum(p_near * dp_near, axis=-1) + jnp.sum(p_far * dp_far, axis=(-2, -1))
    ds_near = rounded(p_near * (dp_near - delta[..., None]) * factor)
    pb_near = rounded(p_near)
    dq_near = jnp.einsum("rhqk,hkd->rhqd", ds_near, k_heads, preferred_element_type=jnp.float32)
    dk_near = jnp.einsum("rhqk,rhqd->hkd", ds_near, q_tiles, preferred_element_type=jnp.float32)
    dv_near = jnp.einsum("rhqk,rhqd->hkd", pb_near, g_tiles, preferred_element_type=jnp.float32)
    dq_near, dk_near, dv_near = (dq_near, dk_near, dv_near)
    ds_far = rounded(p_far * (dp_far - delta[..., None, None]) * factor)
    pb_far = rounded(p_far)
    dq_far = jnp.einsum("rhqck,hckd->rhqd", ds_far, far_k, preferred_element_type=jnp.float32)
    dq_wide = merge_heads(from_tiles(dq_near + dq_far))
    q_dot = jnp.sum(q_gain * dq_wide * q_wide, axis=1)
    dq_wide, q_dot = (dq_wide, q_dot)
    dk_far = jnp.einsum("rhqck,rhqd->hckd", ds_far, q_tiles, preferred_element_type=jnp.float32)
    dv_far = jnp.einsum("rhqck,rhqd->hckd", pb_far, g_tiles, preferred_element_type=jnp.float32)
    grads = jnp.stack((dk_far, dv_far), axis=2).reshape(n_slot, 2, TILE, HD)
    sending = jnp.zeros((n_buffer, 2, TILE, HD), jnp.float32).at[position].set(grads)
    returned = lax.all_to_all(
        sending.reshape(n_ctx, capacity, 2, TILE, HD),
        "ctx",
        split_axis=0,
        concat_axis=0,
        tiled=True,
    ).reshape(n_buffer, 2, TILE, HD)
    far_sums = table_sum(taken, returned, heads_dev, qt_dev)
    dk_wide = merge_heads(dk_near + far_sums[0])
    dv_heads = dv_near + far_sums[1]
    k_dot = jnp.sum(k_gain * dk_wide * k_wide, axis=1)
    q_dot, k_dot = lax.psum((q_dot, k_dot), "head")
    dq_result = finish_norm(q_wide, q_scale, q_gain, dq_wide, q_dot, width_all)
    dk_result = finish_norm(k_wide, k_scale, k_gain, dk_wide, k_dot, width_all)
    return (dq_result, dk_result, merge_heads(dv_heads).astype(jnp.bfloat16))


VMEM_BYTES = 48 * 2**20
PIECES = 4
STRIP = 64
IN_VMEM = pl.BlockSpec(memory_space=pltpu.VMEM)
IN_SMEM = pl.BlockSpec(memory_space=pltpu.SMEM)


def owners_of(group, n_ctx, heads_dev):
    places = [(4 * head + 1) * n_ctx // (4 * heads_dev) for head in range(heads_dev)]
    return [n_ctx - 1 - place if group % 2 else place for place in places]


def head_at(place, group, n_ctx, heads_dev):
    even = jnp.where(group % 2 == 1, n_ctx - 1 - place, place)
    head = -1
    for index, owner in enumerate(owners_of(0, n_ctx, heads_dev)):
        head = jnp.where(even == owner, index, head)
    return head


def pairs_to_owner(mask, n_ctx, n_head, heads_dev):
    pairs = []
    for group in range(n_head):
        owners = owners_of(group, n_ctx, heads_dev)
        for block in range(n_ctx):
            if block ^ mask in owners:
                pairs.append((block * n_head + group, (block ^ mask) * n_head + group))
    return pairs


def there_masks(n_ctx):
    return list(range(n_ctx - 1, 2, -1)) + [1, 2, 0]


def back_masks(n_ctx):
    return list(range(n_ctx // 2 - 1, 0, -1)) + list(range(n_ctx - 1, n_ctx // 2 - 1, -1)) + [0]


def move(masks, arrays, back, n_ctx, n_head, heads_dev):
    moved = []
    for mask, array in zip(masks, arrays):
        pairs = pairs_to_owner(mask, n_ctx, n_head, heads_dev)
        if back:
            pairs = [(b, a) for a, b in pairs]
        moved.append(lax.ppermute(array, ("ctx", "head"), pairs) if mask else array)
    return moved


def column(row, width):
    return jnp.broadcast_to(row, (width, row.shape[1])).T


def row_sums(wide):
    total = wide[:, :HD]
    for at in range(HD, wide.shape[1], HD):
        total = total + wide[:, at : at + HD]
    return jnp.sum(total.T, axis=0, keepdims=True)


def pack_kernel(n_ctx, heads_dev, *refs):
    inputs, square_ref, outs = refs[:4], refs[4], refs[5 : 5 + n_ctx]
    held, sems = refs[5 + n_ctx :]
    rows = held.shape[1]
    piece = rows // PIECES
    block, group = lax.axis_index("ctx"), lax.axis_index("head")

    def copy(at, part):
        place = pl.ds(part * piece, piece)
        return pltpu.make_async_copy(
            inputs[at].at[place, :], held.at[at, place, :], sems.at[at, part]
        )

    for at in range(4):
        for part in range(PIECES):
            copy(at, part).start()
    for at in range(4):
        for part in range(PIECES):
            copy(at, part).wait()
    for mask, out in zip(there_masks(n_ctx), outs):
        head = head_at(block ^ mask, group, n_ctx, heads_dev)

        @pl.when(head >= 0)
        def _(head=head, out=out):
            place = pl.ds(pl.multiple_of(head * HD, HD), HD)
            for at in range(4):
                out[at] = held[at, :, place]

    for at in range(2):
        wide = held[at].astype(jnp.float32)
        square_ref[at : at + 1, :] = row_sums(wide * wide)


def pack(arrays, n_ctx):
    rows, width_dev = arrays[0].shape
    result = pl.pallas_call(
        functools.partial(pack_kernel, n_ctx, width_dev // HD),
        out_shape=[jax.ShapeDtypeStruct((2, rows), jnp.float32)]
        + [jax.ShapeDtypeStruct((4, rows, HD), jnp.bfloat16)] * n_ctx,
        in_specs=[pl.BlockSpec(memory_space=pltpu.HBM)] * 4,
        out_specs=[IN_VMEM] * (n_ctx + 1),
        scratch_shapes=[
            pltpu.VMEM((4, rows, width_dev), jnp.bfloat16),
            pltpu.SemaphoreType.DMA((4, PIECES)),
        ],
        compiler_params=pltpu.CompilerParams(vmem_limit_bytes=VMEM_BYTES),
    )(*[pltpu.with_memory_space_constraint(array, pltpu.HBM) for array in arrays])
    return result[0], result[1:]


def attend_kernel(n_ctx, heads_dev, picks, scale_ref, q_gain, k_gain, *refs):
    messages = dict(zip(there_masks(n_ctx), refs[:n_ctx]))
    outs = dict(zip(back_masks(n_ctx), refs[n_ctx : 2 * n_ctx]))
    scratch = refs[2 * n_ctx :]
    q_ref, qt_ref, g_ref, gt_ref, k_ref, kt_ref, v_ref = scratch[:7]
    dq_ref, dk_ref, dv_ref, kt_picked, k_picked, v_picked = scratch[7:13]
    buffers = (scratch[13:18], scratch[18:23])
    rows = messages[0].shape[1]
    remote_count = picks.shape[1]
    near = rows // TILE
    n_keys = near + remote_count
    n_strips = n_keys * TILE // STRIP
    factor = 1.0 / math.sqrt(HD)
    to_base2 = factor * math.log2(math.e)
    own_block = lax.axis_index("ctx")
    own_head = head_at(own_block, lax.axis_index("head"), n_ctx, heads_dev)

    def rows_of(block):
        return pl.ds(pl.multiple_of(block * rows, rows), rows)

    def places_of(block):
        return [
            pl.ds(pl.multiple_of(block * rows + tile * TILE, TILE), TILE) for tile in range(near)
        ] + [
            pl.ds(pl.multiple_of(picks[block, slot] * TILE, TILE), TILE)
            for slot in range(remote_count)
        ]

    def prepare(mask, q_factor, k_factor):
        message = messages[mask]
        block = own_block ^ mask
        place = rows_of(block)
        q_t = message[0].T.astype(jnp.float32) * scale_ref[block, 0:1, :] * q_factor
        k_t = message[1].T.astype(jnp.float32) * scale_ref[block, 1:2, :] * k_factor
        qt_ref[mask] = q_t.astype(jnp.bfloat16)
        kt_ref[:, place] = k_t.astype(jnp.bfloat16)
        q_ref[mask] = q_t.astype(jnp.bfloat16).T
        k_ref[place, :] = k_t.astype(jnp.bfloat16).T
        v_ref[place, :] = message[2]
        g_ref[mask] = message[3]
        gt_ref[mask] = message[3].T

    def tiles(first, count=1):
        return slice(first * TILE, (first + count) * TILE)

    def scores(mask, group, places, buffer):
        weight_ref, dprob_ref, stat_ref = buffer[:3]
        for slot in group:
            k_picked[tiles(slot), :] = k_ref[places[slot], :]
            v_picked[tiles(slot), :] = v_ref[places[slot], :]
        picked = tiles(group[0], len(group))
        score_all = jnp.dot(
            k_picked[picked, :], qt_ref[mask], preferred_element_type=jnp.float32
        )
        dprob_all = jnp.dot(
            v_picked[picked, :], gt_ref[mask], preferred_element_type=jnp.float32
        )
        for at in range(len(group) * TILE // STRIP):
            strip = group[0] * TILE // STRIP + at
            part = slice(at * STRIP, (at + 1) * STRIP)
            score = score_all[part, :]
            dprob = dprob_all[part, :]
            top = jnp.max(score, axis=0, keepdims=True)
            weight = jnp.exp2((score - top) * to_base2)
            weight_ref[strip] = weight
            dprob_ref[strip] = dprob
            stat_ref[0, strip : strip + 1, :] = top * to_base2
            stat_ref[1, strip : strip + 1, :] = jnp.sum(weight, axis=0, keepdims=True)
            stat_ref[2, strip : strip + 1, :] = jnp.sum(weight * dprob, axis=0, keepdims=True)

    def settle(buffer):
        stat_ref = buffer[2]
        tops = stat_ref[0, :n_strips, :]
        shares = jnp.exp2(tops - jnp.max(tops, axis=0, keepdims=True))
        total = jnp.sum(shares * stat_ref[1, :n_strips, :], axis=0, keepdims=True)
        mixed = jnp.sum(shares * stat_ref[2, :n_strips, :], axis=0, keepdims=True)
        inverse = 1.0 / total
        return shares * inverse, mixed * inverse

    def gradients(group, buffer, shares, delta):
        weight_ref, dprob_ref, _, ds_ref, pb_ref = buffer
        for strip in range(group[0] * TILE // STRIP, (group[-1] + 1) * TILE // STRIP):
            part = slice(strip * STRIP, (strip + 1) * STRIP)
            prob = weight_ref[strip] * shares[strip : strip + 1, :]
            pb_ref[part, :] = prob.astype(jnp.bfloat16)
            ds_ref[part, :] = (prob * (dprob_ref[strip] - delta)).astype(jnp.bfloat16)

    def products(mask, group, places, buffer):
        ds_ref, pb_ref = buffer[3:]
        picked = tiles(group[0], len(group))
        dk = jnp.dot(ds_ref[picked, :], q_ref[mask], preferred_element_type=jnp.float32)
        dv = jnp.dot(pb_ref[picked, :], g_ref[mask], preferred_element_type=jnp.float32)
        for at, slot in enumerate(group):
            dk_ref[places[slot], :] += dk[tiles(at), :]
            dv_ref[places[slot], :] += dv[tiles(at), :]
            kt_picked[:, tiles(slot)] = kt_ref[:, places[slot]]

    def query_gradient(mask, buffer):
        dq_t = jnp.dot(kt_picked[...], buffer[3][...], preferred_element_type=jnp.float32)
        dq_ref[mask] = (dq_t * factor).astype(jnp.bfloat16).T

    groups = [range(first, min(first + 3, n_keys)) for first in range(0, n_keys, 3)]

    def step(now, before, after):
        if now is not None:
            shares, delta = settle(now[1])
        if before is not None:
            before_places = places_of(own_block ^ before[0])
        if after is not None:
            after_places = places_of(own_block ^ after[0])
        for group in groups:
            if before is not None:
                products(before[0], group, before_places, before[1])
            if now is not None:
                gradients(group, now[1], shares, delta)
            if after is not None:
                scores(after[0], group, after_places, after[1])
        if before is not None:
            query_gradient(*before)

    @pl.when(own_head >= 0)
    def _():
        q_factor = column(q_gain[pl.ds(own_head, 1), :], rows)
        k_factor = column(k_gain[pl.ds(own_head, 1), :], rows)
        for mask in range(n_ctx):
            prepare(mask, q_factor, k_factor)
        dk_ref[...] = jnp.zeros_like(dk_ref)
        dv_ref[...] = jnp.zeros_like(dv_ref)
        even, odd = buffers
        step(None, None, (0, even))
        step((0, even), None, (1, odd))

        def two(pair, carry):
            mask = 2 * pair
            step((mask + 1, odd), (mask, even), (mask + 2, even))
            step((mask + 2, even), (mask + 1, odd), (mask + 3, odd))
            return carry

        lax.fori_loop(0, n_ctx // 2 - 1, two, 0)
        step((n_ctx - 1, odd), (n_ctx - 2, even), None)
        step(None, (n_ctx - 1, odd), None)
        for mask in range(n_ctx):
            place = rows_of(own_block ^ mask)
            outs[mask][0] = dq_ref[mask]
            outs[mask][1] = (dk_ref[place, :] * factor).astype(jnp.bfloat16)
            outs[mask][2] = dv_ref[place, :].astype(jnp.bfloat16)


def attend(picks, scales, q_gain, k_gain, messages, n_ctx):
    rows = messages[0].shape[1]
    tokens = n_ctx * rows
    n_keys = rows // TILE + picks.shape[1]
    n_strips = n_keys * TILE // STRIP
    by_block = pltpu.VMEM((n_ctx, rows, HD), jnp.bfloat16)
    by_block_t = pltpu.VMEM((n_ctx, HD, rows), jnp.bfloat16)
    buffer = [
        pltpu.VMEM((n_strips, STRIP, rows), jnp.float32),
        pltpu.VMEM((n_strips, STRIP, rows), jnp.float32),
        pltpu.VMEM((3, -(-n_strips // 8) * 8, rows), jnp.float32),
        pltpu.VMEM((n_keys * TILE, rows), jnp.bfloat16),
        pltpu.VMEM((n_keys * TILE, rows), jnp.bfloat16),
    ]
    return pl.pallas_call(
        functools.partial(attend_kernel, n_ctx, q_gain.shape[0]),
        out_shape=[jax.ShapeDtypeStruct((3, rows, HD), jnp.bfloat16)] * n_ctx,
        in_specs=[IN_SMEM] + [IN_VMEM] * (3 + n_ctx),
        out_specs=[IN_VMEM] * n_ctx,
        scratch_shapes=[
            by_block,
            by_block_t,
            by_block,
            by_block_t,
            pltpu.VMEM((tokens, HD), jnp.bfloat16),
            pltpu.VMEM((HD, tokens), jnp.bfloat16),
            pltpu.VMEM((tokens, HD), jnp.bfloat16),
            by_block,
            pltpu.VMEM((tokens, HD), jnp.float32),
            pltpu.VMEM((tokens, HD), jnp.float32),
            pltpu.VMEM((HD, n_keys * TILE), jnp.bfloat16),
            pltpu.VMEM((n_keys * TILE, HD), jnp.bfloat16),
            pltpu.VMEM((n_keys * TILE, HD), jnp.bfloat16),
        ]
        + buffer
        + buffer,
        compiler_params=pltpu.CompilerParams(vmem_limit_bytes=VMEM_BYTES),
    )(picks, scales, q_gain, k_gain, *messages)


def gather_kernel(n_ctx, heads_dev, q_ref, k_ref, q_gain, k_gain, *refs):
    slots = refs[:n_ctx]
    dot_ref, dq_ref, dk_ref, dv_out, dv_ref, sems = refs[n_ctx:]
    piece = dv_ref.shape[0] // PIECES
    block, group = lax.axis_index("ctx"), lax.axis_index("head")

    def spread(at, out):
        for mask, slot in zip(back_masks(n_ctx), slots):
            head = head_at(block ^ mask, group, n_ctx, heads_dev)

            @pl.when(head >= 0)
            def _(head=head, slot=slot):
                place = pl.ds(pl.multiple_of(head * HD, HD), HD)
                out[:, place] = slot[at]

    spread(2, dv_ref)
    places = [pl.ds(part * piece, piece) for part in range(PIECES)]
    copies = [
        pltpu.make_async_copy(dv_ref.at[place, :], dv_out.at[place, :], sems.at[part])
        for part, place in enumerate(places)
    ]
    for copy in copies:
        copy.start()
    for at, (wide_ref, pre_ref, gain) in enumerate(
        ((dq_ref, q_ref, q_gain), (dk_ref, k_ref, k_gain))
    ):
        spread(at, wide_ref)
        terms = gain[...] * wide_ref[...].astype(jnp.float32) * pre_ref[...].astype(jnp.float32)
        dot_ref[at : at + 1, :] = row_sums(terms)
    for copy in copies:
        copy.wait()


def finish_kernel(width_all, q_ref, k_ref, q_gain, k_gain, scale_ref, dot_ref, *refs):
    dq_ref, dk_ref, dq_out, dk_out, held, sems = refs
    piece = q_ref.shape[0] // PIECES
    scales = scale_ref[lax.axis_index("ctx")]
    backs = scales**3 * (dot_ref[...] / width_all)
    copies = []
    for at, (pre_ref, gain, grad_ref, out) in enumerate(
        ((q_ref, q_gain, dq_ref, dq_out), (k_ref, k_gain, dk_ref, dk_out))
    ):
        scale_all = column(scales[at : at + 1, :], HD)
        back_all = column(backs[at : at + 1, :], HD)
        for part in range(PIECES):
            rows = slice(part * piece, (part + 1) * piece)
            scale, back = scale_all[rows, :], back_all[rows, :]
            for first in range(0, pre_ref.shape[1], HD):
                place = slice(first, first + HD)
                wide = pre_ref[rows, place].astype(jnp.float32)
                grad = grad_ref[rows, place].astype(jnp.float32)
                result = scale * gain[:, place] * grad - wide * back
                held[at, rows, place] = result.astype(jnp.bfloat16)
            copies.append(
                pltpu.make_async_copy(held.at[at, rows, :], out.at[rows, :], sems.at[at, part])
            )
            copies[-1].start()
    for copy in copies:
        copy.wait()


def heads_to_owners(q_pre, k_pre, values, out_grad, q_gain, k_gain, selected):
    n_ctx = lax.axis_size("ctx")
    n_head = lax.axis_size("head")
    rows, width_dev = q_pre.shape
    width_all = width_dev * n_head
    heads_dev = width_dev // HD
    remote_count = selected.shape[2]
    sizes = (n_ctx, n_head, heads_dev)
    params = pltpu.CompilerParams(vmem_limit_bytes=VMEM_BYTES)

    by_row = jax.ShapeDtypeStruct((2, rows), jnp.float32)
    wide = jax.ShapeDtypeStruct((rows, width_dev), jnp.bfloat16)

    squares, sent = pack((q_pre, k_pre, values, out_grad), n_ctx)
    messages = move(there_masks(n_ctx), sent, False, *sizes)

    wishes = selected[0].reshape(1, -1).astype(jnp.float32)
    wishes = jnp.pad(wishes, ((0, 0), (0, rows - wishes.shape[1])))
    small = jnp.concatenate((lax.psum(squares, "head"), wishes), axis=0)
    small = jnp.broadcast_to(small[None], (n_ctx,) + small.shape)
    small = lax.all_to_all(small, "ctx", split_axis=0, concat_axis=0, tiled=True)
    scales = lax.rsqrt(small[:, :2] / width_all + epsilon)
    own_head = head_at(lax.axis_index("ctx"), lax.axis_index("head"), n_ctx, heads_dev)
    first = jnp.maximum(own_head, 0) * remote_count
    picks = lax.dynamic_slice_in_dim(small[:, 2], first, remote_count, 1).astype(jnp.int32)

    q_gains = q_gain.reshape(heads_dev, HD)
    k_gains = k_gain.reshape(heads_dev, HD)
    results = attend(picks, scales, q_gains, k_gains, messages, n_ctx)
    slots = move(back_masks(n_ctx), results, True, *sizes)

    pres = (q_pre, k_pre, q_gain[None], k_gain[None])
    dots, dq_wide, dk_wide, dv = pl.pallas_call(
        functools.partial(gather_kernel, n_ctx, heads_dev),
        out_shape=[by_row, wide, wide, wide],
        in_specs=[IN_VMEM] * (4 + n_ctx),
        out_specs=[IN_VMEM] * 3 + [pl.BlockSpec(memory_space=pltpu.HBM)],
        scratch_shapes=[
            pltpu.VMEM((rows, width_dev), jnp.bfloat16),
            pltpu.SemaphoreType.DMA((PIECES,)),
        ],
        compiler_params=params,
    )(*pres, *slots)
    dots = lax.psum(dots, "head")
    dq, dk = pl.pallas_call(
        functools.partial(finish_kernel, width_all),
        out_shape=[wide, wide],
        in_specs=[IN_VMEM] * 8,
        out_specs=[pl.BlockSpec(memory_space=pltpu.HBM)] * 2,
        scratch_shapes=[
            pltpu.VMEM((2, rows, width_dev), jnp.bfloat16),
            pltpu.SemaphoreType.DMA((2, PIECES)),
        ],
        compiler_params=params,
    )(*pres, scales, dots, dq_wide, dk_wide)
    return dq, dk, dv


def on_device(q_pre, k_pre, values, out_grad, q_gain, k_gain, selected):
    n_ctx = lax.axis_size("ctx")
    tiles_dev, heads_dev, remote_count = selected.shape
    capacity = -(-heads_dev * remote_count // (n_ctx - 1))
    by_head = (n_ctx - 1) * tiles_dev * 7
    by_tile = (n_ctx - 1) * capacity * 6
    paired = n_ctx & (n_ctx - 1) == 0 and n_ctx >= max(heads_dev, 4)
    plan = heads_to_owners if paired and by_head <= by_tile else tiles_to_queries
    return plan(q_pre, k_pre, values, out_grad, q_gain, k_gain, selected)


def solution(mesh):
    placed = (
        P("ctx", "head"),
        P("ctx", "head"),
        P("ctx", "head"),
        P("ctx", "head"),
        P("head"),
        P("head"),
        P("ctx", "head", None),
    )
    return jax.shard_map(
        on_device,
        mesh=mesh,
        in_specs=placed,
        out_specs=(P("ctx", "head"), P("ctx", "head"), P("ctx", "head")),
        check_vma=False,
    )
```

```python
import functools
import math

import jax
import jax.numpy as jnp
from jax import lax
from jax.experimental import pallas as pl
from jax.experimental.pallas import tpu as pltpu
from jax.sharding import PartitionSpec as P

HD = 128
TILE = 128


epsilon = 1e-06


def split_heads(array, heads_dev):
    return array.reshape(array.shape[0], heads_dev, HD).transpose(1, 0, 2)


def merge_heads(array):
    heads_dev, tok_dev, depth = array.shape
    return array.transpose(1, 0, 2).reshape(tok_dev, heads_dev * depth)


def per_tile(array, qt_dev):
    heads_dev, tok_dev, depth = array.shape
    return array.reshape(heads_dev, qt_dev, TILE, depth).transpose(1, 0, 2, 3)


def from_tiles(array):
    qt_dev, heads_dev, rows_tile, depth = array.shape
    return array.transpose(1, 0, 2, 3).reshape(heads_dev, qt_dev * rows_tile, depth)


def table_sum(taken, pieces, heads_dev, qt_dev):
    flat_pieces = pieces.reshape(pieces.shape[0], -1)
    summed = jnp.dot(
        taken, flat_pieces, precision=lax.Precision.HIGHEST, preferred_element_type=jnp.float32
    )
    summed = summed.reshape(heads_dev, qt_dev, 2, TILE, HD).transpose(2, 0, 1, 3, 4)
    return summed.reshape(2, heads_dev, qt_dev * TILE, HD)


def rounded(array):
    return array.astype(jnp.bfloat16)


def finish_norm(wide, scale, gain, grad, dot_sum, width_all):
    return (scale * gain * grad - wide * scale**3 * (dot_sum / width_all)[:, None]).astype(
        jnp.bfloat16
    )


def tiles_to_queries(q_pre, k_pre, values, out_grad, q_gain, k_gain, selected):
    n_ctx = lax.axis_size("ctx")
    tok_dev, width_dev = q_pre.shape
    width_all = width_dev * lax.axis_size("head")
    heads_dev = width_dev // HD
    qt_dev = tok_dev // TILE
    remote_count = selected.shape[2]
    factor = 1.0 / math.sqrt(HD)
    q_wide = q_pre.astype(jnp.float32)
    k_wide = k_pre.astype(jnp.float32)
    q_square, k_square = lax.psum(
        (jnp.sum(q_wide * q_wide, axis=1), jnp.sum(k_wide * k_wide, axis=1)), "head"
    )
    q_scale = lax.rsqrt(q_square / width_all + epsilon)[:, None]
    k_scale = lax.rsqrt(k_square / width_all + epsilon)[:, None]
    q_heads = split_heads(rounded(q_wide * q_scale * q_gain), heads_dev)
    k_heads = split_heads(rounded(k_wide * k_scale * k_gain), heads_dev)
    v_heads = split_heads(values, heads_dev)
    g_heads = split_heads(out_grad, heads_dev)
    q_tiles = per_tile(q_heads, qt_dev)
    g_tiles = per_tile(g_heads, qt_dev)
    k_table = k_heads.reshape(heads_dev * qt_dev, TILE, HD)
    v_table = v_heads.reshape(heads_dev * qt_dev, TILE, HD)
    flat_sel = selected[0].reshape(-1)
    n_slot = flat_sel.shape[0]
    capacity = -(-n_slot // (n_ctx - 1))
    n_buffer = n_ctx * capacity
    owners = flat_sel // qt_dev
    head_of = jnp.arange(n_slot, dtype=jnp.int32) // remote_count
    codes = head_of * qt_dev + flat_sel % qt_dev
    matches = (owners[:, None] == jnp.arange(n_ctx, dtype=jnp.int32)[None, :]).astype(jnp.int32)
    ranks = jnp.sum((jnp.cumsum(matches, axis=0) - matches) * matches, axis=1)
    position = owners * capacity + ranks
    placed = position[None, :] == jnp.arange(n_buffer, dtype=jnp.int32)[:, None]
    request = jnp.sum(jnp.where(placed, codes[None, :] + 1, 0), axis=1) - 1
    asked = lax.all_to_all(
        request.reshape(n_ctx, capacity), "ctx", split_axis=0, concat_axis=0, tiled=True
    ).reshape(n_buffer)
    clipped = jnp.maximum(asked, 0)
    taken = (asked[None, :] == jnp.arange(heads_dev * qt_dev, dtype=jnp.int32)[:, None]).astype(
        jnp.float32
    )
    s_near = (
        jnp.einsum("rhqd,hkd->rhqk", q_tiles, k_heads, preferred_element_type=jnp.float32) * factor
    )
    dp_near = jnp.einsum("rhqd,hkd->rhqk", g_tiles, v_heads, preferred_element_type=jnp.float32)
    near_top = jnp.max(s_near, axis=-1)
    outgoing = jnp.stack((k_table[clipped], v_table[clipped]), axis=1).reshape(
        n_ctx, capacity, 2, TILE, HD
    )
    incoming = lax.all_to_all(outgoing, "ctx", split_axis=0, concat_axis=0, tiled=True).reshape(
        n_buffer, 2, TILE, HD
    )
    slot_kv = incoming[position].reshape(heads_dev, remote_count, 2, TILE, HD)
    far_k = slot_kv[:, :, 0]
    far_v = slot_kv[:, :, 1]
    s_far = (
        jnp.einsum("rhqd,hckd->rhqck", q_tiles, far_k, preferred_element_type=jnp.float32) * factor
    )
    dp_far = jnp.einsum("rhqd,hckd->rhqck", g_tiles, far_v, preferred_element_type=jnp.float32)
    row_top = jnp.maximum(near_top, jnp.max(s_far, axis=(-2, -1)))
    totals = jnp.sum(jnp.exp(s_near - row_top[..., None]), axis=-1) + jnp.sum(
        jnp.exp(s_far - row_top[..., None, None]), axis=(-2, -1)
    )
    lse = row_top + jnp.log(totals)
    p_near = jnp.exp(s_near - lse[..., None])
    p_far = jnp.exp(s_far - lse[..., None, None])
    delta = jnp.sum(p_near * dp_near, axis=-1) + jnp.sum(p_far * dp_far, axis=(-2, -1))
    ds_near = rounded(p_near * (dp_near - delta[..., None]) * factor)
    pb_near = rounded(p_near)
    dq_near = jnp.einsum("rhqk,hkd->rhqd", ds_near, k_heads, preferred_element_type=jnp.float32)
    dk_near = jnp.einsum("rhqk,rhqd->hkd", ds_near, q_tiles, preferred_element_type=jnp.float32)
    dv_near = jnp.einsum("rhqk,rhqd->hkd", pb_near, g_tiles, preferred_element_type=jnp.float32)
    dq_near, dk_near, dv_near = (dq_near, dk_near, dv_near)
    ds_far = rounded(p_far * (dp_far - delta[..., None, None]) * factor)
    pb_far = rounded(p_far)
    dq_far = jnp.einsum("rhqck,hckd->rhqd", ds_far, far_k, preferred_element_type=jnp.float32)
    dq_wide = merge_heads(from_tiles(dq_near + dq_far))
    q_dot = jnp.sum(q_gain * dq_wide * q_wide, axis=1)
    dq_wide, q_dot = (dq_wide, q_dot)
    dk_far = jnp.einsum("rhqck,rhqd->hckd", ds_far, q_tiles, preferred_element_type=jnp.float32)
    dv_far = jnp.einsum("rhqck,rhqd->hckd", pb_far, g_tiles, preferred_element_type=jnp.float32)
    grads = jnp.stack((dk_far, dv_far), axis=2).reshape(n_slot, 2, TILE, HD)
    sending = jnp.zeros((n_buffer, 2, TILE, HD), jnp.float32).at[position].set(grads)
    returned = lax.all_to_all(
        sending.reshape(n_ctx, capacity, 2, TILE, HD),
        "ctx",
        split_axis=0,
        concat_axis=0,
        tiled=True,
    ).reshape(n_buffer, 2, TILE, HD)
    far_sums = table_sum(taken, returned, heads_dev, qt_dev)
    dk_wide = merge_heads(dk_near + far_sums[0])
    dv_heads = dv_near + far_sums[1]
    k_dot = jnp.sum(k_gain * dk_wide * k_wide, axis=1)
    q_dot, k_dot = lax.psum((q_dot, k_dot), "head")
    dq_result = finish_norm(q_wide, q_scale, q_gain, dq_wide, q_dot, width_all)
    dk_result = finish_norm(k_wide, k_scale, k_gain, dk_wide, k_dot, width_all)
    return (dq_result, dk_result, merge_heads(dv_heads).astype(jnp.bfloat16))


VMEM_BYTES = 48 * 2**20
PIECES = 4
STRIP = 64
IN_VMEM = pl.BlockSpec(memory_space=pltpu.VMEM)
IN_SMEM = pl.BlockSpec(memory_space=pltpu.SMEM)


def owners_of(group, n_ctx, heads_dev):
    places = [(4 * head + 1) * n_ctx // (4 * heads_dev) for head in range(heads_dev)]
    return [n_ctx - 1 - place if group % 2 else place for place in places]


def head_at(place, group, n_ctx, heads_dev):
    even = jnp.where(group % 2 == 1, n_ctx - 1 - place, place)
    head = -1
    for index, owner in enumerate(owners_of(0, n_ctx, heads_dev)):
        head = jnp.where(even == owner, index, head)
    return head


def pairs_to_owner(mask, n_ctx, n_head, heads_dev):
    pairs = []
    for group in range(n_head):
        owners = owners_of(group, n_ctx, heads_dev)
        for block in range(n_ctx):
            if block ^ mask in owners:
                pairs.append((block * n_head + group, (block ^ mask) * n_head + group))
    return pairs


def there_masks(n_ctx):
    return list(range(n_ctx - 1, 2, -1)) + [1, 2, 0]


def back_masks(n_ctx):
    half = n_ctx // 2
    far = list(range(n_ctx - 1, half + 1, -1)) + [half, half + 1]
    return list(range(half - 1, 0, -1)) + far + [0]


def move(masks, arrays, back, n_ctx, n_head, heads_dev):
    moved = []
    for mask, array in zip(masks, arrays):
        pairs = pairs_to_owner(mask, n_ctx, n_head, heads_dev)
        if back:
            pairs = [(b, a) for a, b in pairs]
        moved.append(lax.ppermute(array, ("ctx", "head"), pairs) if mask else array)
    return moved


def column(row, width):
    return jnp.broadcast_to(row, (width, row.shape[1])).T


def row_sums(wide):
    total = wide[:, :HD]
    for at in range(HD, wide.shape[1], HD):
        total = total + wide[:, at : at + HD]
    return jnp.sum(total.T, axis=0, keepdims=True)


def pack_kernel(n_ctx, heads_dev, *refs):
    inputs, square_ref, outs = refs[:4], refs[4], refs[5 : 5 + n_ctx]
    held, sems = refs[5 + n_ctx :]
    rows = held.shape[1]
    piece = rows // PIECES
    block, group = lax.axis_index("ctx"), lax.axis_index("head")

    def copy(at, part):
        place = pl.ds(part * piece, piece)
        return pltpu.make_async_copy(
            inputs[at].at[place, :], held.at[at, place, :], sems.at[at, part]
        )

    for at in range(4):
        for part in range(PIECES):
            copy(at, part).start()
    for at in range(4):
        for part in range(PIECES):
            copy(at, part).wait()
    for mask, out in zip(there_masks(n_ctx), outs):
        head = head_at(block ^ mask, group, n_ctx, heads_dev)

        @pl.when(head >= 0)
        def _(head=head, out=out):
            place = pl.ds(pl.multiple_of(head * HD, HD), HD)
            for at in range(4):
                out[at] = held[at, :, place]

    for at in range(2):
        wide = held[at].astype(jnp.float32)
        square_ref[at : at + 1, :] = row_sums(wide * wide)


def pack(arrays, n_ctx):
    rows, width_dev = arrays[0].shape
    result = pl.pallas_call(
        functools.partial(pack_kernel, n_ctx, width_dev // HD),
        out_shape=[jax.ShapeDtypeStruct((2, rows), jnp.float32)]
        + [jax.ShapeDtypeStruct((4, rows, HD), jnp.bfloat16)] * n_ctx,
        in_specs=[pl.BlockSpec(memory_space=pltpu.HBM)] * 4,
        out_specs=[IN_VMEM] * (n_ctx + 1),
        scratch_shapes=[
            pltpu.VMEM((4, rows, width_dev), jnp.bfloat16),
            pltpu.SemaphoreType.DMA((4, PIECES)),
        ],
        compiler_params=pltpu.CompilerParams(vmem_limit_bytes=VMEM_BYTES),
    )(*[pltpu.with_memory_space_constraint(array, pltpu.HBM) for array in arrays])
    return result[0], result[1:]


def attend_kernel(n_ctx, heads_dev, picks, scale_ref, q_gain, k_gain, *refs):
    messages = dict(zip(there_masks(n_ctx), refs[:n_ctx]))
    outs = dict(zip(back_masks(n_ctx), refs[n_ctx : 2 * n_ctx]))
    scratch = refs[2 * n_ctx :]
    q_ref, qt_ref, g_ref, gt_ref, k_ref, kt_ref, v_ref = scratch[:7]
    dq_ref, dk_ref, dv_ref, kt_picked, k_picked, v_picked = scratch[7:13]
    buffers = (scratch[13:18], scratch[18:23])
    rows = messages[0].shape[1]
    remote_count = picks.shape[1]
    near = rows // TILE
    n_keys = near + remote_count
    n_strips = n_keys * TILE // STRIP
    factor = 1.0 / math.sqrt(HD)
    to_base2 = factor * math.log2(math.e)
    own_block = lax.axis_index("ctx")
    own_head = head_at(own_block, lax.axis_index("head"), n_ctx, heads_dev)

    def rows_of(block):
        return pl.ds(pl.multiple_of(block * rows, rows), rows)

    def places_of(block):
        return [
            pl.ds(pl.multiple_of(block * rows + tile * TILE, TILE), TILE) for tile in range(near)
        ] + [
            pl.ds(pl.multiple_of(picks[block, slot] * TILE, TILE), TILE)
            for slot in range(remote_count)
        ]

    def prepare(mask, q_factor, k_factor):
        message = messages[mask]
        block = own_block ^ mask
        place = rows_of(block)
        q_t = message[0].T.astype(jnp.float32) * scale_ref[block, 0:1, :] * q_factor
        k_t = message[1].T.astype(jnp.float32) * scale_ref[block, 1:2, :] * k_factor
        qt_ref[mask] = q_t.astype(jnp.bfloat16)
        kt_ref[:, place] = k_t.astype(jnp.bfloat16)
        q_ref[mask] = q_t.astype(jnp.bfloat16).T
        k_ref[place, :] = k_t.astype(jnp.bfloat16).T
        v_ref[place, :] = message[2]
        g_ref[mask] = message[3]
        gt_ref[mask] = message[3].T

    def tiles(first, count=1):
        return slice(first * TILE, (first + count) * TILE)

    def scores(mask, group, places, buffer):
        weight_ref, dprob_ref, stat_ref = buffer[:3]
        for slot in group:
            k_picked[tiles(slot), :] = k_ref[places[slot], :]
            v_picked[tiles(slot), :] = v_ref[places[slot], :]
        picked = tiles(group[0], len(group))
        score_all = jnp.dot(
            k_picked[picked, :], qt_ref[mask], preferred_element_type=jnp.float32
        )
        dprob_all = jnp.dot(
            v_picked[picked, :], gt_ref[mask], preferred_element_type=jnp.float32
        )
        for at in range(len(group) * TILE // STRIP):
            strip = group[0] * TILE // STRIP + at
            part = slice(at * STRIP, (at + 1) * STRIP)
            score = score_all[part, :]
            dprob = dprob_all[part, :]
            top = jnp.max(score, axis=0, keepdims=True)
            weight = jnp.exp2((score - top) * to_base2)
            weight_ref[strip] = weight
            dprob_ref[strip] = dprob
            stat_ref[0, strip : strip + 1, :] = top * to_base2
            stat_ref[1, strip : strip + 1, :] = jnp.sum(weight, axis=0, keepdims=True)
            stat_ref[2, strip : strip + 1, :] = jnp.sum(weight * dprob, axis=0, keepdims=True)

    def settle(buffer):
        stat_ref = buffer[2]
        tops = stat_ref[0, :n_strips, :]
        shares = jnp.exp2(tops - jnp.max(tops, axis=0, keepdims=True))
        total = jnp.sum(shares * stat_ref[1, :n_strips, :], axis=0, keepdims=True)
        mixed = jnp.sum(shares * stat_ref[2, :n_strips, :], axis=0, keepdims=True)
        inverse = 1.0 / total
        return shares * inverse, mixed * inverse

    def gradients(group, buffer, shares, delta):
        weight_ref, dprob_ref, _, ds_ref, pb_ref = buffer
        for strip in range(group[0] * TILE // STRIP, (group[-1] + 1) * TILE // STRIP):
            part = slice(strip * STRIP, (strip + 1) * STRIP)
            prob = weight_ref[strip] * shares[strip : strip + 1, :]
            pb_ref[part, :] = prob.astype(jnp.bfloat16)
            ds_ref[part, :] = (prob * (dprob_ref[strip] - delta)).astype(jnp.bfloat16)

    def products(mask, group, places, buffer):
        ds_ref, pb_ref = buffer[3:]
        picked = tiles(group[0], len(group))
        dk = jnp.dot(ds_ref[picked, :], q_ref[mask], preferred_element_type=jnp.float32)
        dv = jnp.dot(pb_ref[picked, :], g_ref[mask], preferred_element_type=jnp.float32)
        for at, slot in enumerate(group):
            dk_ref[places[slot], :] += dk[tiles(at), :]
            dv_ref[places[slot], :] += dv[tiles(at), :]
            kt_picked[:, tiles(slot)] = kt_ref[:, places[slot]]

    def query_gradient(mask, buffer):
        dq_t = jnp.dot(kt_picked[...], buffer[3][...], preferred_element_type=jnp.float32)
        dq_ref[mask] = (dq_t * factor).astype(jnp.bfloat16).T

    groups = [range(first, min(first + 3, n_keys)) for first in range(0, n_keys, 3)]

    def step(now, before, after):
        if now is not None:
            shares, delta = settle(now[1])
        if before is not None:
            before_places = places_of(own_block ^ before[0])
        if after is not None:
            after_places = places_of(own_block ^ after[0])
        for group in groups:
            if before is not None:
                products(before[0], group, before_places, before[1])
            if now is not None:
                gradients(group, now[1], shares, delta)
            if after is not None:
                scores(after[0], group, after_places, after[1])
        if before is not None:
            query_gradient(*before)

    @pl.when(own_head >= 0)
    def _():
        q_factor = column(q_gain[pl.ds(own_head, 1), :], rows)
        k_factor = column(k_gain[pl.ds(own_head, 1), :], rows)
        for mask in range(n_ctx):
            prepare(mask, q_factor, k_factor)
        dk_ref[...] = jnp.zeros_like(dk_ref)
        dv_ref[...] = jnp.zeros_like(dv_ref)
        even, odd = buffers
        step(None, None, (0, even))
        step((0, even), None, (1, odd))

        def two(pair, carry):
            mask = 2 * pair
            step((mask + 1, odd), (mask, even), (mask + 2, even))
            step((mask + 2, even), (mask + 1, odd), (mask + 3, odd))
            return carry

        lax.fori_loop(0, n_ctx // 2 - 1, two, 0)
        step((n_ctx - 1, odd), (n_ctx - 2, even), None)
        step(None, (n_ctx - 1, odd), None)
        for mask in range(n_ctx):
            place = rows_of(own_block ^ mask)
            outs[mask][0] = dq_ref[mask]
            outs[mask][1] = (dk_ref[place, :] * factor).astype(jnp.bfloat16)
            outs[mask][2] = dv_ref[place, :].astype(jnp.bfloat16)


def attend(picks, scales, q_gain, k_gain, messages, n_ctx):
    rows = messages[0].shape[1]
    tokens = n_ctx * rows
    n_keys = rows // TILE + picks.shape[1]
    n_strips = n_keys * TILE // STRIP
    by_block = pltpu.VMEM((n_ctx, rows, HD), jnp.bfloat16)
    by_block_t = pltpu.VMEM((n_ctx, HD, rows), jnp.bfloat16)
    buffer = [
        pltpu.VMEM((n_strips, STRIP, rows), jnp.float32),
        pltpu.VMEM((n_strips, STRIP, rows), jnp.float32),
        pltpu.VMEM((3, -(-n_strips // 8) * 8, rows), jnp.float32),
        pltpu.VMEM((n_keys * TILE, rows), jnp.bfloat16),
        pltpu.VMEM((n_keys * TILE, rows), jnp.bfloat16),
    ]
    return pl.pallas_call(
        functools.partial(attend_kernel, n_ctx, q_gain.shape[0]),
        out_shape=[jax.ShapeDtypeStruct((3, rows, HD), jnp.bfloat16)] * n_ctx,
        in_specs=[IN_SMEM] + [IN_VMEM] * (3 + n_ctx),
        out_specs=[IN_VMEM] * n_ctx,
        scratch_shapes=[
            by_block,
            by_block_t,
            by_block,
            by_block_t,
            pltpu.VMEM((tokens, HD), jnp.bfloat16),
            pltpu.VMEM((HD, tokens), jnp.bfloat16),
            pltpu.VMEM((tokens, HD), jnp.bfloat16),
            by_block,
            pltpu.VMEM((tokens, HD), jnp.float32),
            pltpu.VMEM((tokens, HD), jnp.float32),
            pltpu.VMEM((HD, n_keys * TILE), jnp.bfloat16),
            pltpu.VMEM((n_keys * TILE, HD), jnp.bfloat16),
            pltpu.VMEM((n_keys * TILE, HD), jnp.bfloat16),
        ]
        + buffer
        + buffer,
        compiler_params=pltpu.CompilerParams(vmem_limit_bytes=VMEM_BYTES),
    )(picks, scales, q_gain, k_gain, *messages)


def gather_kernel(n_ctx, heads_dev, q_ref, k_ref, q_gain, k_gain, *refs):
    slots = refs[:n_ctx]
    dot_ref, dq_ref, dk_ref, dv_out, dv_ref, sems = refs[n_ctx:]
    piece = dv_ref.shape[0] // PIECES
    block, group = lax.axis_index("ctx"), lax.axis_index("head")

    def spread(at, out):
        for mask, slot in zip(back_masks(n_ctx), slots):
            head = head_at(block ^ mask, group, n_ctx, heads_dev)

            @pl.when(head >= 0)
            def _(head=head, slot=slot):
                place = pl.ds(pl.multiple_of(head * HD, HD), HD)
                out[:, place] = slot[at]

    spread(2, dv_ref)
    places = [pl.ds(part * piece, piece) for part in range(PIECES)]
    copies = [
        pltpu.make_async_copy(dv_ref.at[place, :], dv_out.at[place, :], sems.at[part])
        for part, place in enumerate(places)
    ]
    for copy in copies:
        copy.start()
    for at, (wide_ref, pre_ref, gain) in enumerate(
        ((dq_ref, q_ref, q_gain), (dk_ref, k_ref, k_gain))
    ):
        spread(at, wide_ref)
        terms = gain[...] * wide_ref[...].astype(jnp.float32) * pre_ref[...].astype(jnp.float32)
        dot_ref[at : at + 1, :] = row_sums(terms)
    for copy in copies:
        copy.wait()


def finish_kernel(width_all, q_ref, k_ref, q_gain, k_gain, scale_ref, dot_ref, *refs):
    dq_ref, dk_ref, dq_out, dk_out, held, sems = refs
    piece = q_ref.shape[0] // PIECES
    scales = scale_ref[lax.axis_index("ctx")]
    backs = scales**3 * (dot_ref[...] / width_all)
    copies = []
    for at, (pre_ref, gain, grad_ref, out) in enumerate(
        ((q_ref, q_gain, dq_ref, dq_out), (k_ref, k_gain, dk_ref, dk_out))
    ):
        scale_all = column(scales[at : at + 1, :], HD)
        back_all = column(backs[at : at + 1, :], HD)
        for part in range(PIECES):
            rows = slice(part * piece, (part + 1) * piece)
            scale, back = scale_all[rows, :], back_all[rows, :]
            for first in range(0, pre_ref.shape[1], HD):
                place = slice(first, first + HD)
                wide = pre_ref[rows, place].astype(jnp.float32)
                grad = grad_ref[rows, place].astype(jnp.float32)
                result = scale * gain[:, place] * grad - wide * back
                held[at, rows, place] = result.astype(jnp.bfloat16)
            copies.append(
                pltpu.make_async_copy(held.at[at, rows, :], out.at[rows, :], sems.at[at, part])
            )
            copies[-1].start()
    for copy in copies:
        copy.wait()


def heads_to_owners(q_pre, k_pre, values, out_grad, q_gain, k_gain, selected):
    n_ctx = lax.axis_size("ctx")
    n_head = lax.axis_size("head")
    rows, width_dev = q_pre.shape
    width_all = width_dev * n_head
    heads_dev = width_dev // HD
    remote_count = selected.shape[2]
    sizes = (n_ctx, n_head, heads_dev)
    params = pltpu.CompilerParams(vmem_limit_bytes=VMEM_BYTES)

    by_row = jax.ShapeDtypeStruct((2, rows), jnp.float32)
    wide = jax.ShapeDtypeStruct((rows, width_dev), jnp.bfloat16)

    squares, sent = pack((q_pre, k_pre, values, out_grad), n_ctx)
    messages = move(there_masks(n_ctx), sent, False, *sizes)

    wishes = selected[0].reshape(1, -1).astype(jnp.float32)
    wishes = jnp.pad(wishes, ((0, 0), (0, rows - wishes.shape[1])))
    small = jnp.concatenate((lax.psum(squares, "head"), wishes), axis=0)
    small = jnp.broadcast_to(small[None], (n_ctx,) + small.shape)
    small = lax.all_to_all(small, "ctx", split_axis=0, concat_axis=0, tiled=True)
    scales = lax.rsqrt(small[:, :2] / width_all + epsilon)
    own_head = head_at(lax.axis_index("ctx"), lax.axis_index("head"), n_ctx, heads_dev)
    first = jnp.maximum(own_head, 0) * remote_count
    picks = lax.dynamic_slice_in_dim(small[:, 2], first, remote_count, 1).astype(jnp.int32)

    q_gains = q_gain.reshape(heads_dev, HD)
    k_gains = k_gain.reshape(heads_dev, HD)
    results = attend(picks, scales, q_gains, k_gains, messages, n_ctx)
    slots = move(back_masks(n_ctx), results, True, *sizes)

    pres = (q_pre, k_pre, q_gain[None], k_gain[None])
    dots, dq_wide, dk_wide, dv = pl.pallas_call(
        functools.partial(gather_kernel, n_ctx, heads_dev),
        out_shape=[by_row, wide, wide, wide],
        in_specs=[IN_VMEM] * (4 + n_ctx),
        out_specs=[IN_VMEM] * 3 + [pl.BlockSpec(memory_space=pltpu.HBM)],
        scratch_shapes=[
            pltpu.VMEM((rows, width_dev), jnp.bfloat16),
            pltpu.SemaphoreType.DMA((PIECES,)),
        ],
        compiler_params=params,
    )(*pres, *slots)
    dots = lax.psum(dots, "head")
    dq, dk = pl.pallas_call(
        functools.partial(finish_kernel, width_all),
        out_shape=[wide, wide],
        in_specs=[IN_VMEM] * 8,
        out_specs=[pl.BlockSpec(memory_space=pltpu.HBM)] * 2,
        scratch_shapes=[
            pltpu.VMEM((2, rows, width_dev), jnp.bfloat16),
            pltpu.SemaphoreType.DMA((2, PIECES)),
        ],
        compiler_params=params,
    )(*pres, scales, dots, dq_wide, dk_wide)
    return dq, dk, dv


def on_device(q_pre, k_pre, values, out_grad, q_gain, k_gain, selected):
    n_ctx = lax.axis_size("ctx")
    tiles_dev, heads_dev, remote_count = selected.shape
    capacity = -(-heads_dev * remote_count // (n_ctx - 1))
    by_head = (n_ctx - 1) * tiles_dev * 7
    by_tile = (n_ctx - 1) * capacity * 6
    paired = n_ctx & (n_ctx - 1) == 0 and n_ctx >= max(heads_dev, 4)
    plan = heads_to_owners if paired and by_head <= by_tile else tiles_to_queries
    return plan(q_pre, k_pre, values, out_grad, q_gain, k_gain, selected)


def solution(mesh):
    placed = (
        P("ctx", "head"),
        P("ctx", "head"),
        P("ctx", "head"),
        P("ctx", "head"),
        P("head"),
        P("head"),
        P("ctx", "head", None),
    )
    return jax.shard_map(
        on_device,
        mesh=mesh,
        in_specs=placed,
        out_specs=(P("ctx", "head"), P("ctx", "head"), P("ctx", "head")),
        check_vma=False,
    )
```
